256 devices in a mesh: tower: 2 (over core), shard: 128 (over x, y, z).
Axes of the slice: x: 4, y: 4, z: 8, core: 2. Of those that a mesh axis runs over, the one named last changes fastest.
Arguments:
- history: int32 [1024, 64], P(('tower', 'shard')), may hold values from 0 to 65663, as said below
- item_ids: int32 [1024], P(('tower', 'shard')), may hold values from 0 to 65663, as said below
- hot_table: float32 [128, 256], replicated, may hold values from -6 to 6
- rare_table: float32 [65536, 256], P('shard'), may hold values from -6 to 6
- in_proj: bfloat16 [256, 1024], replicated, may hold values from -0.375 to 0.375
- pos_embed: bfloat16 [64, 1024], replicated, may hold values from -3 to 3
- norm_gain: float32 [1024], replicated, may hold values from 0.5 to 1.5
- w_query: bfloat16 [1024, 1024], replicated, may hold values from -0.1875 to 0.1875
- w_key: bfloat16 [1024, 1024], replicated, may hold values from -0.1875 to 0.1875
- w_value: bfloat16 [1024, 1024], replicated, may hold values from -0.1875 to 0.1875
- w_out: bfloat16 [1024, 1024], replicated, may hold values from -0.1875 to 0.1875
- out_gain: float32 [1024], replicated, may hold values from 0.5 to 1.5
- item_w1: bfloat16 [256, 1024], replicated, may hold values from -0.375 to 0.375
- item_w2: bfloat16 [1024, 1024], replicated, may hold values from -0.1875 to 0.1875
- item_gain: float32 [1024], replicated, may hold values from 0.5 to 1.5
Outputs:
- grad_hot: float32 [128, 256], replicated
- grad_rare: float32 [65536, 256], P('shard')
- loss: float32 [], replicated
The draws below stay inside these ranges and needn't reach their ends.
Inputs may be any that keep to these rules, and one draw needn't show every extreme that they name: An id below 128 names hot row id; another id i names rare row i - 128, held by shard index (i - 128) // 512. Among the history and item ids of one device's 4 users (aligned blocks) at most 5 rare ids fall on one shard index, and exactly 5 on one. `item_ids`: same rule as history, counted together with it.
All inputs are finite; a program needn't handle non-finite values.
Results may differ from the reference program's by a relative error of at most 0.019.
Values may be sent and summed in bfloat16 or wider, within the bound.
No kernel may reach another device: no remote copies, remote signals or barrier semaphores. Data moves between devices by JAX's collectives and lax.ppermute only.
A program may use at most 128 MiB of HBM per device.

```python
import math
import jax
import jax.numpy as jnp
from jax import lax

D = 1024
EMB = 256
HEAD_DIM = 64
HIST = 64
B_DEV = 4
HOT = 128
RARE_DEV = 512
CAP = 5
OWNERS = 128
USERS = 1024
RARE_ROWS = 65536


def draw_lookups(key):
    blocks = USERS // B_DEV
    span = B_DEV * (HIST + 1)

    def one_block(block_key):
        keys = jax.random.split(block_key, 6)
        first = jax.random.randint(keys[0], (), 0, OWNERS)
        others = (first + 1 + jnp.arange(OWNERS - 1)) % OWNERS
        shuffled = jax.random.permutation(keys[1], jnp.repeat(others, CAP))
        owner = jnp.concatenate([jnp.full((CAP,), first), shuffled])[:span]
        rare = (jnp.arange(span) < CAP) | (jax.random.randint(keys[2], (span,), 0, 4) > 0)
        local_row = jax.random.randint(keys[3], (span,), 0, RARE_DEV)
        hot_id = jax.random.randint(keys[4], (span,), 0, HOT)
        ids = jnp.where(rare, HOT + owner * RARE_DEV + local_row, hot_id)
        return ids[jax.random.permutation(keys[5], span)]
    return jax.vmap(one_block)(jax.random.split(key, blocks)).astype(jnp.int32)


def draw_history(key, part):
    ids = draw_lookups(key)
    return ids[:, :B_DEV * HIST].reshape(USERS, HIST)


def draw_item_ids(key, part):
    ids = draw_lookups(key)
    return ids[:, B_DEV * HIST:].reshape(USERS)


def block_scale(own_key, dims, pieces, low, largest):
    level = 1.0
    for position, blocks in pieces:
        steps = jax.random.uniform(jax.random.fold_in(jax.random.fold_in(own_key, 6), position), (blocks,), jnp.float32, low / len(pieces), largest / len(pieces))
        level = level * jnp.repeat(jnp.exp(steps), dims[position] // blocks).reshape((-1,) + (1,) * (len(dims) - 1 - position))
    return level


def gaussian(stream_key, extent, deviation, most, pieces=(), held_as=jnp.bfloat16):
    level = block_scale(stream_key, extent, pieces, -0.22, 0.18) if pieces else 1.0
    array = jax.random.normal(stream_key, extent, jnp.float32) * deviation * level
    return jnp.minimum(jnp.maximum(array, -most), most).astype(held_as)


def setup_inputs(seed: int = 0) -> dict:
    streams_of = jax.random.split(jax.random.key(seed), 16)
    return {
        "history": draw_history(jax.random.fold_in(streams_of[15], 71), 0),
        "item_ids": draw_item_ids(jax.random.fold_in(streams_of[15], 71), 0),
        "hot_table": gaussian(streams_of[2], (HOT, EMB), 1.0, 6.0, (), jnp.float32),
        "rare_table": gaussian(streams_of[3], (RARE_ROWS, EMB), 1.0, 6.0, ((0, 128),), jnp.float32),
        "in_proj": gaussian(streams_of[4], (EMB, D), EMB ** -0.5, 0.375),
        "pos_embed": gaussian(streams_of[5], (HIST, D), 0.5, 3.0),
        "norm_gain": jnp.clip(1.0 + 0.1 * jax.random.normal(streams_of[6], (D,), jnp.float32), 0.5, 1.5),
        "w_query": gaussian(streams_of[7], (D, D), D ** -0.5, 0.1875),
        "w_key": gaussian(streams_of[8], (D, D), D ** -0.5, 0.1875),
        "w_value": gaussian(streams_of[9], (D, D), D ** -0.5, 0.1875),
        "w_out": gaussian(streams_of[10], (D, D), D ** -0.5, 0.1875),
        "out_gain": jnp.clip(1.0 + 0.1 * jax.random.normal(streams_of[11], (D,), jnp.float32), 0.5, 1.5),
        "item_w1": gaussian(streams_of[12], (EMB, D), EMB ** -0.5, 0.375),
        "item_w2": gaussian(streams_of[13], (D, D), D ** -0.5, 0.1875),
        "item_gain": jnp.clip(1.0 + 0.1 * jax.random.normal(streams_of[14], (D,), jnp.float32), 0.5, 1.5),
    }


EPS = 1e-06

def rms_scale(values, gain):
    return values * lax.rsqrt(lax.optimization_barrier(jnp.mean(values * values, axis=-1, keepdims=True)) + EPS) * gain

def user_tower(rows, in_proj, pos_embed, norm_gain, w_query, w_key, w_value, w_out, out_gain):
    users, hist, emb = rows.shape
    width = in_proj.shape[1]
    heads = width // HEAD_DIM
    flat = rows.reshape(users * hist, emb).astype(jnp.bfloat16)
    hidden = jnp.dot(flat, in_proj, preferred_element_type=jnp.float32).reshape(users, hist, width)
    hidden = hidden + pos_embed.astype(jnp.float32)[None]
    normed = rms_scale(hidden, norm_gain).astype(jnp.bfloat16)
    flat_normed = normed.reshape(users * hist, width)
    keys = jnp.dot(flat_normed, w_key, preferred_element_type=jnp.float32).astype(jnp.bfloat16)
    keys = keys.reshape(users, hist, heads, HEAD_DIM)
    values = jnp.dot(flat_normed, w_value, preferred_element_type=jnp.float32).astype(jnp.bfloat16)
    values = values.reshape(users, hist, heads, HEAD_DIM)
    query = jnp.dot(normed[:, -1], w_query, preferred_element_type=jnp.float32).astype(jnp.bfloat16)
    query = query.reshape(users, heads, HEAD_DIM)
    scores = jnp.einsum('uhd,ushd->uhs', query, keys, preferred_element_type=jnp.float32) / math.sqrt(HEAD_DIM)
    weights = jax.nn.softmax(scores, axis=-1).astype(jnp.bfloat16)
    attended = jnp.einsum('uhs,ushd->uhd', weights, values, preferred_element_type=jnp.float32)
    attended = attended.astype(jnp.bfloat16).reshape(users, width)
    mixed = hidden[:, -1] + jnp.dot(attended, w_out, preferred_element_type=jnp.float32)
    return rms_scale(mixed, out_gain).astype(jnp.bfloat16)

def item_tower(rows, item_w1, item_w2, item_gain):
    inner = jax.nn.silu(jnp.dot(rows.astype(jnp.bfloat16), item_w1, preferred_element_type=jnp.float32))
    outer = jnp.dot(inner.astype(jnp.bfloat16), item_w2, preferred_element_type=jnp.float32)
    return rms_scale(outer, item_gain).astype(jnp.bfloat16)

def lookup(ids, hot_table, rare_table):
    hot_count = hot_table.shape[0]
    is_rare = ids >= hot_count
    rare_rows = rare_table[jnp.where(is_rare, ids - hot_count, 0)]
    hot_rows = hot_table[jnp.where(is_rare, 0, ids)]
    return jnp.where(is_rare[..., None], rare_rows, hot_rows)

def add_rows(grad_hot, grad_rare, ids, grads):
    hot_count = grad_hot.shape[0]
    rare_count = grad_rare.shape[0]
    is_rare = ids >= hot_count
    grad_hot = grad_hot.at[jnp.where(is_rare, hot_count, ids)].add(grads, mode='drop')
    grad_rare = grad_rare.at[jnp.where(is_rare, ids - hot_count, rare_count)].add(grads, mode='drop')
    return (grad_hot, grad_rare)

def reference(history, item_ids, hot_table, rare_table, in_proj, pos_embed, norm_gain, w_query, w_key, w_value, w_out, out_gain, item_w1, item_w2, item_gain):
    users = history.shape[0]
    blocks = users // B_DEV
    width = in_proj.shape[1]
    scale = 4.0 / math.sqrt(width)

    def user_side(rows):
        return user_tower(rows, in_proj, pos_embed, norm_gain, w_query, w_key, w_value, w_out, out_gain)

    def item_side(rows):
        return item_tower(rows, item_w1, item_w2, item_gain)
    grouped = history.reshape(blocks, B_DEV, HIST)
    user_vec = lax.map(lambda ids: user_side(lookup(ids, hot_table, rare_table)), grouped).reshape(users, width)
    item_rows = lookup(item_ids, hot_table, rare_table)
    item_vec, pull_item = jax.vjp(item_side, item_rows)
    logits = scale * jnp.dot(user_vec, item_vec.T, preferred_element_type=jnp.float32)
    top = lax.optimization_barrier(jnp.max(logits, axis=1, keepdims=True))
    normalizer = top + jnp.log(lax.optimization_barrier(jnp.sum(jnp.exp(logits - top), axis=1, keepdims=True)))
    loss = jnp.sum(normalizer[:, 0] - jnp.diagonal(logits)) / users
    target = jnp.eye(users, dtype=jnp.float32)
    slope = (jnp.exp(logits - normalizer) - target).astype(jnp.bfloat16)
    d_user = (scale * jnp.dot(slope, item_vec, preferred_element_type=jnp.float32)).astype(jnp.bfloat16)
    d_item = (scale * jnp.dot(slope.T, user_vec, preferred_element_type=jnp.float32)).astype(jnp.bfloat16)
    d_item_rows, = pull_item(d_item)
    grad_hot = jnp.zeros((HOT, EMB), jnp.float32)
    grad_rare = jnp.zeros((RARE_ROWS, EMB), jnp.float32)
    grad_hot, grad_rare = add_rows(grad_hot, grad_rare, item_ids, d_item_rows)

    def backward_block(carry, inputs):
        ids, cotangent = inputs
        rows = lookup(ids, hot_table, rare_table)
        unused, pull_user = jax.vjp(user_side, rows)
        d_rows, = pull_user(cotangent)
        return (add_rows(carry[0], carry[1], ids.reshape(-1), d_rows.reshape(-1, EMB)), None)
    (grad_hot, grad_rare), unused = lax.scan(backward_block, (grad_hot, grad_rare), (grouped, d_user.reshape(blocks, B_DEV, width)))
    return (grad_hot, grad_rare, loss)
```

```python
import functools
import math

import jax
import jax.numpy as jnp
from jax import lax
from jax.experimental import pallas as pl
from jax.experimental.pallas import tpu as pltpu
from jax.sharding import PartitionSpec as P

HEAD_DIM = 64
EPS = 1e-06
SLOTS = 8
PAD = 16
BF = jnp.bfloat16
F32 = jnp.float32
VMEM = pl.BlockSpec(memory_space=pltpu.VMEM)
SMEM = pl.BlockSpec(memory_space=pltpu.SMEM)
HBM = pl.BlockSpec(memory_space=pl.ANY)
NT = (((1,), (1,)), ((), ()))
TN = (((0,), (0,)), ((), ()))


def dot(a, b):
    return jnp.dot(a, b, preferred_element_type=F32)


def dot_nt(a, b):
    return lax.dot_general(a, b, NT, preferred_element_type=F32)


def dot_tn(a, b):
    return lax.dot_general(a, b, TN, preferred_element_type=F32)


def iota(shape, axis):
    return lax.broadcasted_iota(jnp.int32, shape, axis)


def one_hot(mask):
    return jnp.where(mask, 1.0, 0.0).astype(BF)


def params(mib):
    return pltpu.CompilerParams(vmem_limit_bytes=mib * 1024 * 1024)


def index_kernel(hot_count, rare_count, owners, ids_ref, request_ref, row_ref, column_ref):
    ids = ids_ref[...]
    span = ids.shape[1]
    is_rare = ids >= hot_count
    index = ids - hot_count
    owner = jnp.where(is_rare, index // rare_count, -1)
    local = jnp.where(is_rare, index % rare_count, 0)
    hits = iota((owners, span), 0) == owner
    before = one_hot(iota((span, span), 0) < iota((span, span), 1))
    earlier = dot(one_hot(hits), before)
    position = jnp.sum(jnp.where(hits, earlier, 0.0), axis=0, keepdims=True).astype(jnp.int32)
    column = jnp.where(
        is_rare, owner * SLOTS + position, jnp.where(ids >= 0, owners * SLOTS + ids, -1)
    )
    row_ref[...] = jnp.broadcast_to(column, row_ref.shape)
    column_ref[...] = jnp.transpose(
        jnp.broadcast_to(column.astype(F32), (128, span))
    ).astype(jnp.int32)
    spread = one_hot(iota((owners * SLOTS, span), 0) == column)
    value = local + 1
    high = jnp.broadcast_to((value // 2).astype(F32), (128, span)).astype(BF)
    low = jnp.broadcast_to((value % 2).astype(F32), (128, span)).astype(BF)
    request_ref[...] = (2.0 * dot_nt(spread, high) + dot_nt(spread, low) - 1.0).astype(jnp.int32)


def serve_kernel(asked_ref, table_ref, served_ref, row_ref):
    asked = asked_ref[...]
    rows = table_ref.shape[0]
    lanes = iota(asked.shape, 1)
    picks = jnp.concatenate(
        [one_hot(asked == lanes + 128 * j) for j in range(rows // 128)], axis=1
    )
    served_ref[...] = dot(picks, table_ref[...].astype(BF)).astype(BF)
    row_ref[...] = jnp.transpose(asked.astype(F32))[0:8].astype(jnp.int32)


def head_mask(heads, width):
    return iota((heads, width), 1) // HEAD_DIM == iota((heads, width), 0)


def spread_heads(values, mask, users):
    return jnp.concatenate(
        [jnp.where(mask, values[u : u + 1], 0.0) for u in range(users)], axis=0
    ).astype(BF)


def join_heads(full, mask, users):
    heads = mask.shape[0]
    parts = [
        jnp.sum(
            jnp.where(mask, full[u * heads : (u + 1) * heads], 0.0), axis=0, keepdims=True
        )
        for u in range(users)
    ]
    return jnp.concatenate(parts + [jnp.zeros((PAD - users, full.shape[1]), F32)], axis=0)


def forward_kernel(
    users,
    fetched_ref,
    hot_ref,
    column_ref,
    pos_ref,
    norm_gain_ref,
    out_gain_ref,
    item_gain_ref,
    in_proj_hbm,
    w_query_hbm,
    w_key_hbm,
    w_value_hbm,
    w_out_hbm,
    item_w1_hbm,
    item_w2_hbm,
    user_vec_ref,
    item_vec_ref,
    hidden_ref,
    normed_ref,
    qk_ref,
    weights_ref,
    mixed_ref,
    inner_ref,
    outer_ref,
    in_proj,
    w_query,
    w_key,
    w_value,
    w_out,
    item_w1,
    item_w2,
    sems,
):
    sources = (in_proj_hbm, w_query_hbm, w_key_hbm, w_value_hbm, w_out_hbm, item_w1_hbm, item_w2_hbm)
    targets = (in_proj, w_query, w_key, w_value, w_out, item_w1, item_w2)
    copies = [
        pltpu.make_async_copy(s, t, sems.at[i]) for i, (s, t) in enumerate(zip(sources, targets))
    ]
    for copy in copies:
        copy.start()
    hist, width = pos_ref.shape
    heads = width // HEAD_DIM
    span = users * hist
    slots = fetched_ref.shape[0]
    column = column_ref[0 : span + PAD, :]
    lanes = iota(column.shape, 1)
    picks = jnp.concatenate(
        [one_hot(column == lanes + 128 * j) for j in range(slots // 128)], axis=1
    )
    hot_picks = one_hot(column == lanes + slots)
    rows = (dot(picks, fetched_ref[...]) + dot(hot_picks, hot_ref[...].astype(BF))).astype(BF)
    copies[0].wait()
    pos = pos_ref[...].astype(F32)
    hidden = dot(rows[0:span], in_proj[...]) + jnp.concatenate([pos] * users, axis=0)
    hidden_ref[...] = hidden
    scale = lax.rsqrt(jnp.mean(hidden * hidden, axis=-1, keepdims=True) + EPS)
    normed = (hidden * scale * norm_gain_ref[...]).astype(BF)
    normed_ref[...] = normed
    last = jnp.concatenate(
        [normed_ref[(u + 1) * hist - 1 : (u + 1) * hist, :].astype(F32) for u in range(users)]
        + [jnp.zeros((PAD - users, width), F32)],
        axis=0,
    ).astype(BF)
    mask = head_mask(heads, width)
    copies[1].wait()
    query = dot(last, w_query[...]).astype(BF).astype(F32)
    copies[2].wait()
    qk = dot_nt(spread_heads(query, mask, users), w_key[...]).astype(BF)
    qk_ref[...] = qk
    mixes = []
    for u in range(users):
        own = normed[u * hist : (u + 1) * hist]
        scores = dot_nt(qk[u * heads : (u + 1) * heads], own) * (1.0 / math.sqrt(HEAD_DIM))
        raised = jnp.exp(scores - jnp.max(scores, axis=1, keepdims=True))
        weights = raised / jnp.sum(raised, axis=1, keepdims=True)
        weights_ref[u * heads : (u + 1) * heads, :] = weights
        mixes.append(dot(weights.astype(BF), own))
    mixes = jnp.concatenate(mixes, axis=0).astype(BF)
    copies[3].wait()
    attended = join_heads(dot(mixes, w_value[...]), mask, users).astype(BF)
    copies[4].wait()
    hidden_last = jnp.concatenate(
        [hidden_ref[(u + 1) * hist - 1 : (u + 1) * hist, :] for u in range(users)]
        + [jnp.zeros((PAD - users, width), F32)],
        axis=0,
    )
    mixed = hidden_last + dot(attended, w_out[...])
    mixed_ref[...] = mixed
    scale = lax.rsqrt(jnp.mean(mixed * mixed, axis=-1, keepdims=True) + EPS)
    user_vec_ref[...] = (mixed * scale * out_gain_ref[...]).astype(BF)
    copies[5].wait()
    inner = dot(rows[span : span + PAD], item_w1[...])
    inner_ref[...] = inner
    copies[6].wait()
    outer = dot((inner * jax.nn.sigmoid(inner)).astype(BF), item_w2[...])
    outer_ref[...] = outer
    scale = lax.rsqrt(jnp.mean(outer * outer, axis=-1, keepdims=True) + EPS)
    item_vec_ref[...] = (outer * scale * item_gain_ref[...]).astype(BF)


def softmax_step(users, scale, base, user_all, item_all, user_vec, item_vec, logits, d_user, d_item, loss):
    total = user_all.shape[0]
    chunk = 256
    top = jnp.full((1, total), -jnp.inf, F32)
    for c in range(total // chunk):
        part = scale * dot_nt(item_all[c * chunk : (c + 1) * chunk, :], user_all[...])
        logits[c * chunk : (c + 1) * chunk, :] = part
        top = jnp.maximum(top, jnp.max(part, axis=0, keepdims=True))
    count = jnp.zeros((1, total), F32)
    for c in range(total // chunk):
        part = logits[c * chunk : (c + 1) * chunk, :]
        count = count + jnp.sum(jnp.exp(part - top), axis=0, keepdims=True)
    normalizer = top + jnp.log(count)
    rows = iota((PAD, total), 0)
    valid = rows < users
    target = iota((PAD, total), 1) == rows + base
    one = jnp.where(target, 1.0, 0.0)
    item_logits = scale * dot_nt(item_vec[...], user_all[...])
    slope = jnp.where(valid, jnp.exp(item_logits - normalizer) - one, 0.0).astype(BF)
    d_item[...] = (scale * dot(slope, user_all[...])).astype(BF).astype(F32)
    user_logits = scale * dot_nt(user_vec[...], item_all[...])
    top = jnp.max(user_logits, axis=1, keepdims=True)
    normalizer = top + jnp.log(jnp.sum(jnp.exp(user_logits - top), axis=1, keepdims=True))
    slope = jnp.where(valid, jnp.exp(user_logits - normalizer) - one, 0.0).astype(BF)
    d_user[...] = (scale * dot(slope, item_all[...])).astype(BF).astype(F32)
    each = jnp.sum(jnp.where(valid & target, normalizer - user_logits, 0.0), axis=1, keepdims=True)
    loss[...] = jnp.broadcast_to(jnp.sum(each, axis=0, keepdims=True), loss.shape)


def norm_backward(values, cotangent, gain):
    inverse = lax.rsqrt(jnp.mean(values * values, axis=-1, keepdims=True) + EPS)
    pulled = cotangent * gain
    along = jnp.mean(pulled * values, axis=-1, keepdims=True)
    return inverse * pulled - values * (inverse * inverse * inverse * along)


def backward_kernel(
    users,
    loss_scale,
    place_ref,
    gathered_ref,
    swapped_ref,
    user_vec_ref,
    item_vec_ref,
    hidden_ref,
    normed_ref,
    qk_ref,
    weights_ref,
    mixed_ref,
    inner_ref,
    outer_ref,
    row_ref,
    norm_gain_ref,
    out_gain_ref,
    item_gain_ref,
    in_proj_hbm,
    w_query_hbm,
    w_key_hbm,
    w_value_hbm,
    w_out_hbm,
    item_w1_hbm,
    item_w2_hbm,
    outgoing_ref,
    hot_ref,
    in_proj,
    w_query,
    w_key,
    w_value,
    w_out,
    item_w1,
    item_w2,
    logits,
    d_user,
    d_item,
    loss,
    d_normed,
    sems,
):
    sources = (in_proj_hbm, w_query_hbm, w_key_hbm, w_value_hbm, w_out_hbm, item_w1_hbm, item_w2_hbm)
    targets = (in_proj, w_query, w_key, w_value, w_out, item_w1, item_w2)
    copies = [
        pltpu.make_async_copy(s, t, sems.at[i]) for i, (s, t) in enumerate(zip(sources, targets))
    ]
    for copy in copies:
        copy.start()
    own = (user_vec_ref, item_vec_ref, logits, d_user, d_item, loss)

    @pl.when(place_ref[0] == 0)
    def _():
        softmax_step(users, loss_scale, place_ref[1], gathered_ref, swapped_ref, *own)

    @pl.when(place_ref[0] != 0)
    def _():
        softmax_step(users, loss_scale, place_ref[1], swapped_ref, gathered_ref, *own)

    for copy in copies:
        copy.wait()
    span, width = hidden_ref.shape
    hist = span // users
    heads = width // HEAD_DIM
    mask = head_mask(heads, width)
    d_mixed = norm_backward(mixed_ref[...], d_user[...], out_gain_ref[...])
    d_attended = dot_nt(d_mixed.astype(BF), w_out[...])
    d_mixes = dot_nt(spread_heads(d_attended, mask, users), w_value[...]).astype(BF)
    d_qk = []
    for u in range(users):
        own = normed_ref[u * hist : (u + 1) * hist, :]
        weights = weights_ref[u * heads : (u + 1) * heads, :]
        pulled = d_mixes[u * heads : (u + 1) * heads]
        d_weights = dot_nt(pulled, own)
        d_scores = weights * (d_weights - jnp.sum(weights * d_weights, axis=1, keepdims=True))
        d_scores = (d_scores * (1.0 / math.sqrt(HEAD_DIM))).astype(BF)
        d_normed[u * hist : (u + 1) * hist, :] = dot_tn(weights.astype(BF), pulled) + dot_tn(
            d_scores, qk_ref[u * heads : (u + 1) * heads, :]
        )
        d_qk.append(dot(d_scores, own))
    d_qk = jnp.concatenate(d_qk, axis=0).astype(BF)
    d_query = join_heads(dot(d_qk, w_key[...]), mask, users).astype(BF)
    d_last = dot_nt(d_query, w_query[...])
    for u in range(users):
        at = slice((u + 1) * hist - 1, (u + 1) * hist)
        d_normed[at, :] = d_normed[at, :] + d_last[u : u + 1]
    d_normed[...] = norm_backward(hidden_ref[...], d_normed[...], norm_gain_ref[...])
    for u in range(users):
        at = slice((u + 1) * hist - 1, (u + 1) * hist)
        d_normed[at, :] = d_normed[at, :] + d_mixed[u : u + 1]
    d_rows = dot_nt(d_normed[...].astype(BF), in_proj[...])
    d_outer = norm_backward(outer_ref[...], d_item[...], item_gain_ref[...])
    inner = inner_ref[...]
    gate = jax.nn.sigmoid(inner)
    d_inner = dot_nt(d_outer.astype(BF), item_w2[...]) * (gate * (1.0 + inner * (1.0 - gate)))
    d_items = dot_nt(d_inner.astype(BF), item_w1[...])
    wide = row_ref.shape[1]
    d_all = jnp.concatenate(
        [d_rows, d_items, jnp.zeros((wide - span - PAD, d_rows.shape[1]), F32)], axis=0
    ).astype(BF)
    slots = outgoing_ref.shape[0]
    hot_count = hot_ref.shape[0] - 16
    column = row_ref[0:1, :]
    outgoing_ref[...] = dot(one_hot(iota((slots, wide), 0) == column), d_all).astype(BF)
    hot = dot(one_hot(iota((hot_count, wide), 0) + slots == column), d_all)
    half = hot_count // 2
    hot_ref[0:half, :] = hot[0:half]
    hot_ref[half : half + 8, :] = loss[...]
    hot_ref[half + 8 : 2 * half + 8, :] = hot[half:]
    hot_ref[2 * half + 8 :, :] = jnp.zeros_like(loss)


def scatter_kernel(returned_ref, row_ref, part_ref):
    rows = part_ref.shape[0]
    slots = returned_ref.shape[0]
    picks = one_hot(iota((rows, slots), 0) == row_ref[0:1, :])
    part_ref[...] = dot(picks, returned_ref[...]).astype(BF)


def shards(
    history,
    item_ids,
    hot_table,
    rare_table,
    in_proj,
    pos_embed,
    norm_gain,
    w_query,
    w_key,
    w_value,
    w_out,
    out_gain,
    item_w1,
    item_w2,
    item_gain,
):
    users, hist = history.shape
    hot_count, emb = hot_table.shape
    rare_count = rare_table.shape[0]
    width = in_proj.shape[1]
    heads = width // HEAD_DIM
    scale = 4.0 / math.sqrt(width)
    owners = lax.axis_size("shard")
    towers = lax.axis_size("tower")
    tower = lax.axis_index("tower")
    total = users * towers * owners
    slots = owners * SLOTS
    span = users * hist
    wide = -(-(span + PAD) // 128) * 128
    swap = [(i, towers - 1 - i) for i in range(towers)]
    shape = jax.ShapeDtypeStruct

    ids = jnp.concatenate(
        [history.reshape(-1), item_ids, jnp.full((wide - span - users,), -1, jnp.int32)]
    ).reshape(1, wide)
    request, row, column = pl.pallas_call(
        functools.partial(index_kernel, hot_count, rare_count, owners),
        out_shape=(
            shape((slots, 128), jnp.int32),
            shape((8, wide), jnp.int32),
            shape((wide, 128), jnp.int32),
        ),
        in_specs=[VMEM],
        out_specs=(VMEM, VMEM, VMEM),
        compiler_params=params(24),
        name="index",
    )(ids)
    asked = lax.all_to_all(request, "shard", split_axis=0, concat_axis=0, tiled=True)
    served, asked_row = pl.pallas_call(
        serve_kernel,
        out_shape=(shape((slots, emb), BF), shape((8, slots), jnp.int32)),
        in_specs=[VMEM, VMEM],
        out_specs=(VMEM, VMEM),
        compiler_params=params(24),
        name="serve",
    )(asked, rare_table)
    fetched = lax.all_to_all(served, "shard", split_axis=0, concat_axis=0, tiled=True)

    weights = (in_proj, w_query, w_key, w_value, w_out, item_w1, item_w2)
    gains = tuple(g.reshape(1, width) for g in (norm_gain, out_gain, item_gain))
    weight_scratch = [pltpu.VMEM(w.shape, w.dtype) for w in weights]
    sems = pltpu.SemaphoreType.DMA((len(weights),))
    user_vec, item_vec, *kept = pl.pallas_call(
        functools.partial(forward_kernel, users),
        out_shape=(
            shape((PAD, width), BF),
            shape((PAD, width), BF),
            shape((span, width), F32),
            shape((span, width), BF),
            shape((users * heads, width), BF),
            shape((users * heads, hist), F32),
            shape((PAD, width), F32),
            shape((PAD, width), F32),
            shape((PAD, width), F32),
        ),
        in_specs=[VMEM] * 7 + [HBM] * 7,
        out_specs=(VMEM,) * 9,
        scratch_shapes=weight_scratch + [sems],
        compiler_params=params(40),
        name="forward",
    )(fetched, hot_table, column, pos_embed, *gains, *weights)

    is_first = tower == 0
    mine_user, mine_item = user_vec[:users], item_vec[:users]
    kept_vec = jnp.where(is_first, mine_user, mine_item)
    other_vec = lax.ppermute(jnp.where(is_first, mine_item, mine_user), "tower", swap)
    chip = jnp.concatenate(
        [jnp.where(is_first, kept_vec, other_vec), jnp.where(is_first, other_vec, kept_vec)], axis=0
    )
    spread = jnp.broadcast_to(chip[None], (owners, towers * users, width)).reshape(total, width)
    gathered = lax.all_to_all(spread, "shard", split_axis=0, concat_axis=0, tiled=True)
    swapped = lax.ppermute(gathered, "tower", swap)
    base = lax.axis_index("shard") * (towers * users) + tower * users
    place = jnp.stack([tower, base]).astype(jnp.int32)

    half = hot_count // 2 + 8
    outgoing, hot = pl.pallas_call(
        functools.partial(backward_kernel, users, scale),
        out_shape=(shape((slots, emb), BF), shape((2 * half, emb), F32)),
        in_specs=[SMEM] + [VMEM] * 15 + [HBM] * 7,
        out_specs=(VMEM, VMEM),
        scratch_shapes=weight_scratch
        + [
            pltpu.VMEM((total, total), F32),
            pltpu.VMEM((PAD, width), F32),
            pltpu.VMEM((PAD, width), F32),
            pltpu.VMEM((8, emb), F32),
            pltpu.VMEM((span, width), F32),
            sems,
        ],
        compiler_params=params(48),
        name="backward",
    )(place, gathered, swapped, user_vec, item_vec, *kept, row, *gains, *weights)

    returned = lax.all_to_all(outgoing, "shard", split_axis=0, concat_axis=0, tiled=True)

    lower, upper = hot[:half], hot[half:]
    mine = jnp.where(is_first, lower, upper)
    mine = mine + lax.ppermute(jnp.where(is_first, upper, lower), "tower", swap)
    step = 1
    while step < owners:
        mine = mine + lax.ppermute(mine, "shard", [(i, i ^ step) for i in range(owners)])
        step *= 2
    other = lax.ppermute(mine, "tower", swap)
    lower = jnp.where(is_first, mine, other)
    upper = jnp.where(is_first, other, mine)
    hot_total = jnp.concatenate([lower[: half - 8], upper[: half - 8]], axis=0)
    loss_total = lower[half - 8, 0]

    part = pl.pallas_call(
        scatter_kernel,
        out_shape=shape((rare_count, emb), BF),
        in_specs=[VMEM, VMEM],
        out_specs=VMEM,
        compiler_params=params(24),
        name="scatter",
    )(returned, asked_row)
    rare_grad = part.astype(F32) + lax.ppermute(part, "tower", swap).astype(F32)
    return (hot_total, rare_grad, loss_total / total)


def solution(mesh):
    return jax.shard_map(
        shards,
        mesh=mesh,
        in_specs=(
            P(("tower", "shard"), None),
            P(("tower", "shard")),
            P(),
            P("shard", None),
            P(),
            P(),
            P(),
            P(),
            P(),
            P(),
            P(),
            P(),
            P(),
            P(),
            P(),
        ),
        out_specs=(P(), P("shard", None), P()),
        check_vma=False,
    )
```

```python
import functools
import math

import jax
import jax.numpy as jnp
from jax import lax
from jax.experimental import pallas as pl
from jax.experimental.pallas import tpu as pltpu
from jax.sharding import Mesh
from jax.sharding import PartitionSpec as P

HEAD_DIM = 64
EPS = 1e-06
SLOTS = 8
HOT_SLOT = 5
SHARD = ("x", "y", "z")
PAD = 16
BF = jnp.bfloat16
F32 = jnp.float32
VMEM = pl.BlockSpec(memory_space=pltpu.VMEM)
SMEM = pl.BlockSpec(memory_space=pltpu.SMEM)
HBM = pl.BlockSpec(memory_space=pltpu.HBM)
NT = (((1,), (1,)), ((), ()))
TN = (((0,), (0,)), ((), ()))


def dot(a, b):
    return jnp.dot(a, b, preferred_element_type=F32)


def dot_nt(a, b):
    return lax.dot_general(a, b, NT, preferred_element_type=F32)


def dot_tn(a, b):
    return lax.dot_general(a, b, TN, preferred_element_type=F32)


def iota(shape, axis):
    return lax.broadcasted_iota(jnp.int32, shape, axis)


def one_hot(mask):
    return jnp.where(mask, 1.0, 0.0).astype(BF)


def params(mib):
    return pltpu.CompilerParams(vmem_limit_bytes=mib * 1024 * 1024)


def copies_of(pairs, sems):
    copies = [pltpu.make_async_copy(a, b, sems.at[i]) for i, (a, b) in enumerate(pairs)]
    for copy in copies:
        copy.start()
    return copies


def index_kernel(
    rare_count, owners, history_ref, items_ref, request_ref, row_hbm, column_hbm, row, column, sems
):
    hot_count = owners
    users = history_ref.shape[0]
    span = row.shape[1]
    parts = [history_ref[u : u + 1, :] for u in range(users)] + [items_ref[...]]
    filled = sum(p.shape[1] for p in parts)
    ids = jnp.concatenate(parts + [jnp.full((1, span - filled), -1, jnp.int32)], axis=1)
    is_rare = ids >= hot_count
    index = ids - hot_count
    owner = jnp.where(is_rare, index // rare_count, -1)
    value = jnp.where(is_rare, index % rare_count + 1, 0).astype(F32)
    hits = iota((owners, span), 0) == owner
    before = one_hot(iota((span, span), 0) < iota((span, span), 1))
    earlier = dot(one_hot(hits), before)
    position = jnp.sum(jnp.where(hits, earlier, 0.0), axis=0, keepdims=True).astype(jnp.int32)
    places = jnp.where(
        is_rare, owner * SLOTS + position, jnp.where(ids >= 0, ids * SLOTS + HOT_SLOT, -1)
    )
    row[...] = jnp.broadcast_to(places, row.shape)
    column[...] = jnp.transpose(jnp.broadcast_to(places.astype(F32), (128, span))).astype(jnp.int32)
    copies = copies_of([(row, row_hbm), (column, column_hbm)], sems)
    order = jnp.where(hits, earlier, -1.0)
    lanes = iota(request_ref.shape, 1)
    request = jnp.zeros(request_ref.shape, F32)
    for slot in range(HOT_SLOT):
        wanted = jnp.sum(jnp.where(order == float(slot), value, 0.0), axis=1, keepdims=True)
        request = jnp.where(lanes == slot, wanted, request)
    request_ref[...] = request.astype(jnp.int32)
    for copy in copies:
        copy.wait()


def serve_kernel(asked_ref, table_hbm, served_hbm, row_hbm, table, served, row, sems):
    load = pltpu.make_async_copy(table_hbm, table, sems.at[0])
    load.start()
    slots = served.shape[0]
    sources = asked_ref.shape[0]
    asked = asked_ref[...]
    high = (asked // 2).astype(F32).astype(BF)
    low = (asked % 2).astype(F32).astype(BF)
    expand = one_hot(iota((slots, sources), 0) // SLOTS == iota((slots, sources), 1))
    wide = 2.0 * dot(expand, high) + dot(expand, low)
    mine = iota(wide.shape, 1) == iota(wide.shape, 0) % SLOTS
    index = jnp.sum(jnp.where(mine, wide, 0.0), axis=1, keepdims=True) - 1.0
    index = jnp.broadcast_to(index, wide.shape)
    row[...] = jnp.transpose(index)[0:8].astype(jnp.int32)
    keep = pltpu.make_async_copy(row, row_hbm, sems.at[1])
    keep.start()
    index = index.astype(jnp.int32)
    lanes = iota(index.shape, 1)
    rows = table.shape[0]
    picks = jnp.concatenate(
        [one_hot(index == lanes + 128 * j) for j in range(rows // 128)], axis=1
    )
    load.wait()
    known = table[...].astype(BF)
    chunk = slots // 4
    copies = []
    for c in range(4):
        at = pl.ds(c * chunk, chunk)
        served[at, :] = dot(picks[c * chunk : (c + 1) * chunk], known).astype(BF)
        copies.append(pltpu.make_async_copy(served.at[at], served_hbm.at[at], sems.at[2 + c]))
        copies[-1].start()
    keep.wait()
    for copy in copies:
        copy.wait()


def head_mask(heads, width):
    return iota((heads, width), 1) // HEAD_DIM == iota((heads, width), 0)


def spread_heads(values, mask, users):
    return jnp.concatenate(
        [jnp.where(mask, values[u : u + 1], 0.0) for u in range(users)], axis=0
    ).astype(BF)


def join_heads(full, mask, users):
    heads = mask.shape[0]
    parts = [
        jnp.sum(
            jnp.where(mask, full[u * heads : (u + 1) * heads], 0.0), axis=0, keepdims=True
        )
        for u in range(users)
    ]
    return jnp.concatenate(parts + [jnp.zeros((PAD - users, full.shape[1]), F32)], axis=0)


def forward_kernel(
    users,
    fetched_ref,
    norm_gain_ref,
    out_gain_ref,
    item_gain_ref,
    *refs,
):
    sources, refs = refs[:10], refs[10:]
    vectors_ref, kept_hbm, refs = refs[0], refs[1:8], refs[8:]
    targets, kept, (in_sems, out_sems) = refs[:10], refs[10:17], refs[17:]
    hot, column_of, pos_of, in_proj, w_query, w_key, w_value, w_out, item_w1, item_w2 = targets
    hidden_ref, normed_ref, qk_ref, weights_ref, mixed_ref, inner_ref, outer_ref = kept
    copies = copies_of(zip(sources, targets), in_sems)
    saves = [
        pltpu.make_async_copy(a, b, out_sems.at[i]) for i, (a, b) in enumerate(zip(kept, kept_hbm))
    ]
    hist, width = pos_of.shape
    heads = width // HEAD_DIM
    span = users * hist
    slots = fetched_ref.shape[0]
    copies[0].wait()
    copies[1].wait()
    column = column_of[0 : span + PAD, :]
    lanes = iota(column.shape, 1)
    picks = jnp.concatenate(
        [one_hot(column == lanes + 128 * j) for j in range(slots // 128)], axis=1
    )
    hot_picks = one_hot(column == lanes * SLOTS + HOT_SLOT)
    rows = (dot(picks, fetched_ref[...]) + dot(hot_picks, hot[...].astype(BF))).astype(BF)
    copies[2].wait()
    copies[3].wait()
    pos = pos_of[...].astype(F32)
    hidden = dot(rows[0:span], in_proj[...]) + jnp.concatenate([pos] * users, axis=0)
    hidden_ref[...] = hidden
    saves[0].start()
    scale = lax.rsqrt(jnp.mean(hidden * hidden, axis=-1, keepdims=True) + EPS)
    normed = (hidden * scale * norm_gain_ref[...]).astype(BF)
    normed_ref[...] = normed
    saves[1].start()
    last = jnp.concatenate(
        [normed[(u + 1) * hist - PAD : (u + 1) * hist].astype(F32)[PAD - 1 :] for u in range(users)]
        + [jnp.zeros((PAD - users, width), F32)],
        axis=0,
    ).astype(BF)
    mask = head_mask(heads, width)
    copies[4].wait()
    query = dot(last, w_query[...]).astype(BF).astype(F32)
    copies[5].wait()
    qk = dot_nt(spread_heads(query, mask, users), w_key[...]).astype(BF)
    qk_ref[...] = qk
    saves[2].start()
    mixes = []
    for u in range(users):
        own = normed[u * hist : (u + 1) * hist]
        scores = dot_nt(qk[u * heads : (u + 1) * heads], own) * (1.0 / math.sqrt(HEAD_DIM))
        raised = jnp.exp(scores - jnp.max(scores, axis=1, keepdims=True))
        weights = raised / jnp.sum(raised, axis=1, keepdims=True)
        weights_ref[u * heads : (u + 1) * heads, :] = weights
        mixes.append(dot(weights.astype(BF), own))
    saves[3].start()
    mixes = jnp.concatenate(mixes, axis=0).astype(BF)
    copies[6].wait()
    attended = join_heads(dot(mixes, w_value[...]), mask, users).astype(BF)
    copies[7].wait()
    hidden_last = jnp.concatenate(
        [hidden_ref[(u + 1) * hist - 1 : (u + 1) * hist, :] for u in range(users)]
        + [jnp.zeros((PAD - users, width), F32)],
        axis=0,
    )
    mixed = hidden_last + dot(attended, w_out[...])
    mixed_ref[...] = mixed
    saves[4].start()
    scale = lax.rsqrt(jnp.mean(mixed * mixed, axis=-1, keepdims=True) + EPS)
    user_vec = mixed * scale * out_gain_ref[...]
    copies[8].wait()
    inner = dot(rows[span : span + PAD], item_w1[...])
    inner_ref[...] = inner
    saves[5].start()
    copies[9].wait()
    outer = dot((inner * jax.nn.sigmoid(inner)).astype(BF), item_w2[...])
    outer_ref[...] = outer
    saves[6].start()
    scale = lax.rsqrt(jnp.mean(outer * outer, axis=-1, keepdims=True) + EPS)
    item_vec = outer * scale * item_gain_ref[...]
    both = jnp.concatenate([user_vec[0:users], item_vec[0:users]], axis=0)
    peers = vectors_ref.shape[0] // (2 * users)
    vectors_ref[...] = jnp.concatenate([both] * peers, axis=0).astype(BF)
    for save in saves:
        save.wait()


def arrange_kernel(users, vectors_ref, spread_ref):
    vectors = vectors_ref[...]
    rows, width = vectors.shape
    half = rows // 2
    out = iota((half, rows), 0)
    source = out // users * (2 * users) + out % users
    at = iota((half, rows), 1)
    user_rows = dot(one_hot(at == source), vectors).astype(BF)
    item_rows = dot(one_hot(at == source + users), vectors).astype(BF)
    for peer in range(spread_ref.shape[0] // half):
        spread_ref[peer * half : (peer + 1) * half, 0:width] = user_rows
        spread_ref[peer * half : (peer + 1) * half, width : 2 * width] = item_rows


def softmax_step(users, scale, base, parts, vectors, logits):
    rows, width = parts[0].shape
    width //= 2
    total = rows * len(parts)
    chunk = 256
    tops = [jnp.full((1, rows), -jnp.inf, F32) for _ in parts]
    for i, items in enumerate(parts):
        for c in range(0, rows, chunk):
            some = items[c : c + chunk, width:]
            for j, part in enumerate(parts):
                here = scale * dot_nt(some, part[:, :width])
                logits[i * rows + c : i * rows + c + chunk, j * rows : (j + 1) * rows] = here
                tops[j] = jnp.maximum(tops[j], jnp.max(here, axis=0, keepdims=True))
    top = jnp.concatenate(tops, axis=1)
    count = jnp.zeros((1, total), F32)
    for c in range(0, total, chunk):
        here = logits[c : c + chunk, :]
        count = count + jnp.sum(jnp.exp(here - top), axis=0, keepdims=True)
    normalizer = top + jnp.log(count)
    none = jnp.zeros((PAD - users, width), F32)
    user_vec = jnp.concatenate([vectors[0:users], none], axis=0).astype(BF)
    item_vec = jnp.concatenate([vectors[users : 2 * users], none], axis=0).astype(BF)
    lines = iota((PAD, total), 0)
    valid = lines < users
    target = iota((PAD, total), 1) == lines + base
    one = jnp.where(target, 1.0, 0.0)

    def against(vec, at):
        return scale * jnp.concatenate([dot_nt(vec, p[:, at]) for p in parts], axis=1)

    def pulled(slope, at):
        sums = [dot(slope[:, j * rows : (j + 1) * rows], p[:, at]) for j, p in enumerate(parts)]
        return (scale * sum(sums)).astype(BF).astype(F32)

    of_users, of_items = slice(0, width), slice(width, 2 * width)
    item_logits = against(item_vec, of_users)
    slope = jnp.where(valid, jnp.exp(item_logits - normalizer) - one, 0.0).astype(BF)
    d_item = pulled(slope, of_users)
    user_logits = against(user_vec, of_items)
    top = jnp.max(user_logits, axis=1, keepdims=True)
    normalizer = top + jnp.log(jnp.sum(jnp.exp(user_logits - top), axis=1, keepdims=True))
    slope = jnp.where(valid, jnp.exp(user_logits - normalizer) - one, 0.0).astype(BF)
    d_user = pulled(slope, of_items)
    each = jnp.sum(jnp.where(valid & target, normalizer - user_logits, 0.0), axis=1, keepdims=True)
    return d_user, d_item, jnp.sum(each, axis=0, keepdims=True)


def norm_backward(values, cotangent, gain):
    inverse = lax.rsqrt(jnp.mean(values * values, axis=-1, keepdims=True) + EPS)
    pulled = cotangent * gain
    along = jnp.mean(pulled * values, axis=-1, keepdims=True)
    return inverse * pulled - values * (inverse * inverse * inverse * along)


def backward_kernel(
    users,
    loss_scale,
    base_ref,
    gathered_ref,
    swapped_ref,
    norm_gain_ref,
    out_gain_ref,
    item_gain_ref,
    *refs,
):
    sources, refs = refs[:16], refs[16:]
    (outgoing_hbm, loss_ref), refs = refs[:2], refs[2:]
    targets, (outgoing, logits, d_normed, in_sems, out_sems) = refs[:16], refs[16:]
    vectors_ref, row_ref = targets[:2]
    hidden_ref, normed_ref, qk_ref, weights_ref, mixed_ref, inner_ref, outer_ref = targets[2:9]
    in_proj, w_query, w_key, w_value, w_out, item_w1, item_w2 = targets[9:]
    copies = copies_of(zip(sources, targets), in_sems)
    copies[0].wait()
    vectors = vectors_ref[0:PAD, :].astype(F32)
    d_user, d_item, loss = softmax_step(
        users, loss_scale, base_ref[0], (gathered_ref, swapped_ref), vectors, logits
    )
    loss_ref[...] = jnp.broadcast_to(loss, loss_ref.shape)
    for copy in copies[1:]:
        copy.wait()
    span, width = hidden_ref.shape
    hist = span // users
    heads = width // HEAD_DIM
    mask = head_mask(heads, width)
    d_mixed = norm_backward(mixed_ref[...], d_user, out_gain_ref[...])
    d_attended = dot_nt(d_mixed.astype(BF), w_out[...])
    d_mixes = dot_nt(spread_heads(d_attended, mask, users), w_value[...]).astype(BF)
    d_qk = []
    for u in range(users):
        own = normed_ref[u * hist : (u + 1) * hist, :]
        weights = weights_ref[u * heads : (u + 1) * heads, :]
        pulled = d_mixes[u * heads : (u + 1) * heads]
        d_weights = dot_nt(pulled, own)
        d_scores = weights * (d_weights - jnp.sum(weights * d_weights, axis=1, keepdims=True))
        d_scores = (d_scores * (1.0 / math.sqrt(HEAD_DIM))).astype(BF)
        d_normed[u * hist : (u + 1) * hist, :] = dot_tn(weights.astype(BF), pulled) + dot_tn(
            d_scores, qk_ref[u * heads : (u + 1) * heads, :]
        )
        d_qk.append(dot(d_scores, own))
    d_qk = jnp.concatenate(d_qk, axis=0).astype(BF)
    d_query = join_heads(dot(d_qk, w_key[...]), mask, users).astype(BF)
    d_last = dot_nt(d_query, w_query[...])
    for u in range(users):
        at = slice((u + 1) * hist - 1, (u + 1) * hist)
        d_normed[at, :] = d_normed[at, :] + d_last[u : u + 1]
    d_normed[...] = norm_backward(hidden_ref[...], d_normed[...], norm_gain_ref[...])
    for u in range(users):
        at = slice((u + 1) * hist - 1, (u + 1) * hist)
        d_normed[at, :] = d_normed[at, :] + d_mixed[u : u + 1]
    d_rows = dot_nt(d_normed[...].astype(BF), in_proj[...])
    d_outer = norm_backward(outer_ref[...], d_item, item_gain_ref[...])
    inner = inner_ref[...]
    gate = jax.nn.sigmoid(inner)
    d_inner = dot_nt(d_outer.astype(BF), item_w2[...]) * (gate * (1.0 + inner * (1.0 - gate)))
    d_items = dot_nt(d_inner.astype(BF), item_w1[...])
    wide = row_ref.shape[1]
    d_all = jnp.concatenate(
        [d_rows, d_items, jnp.zeros((wide - span - PAD, d_rows.shape[1]), F32)], axis=0
    ).astype(BF)
    slots = outgoing.shape[0]
    column = row_ref[0:1, :]
    chunk = slots // 4
    saves = []
    for c in range(4):
        at = pl.ds(c * chunk, chunk)
        picks = one_hot(iota((chunk, wide), 0) + c * chunk == column)
        outgoing[at, :] = dot(picks, d_all).astype(BF)
        saves.append(pltpu.make_async_copy(outgoing.at[at], outgoing_hbm.at[at], out_sems.at[c]))
        saves[-1].start()
    for save in saves:
        save.wait()


def scatter_kernel(returned_ref, row_ref, loss_ref, part_ref, hot_ref):
    rows, emb = part_ref.shape
    slots = returned_ref.shape[0]
    returned = returned_ref[...]
    picks = one_hot(iota((rows, slots), 0) == row_ref[0:1, :])
    part_ref[...] = dot(picks, returned).astype(BF)
    hot = dot(one_hot(iota((PAD, slots), 1) % SLOTS == HOT_SLOT), returned)
    hot_ref[:, 0:emb] = hot[0:1]
    hot_ref[:, emb:] = loss_ref[0:1, :]


def shards(
    history,
    item_ids,
    hot_table,
    rare_table,
    in_proj,
    pos_embed,
    norm_gain,
    w_query,
    w_key,
    w_value,
    w_out,
    out_gain,
    item_w1,
    item_w2,
    item_gain,
):
    users, hist = history.shape
    emb = hot_table.shape[1]
    rare_count = rare_table.shape[0]
    width = in_proj.shape[1]
    heads = width // HEAD_DIM
    scale = 4.0 / math.sqrt(width)
    owners = lax.axis_size(SHARD)
    towers = lax.axis_size("tower")
    near = lax.axis_size("z")
    total = users * towers * owners
    slots = owners * SLOTS
    span = users * hist
    wide = -(-(span + PAD) // 128) * 128
    swap = [(i, towers - 1 - i) for i in range(towers)]
    shape = jax.ShapeDtypeStruct
    sems = lambda n: pltpu.SemaphoreType.DMA((n,))
    like = lambda arrays: [pltpu.VMEM(a.shape, a.dtype) for a in arrays]
    exchange = functools.partial(lax.all_to_all, split_axis=0, concat_axis=0, tiled=True)

    places = (shape((8, wide), jnp.int32), shape((wide, 128), jnp.int32))
    request, row, column = pl.pallas_call(
        functools.partial(index_kernel, rare_count, owners),
        out_shape=(shape((owners, 128), jnp.int32),) + places,
        in_specs=[VMEM, VMEM],
        out_specs=(VMEM, HBM, HBM),
        scratch_shapes=like(places) + [sems(2)],
        compiler_params=params(24),
        name="index",
    )(history, item_ids.reshape(1, users))
    asked = exchange(request, SHARD)
    served_shapes = (shape((slots, emb), BF), shape((8, slots), jnp.int32))
    served, asked_row = pl.pallas_call(
        serve_kernel,
        out_shape=served_shapes,
        in_specs=[VMEM, HBM],
        out_specs=(HBM, HBM),
        scratch_shapes=like((rare_table,) + served_shapes) + [sems(6)],
        compiler_params=params(24),
        name="serve",
    )(asked, rare_table)
    fetched = exchange(served, SHARD)

    weights = (in_proj, w_query, w_key, w_value, w_out, item_w1, item_w2)
    gains = tuple(g.reshape(1, width) for g in (norm_gain, out_gain, item_gain))
    kept_shapes = (
        shape((span, width), F32),
        shape((span, width), BF),
        shape((users * heads, width), BF),
        shape((users * heads, hist), F32),
        shape((PAD, width), F32),
        shape((PAD, width), F32),
        shape((PAD, width), F32),
    )
    loads = (hot_table, column, pos_embed) + weights
    vectors, *kept = pl.pallas_call(
        functools.partial(forward_kernel, users),
        out_shape=(shape((near * 2 * users, width), BF),) + kept_shapes,
        in_specs=[VMEM] * 4 + [HBM] * len(loads),
        out_specs=(VMEM,) + (HBM,) * len(kept_shapes),
        scratch_shapes=like(loads + kept_shapes) + [sems(len(loads)), sems(len(kept_shapes))],
        compiler_params=params(40),
        name="forward",
    )(fetched, *gains, *loads)

    near_vectors = exchange(vectors, "z")
    spread = pl.pallas_call(
        functools.partial(arrange_kernel, users),
        out_shape=shape((owners * users, 2 * width), BF),
        in_specs=[VMEM],
        out_specs=VMEM,
        compiler_params=params(24),
        name="arrange",
    )(near_vectors)
    gathered = exchange(spread, ("x", "y"))
    swapped = lax.ppermute(gathered, "tower", swap)
    base = (lax.axis_index(SHARD) * users).astype(jnp.int32).reshape(1)

    loads = (vectors, row) + tuple(kept) + weights
    outgoing, loss = pl.pallas_call(
        functools.partial(backward_kernel, users, scale),
        out_shape=(shape((slots, emb), BF), shape((8, 128), F32)),
        in_specs=[SMEM] + [VMEM] * 5 + [HBM] * len(loads),
        out_specs=(HBM, VMEM),
        scratch_shapes=like(loads)
        + [
            pltpu.VMEM((slots, emb), BF),
            pltpu.VMEM((total, total), F32),
            pltpu.VMEM((span, width), F32),
            sems(len(loads)),
            sems(4),
        ],
        compiler_params=params(48),
        name="backward",
    )(base, gathered, swapped, *gains, *loads)

    returned = exchange(outgoing, SHARD)
    part, mine = pl.pallas_call(
        scatter_kernel,
        out_shape=(shape((rare_count, emb), BF), shape((1, emb + 128), F32)),
        in_specs=[VMEM, VMEM, VMEM],
        out_specs=(VMEM, VMEM),
        compiler_params=params(24),
        name="scatter",
    )(returned, asked_row, loss)
    mine = mine + lax.ppermute(mine, "tower", swap)
    rare_grad = part.astype(F32) + lax.ppermute(part, "tower", swap).astype(F32)
    sums = exchange(jnp.broadcast_to(mine, (owners, emb + 128)), SHARD)
    return (sums[:, :emb], rare_grad, jnp.sum(sums[:, emb]) / total)


def solution(mesh):
    sizes = (mesh.shape["tower"], 4, 4, mesh.shape["shard"] // 16)
    mesh = Mesh(mesh.devices.reshape(sizes), ("tower",) + SHARD)
    return jax.shard_map(
        shards,
        mesh=mesh,
        in_specs=(
            P(("tower",) + SHARD, None),
            P(("tower",) + SHARD),
            P(),
            P(SHARD, None),
            P(),
            P(),
            P(),
            P(),
            P(),
            P(),
            P(),
            P(),
            P(),
            P(),
            P(),
        ),
        out_specs=(P(), P(SHARD, None), P()),
        check_vma=False,
    )
```

```python
import functools
import math

import jax
import jax.numpy as jnp
from jax import lax
from jax.experimental import pallas as pl
from jax.experimental.pallas import tpu as pltpu
from jax.sharding import Mesh
from jax.sharding import PartitionSpec as P

HEAD_DIM = 64
EPS = 1e-06
SLOTS = 8
HOT_SLOT = 5
SHARD = ("x", "y", "z")
FULL = 62
PAD = 16
BF = jnp.bfloat16
F32 = jnp.float32
VMEM = pl.BlockSpec(memory_space=pltpu.VMEM)
SMEM = pl.BlockSpec(memory_space=pltpu.SMEM)
HBM = pl.BlockSpec(memory_space=pltpu.HBM)
NT = (((1,), (1,)), ((), ()))
TN = (((0,), (0,)), ((), ()))


def dot(a, b):
    return jnp.dot(a, b, preferred_element_type=F32)


def dot_nt(a, b):
    return lax.dot_general(a, b, NT, preferred_element_type=F32)


def dot_tn(a, b):
    return lax.dot_general(a, b, TN, preferred_element_type=F32)


def iota(shape, axis):
    return lax.broadcasted_iota(jnp.int32, shape, axis)


def one_hot(mask):
    return jnp.where(mask, 1.0, 0.0).astype(BF)


def params(mib):
    return pltpu.CompilerParams(vmem_limit_bytes=mib * 1024 * 1024)


def copies_of(pairs, sems):
    copies = [pltpu.make_async_copy(a, b, sems.at[i]) for i, (a, b) in enumerate(pairs)]
    for copy in copies:
        copy.start()
    return copies


def index_kernel(
    owners,
    history_hbm,
    items_hbm,
    table_hbm,
    request_ref,
    known_ref,
    row_hbm,
    column_hbm,
    history_ref,
    items_ref,
    table,
    row,
    column,
    sems,
):
    loads = copies_of(
        [(history_hbm, history_ref), (items_hbm, items_ref), (table_hbm, table)], sems
    )
    loads[0].wait()
    loads[1].wait()
    hot_count = owners
    rare_count = table.shape[0]
    users = history_ref.shape[0]
    span = row.shape[1]
    parts = [history_ref[u : u + 1, :] for u in range(users)] + [items_ref[...]]
    filled = sum(p.shape[1] for p in parts)
    ids = jnp.concatenate(parts + [jnp.full((1, span - filled), -1, jnp.int32)], axis=1)
    is_rare = ids >= hot_count
    index = ids - hot_count
    owner = jnp.where(is_rare, index // rare_count, -1)
    value = jnp.where(is_rare, index % rare_count + 1, 0).astype(F32)
    hits = iota((owners, span), 0) == owner
    before = one_hot(iota((span, span), 0) < iota((span, span), 1))
    earlier = dot(one_hot(hits), before)
    position = jnp.sum(jnp.where(hits, earlier, 0.0), axis=0, keepdims=True).astype(jnp.int32)
    places = jnp.where(
        is_rare, owner * SLOTS + position, jnp.where(ids >= 0, ids * SLOTS + HOT_SLOT, -1)
    )
    row[...] = jnp.broadcast_to(places, row.shape)
    column[...] = jnp.transpose(jnp.broadcast_to(places.astype(F32), (128, span))).astype(jnp.int32)
    copies = [
        pltpu.make_async_copy(row, row_hbm, sems.at[3]),
        pltpu.make_async_copy(column, column_hbm, sems.at[4]),
    ]
    for copy in copies:
        copy.start()
    order = jnp.where(hits, earlier, -1.0)
    lanes = iota(request_ref.shape, 1)
    request = jnp.zeros(request_ref.shape, F32)
    for slot in range(HOT_SLOT):
        wanted = jnp.sum(jnp.where(order == float(slot), value, 0.0), axis=1, keepdims=True)
        request = jnp.where(lanes == slot, wanted, request)
    request_ref[...] = request.astype(jnp.int32)
    loads[2].wait()
    known_ref[...] = table[...].astype(BF)
    for copy in copies:
        copy.wait()


def serve_kernel(asked_ref, known_ref, served, row_hbm, row, sem):
    slots = served.shape[0]
    sources = asked_ref.shape[0]
    asked = asked_ref[...]
    high = (asked // 2).astype(F32).astype(BF)
    low = (asked % 2).astype(F32).astype(BF)
    expand = one_hot(iota((slots, sources), 0) // SLOTS == iota((slots, sources), 1))
    wide = 2.0 * dot(expand, high) + dot(expand, low)
    mine = iota(wide.shape, 1) == iota(wide.shape, 0) % SLOTS
    index = jnp.sum(jnp.where(mine, wide, 0.0), axis=1, keepdims=True) - 1.0
    index = jnp.broadcast_to(index, wide.shape)
    row[...] = jnp.transpose(index)[0:8].astype(jnp.int32)
    keep = pltpu.make_async_copy(row, row_hbm, sem)
    keep.start()
    index = index.astype(jnp.int32)
    lanes = iota(index.shape, 1)
    rows = known_ref.shape[0]
    picks = jnp.concatenate(
        [one_hot(index == lanes + 128 * j) for j in range(rows // 128)], axis=1
    )
    served[...] = dot(picks, known_ref[...]).astype(BF)
    keep.wait()


def head_mask(heads, width):
    return iota((heads, width), 1) // HEAD_DIM == iota((heads, width), 0)


def spread_heads(values, mask, users):
    return jnp.concatenate(
        [jnp.where(mask, values[u : u + 1], 0.0) for u in range(users)], axis=0
    ).astype(BF)


def join_heads(full, mask, users):
    heads = mask.shape[0]
    parts = [
        jnp.sum(
            jnp.where(mask, full[u * heads : (u + 1) * heads], 0.0), axis=0, keepdims=True
        )
        for u in range(users)
    ]
    return jnp.concatenate(parts + [jnp.zeros((PAD - users, full.shape[1]), F32)], axis=0)


def forward_kernel(
    users,
    *refs,
):
    sources, refs = refs[:14], refs[14:]
    vectors_ref, kept_hbm, refs = refs[0], refs[1:8], refs[8:]
    targets, kept, (in_sems, out_sems) = refs[:14], refs[14:21], refs[21:]
    column_of, fetched_ref, hot, pos_of, norm_gain_ref, out_gain_ref, item_gain_ref = targets[:7]
    in_proj, w_query, w_key, w_value, w_out, item_w1, item_w2 = targets[7:]
    hidden_ref, normed_ref, qk_ref, weights_ref, mixed_ref, inner_ref, outer_ref = kept
    copies = copies_of(zip(sources, targets), in_sems)
    saves = [
        pltpu.make_async_copy(a, b, out_sems.at[i]) for i, (a, b) in enumerate(zip(kept, kept_hbm))
    ]
    hist, width = pos_of.shape
    heads = width // HEAD_DIM
    span = users * hist
    slots = fetched_ref.shape[0]
    copies[0].wait()
    column = column_of[0 : span + PAD, :]
    lanes = iota(column.shape, 1)
    picks = jnp.concatenate(
        [one_hot(column == lanes + 128 * j) for j in range(slots // 128)], axis=1
    )
    hot_picks = one_hot(column == lanes * SLOTS + HOT_SLOT)
    copies[1].wait()
    copies[2].wait()
    rows = (dot(picks, fetched_ref[...]) + dot(hot_picks, hot[...].astype(BF))).astype(BF)
    for copy in copies[3:8]:
        copy.wait()
    pos = pos_of[...].astype(F32)
    hidden = dot(rows[0:span], in_proj[...]) + jnp.concatenate([pos] * users, axis=0)
    hidden_ref[...] = hidden
    saves[0].start()
    scale = lax.rsqrt(jnp.mean(hidden * hidden, axis=-1, keepdims=True) + EPS)
    normed = (hidden * scale * norm_gain_ref[...]).astype(BF)
    normed_ref[...] = normed
    saves[1].start()
    last = jnp.concatenate(
        [normed[(u + 1) * hist - PAD : (u + 1) * hist].astype(F32)[PAD - 1 :] for u in range(users)]
        + [jnp.zeros((PAD - users, width), F32)],
        axis=0,
    ).astype(BF)
    mask = head_mask(heads, width)
    copies[8].wait()
    query = dot(last, w_query[...]).astype(BF).astype(F32)
    copies[9].wait()
    qk = dot_nt(spread_heads(query, mask, users), w_key[...]).astype(BF)
    qk_ref[...] = qk
    saves[2].start()
    mixes = []
    for u in range(users):
        own = normed[u * hist : (u + 1) * hist]
        scores = dot_nt(qk[u * heads : (u + 1) * heads], own) * (1.0 / math.sqrt(HEAD_DIM))
        raised = jnp.exp(scores - jnp.max(scores, axis=1, keepdims=True))
        weights = raised / jnp.sum(raised, axis=1, keepdims=True)
        weights_ref[u * heads : (u + 1) * heads, :] = weights
        mixes.append(dot(weights.astype(BF), own))
    saves[3].start()
    mixes = jnp.concatenate(mixes, axis=0).astype(BF)
    copies[10].wait()
    attended = join_heads(dot(mixes, w_value[...]), mask, users).astype(BF)
    copies[11].wait()
    hidden_last = jnp.concatenate(
        [hidden_ref[(u + 1) * hist - 1 : (u + 1) * hist, :] for u in range(users)]
        + [jnp.zeros((PAD - users, width), F32)],
        axis=0,
    )
    mixed = hidden_last + dot(attended, w_out[...])
    mixed_ref[...] = mixed
    saves[4].start()
    scale = lax.rsqrt(jnp.mean(mixed * mixed, axis=-1, keepdims=True) + EPS)
    user_vec = mixed * scale * out_gain_ref[...]
    copies[12].wait()
    inner = dot(rows[span : span + PAD], item_w1[...])
    inner_ref[...] = inner
    saves[5].start()
    copies[13].wait()
    outer = dot((inner * jax.nn.sigmoid(inner)).astype(BF), item_w2[...])
    outer_ref[...] = outer
    saves[6].start()
    scale = lax.rsqrt(jnp.mean(outer * outer, axis=-1, keepdims=True) + EPS)
    item_vec = outer * scale * item_gain_ref[...]
    both = jnp.concatenate([user_vec[0:users], item_vec[0:users]], axis=0)
    peers = vectors_ref.shape[0] // (2 * users)
    vectors_ref[...] = jnp.concatenate([both] * peers, axis=0).astype(BF)
    for save in saves:
        save.wait()


def arrange_kernel(users, vectors_ref, spread_ref):
    vectors = vectors_ref[...]
    rows, width = vectors.shape
    half = rows // 2
    out = iota((half, rows), 0)
    source = out // users * (2 * users) + out % users
    at = iota((half, rows), 1)
    user_rows = dot(one_hot(at == source), vectors).astype(BF)
    item_rows = dot(one_hot(at == source + users), vectors).astype(BF)
    for peer in range(spread_ref.shape[0] // half):
        spread_ref[peer * half : (peer + 1) * half, 0:width] = user_rows
        spread_ref[peer * half : (peer + 1) * half, width : 2 * width] = item_rows


def softmax_step(users, scale, base, parts, vectors, logits):
    rows, width = parts[0].shape
    width //= 2
    total = rows * len(parts)
    chunk = 256
    tops = [jnp.full((1, rows), -jnp.inf, F32) for _ in parts]
    for i, items in enumerate(parts):
        for c in range(0, rows, chunk):
            some = items[c : c + chunk, width:]
            for j, part in enumerate(parts):
                here = scale * dot_nt(some, part[:, :width])
                logits[i * rows + c : i * rows + c + chunk, j * rows : (j + 1) * rows] = here
                tops[j] = jnp.maximum(tops[j], jnp.max(here, axis=0, keepdims=True))
    top = jnp.concatenate(tops, axis=1)
    count = jnp.zeros((1, total), F32)
    for c in range(0, total, chunk):
        here = logits[c : c + chunk, :]
        count = count + jnp.sum(jnp.exp(here - top), axis=0, keepdims=True)
    normalizer = top + jnp.log(count)
    none = jnp.zeros((PAD - users, width), F32)
    user_vec = jnp.concatenate([vectors[0:users], none], axis=0).astype(BF)
    item_vec = jnp.concatenate([vectors[users : 2 * users], none], axis=0).astype(BF)
    lines = iota((PAD, total), 0)
    valid = lines < users
    target = iota((PAD, total), 1) == lines + base
    one = jnp.where(target, 1.0, 0.0)

    def against(vec, at):
        return scale * jnp.concatenate([dot_nt(vec, p[:, at]) for p in parts], axis=1)

    def pulled(slope, at):
        sums = [dot(slope[:, j * rows : (j + 1) * rows], p[:, at]) for j, p in enumerate(parts)]
        return (scale * sum(sums)).astype(BF).astype(F32)

    of_users, of_items = slice(0, width), slice(width, 2 * width)
    item_logits = against(item_vec, of_users)
    slope = jnp.where(valid, jnp.exp(item_logits - normalizer) - one, 0.0).astype(BF)
    d_item = pulled(slope, of_users)
    user_logits = against(user_vec, of_items)
    top = jnp.max(user_logits, axis=1, keepdims=True)
    normalizer = top + jnp.log(jnp.sum(jnp.exp(user_logits - top), axis=1, keepdims=True))
    slope = jnp.where(valid, jnp.exp(user_logits - normalizer) - one, 0.0).astype(BF)
    d_user = pulled(slope, of_items)
    each = jnp.sum(jnp.where(valid & target, normalizer - user_logits, 0.0), axis=1, keepdims=True)
    return d_user, d_item, jnp.sum(each, axis=0, keepdims=True)


def norm_backward(values, cotangent, gain):
    inverse = lax.rsqrt(jnp.mean(values * values, axis=-1, keepdims=True) + EPS)
    pulled = cotangent * gain
    along = jnp.mean(pulled * values, axis=-1, keepdims=True)
    return inverse * pulled - values * (inverse * inverse * inverse * along)


def backward_kernel(
    users,
    loss_scale,
    base_ref,
    gathered_ref,
    swapped_ref,
    *refs,
):
    sources, refs = refs[:19], refs[19:]
    (outgoing_hbm, loss_ref), refs = refs[:2], refs[2:]
    targets, (outgoing, logits, d_normed, in_sems, out_sems) = refs[:19], refs[19:]
    vectors_ref, row_ref = targets[:2]
    norm_gain_ref, out_gain_ref, item_gain_ref = targets[2:5]
    hidden_ref, normed_ref, qk_ref, weights_ref, mixed_ref, inner_ref, outer_ref = targets[5:12]
    in_proj, w_query, w_key, w_value, w_out, item_w1, item_w2 = targets[12:]
    copies = copies_of(zip(sources, targets), in_sems)
    copies[0].wait()
    vectors = vectors_ref[0:PAD, :].astype(F32)
    d_user, d_item, loss = softmax_step(
        users, loss_scale, base_ref[0], (gathered_ref, swapped_ref), vectors, logits
    )
    loss_ref[...] = jnp.broadcast_to(loss, loss_ref.shape)
    for copy in copies[1:]:
        copy.wait()
    span, width = hidden_ref.shape
    hist = span // users
    heads = width // HEAD_DIM
    mask = head_mask(heads, width)
    d_mixed = norm_backward(mixed_ref[...], d_user, out_gain_ref[...])
    d_attended = dot_nt(d_mixed.astype(BF), w_out[...])
    d_mixes = dot_nt(spread_heads(d_attended, mask, users), w_value[...]).astype(BF)
    d_qk = []
    for u in range(users):
        own = normed_ref[u * hist : (u + 1) * hist, :]
        weights = weights_ref[u * heads : (u + 1) * heads, :]
        pulled = d_mixes[u * heads : (u + 1) * heads]
        d_weights = dot_nt(pulled, own)
        d_scores = weights * (d_weights - jnp.sum(weights * d_weights, axis=1, keepdims=True))
        d_scores = (d_scores * (1.0 / math.sqrt(HEAD_DIM))).astype(BF)
        d_normed[u * hist : (u + 1) * hist, :] = dot_tn(weights.astype(BF), pulled) + dot_tn(
            d_scores, qk_ref[u * heads : (u + 1) * heads, :]
        )
        d_qk.append(dot(d_scores, own))
    d_qk = jnp.concatenate(d_qk, axis=0).astype(BF)
    d_query = join_heads(dot(d_qk, w_key[...]), mask, users).astype(BF)
    d_last = dot_nt(d_query, w_query[...])
    for u in range(users):
        at = slice((u + 1) * hist - 1, (u + 1) * hist)
        d_normed[at, :] = d_normed[at, :] + d_last[u : u + 1]
    d_normed[...] = norm_backward(hidden_ref[...], d_normed[...], norm_gain_ref[...])
    for u in range(users):
        at = slice((u + 1) * hist - 1, (u + 1) * hist)
        d_normed[at, :] = d_normed[at, :] + d_mixed[u : u + 1]
    d_rows = dot_nt(d_normed[...].astype(BF), in_proj[...])
    d_outer = norm_backward(outer_ref[...], d_item, item_gain_ref[...])
    inner = inner_ref[...]
    gate = jax.nn.sigmoid(inner)
    d_inner = dot_nt(d_outer.astype(BF), item_w2[...]) * (gate * (1.0 + inner * (1.0 - gate)))
    d_items = dot_nt(d_inner.astype(BF), item_w1[...])
    wide = row_ref.shape[1]
    d_all = jnp.concatenate(
        [d_rows, d_items, jnp.zeros((wide - span - PAD, d_rows.shape[1]), F32)], axis=0
    ).astype(BF)
    slots = outgoing.shape[0]
    column = row_ref[0:1, :]
    chunk = slots // 4
    saves = []
    for c in range(4):
        at = pl.ds(c * chunk, chunk)
        picks = one_hot(iota((chunk, wide), 0) + c * chunk == column)
        outgoing[at, :] = dot(picks, d_all).astype(BF)
        saves.append(pltpu.make_async_copy(outgoing.at[at], outgoing_hbm.at[at], out_sems.at[c]))
        saves[-1].start()
    for save in saves:
        save.wait()


def scatter_kernel(returned_ref, row_ref, loss_ref, part_ref, hot_ref):
    rows, emb = part_ref.shape
    slots = returned_ref.shape[0]
    returned = returned_ref[...]
    picks = one_hot(iota((rows, slots), 0) == row_ref[0:1, :])
    part_ref[...] = dot(picks, returned).astype(BF)
    hot = dot(one_hot(iota((PAD, slots), 1) % SLOTS == HOT_SLOT), returned)
    hot_ref[:, 0:emb] = hot[0:1]
    hot_ref[:, emb:] = loss_ref[0:1, :]


def shards(
    history,
    item_ids,
    hot_table,
    rare_table,
    in_proj,
    pos_embed,
    norm_gain,
    w_query,
    w_key,
    w_value,
    w_out,
    out_gain,
    item_w1,
    item_w2,
    item_gain,
):
    users, hist = history.shape
    emb = hot_table.shape[1]
    rare_count = rare_table.shape[0]
    width = in_proj.shape[1]
    heads = width // HEAD_DIM
    scale = 4.0 / math.sqrt(width)
    owners = lax.axis_size(SHARD)
    towers = lax.axis_size("tower")
    near = lax.axis_size("z")
    total = users * towers * owners
    slots = owners * SLOTS
    span = users * hist
    wide = -(-(span + PAD) // 128) * 128
    swap = [(i, towers - 1 - i) for i in range(towers)]
    shape = jax.ShapeDtypeStruct
    sems = lambda n: pltpu.SemaphoreType.DMA((n,))
    like = lambda arrays: [pltpu.VMEM(a.shape, a.dtype) for a in arrays]
    exchange = functools.partial(lax.all_to_all, split_axis=0, concat_axis=0, tiled=True)

    places = (shape((8, wide), jnp.int32), shape((wide, 128), jnp.int32))
    loads = (history, item_ids.reshape(1, users), rare_table)
    request, known, row, column = pl.pallas_call(
        functools.partial(index_kernel, owners),
        out_shape=(shape((owners, 128), jnp.int32), shape((rare_count, emb), BF)) + places,
        in_specs=[HBM] * 3,
        out_specs=(VMEM, VMEM, HBM, HBM),
        scratch_shapes=like(loads + places) + [sems(5)],
        compiler_params=params(FULL - 2),
        name="index",
    )(*loads)
    asked = exchange(request, SHARD)
    served_shapes = (shape((slots, emb), BF), shape((8, slots), jnp.int32))
    served, asked_row = pl.pallas_call(
        serve_kernel,
        out_shape=served_shapes,
        in_specs=[VMEM, VMEM],
        out_specs=(VMEM, HBM),
        scratch_shapes=like(served_shapes[1:]) + [pltpu.SemaphoreType.DMA],
        compiler_params=params(24),
        name="serve",
    )(asked, known)
    fetched = exchange(served, SHARD)

    weights = (in_proj, w_query, w_key, w_value, w_out, item_w1, item_w2)
    gains = tuple(g.reshape(1, width) for g in (norm_gain, out_gain, item_gain))
    kept_shapes = (
        shape((span, width), F32),
        shape((span, width), BF),
        shape((users * heads, width), BF),
        shape((users * heads, hist), F32),
        shape((PAD, width), F32),
        shape((PAD, width), F32),
        shape((PAD, width), F32),
    )
    loads = (column, fetched, hot_table, pos_embed) + gains + weights
    vectors, *kept = pl.pallas_call(
        functools.partial(forward_kernel, users),
        out_shape=(shape((near * 2 * users, width), BF),) + kept_shapes,
        in_specs=[HBM] * len(loads),
        out_specs=(VMEM,) + (HBM,) * len(kept_shapes),
        scratch_shapes=like(loads + kept_shapes) + [sems(len(loads)), sems(len(kept_shapes))],
        compiler_params=params(FULL),
        name="forward",
    )(*loads)

    near_vectors = exchange(vectors, "z")
    spread = pl.pallas_call(
        functools.partial(arrange_kernel, users),
        out_shape=shape((owners * users, 2 * width), BF),
        in_specs=[VMEM],
        out_specs=VMEM,
        compiler_params=params(24),
        name="arrange",
    )(near_vectors)
    gathered = exchange(spread, ("x", "y"))
    swapped = lax.ppermute(gathered, "tower", swap)
    base = (lax.axis_index(SHARD) * users).astype(jnp.int32).reshape(1)

    loads = (vectors, row) + gains + tuple(kept) + weights
    outgoing, loss = pl.pallas_call(
        functools.partial(backward_kernel, users, scale),
        out_shape=(shape((slots, emb), BF), shape((8, 128), F32)),
        in_specs=[SMEM, VMEM, VMEM] + [HBM] * len(loads),
        out_specs=(HBM, VMEM),
        scratch_shapes=like(loads)
        + [
            pltpu.VMEM((slots, emb), BF),
            pltpu.VMEM((total, total), F32),
            pltpu.VMEM((span, width), F32),
            sems(len(loads)),
            sems(4),
        ],
        compiler_params=params(FULL - 4),
        name="backward",
    )(base, gathered, swapped, *loads)

    returned = exchange(outgoing, SHARD)
    part, mine = pl.pallas_call(
        scatter_kernel,
        out_shape=(shape((rare_count, emb), BF), shape((1, emb + 128), F32)),
        in_specs=[VMEM, VMEM, VMEM],
        out_specs=(VMEM, VMEM),
        compiler_params=params(24),
        name="scatter",
    )(returned, asked_row, loss)
    mine = mine + lax.ppermute(mine, "tower", swap)
    rare_grad = part.astype(F32) + lax.ppermute(part, "tower", swap).astype(F32)
    sums = exchange(jnp.broadcast_to(mine, (owners, emb + 128)), SHARD)
    return (sums[:, :emb], rare_grad, jnp.sum(sums[:, emb]) / total)


def solution(mesh):
    sizes = (mesh.shape["tower"], 4, 4, mesh.shape["shard"] // 16)
    mesh = Mesh(mesh.devices.reshape(sizes), ("tower",) + SHARD)
    return jax.shard_map(
        shards,
        mesh=mesh,
        in_specs=(
            P(("tower",) + SHARD, None),
            P(("tower",) + SHARD),
            P(),
            P(SHARD, None),
            P(),
            P(),
            P(),
            P(),
            P(),
            P(),
            P(),
            P(),
            P(),
            P(),
            P(),
        ),
        out_specs=(P(), P(SHARD, None), P()),
        check_vma=False,
    )
```

```python
import functools
import math

import jax
import jax.numpy as jnp
from jax import lax
from jax.experimental import pallas as pl
from jax.experimental.pallas import tpu as pltpu
from jax.sharding import Mesh
from jax.sharding import PartitionSpec as P

HEAD_DIM = 64
EPS = 1e-06
SLOTS = 8
HOT_SLOT = 5
SHARD = ("x", "y", "z")
PAD = 16
BF = jnp.bfloat16
F32 = jnp.float32
VMEM = pl.BlockSpec(memory_space=pltpu.VMEM)
SMEM = pl.BlockSpec(memory_space=pltpu.SMEM)
HBM = pl.BlockSpec(memory_space=pltpu.HBM)
NT = (((1,), (1,)), ((), ()))
TN = (((0,), (0,)), ((), ()))


def dot(a, b):
    return jnp.dot(a, b, preferred_element_type=F32)


def dot_nt(a, b):
    return lax.dot_general(a, b, NT, preferred_element_type=F32)


def dot_tn(a, b):
    return lax.dot_general(a, b, TN, preferred_element_type=F32)


def iota(shape, axis):
    return lax.broadcasted_iota(jnp.int32, shape, axis)


def one_hot(mask):
    return jnp.where(mask, 1.0, 0.0).astype(BF)


def params(mib):
    return pltpu.CompilerParams(vmem_limit_bytes=mib * 1024 * 1024)


def copies_of(pairs, sems):
    copies = [pltpu.make_async_copy(a, b, sems.at[i]) for i, (a, b) in enumerate(pairs)]
    for copy in copies:
        copy.start()
    return copies


def index_kernel(
    owners,
    history_hbm,
    items_hbm,
    table_hbm,
    request_ref,
    known_ref,
    row,
    column,
    history_ref,
    items_ref,
    table,
    sems,
):
    loads = copies_of(
        [(history_hbm, history_ref), (items_hbm, items_ref), (table_hbm, table)], sems
    )
    loads[0].wait()
    loads[1].wait()
    hot_count = owners
    rare_count = table.shape[0]
    users = history_ref.shape[0]
    span = row.shape[1]
    parts = [history_ref[u : u + 1, :] for u in range(users)] + [items_ref[...]]
    filled = sum(p.shape[1] for p in parts)
    ids = jnp.concatenate(parts + [jnp.full((1, span - filled), -1, jnp.int32)], axis=1)
    is_rare = ids >= hot_count
    index = ids - hot_count
    owner = jnp.where(is_rare, index // rare_count, -1)
    value = jnp.where(is_rare, index % rare_count + 1, 0).astype(F32)
    hits = iota((owners, span), 0) == owner
    before = one_hot(iota((span, span), 0) < iota((span, span), 1))
    earlier = dot(one_hot(hits), before)
    position = jnp.sum(jnp.where(hits, earlier, 0.0), axis=0, keepdims=True).astype(jnp.int32)
    places = jnp.where(
        is_rare, owner * SLOTS + position, jnp.where(ids >= 0, ids * SLOTS + HOT_SLOT, -1)
    )
    row[...] = jnp.broadcast_to(places, row.shape)
    column[...] = jnp.transpose(jnp.broadcast_to(places.astype(F32), (128, span))).astype(jnp.int32)
    order = jnp.where(hits, earlier, -1.0)
    lanes = iota(request_ref.shape, 1)
    request = jnp.zeros(request_ref.shape, F32)
    for slot in range(HOT_SLOT):
        wanted = jnp.sum(jnp.where(order == float(slot), value, 0.0), axis=1, keepdims=True)
        request = jnp.where(lanes == slot, wanted, request)
    request_ref[...] = request.astype(jnp.int32)
    loads[2].wait()
    known_ref[...] = table[...].astype(BF)


def serve_kernel(asked_ref, known_ref, served, row):
    slots = served.shape[0]
    sources = asked_ref.shape[0]
    asked = asked_ref[...]
    high = (asked // 2).astype(F32).astype(BF)
    low = (asked % 2).astype(F32).astype(BF)
    expand = one_hot(iota((slots, sources), 0) // SLOTS == iota((slots, sources), 1))
    wide = 2.0 * dot(expand, high) + dot(expand, low)
    mine = iota(wide.shape, 1) == iota(wide.shape, 0) % SLOTS
    index = jnp.sum(jnp.where(mine, wide, 0.0), axis=1, keepdims=True) - 1.0
    index = jnp.broadcast_to(index, wide.shape)
    row[...] = jnp.transpose(index)[0:8].astype(jnp.int32)
    index = index.astype(jnp.int32)
    lanes = iota(index.shape, 1)
    rows = known_ref.shape[0]
    picks = jnp.concatenate(
        [one_hot(index == lanes + 128 * j) for j in range(rows // 128)], axis=1
    )
    served[...] = dot(picks, known_ref[...]).astype(BF)


def prefetch_kernel(count, after_ref, *refs):
    copies = copies_of(zip(refs[:count], refs[count : 2 * count]), refs[2 * count])
    for copy in copies:
        copy.wait()


def head_mask(heads, width):
    return iota((heads, width), 1) // HEAD_DIM == iota((heads, width), 0)


def spread_heads(values, mask, users):
    return jnp.concatenate(
        [jnp.where(mask, values[u : u + 1], 0.0) for u in range(users)], axis=0
    ).astype(BF)


def join_heads(full, mask, users):
    heads = mask.shape[0]
    parts = [
        jnp.sum(
            jnp.where(mask, full[u * heads : (u + 1) * heads], 0.0), axis=0, keepdims=True
        )
        for u in range(users)
    ]
    return jnp.concatenate(parts + [jnp.zeros((PAD - users, full.shape[1]), F32)], axis=0)


def forward_kernel(users, *refs):
    column_of, fetched_ref, hot, pos_of, norm_gain_ref, out_gain_ref, item_gain_ref = refs[:7]
    in_proj, w_query, w_key, w_value, w_out, item_w1, item_w2 = refs[7:14]
    vectors_ref, hidden_ref, normed_ref, qk_ref, weights_ref, mixed_ref, inner_ref, outer_ref = refs[14:]
    hist, width = pos_of.shape
    heads = width // HEAD_DIM
    span = users * hist
    slots = fetched_ref.shape[0]
    column = column_of[0 : span + PAD, :]
    lanes = iota(column.shape, 1)
    picks = jnp.concatenate(
        [one_hot(column == lanes + 128 * j) for j in range(slots // 128)], axis=1
    )
    hot_picks = one_hot(column == lanes * SLOTS + HOT_SLOT)
    rows = (dot(picks, fetched_ref[...]) + dot(hot_picks, hot[...].astype(BF))).astype(BF)
    pos = pos_of[...].astype(F32)
    hidden = dot(rows[0:span], in_proj[...]) + jnp.concatenate([pos] * users, axis=0)
    hidden_ref[...] = hidden
    scale = lax.rsqrt(jnp.mean(hidden * hidden, axis=-1, keepdims=True) + EPS)
    normed = (hidden * scale * norm_gain_ref[...]).astype(BF)
    normed_ref[...] = normed
    last = jnp.concatenate(
        [normed[(u + 1) * hist - PAD : (u + 1) * hist].astype(F32)[PAD - 1 :] for u in range(users)]
        + [jnp.zeros((PAD - users, width), F32)],
        axis=0,
    ).astype(BF)
    mask = head_mask(heads, width)
    query = dot(last, w_query[...]).astype(BF).astype(F32)
    qk = dot_nt(spread_heads(query, mask, users), w_key[...]).astype(BF)
    qk_ref[...] = qk
    mixes = []
    for u in range(users):
        own = normed[u * hist : (u + 1) * hist]
        scores = dot_nt(qk[u * heads : (u + 1) * heads], own) * (1.0 / math.sqrt(HEAD_DIM))
        raised = jnp.exp(scores - jnp.max(scores, axis=1, keepdims=True))
        weights = raised / jnp.sum(raised, axis=1, keepdims=True)
        weights_ref[u * heads : (u + 1) * heads, :] = weights
        mixes.append(dot(weights.astype(BF), own))
    mixes = jnp.concatenate(mixes, axis=0).astype(BF)
    attended = join_heads(dot(mixes, w_value[...]), mask, users).astype(BF)
    hidden_last = jnp.concatenate(
        [hidden_ref[(u + 1) * hist - 1 : (u + 1) * hist, :] for u in range(users)]
        + [jnp.zeros((PAD - users, width), F32)],
        axis=0,
    )
    mixed = hidden_last + dot(attended, w_out[...])
    mixed_ref[...] = mixed
    scale = lax.rsqrt(jnp.mean(mixed * mixed, axis=-1, keepdims=True) + EPS)
    user_vec = mixed * scale * out_gain_ref[...]
    inner = dot(rows[span : span + PAD], item_w1[...])
    inner_ref[...] = inner
    outer = dot((inner * jax.nn.sigmoid(inner)).astype(BF), item_w2[...])
    outer_ref[...] = outer
    scale = lax.rsqrt(jnp.mean(outer * outer, axis=-1, keepdims=True) + EPS)
    item_vec = outer * scale * item_gain_ref[...]
    both = jnp.concatenate([user_vec[0:users], item_vec[0:users]], axis=0)
    peers = vectors_ref.shape[0] // (2 * users)
    vectors_ref[...] = jnp.concatenate([both] * peers, axis=0).astype(BF)


def arrange_kernel(users, vectors_ref, spread_ref):
    vectors = vectors_ref[...]
    rows, width = vectors.shape
    half = rows // 2
    out = iota((half, rows), 0)
    source = out // users * (2 * users) + out % users
    at = iota((half, rows), 1)
    user_rows = dot(one_hot(at == source), vectors).astype(BF)
    item_rows = dot(one_hot(at == source + users), vectors).astype(BF)
    for peer in range(spread_ref.shape[0] // half):
        spread_ref[peer * half : (peer + 1) * half, 0:width] = user_rows
        spread_ref[peer * half : (peer + 1) * half, width : 2 * width] = item_rows


def softmax_step(users, scale, base, parts, vectors, logits):
    rows, width = parts[0].shape
    width //= 2
    total = rows * len(parts)
    chunk = 256
    tops = [jnp.full((1, rows), -jnp.inf, F32) for _ in parts]
    for i, items in enumerate(parts):
        for c in range(0, rows, chunk):
            some = items[c : c + chunk, width:]
            for j, part in enumerate(parts):
                here = scale * dot_nt(some, part[:, :width])
                logits[i * rows + c : i * rows + c + chunk, j * rows : (j + 1) * rows] = here
                tops[j] = jnp.maximum(tops[j], jnp.max(here, axis=0, keepdims=True))
    top = jnp.concatenate(tops, axis=1)
    count = jnp.zeros((1, total), F32)
    for c in range(0, total, chunk):
        here = logits[c : c + chunk, :]
        count = count + jnp.sum(jnp.exp(here - top), axis=0, keepdims=True)
    normalizer = top + jnp.log(count)
    none = jnp.zeros((PAD - users, width), F32)
    user_vec = jnp.concatenate([vectors[0:users], none], axis=0).astype(BF)
    item_vec = jnp.concatenate([vectors[users : 2 * users], none], axis=0).astype(BF)
    lines = iota((PAD, total), 0)
    valid = lines < users
    target = iota((PAD, total), 1) == lines + base
    one = jnp.where(target, 1.0, 0.0)

    def against(vec, at):
        return scale * jnp.concatenate([dot_nt(vec, p[:, at]) for p in parts], axis=1)

    def pulled(slope, at):
        sums = [dot(slope[:, j * rows : (j + 1) * rows], p[:, at]) for j, p in enumerate(parts)]
        return (scale * sum(sums)).astype(BF).astype(F32)

    of_users, of_items = slice(0, width), slice(width, 2 * width)
    item_logits = against(item_vec, of_users)
    slope = jnp.where(valid, jnp.exp(item_logits - normalizer) - one, 0.0).astype(BF)
    d_item = pulled(slope, of_users)
    user_logits = against(user_vec, of_items)
    top = jnp.max(user_logits, axis=1, keepdims=True)
    normalizer = top + jnp.log(jnp.sum(jnp.exp(user_logits - top), axis=1, keepdims=True))
    slope = jnp.where(valid, jnp.exp(user_logits - normalizer) - one, 0.0).astype(BF)
    d_user = pulled(slope, of_items)
    each = jnp.sum(jnp.where(valid & target, normalizer - user_logits, 0.0), axis=1, keepdims=True)
    return d_user, d_item, jnp.sum(each, axis=0, keepdims=True)


def norm_backward(values, cotangent, gain):
    inverse = lax.rsqrt(jnp.mean(values * values, axis=-1, keepdims=True) + EPS)
    pulled = cotangent * gain
    along = jnp.mean(pulled * values, axis=-1, keepdims=True)
    return inverse * pulled - values * (inverse * inverse * inverse * along)


def backward_kernel(
    users,
    loss_scale,
    base_ref,
    gathered_ref,
    swapped_ref,
    vectors_ref,
    row_ref,
    *refs,
):
    norm_gain_ref, out_gain_ref, item_gain_ref = refs[:3]
    hidden_ref, normed_ref, qk_ref, weights_ref, mixed_ref, inner_ref, outer_ref = refs[3:10]
    in_proj, w_query, w_key, w_value, w_out, item_w1, item_w2 = refs[10:17]
    outgoing, loss_ref, logits, d_normed = refs[17:]
    vectors = vectors_ref[0:PAD, :].astype(F32)
    d_user, d_item, loss = softmax_step(
        users, loss_scale, base_ref[0], (gathered_ref, swapped_ref), vectors, logits
    )
    loss_ref[...] = jnp.broadcast_to(loss, loss_ref.shape)
    span, width = hidden_ref.shape
    hist = span // users
    heads = width // HEAD_DIM
    mask = head_mask(heads, width)
    d_mixed = norm_backward(mixed_ref[...], d_user, out_gain_ref[...])
    d_attended = dot_nt(d_mixed.astype(BF), w_out[...])
    d_mixes = dot_nt(spread_heads(d_attended, mask, users), w_value[...]).astype(BF)
    d_qk = []
    for u in range(users):
        own = normed_ref[u * hist : (u + 1) * hist, :]
        weights = weights_ref[u * heads : (u + 1) * heads, :]
        pulled = d_mixes[u * heads : (u + 1) * heads]
        d_weights = dot_nt(pulled, own)
        d_scores = weights * (d_weights - jnp.sum(weights * d_weights, axis=1, keepdims=True))
        d_scores = (d_scores * (1.0 / math.sqrt(HEAD_DIM))).astype(BF)
        d_normed[u * hist : (u + 1) * hist, :] = dot_tn(weights.astype(BF), pulled) + dot_tn(
            d_scores, qk_ref[u * heads : (u + 1) * heads, :]
        )
        d_qk.append(dot(d_scores, own))
    d_qk = jnp.concatenate(d_qk, axis=0).astype(BF)
    d_query = join_heads(dot(d_qk, w_key[...]), mask, users).astype(BF)
    d_last = dot_nt(d_query, w_query[...])
    for u in range(users):
        at = slice((u + 1) * hist - 1, (u + 1) * hist)
        d_normed[at, :] = d_normed[at, :] + d_last[u : u + 1]
    d_normed[...] = norm_backward(hidden_ref[...], d_normed[...], norm_gain_ref[...])
    for u in range(users):
        at = slice((u + 1) * hist - 1, (u + 1) * hist)
        d_normed[at, :] = d_normed[at, :] + d_mixed[u : u + 1]
    d_rows = dot_nt(d_normed[...].astype(BF), in_proj[...])
    d_outer = norm_backward(outer_ref[...], d_item, item_gain_ref[...])
    inner = inner_ref[...]
    gate = jax.nn.sigmoid(inner)
    d_inner = dot_nt(d_outer.astype(BF), item_w2[...]) * (gate * (1.0 + inner * (1.0 - gate)))
    d_items = dot_nt(d_inner.astype(BF), item_w1[...])
    wide = row_ref.shape[1]
    d_all = jnp.concatenate(
        [d_rows, d_items, jnp.zeros((wide - span - PAD, d_rows.shape[1]), F32)], axis=0
    ).astype(BF)
    slots = outgoing.shape[0]
    column = row_ref[0:1, :]
    picks = one_hot(iota((slots, wide), 0) == column)
    outgoing[...] = dot(picks, d_all).astype(BF)


def scatter_kernel(returned_ref, row_ref, loss_ref, part_ref, hot_ref):
    rows, emb = part_ref.shape
    slots = returned_ref.shape[0]
    returned = returned_ref[...]
    picks = one_hot(iota((rows, slots), 0) == row_ref[0:1, :])
    part_ref[...] = dot(picks, returned).astype(BF)
    hot = dot(one_hot(iota((PAD, slots), 1) % SLOTS == HOT_SLOT), returned)
    hot_ref[:, 0:emb] = hot[0:1]
    hot_ref[:, emb:] = loss_ref[0:1, :]


def shards(
    history,
    item_ids,
    hot_table,
    rare_table,
    in_proj,
    pos_embed,
    norm_gain,
    w_query,
    w_key,
    w_value,
    w_out,
    out_gain,
    item_w1,
    item_w2,
    item_gain,
):
    users, hist = history.shape
    emb = hot_table.shape[1]
    rare_count = rare_table.shape[0]
    width = in_proj.shape[1]
    heads = width // HEAD_DIM
    scale = 4.0 / math.sqrt(width)
    owners = lax.axis_size(SHARD)
    towers = lax.axis_size("tower")
    near = lax.axis_size("z")
    total = users * towers * owners
    slots = owners * SLOTS
    span = users * hist
    wide = -(-(span + PAD) // 128) * 128
    swap = [(i, towers - 1 - i) for i in range(towers)]
    shape = jax.ShapeDtypeStruct
    sems = lambda n: pltpu.SemaphoreType.DMA((n,))
    in_hbm = lambda a: pltpu.with_memory_space_constraint(a, pltpu.HBM)
    in_vmem = lambda a: pltpu.with_memory_space_constraint(a, pltpu.VMEM)
    like = lambda arrays: [pltpu.VMEM(a.shape, a.dtype) for a in arrays]
    exchange = functools.partial(lax.all_to_all, split_axis=0, concat_axis=0, tiled=True)

    loads = (history, item_ids.reshape(1, users), rare_table)
    request, known, row, column = pl.pallas_call(
        functools.partial(index_kernel, owners),
        out_shape=(
            shape((owners, 128), jnp.int32),
            pltpu.VMEM((rare_count, emb), BF),
            pltpu.VMEM((8, wide), jnp.int32),
            pltpu.VMEM((wide, 128), jnp.int32),
        ),
        in_specs=[HBM] * 3,
        out_specs=(VMEM,) * 4,
        scratch_shapes=like(loads) + [sems(3)],
        compiler_params=params(24),
        name="index",
    )(*map(in_hbm, loads))
    asked = exchange(request, SHARD)
    served, asked_row = pl.pallas_call(
        serve_kernel,
        out_shape=(shape((slots, emb), BF), pltpu.VMEM((8, slots), jnp.int32)),
        in_specs=[VMEM, VMEM],
        out_specs=(VMEM, VMEM),
        compiler_params=params(24),
        name="serve",
    )(asked, in_vmem(known))
    fetched = exchange(served, SHARD)

    gains = tuple(g.reshape(1, width) for g in (norm_gain, out_gain, item_gain))
    loads = (in_proj, w_query, w_key, w_value, w_out, item_w1, item_w2, hot_table, pos_embed) + gains
    ready = pl.pallas_call(
        functools.partial(prefetch_kernel, len(loads)),
        out_shape=tuple(pltpu.VMEM(a.shape, a.dtype) for a in loads),
        in_specs=[pl.BlockSpec(memory_space=pl.ANY)] + [HBM] * len(loads),
        out_specs=(VMEM,) * len(loads),
        scratch_shapes=[sems(len(loads))],
        compiler_params=params(8),
        name="prefetch",
    )(served, *map(in_hbm, loads))
    weights, (hot_ready, pos_ready), gains = ready[:7], ready[7:9], ready[9:]

    vectors, *kept = pl.pallas_call(
        functools.partial(forward_kernel, users),
        out_shape=(
            pltpu.VMEM((near * 2 * users, width), BF),
            pltpu.VMEM((span, width), F32),
            pltpu.VMEM((span, width), BF),
            pltpu.VMEM((users * heads, width), BF),
            pltpu.VMEM((users * heads, hist), F32),
            pltpu.VMEM((PAD, width), F32),
            pltpu.VMEM((PAD, width), F32),
            pltpu.VMEM((PAD, width), F32),
        ),
        in_specs=[VMEM] * 14,
        out_specs=(VMEM,) * 8,
        compiler_params=params(24),
        name="forward",
    )(in_vmem(column), fetched, *map(in_vmem, (hot_ready, pos_ready, *gains, *weights)))

    near_vectors = exchange(vectors, "z")
    spread = pl.pallas_call(
        functools.partial(arrange_kernel, users),
        out_shape=shape((owners * users, 2 * width), BF),
        in_specs=[VMEM],
        out_specs=VMEM,
        compiler_params=params(24),
        name="arrange",
    )(near_vectors)
    gathered = exchange(spread, ("x", "y"))
    swapped = lax.ppermute(gathered, "tower", swap)
    base = (lax.axis_index(SHARD) * users).astype(jnp.int32).reshape(1)

    loads = (vectors, row) + tuple(gains) + tuple(kept) + tuple(weights)
    outgoing, loss = pl.pallas_call(
        functools.partial(backward_kernel, users, scale),
        out_shape=(shape((slots, emb), BF), pltpu.VMEM((8, 128), F32)),
        in_specs=[SMEM] + [VMEM] * (2 + len(loads)),
        out_specs=(VMEM, VMEM),
        scratch_shapes=[pltpu.VMEM((total, total), F32), pltpu.VMEM((span, width), F32)],
        compiler_params=params(24),
        name="backward",
    )(base, gathered, swapped, *map(in_vmem, loads))

    returned = exchange(outgoing, SHARD)
    part, mine = pl.pallas_call(
        scatter_kernel,
        out_shape=(shape((rare_count, emb), BF), shape((1, emb + 128), F32)),
        in_specs=[VMEM, VMEM, VMEM],
        out_specs=(VMEM, VMEM),
        compiler_params=params(24),
        name="scatter",
    )(returned, in_vmem(asked_row), in_vmem(loss))
    mine = mine + lax.ppermute(mine, "tower", swap)
    rare_grad = part.astype(F32) + lax.ppermute(part, "tower", swap).astype(F32)
    sums = exchange(jnp.broadcast_to(mine, (owners, emb + 128)), SHARD)
    return (sums[:, :emb], rare_grad, jnp.sum(sums[:, emb]) / total)


def solution(mesh):
    sizes = (mesh.shape["tower"], 4, 4, mesh.shape["shard"] // 16)
    mesh = Mesh(mesh.devices.reshape(sizes), ("tower",) + SHARD)
    return jax.shard_map(
        shards,
        mesh=mesh,
        in_specs=(
            P(("tower",) + SHARD, None),
            P(("tower",) + SHARD),
            P(),
            P(SHARD, None),
            P(),
            P(),
            P(),
            P(),
            P(),
            P(),
            P(),
            P(),
            P(),
            P(),
            P(),
        ),
        out_specs=(P(), P(SHARD, None), P()),
        check_vma=False,
    )
```

```python
import functools
import math

import jax
import jax.numpy as jnp
from jax import lax
from jax.experimental import pallas as pl
from jax.experimental.pallas import tpu as pltpu
from jax.sharding import Mesh
from jax.sharding import PartitionSpec as P

HEAD_DIM = 64
EPS = 1e-06
SLOTS = 8
HOT_SLOT = 5
SHARD = ("x", "y", "z")
PAD = 16
BF = jnp.bfloat16
F32 = jnp.float32
VMEM = pl.BlockSpec(memory_space=pltpu.VMEM)
SMEM = pl.BlockSpec(memory_space=pltpu.SMEM)
HBM = pl.BlockSpec(memory_space=pltpu.HBM)
NT = (((1,), (1,)), ((), ()))
TN = (((0,), (0,)), ((), ()))


def dot(a, b):
    return jnp.dot(a, b, preferred_element_type=F32)


def dot_nt(a, b):
    return lax.dot_general(a, b, NT, preferred_element_type=F32)


def dot_tn(a, b):
    return lax.dot_general(a, b, TN, preferred_element_type=F32)


def iota(shape, axis):
    return lax.broadcasted_iota(jnp.int32, shape, axis)


def one_hot(mask):
    return jnp.where(mask, 1.0, 0.0).astype(BF)


def params(mib):
    return pltpu.CompilerParams(vmem_limit_bytes=mib * 1024 * 1024)


def copies_of(pairs, sems):
    copies = [pltpu.make_async_copy(a, b, sems.at[i]) for i, (a, b) in enumerate(pairs)]
    for copy in copies:
        copy.start()
    return copies


def index_kernel(
    owners,
    history_hbm,
    items_hbm,
    table_hbm,
    request_ref,
    known_ref,
    row_hbm,
    column_hbm,
    history_ref,
    items_ref,
    table,
    row,
    column,
    sems,
):
    loads = copies_of(
        [(history_hbm, history_ref), (items_hbm, items_ref), (table_hbm, table)], sems
    )
    loads[0].wait()
    loads[1].wait()
    hot_count = owners
    rare_count = table.shape[0]
    users = history_ref.shape[0]
    span = row.shape[1]
    parts = [history_ref[u : u + 1, :] for u in range(users)] + [items_ref[...]]
    filled = sum(p.shape[1] for p in parts)
    ids = jnp.concatenate(parts + [jnp.full((1, span - filled), -1, jnp.int32)], axis=1)
    is_rare = ids >= hot_count
    index = ids - hot_count
    owner = jnp.where(is_rare, index // rare_count, -1)
    value = jnp.where(is_rare, index % rare_count + 1, 0).astype(F32)
    hits = iota((owners, span), 0) == owner
    before = one_hot(iota((span, span), 0) < iota((span, span), 1))
    earlier = dot(one_hot(hits), before)
    position = jnp.sum(jnp.where(hits, earlier, 0.0), axis=0, keepdims=True).astype(jnp.int32)
    places = jnp.where(
        is_rare, owner * SLOTS + position, jnp.where(ids >= 0, ids * SLOTS + HOT_SLOT, -1)
    )
    row[...] = jnp.broadcast_to(places, row.shape)
    column[...] = jnp.transpose(jnp.broadcast_to(places.astype(F32), (128, span))).astype(jnp.int32)
    saves = copies_of([(row, row_hbm), (column, column_hbm)], sems.at[pl.ds(3, 2)])
    order = jnp.where(hits, earlier, -1.0)
    lanes = iota(request_ref.shape, 1)
    request = jnp.zeros(request_ref.shape, F32)
    for slot in range(HOT_SLOT):
        wanted = jnp.sum(jnp.where(order == float(slot), value, 0.0), axis=1, keepdims=True)
        request = jnp.where(lanes == slot, wanted, request)
    request_ref[...] = request.astype(jnp.int32)
    loads[2].wait()
    known_ref[...] = table[...].astype(BF)
    for save in saves:
        save.wait()


def serve_kernel(asked_ref, known_ref, served, row_hbm, row, sem):
    slots = served.shape[0]
    sources = asked_ref.shape[0]
    asked = asked_ref[...]
    high = (asked // 2).astype(F32).astype(BF)
    low = (asked % 2).astype(F32).astype(BF)
    expand = one_hot(iota((slots, sources), 0) // SLOTS == iota((slots, sources), 1))
    wide = 2.0 * dot(expand, high) + dot(expand, low)
    mine = iota(wide.shape, 1) == iota(wide.shape, 0) % SLOTS
    index = jnp.sum(jnp.where(mine, wide, 0.0), axis=1, keepdims=True) - 1.0
    index = jnp.broadcast_to(index, wide.shape)
    row[...] = jnp.transpose(index)[0:8].astype(jnp.int32)
    save = pltpu.make_async_copy(row, row_hbm, sem)
    save.start()
    index = index.astype(jnp.int32)
    lanes = iota(index.shape, 1)
    rows = known_ref.shape[0]
    picks = jnp.concatenate(
        [one_hot(index == lanes + 128 * j) for j in range(rows // 128)], axis=1
    )
    served[...] = dot(picks, known_ref[...]).astype(BF)
    save.wait()


def head_mask(heads, width):
    return iota((heads, width), 1) // HEAD_DIM == iota((heads, width), 0)


def spread_heads(values, mask, users):
    return jnp.concatenate(
        [jnp.where(mask, values[u : u + 1], 0.0) for u in range(users)], axis=0
    ).astype(BF)


def join_heads(full, mask, users):
    heads = mask.shape[0]
    parts = [
        jnp.sum(
            jnp.where(mask, full[u * heads : (u + 1) * heads], 0.0), axis=0, keepdims=True
        )
        for u in range(users)
    ]
    return jnp.concatenate(parts + [jnp.zeros((PAD - users, full.shape[1]), F32)], axis=0)


def look_up(column, fetched, hot):
    lanes = iota(column.shape, 1)
    slots = fetched.shape[0]
    picks = jnp.concatenate(
        [one_hot(column == lanes + 128 * j) for j in range(slots // 128)], axis=1
    )
    hot_picks = one_hot(column == lanes * SLOTS + HOT_SLOT)
    return (dot(picks, fetched[...]) + dot(hot_picks, hot[...].astype(BF))).astype(BF)


def item_forward_kernel(users, *refs):
    fetched_ref, sources, refs = refs[0], refs[1:6], refs[6:]
    vectors_ref, kept_hbm, refs = refs[0], refs[1:3], refs[3:]
    targets, kept, (in_sems, out_sems) = refs[:5], refs[5:7], refs[7:]
    column_of, hot, gain, item_w1, item_w2 = targets
    inner_ref, outer_ref = kept
    span = sources[0].shape[0]
    sources = (sources[0].at[pl.ds(span - 128, PAD)],) + tuple(sources[1:])
    copies = copies_of(zip(sources, targets), in_sems)
    copies[0].wait()
    copies[1].wait()
    rows = look_up(column_of[...], fetched_ref, hot)
    copies[2].wait()
    copies[3].wait()
    inner = dot(rows, item_w1[...])
    inner_ref[...] = inner
    gated = (inner * jax.nn.sigmoid(inner)).astype(BF)
    copies[4].wait()
    outer = dot(gated, item_w2[...])
    outer_ref[...] = outer
    saves = copies_of(zip(kept, kept_hbm), out_sems)
    scale = lax.rsqrt(jnp.mean(outer * outer, axis=-1, keepdims=True) + EPS)
    vectors = jnp.where(iota(outer.shape, 0) < users, outer * scale * gain[...], 0.0)
    peers = vectors_ref.shape[0] // 8
    vectors_ref[...] = jnp.concatenate([vectors[0:8]] * peers, axis=0).astype(BF)
    for save in saves:
        save.wait()


def user_forward_kernel(users, *refs):
    fetched_ref, sources, refs = refs[0], refs[1:11], refs[11:]
    vectors_ref, kept_hbm, refs = refs[0], refs[1:6], refs[6:]
    targets, kept, (in_sems, out_sems) = refs[:10], refs[10:15], refs[15:]
    column_of, hot, pos_of, norm_gain_ref, out_gain_ref = targets[:5]
    in_proj, w_query, w_key, w_value, w_out = targets[5:]
    hidden_ref, normed_ref, qk_ref, weights_ref, mixed_ref = kept
    copies = copies_of(zip(sources, targets), in_sems)
    saves = [
        pltpu.make_async_copy(a, b, out_sems.at[i]) for i, (a, b) in enumerate(zip(kept, kept_hbm))
    ]
    hist, width = pos_of.shape
    heads = width // HEAD_DIM
    span = users * hist
    copies[0].wait()
    copies[1].wait()
    rows = look_up(column_of[0:span, :], fetched_ref, hot)
    for copy in copies[2:6]:
        copy.wait()
    pos = pos_of[...].astype(F32)
    hidden = dot(rows, in_proj[...]) + jnp.concatenate([pos] * users, axis=0)
    hidden_ref[...] = hidden
    saves[0].start()
    scale = lax.rsqrt(jnp.mean(hidden * hidden, axis=-1, keepdims=True) + EPS)
    normed = (hidden * scale * norm_gain_ref[...]).astype(BF)
    normed_ref[...] = normed
    saves[1].start()
    last = jnp.concatenate(
        [normed[(u + 1) * hist - PAD : (u + 1) * hist].astype(F32)[PAD - 1 :] for u in range(users)]
        + [jnp.zeros((PAD - users, width), F32)],
        axis=0,
    ).astype(BF)
    mask = head_mask(heads, width)
    copies[6].wait()
    query = dot(last, w_query[...]).astype(BF).astype(F32)
    copies[7].wait()
    qk = dot_nt(spread_heads(query, mask, users), w_key[...]).astype(BF)
    qk_ref[...] = qk
    saves[2].start()
    mixes = []
    for u in range(users):
        own = normed[u * hist : (u + 1) * hist]
        scores = dot_nt(qk[u * heads : (u + 1) * heads], own) * (1.0 / math.sqrt(HEAD_DIM))
        raised = jnp.exp(scores - jnp.max(scores, axis=1, keepdims=True))
        weights = raised / jnp.sum(raised, axis=1, keepdims=True)
        weights_ref[u * heads : (u + 1) * heads, :] = weights
        mixes.append(dot(weights.astype(BF), own))
    saves[3].start()
    mixes = jnp.concatenate(mixes, axis=0).astype(BF)
    copies[8].wait()
    attended = join_heads(dot(mixes, w_value[...]), mask, users).astype(BF)
    copies[9].wait()
    hidden_last = jnp.concatenate(
        [hidden[(u + 1) * hist - 1 : (u + 1) * hist] for u in range(users)]
        + [jnp.zeros((PAD - users, width), F32)],
        axis=0,
    )
    mixed = hidden_last + dot(attended, w_out[...])
    mixed_ref[...] = mixed
    saves[4].start()
    scale = lax.rsqrt(jnp.mean(mixed * mixed, axis=-1, keepdims=True) + EPS)
    vectors_ref[...] = (mixed * scale * out_gain_ref[...]).astype(BF)
    for save in saves:
        save.wait()


def arrange_kernel(users, near, near_ref, vectors_ref, spread_ref):
    total, width = spread_ref.shape
    block = near * users + 8
    at = iota((total, near * 8), 0) % block
    source = jnp.where(at < near * users, at // users * 8 + at % users, -1)
    item_rows = dot(one_hot(iota((total, near * 8), 1) == source), near_ref[...])
    at = iota((total, PAD), 0) % block
    source = jnp.where((at >= near * users) & (at < (near + 1) * users), at - near * users, -1)
    user_rows = dot(one_hot(iota((total, PAD), 1) == source), vectors_ref[...])
    spread_ref[...] = (item_rows + user_rows).astype(BF)


def softmax_kernel(
    users, near, scale, place_ref, gathered_ref, swapped_ref, d_user_ref, d_part_ref, loss_ref
):
    rows, width = gathered_ref.shape
    items = near * users
    block = items + 8
    blocks = rows // block
    mine, plane = place_ref[0], place_ref[1]
    own, other = gathered_ref[...], swapped_ref[...]

    def source_of_users(shape):
        line = iota(shape, 0)
        return line // users * block + items + line % users

    group = (blocks * users, rows)
    at_group = iota(group, 1) == source_of_users(group)
    line = (near * 8, rows)
    at_line = (iota(line, 0) % 8 < users) & (
        iota(line, 1) == mine * block + iota(line, 0) // 8 * users + iota(line, 0) % 8
    )
    self = (PAD, rows)
    at_self = (iota(self, 0) < users) & (iota(self, 1) == mine * block + items + iota(self, 0))
    picked = dot(jnp.concatenate([one_hot(at_group), one_hot(at_line), one_hot(at_self)], axis=0), own)
    own_users = picked[0 : blocks * users].astype(BF)
    line_items = picked[blocks * users : blocks * users + near * 8].astype(BF)
    self_users = picked[blocks * users + near * 8 :].astype(BF)
    other_users = dot(one_hot(at_group), other).astype(BF)
    group_users = jnp.concatenate([own_users, other_users], axis=0)
    total = 2 * blocks * users

    valid = iota((rows, total), 0) % block < items
    first = jnp.where(valid, scale * dot_nt(own, group_users), -jnp.inf)
    second = jnp.where(valid, scale * dot_nt(other, group_users), -jnp.inf)
    top = jnp.maximum(
        jnp.max(first, axis=0, keepdims=True), jnp.max(second, axis=0, keepdims=True)
    )
    count = jnp.sum(jnp.exp(first - top), axis=0, keepdims=True) + jnp.sum(
        jnp.exp(second - top), axis=0, keepdims=True
    )
    normalizer = top + jnp.log(count)
    shape = (near * 8, total)
    which = iota(shape, 0)
    target = (which // 8 == plane) & (iota(shape, 1) == mine * users + which % 8)
    slope = jnp.exp(scale * dot_nt(line_items, group_users) - normalizer)
    slope = jnp.where(which % 8 < users, slope - jnp.where(target, 1.0, 0.0), 0.0).astype(BF)
    d_part_ref[...] = (scale * dot(slope, group_users)).astype(BF)

    shape = (PAD, rows)
    lanes = iota(shape, 1)
    real = lanes % block < items
    valid = iota(shape, 0) < users
    target = lanes == mine * block + plane * users + iota(shape, 0)
    first = jnp.where(real, scale * dot_nt(self_users, own), -jnp.inf)
    second = jnp.where(real, scale * dot_nt(self_users, other), -jnp.inf)
    top = jnp.maximum(
        jnp.max(first, axis=1, keepdims=True), jnp.max(second, axis=1, keepdims=True)
    )
    count = jnp.sum(jnp.exp(first - top), axis=1, keepdims=True) + jnp.sum(
        jnp.exp(second - top), axis=1, keepdims=True
    )
    normalizer = top + jnp.log(count)
    slope = jnp.exp(first - normalizer) - jnp.where(target, 1.0, 0.0)
    d_user = dot(jnp.where(valid, slope, 0.0).astype(BF), own)
    slope = jnp.exp(second - normalizer)
    d_user = d_user + dot(jnp.where(valid, slope, 0.0).astype(BF), other)
    d_user_ref[...] = (scale * d_user).astype(BF).astype(F32)
    each = jnp.sum(jnp.where(valid & target, normalizer - first, 0.0), axis=1, keepdims=True)
    loss_ref[...] = jnp.broadcast_to(jnp.sum(each, axis=0, keepdims=True), loss_ref.shape)


def norm_backward(values, cotangent, gain):
    inverse = lax.rsqrt(jnp.mean(values * values, axis=-1, keepdims=True) + EPS)
    pulled = cotangent * gain
    along = jnp.mean(pulled * values, axis=-1, keepdims=True)
    return inverse * pulled - values * (inverse * inverse * inverse * along)


def user_backward_kernel(users, d_user_ref, *refs):
    sources, d_rows_ref, refs = refs[:12], refs[12], refs[13:]
    targets, (d_normed, sems) = refs[:12], refs[12:]
    mixed_ref, out_gain_ref, w_out, w_value, normed_ref, weights_ref, qk_ref = targets[:7]
    w_key, w_query, hidden_ref, norm_gain_ref, in_proj = targets[7:]
    copies = copies_of(zip(sources, targets), sems)
    span, width = hidden_ref.shape
    hist = span // users
    heads = width // HEAD_DIM
    mask = head_mask(heads, width)
    for copy in copies[:3]:
        copy.wait()
    d_mixed = norm_backward(mixed_ref[...], d_user_ref[...], out_gain_ref[...])
    d_attended = dot_nt(d_mixed.astype(BF), w_out[...])
    copies[3].wait()
    d_mixes = dot_nt(spread_heads(d_attended, mask, users), w_value[...]).astype(BF)
    for copy in copies[4:7]:
        copy.wait()
    d_qk = []
    for u in range(users):
        own = normed_ref[u * hist : (u + 1) * hist, :]
        weights = weights_ref[u * heads : (u + 1) * heads, :]
        pulled = d_mixes[u * heads : (u + 1) * heads]
        d_weights = dot_nt(pulled, own)
        d_scores = weights * (d_weights - jnp.sum(weights * d_weights, axis=1, keepdims=True))
        d_scores = (d_scores * (1.0 / math.sqrt(HEAD_DIM))).astype(BF)
        d_normed[u * hist : (u + 1) * hist, :] = dot_tn(weights.astype(BF), pulled) + dot_tn(
            d_scores, qk_ref[u * heads : (u + 1) * heads, :]
        )
        d_qk.append(dot(d_scores, own))
    d_qk = jnp.concatenate(d_qk, axis=0).astype(BF)
    copies[7].wait()
    d_query = join_heads(dot(d_qk, w_key[...]), mask, users).astype(BF)
    copies[8].wait()
    d_last = dot_nt(d_query, w_query[...])
    for u in range(users):
        at = slice((u + 1) * hist - 1, (u + 1) * hist)
        d_normed[at, :] = d_normed[at, :] + d_last[u : u + 1]
    copies[9].wait()
    copies[10].wait()
    d_normed[...] = norm_backward(hidden_ref[...], d_normed[...], norm_gain_ref[...])
    for u in range(users):
        at = slice((u + 1) * hist - 1, (u + 1) * hist)
        d_normed[at, :] = d_normed[at, :] + d_mixed[u : u + 1]
    copies[11].wait()
    d_rows_ref[...] = dot_nt(d_normed[...].astype(BF), in_proj[...]).astype(BF)


def item_backward_kernel(users, parts_ref, d_rows_ref, *refs):
    sources, outgoing, refs = refs[:6], refs[6], refs[7:]
    targets, sems = refs[:6], refs[6]
    row_ref, gain, outer_ref, inner_ref, item_w2, item_w1 = targets
    copies = copies_of(zip(sources, targets), sems)
    slots = outgoing.shape[0]
    span = d_rows_ref.shape[0]
    wide = row_ref.shape[1]
    peers = parts_ref.shape[0]
    shape = (PAD, peers)
    added = (iota(shape, 1) % 8 == iota(shape, 0)) & (iota(shape, 0) < users)
    d_item = dot(one_hot(added), parts_ref[...]).astype(BF).astype(F32)
    copies[0].wait()
    picks = one_hot(iota((slots, wide), 0) == row_ref[0:1, :])
    total = dot(picks[:, 0:span], d_rows_ref[...])
    copies[1].wait()
    copies[2].wait()
    d_outer = norm_backward(outer_ref[...], d_item, gain[...])
    copies[3].wait()
    inner = inner_ref[...]
    gate = jax.nn.sigmoid(inner)
    copies[4].wait()
    d_inner = dot_nt(d_outer.astype(BF), item_w2[...]) * (gate * (1.0 + inner * (1.0 - gate)))
    copies[5].wait()
    d_items = dot_nt(d_inner.astype(BF), item_w1[...])
    d_items = jnp.concatenate(
        [d_items, jnp.zeros((wide - span - PAD, d_items.shape[1]), F32)], axis=0
    ).astype(BF)
    outgoing[...] = (total + dot(picks[:, span:], d_items)).astype(BF)


def finish_kernel(total, sums_ref, hot_ref, loss_ref):
    emb = hot_ref.shape[1]
    sums = sums_ref[...]
    hot_ref[...] = sums[:, 0:emb]
    loss_ref[...] = jnp.sum(sums[:, emb : emb + 1], axis=0, keepdims=True) / total


def scatter_kernel(returned_ref, row_ref, loss_ref, part_ref, hot_ref):
    rows, emb = part_ref.shape
    slots = returned_ref.shape[0]
    returned = returned_ref[...]
    picks = one_hot(iota((rows, slots), 0) == row_ref[0:1, :])
    part_ref[...] = dot(picks, returned).astype(BF)
    hot = dot(one_hot(iota((PAD, slots), 1) % SLOTS == HOT_SLOT), returned)
    hot_ref[:, 0:emb] = hot[0:1]
    hot_ref[:, emb:] = loss_ref[0:1, :]


def shards(
    history,
    item_ids,
    hot_table,
    rare_table,
    in_proj,
    pos_embed,
    norm_gain,
    w_query,
    w_key,
    w_value,
    w_out,
    out_gain,
    item_w1,
    item_w2,
    item_gain,
):
    users, hist = history.shape
    emb = hot_table.shape[1]
    rare_count = rare_table.shape[0]
    width = in_proj.shape[1]
    heads = width // HEAD_DIM
    scale = 4.0 / math.sqrt(width)
    owners = lax.axis_size(SHARD)
    towers = lax.axis_size("tower")
    near = lax.axis_size("z")
    total = users * towers * owners
    slots = owners * SLOTS
    span = users * hist
    wide = -(-(span + PAD) // 128) * 128
    swap = [(i, towers - 1 - i) for i in range(towers)]
    shape = jax.ShapeDtypeStruct
    sems = lambda n: pltpu.SemaphoreType.DMA((n,))
    hbm = lambda a: pltpu.HBM(a.shape, a.dtype)
    in_hbm = lambda a: pltpu.with_memory_space_constraint(a, pltpu.HBM)
    in_vmem = lambda a: pltpu.with_memory_space_constraint(a, pltpu.VMEM)
    like = lambda arrays: [pltpu.VMEM(a.shape, a.dtype) for a in arrays]
    exchange = functools.partial(lax.all_to_all, split_axis=0, concat_axis=0, tiled=True)

    places = (shape((8, wide), jnp.int32), shape((wide, 128), jnp.int32))
    loads = (history, item_ids.reshape(1, users), rare_table)
    request, known, row, column = pl.pallas_call(
        functools.partial(index_kernel, owners),
        out_shape=(
            shape((owners, 128), jnp.int32),
            pltpu.VMEM((rare_count, emb), BF),
            *map(hbm, places),
        ),
        in_specs=[HBM] * 3,
        out_specs=(VMEM, VMEM, HBM, HBM),
        scratch_shapes=like(loads + places) + [sems(5)],
        compiler_params=params(24),
        name="index",
    )(*map(in_hbm, loads))
    asked = exchange(request, SHARD)
    served, asked_row = pl.pallas_call(
        serve_kernel,
        out_shape=(shape((slots, emb), BF), pltpu.HBM((8, slots), jnp.int32)),
        in_specs=[VMEM, VMEM],
        out_specs=(VMEM, HBM),
        scratch_shapes=[pltpu.VMEM((8, slots), jnp.int32), pltpu.SemaphoreType.DMA],
        compiler_params=params(24),
        name="serve",
    )(asked, in_vmem(known))
    fetched = exchange(served, SHARD)

    norm_gain, out_gain, item_gain = (g.reshape(1, width) for g in (norm_gain, out_gain, item_gain))
    loads = (column, hot_table, item_gain, item_w1, item_w2)
    kept = (shape((PAD, width), F32), shape((PAD, width), F32))
    item_vec, inner, outer = pl.pallas_call(
        functools.partial(item_forward_kernel, users),
        out_shape=(shape((near * 8, width), BF), *map(hbm, kept)),
        in_specs=[VMEM] + [HBM] * 5,
        out_specs=(VMEM, HBM, HBM),
        scratch_shapes=[pltpu.VMEM((PAD, 128), jnp.int32)]
        + like(loads[1:] + kept)
        + [sems(5), sems(2)],
        compiler_params=params(24),
        name="item_forward",
    )(fetched, *map(in_hbm, loads))
    near_items = exchange(item_vec, "z")

    loads = (column, hot_table, pos_embed, norm_gain, out_gain)
    loads += (in_proj, w_query, w_key, w_value, w_out)
    kept = (
        shape((span, width), F32),
        shape((span, width), BF),
        shape((users * heads, width), BF),
        shape((users * heads, hist), F32),
        shape((PAD, width), F32),
    )
    user_vec, hidden, normed, qk, weights, mixed = pl.pallas_call(
        functools.partial(user_forward_kernel, users),
        out_shape=(shape((PAD, width), BF), *map(hbm, kept)),
        in_specs=[VMEM] + [HBM] * len(loads),
        out_specs=(VMEM,) + (HBM,) * len(kept),
        scratch_shapes=like(loads + kept) + [sems(len(loads)), sems(len(kept))],
        compiler_params=params(40),
        name="user_forward",
    )(fetched, *map(in_hbm, loads))

    rows = owners // near * (near * users + 8)
    spread = pl.pallas_call(
        functools.partial(arrange_kernel, users, near),
        out_shape=shape((rows, width), BF),
        in_specs=[VMEM, VMEM],
        out_specs=VMEM,
        compiler_params=params(24),
        name="arrange",
    )(near_items, user_vec)
    gathered = exchange(spread, ("x", "y"))
    swapped = lax.ppermute(gathered, "tower", swap)
    place = jnp.stack([lax.axis_index(("x", "y")), lax.axis_index("z")]).astype(jnp.int32)
    d_user, d_part, loss = pl.pallas_call(
        functools.partial(softmax_kernel, users, near, scale),
        out_shape=(shape((PAD, width), F32), shape((near * 8, width), BF), shape((8, 128), F32)),
        in_specs=[SMEM, VMEM, VMEM],
        out_specs=(VMEM, VMEM, VMEM),
        compiler_params=params(32),
        name="softmax",
    )(place, gathered, swapped)
    parts = exchange(d_part, "z")

    loads = (mixed, out_gain, w_out, w_value, normed, weights, qk)
    loads += (w_key, w_query, hidden, norm_gain, in_proj)
    d_rows = pl.pallas_call(
        functools.partial(user_backward_kernel, users),
        out_shape=shape((span, emb), BF),
        in_specs=[VMEM] + [HBM] * len(loads),
        out_specs=VMEM,
        scratch_shapes=like(loads) + [pltpu.VMEM((span, width), F32), sems(len(loads))],
        compiler_params=params(40),
        name="user_backward",
    )(d_user, *map(in_hbm, loads))
    loads = (row, item_gain, outer, inner, item_w2, item_w1)
    outgoing = pl.pallas_call(
        functools.partial(item_backward_kernel, users),
        out_shape=shape((slots, emb), BF),
        in_specs=[VMEM, VMEM] + [HBM] * len(loads),
        out_specs=VMEM,
        scratch_shapes=like(loads) + [sems(len(loads))],
        compiler_params=params(32),
        name="item_backward",
    )(parts, d_rows, *map(in_hbm, loads))

    returned = exchange(outgoing, SHARD)
    part, mine = pl.pallas_call(
        scatter_kernel,
        out_shape=(shape((rare_count, emb), BF), shape((1, emb + 128), F32)),
        in_specs=[VMEM, VMEM, VMEM],
        out_specs=(VMEM, VMEM),
        compiler_params=params(24),
        name="scatter",
    )(returned, asked_row, loss)
    mine = mine + lax.ppermute(mine, "tower", swap)
    rare_grad = part.astype(F32) + lax.ppermute(part, "tower", swap).astype(F32)
    sums = exchange(jnp.broadcast_to(mine, (owners, emb + 128)), SHARD)
    hot_total, loss_total = pl.pallas_call(
        functools.partial(finish_kernel, total),
        out_shape=(shape((owners, emb), F32), shape((1, 1), F32)),
        in_specs=[VMEM],
        out_specs=(VMEM, VMEM),
        compiler_params=params(24),
        name="finish",
    )(sums)
    return (hot_total, rare_grad, loss_total[0, 0])


def solution(mesh):
    sizes = (mesh.shape["tower"], 4, 4, mesh.shape["shard"] // 16)
    mesh = Mesh(mesh.devices.reshape(sizes), ("tower",) + SHARD)
    return jax.shard_map(
        shards,
        mesh=mesh,
        in_specs=(
            P(("tower",) + SHARD, None),
            P(("tower",) + SHARD),
            P(),
            P(SHARD, None),
            P(),
            P(),
            P(),
            P(),
            P(),
            P(),
            P(),
            P(),
            P(),
            P(),
            P(),
        ),
        out_specs=(P(), P(SHARD, None), P()),
        check_vma=False,
    )
```

```python
import functools
import math

import jax
import jax.numpy as jnp
from jax import lax
from jax.experimental import pallas as pl
from jax.experimental.pallas import tpu as pltpu
from jax.sharding import Mesh
from jax.sharding import PartitionSpec as P

HEAD_DIM = 64
EPS = 1e-06
SLOTS = 8
HOT_SLOT = 5
SHARD = ("x", "y", "z")
PAD = 16
BF = jnp.bfloat16
F32 = jnp.float32
VMEM = pl.BlockSpec(memory_space=pltpu.VMEM)
SMEM = pl.BlockSpec(memory_space=pltpu.SMEM)
HBM = pl.BlockSpec(memory_space=pltpu.HBM)
NT = (((1,), (1,)), ((), ()))
TN = (((0,), (0,)), ((), ()))


def dot(a, b):
    return jnp.dot(a, b, preferred_element_type=F32)


def dot_nt(a, b):
    return lax.dot_general(a, b, NT, preferred_element_type=F32)


def dot_tn(a, b):
    return lax.dot_general(a, b, TN, preferred_element_type=F32)


def iota(shape, axis):
    return lax.broadcasted_iota(jnp.int32, shape, axis)


def one_hot(mask):
    return jnp.where(mask, 1.0, 0.0).astype(BF)


def params(mib):
    return pltpu.CompilerParams(vmem_limit_bytes=mib * 1024 * 1024)


def copies_of(pairs, sems):
    copies = [pltpu.make_async_copy(a, b, sems.at[i]) for i, (a, b) in enumerate(pairs)]
    for copy in copies:
        copy.start()
    return copies


def index_kernel(
    owners,
    history_hbm,
    items_hbm,
    table_hbm,
    request_ref,
    known_ref,
    row_hbm,
    column_hbm,
    history_ref,
    items_ref,
    table,
    row,
    column,
    sems,
):
    loads = copies_of(
        [(history_hbm, history_ref), (items_hbm, items_ref), (table_hbm, table)], sems
    )
    loads[0].wait()
    loads[1].wait()
    hot_count = owners
    rare_count = table.shape[0]
    users = history_ref.shape[0]
    span = row.shape[1]
    parts = [history_ref[u : u + 1, :] for u in range(users)] + [items_ref[...]]
    filled = sum(p.shape[1] for p in parts)
    ids = jnp.concatenate(parts + [jnp.full((1, span - filled), -1, jnp.int32)], axis=1)
    is_rare = ids >= hot_count
    index = ids - hot_count
    owner = jnp.where(is_rare, index // rare_count, -1)
    value = jnp.where(is_rare, index % rare_count + 1, 0).astype(F32)
    hits = iota((owners, span), 0) == owner
    before = one_hot(iota((span, span), 0) < iota((span, span), 1))
    earlier = dot(one_hot(hits), before)
    position = jnp.sum(jnp.where(hits, earlier, 0.0), axis=0, keepdims=True).astype(jnp.int32)
    places = jnp.where(
        is_rare, owner * SLOTS + position, jnp.where(ids >= 0, ids * SLOTS + HOT_SLOT, -1)
    )
    row[...] = jnp.broadcast_to(places, row.shape)
    column[...] = jnp.transpose(jnp.broadcast_to(places.astype(F32), (128, span))).astype(jnp.int32)
    saves = copies_of([(row, row_hbm), (column, column_hbm)], sems.at[pl.ds(3, 2)])
    order = jnp.where(hits, earlier, -1.0)
    lanes = iota(request_ref.shape, 1)
    request = jnp.zeros(request_ref.shape, F32)
    for slot in range(HOT_SLOT):
        wanted = jnp.sum(jnp.where(order == float(slot), value, 0.0), axis=1, keepdims=True)
        request = jnp.where(lanes == slot, wanted, request)
    request_ref[...] = request.astype(jnp.int32)
    loads[2].wait()
    known_ref[...] = table[...].astype(BF)
    for save in saves:
        save.wait()


def serve_kernel(asked_ref, known_ref, served, row_hbm, row, sem):
    slots = served.shape[0]
    sources = asked_ref.shape[0]
    asked = asked_ref[...]
    high = (asked // 2).astype(F32).astype(BF)
    low = (asked % 2).astype(F32).astype(BF)
    expand = one_hot(iota((slots, sources), 0) // SLOTS == iota((slots, sources), 1))
    wide = 2.0 * dot(expand, high) + dot(expand, low)
    mine = iota(wide.shape, 1) == iota(wide.shape, 0) % SLOTS
    index = jnp.sum(jnp.where(mine, wide, 0.0), axis=1, keepdims=True) - 1.0
    index = jnp.broadcast_to(index, wide.shape)
    row[...] = jnp.transpose(index)[0:8].astype(jnp.int32)
    save = pltpu.make_async_copy(row, row_hbm, sem)
    save.start()
    index = index.astype(jnp.int32)
    lanes = iota(index.shape, 1)
    rows = known_ref.shape[0]
    picks = jnp.concatenate(
        [one_hot(index == lanes + 128 * j) for j in range(rows // 128)], axis=1
    )
    served[...] = dot(picks, known_ref[...]).astype(BF)
    save.wait()


def prefetch_kernel(count, after_ref, *refs):
    copies = copies_of(zip(refs[:count], refs[count : 2 * count]), refs[2 * count])
    for copy in copies:
        copy.wait()


def head_mask(heads, width):
    return iota((heads, width), 1) // HEAD_DIM == iota((heads, width), 0)


def spread_heads(values, mask, users):
    return jnp.concatenate(
        [jnp.where(mask, values[u : u + 1], 0.0) for u in range(users)], axis=0
    ).astype(BF)


def join_heads(full, mask, users):
    heads = mask.shape[0]
    parts = [
        jnp.sum(
            jnp.where(mask, full[u * heads : (u + 1) * heads], 0.0), axis=0, keepdims=True
        )
        for u in range(users)
    ]
    return jnp.concatenate(parts + [jnp.zeros((PAD - users, full.shape[1]), F32)], axis=0)


def look_up(column, fetched, hot):
    lanes = iota(column.shape, 1)
    slots = fetched.shape[0]
    picks = jnp.concatenate(
        [one_hot(column == lanes + 128 * j) for j in range(slots // 128)], axis=1
    )
    hot_picks = one_hot(column == lanes * SLOTS + HOT_SLOT)
    return (dot(picks, fetched[...]) + dot(hot_picks, hot[...].astype(BF))).astype(BF)


def item_forward_kernel(users, *refs):
    fetched_ref, column_ref, hot_ref, item_w2, refs = *refs[:4], refs[4:]
    sources, refs = refs[:4], refs[4:]
    vectors_ref, kept_hbm, refs = refs[0], refs[1:3], refs[3:]
    ahead, refs = refs[:2], refs[2:]
    targets, kept, (in_sems, out_sems) = refs[:2], refs[2:4], refs[4:]
    item_w1, gain = targets
    inner_ref, outer_ref = kept
    copies = copies_of(zip(sources, tuple(targets) + tuple(ahead)), in_sems)
    span = column_ref.shape[0] - 128
    rows = look_up(column_ref[span : span + PAD, :], fetched_ref, hot_ref)
    copies[0].wait()
    copies[1].wait()
    inner = dot(rows, item_w1[...])
    inner_ref[...] = inner
    gated = (inner * jax.nn.sigmoid(inner)).astype(BF)
    outer = dot(gated, item_w2[...])
    outer_ref[...] = outer
    saves = copies_of(zip(kept, kept_hbm), out_sems)
    scale = lax.rsqrt(jnp.mean(outer * outer, axis=-1, keepdims=True) + EPS)
    vectors = jnp.where(iota(outer.shape, 0) < users, outer * scale * gain[...], 0.0)
    peers = vectors_ref.shape[0] // 8
    vectors_ref[...] = jnp.concatenate([vectors[0:8]] * peers, axis=0).astype(BF)
    for copy in copies[2:] + saves:
        copy.wait()


def user_forward_kernel(users, *refs):
    fetched_ref, column_ref, hot_ref, in_proj, pos_of, refs = *refs[:5], refs[5:]
    sources, refs = refs[:6], refs[6:]
    vectors_ref, kept_hbm, refs = refs[0], refs[1:6], refs[6:]
    targets, kept, (in_sems, out_sems) = refs[:6], refs[6:11], refs[11:]
    norm_gain_ref, w_query, w_key, w_value, w_out, out_gain_ref = targets
    hidden_ref, normed_ref, qk_ref, weights_ref, mixed_ref = kept
    copies = copies_of(zip(sources, targets), in_sems)
    saves = [
        pltpu.make_async_copy(a, b, out_sems.at[i]) for i, (a, b) in enumerate(zip(kept, kept_hbm))
    ]
    hist, width = pos_of.shape
    heads = width // HEAD_DIM
    span = users * hist
    rows = look_up(column_ref[0:span, :], fetched_ref, hot_ref)
    pos = pos_of[...].astype(F32)
    hidden = dot(rows, in_proj[...]) + jnp.concatenate([pos] * users, axis=0)
    copies[0].wait()
    hidden_ref[...] = hidden
    saves[0].start()
    scale = lax.rsqrt(jnp.mean(hidden * hidden, axis=-1, keepdims=True) + EPS)
    normed = (hidden * scale * norm_gain_ref[...]).astype(BF)
    normed_ref[...] = normed
    saves[1].start()
    last = jnp.concatenate(
        [normed[(u + 1) * hist - PAD : (u + 1) * hist].astype(F32)[PAD - 1 :] for u in range(users)]
        + [jnp.zeros((PAD - users, width), F32)],
        axis=0,
    ).astype(BF)
    mask = head_mask(heads, width)
    copies[1].wait()
    query = dot(last, w_query[...]).astype(BF).astype(F32)
    copies[2].wait()
    qk = dot_nt(spread_heads(query, mask, users), w_key[...]).astype(BF)
    qk_ref[...] = qk
    saves[2].start()
    mixes = []
    for u in range(users):
        own = normed[u * hist : (u + 1) * hist]
        scores = dot_nt(qk[u * heads : (u + 1) * heads], own) * (1.0 / math.sqrt(HEAD_DIM))
        raised = jnp.exp(scores - jnp.max(scores, axis=1, keepdims=True))
        weights = raised / jnp.sum(raised, axis=1, keepdims=True)
        weights_ref[u * heads : (u + 1) * heads, :] = weights
        mixes.append(dot(weights.astype(BF), own))
    saves[3].start()
    mixes = jnp.concatenate(mixes, axis=0).astype(BF)
    copies[3].wait()
    attended = join_heads(dot(mixes, w_value[...]), mask, users).astype(BF)
    copies[4].wait()
    copies[5].wait()
    hidden_last = jnp.concatenate(
        [hidden[(u + 1) * hist - 1 : (u + 1) * hist] for u in range(users)]
        + [jnp.zeros((PAD - users, width), F32)],
        axis=0,
    )
    mixed = hidden_last + dot(attended, w_out[...])
    mixed_ref[...] = mixed
    saves[4].start()
    scale = lax.rsqrt(jnp.mean(mixed * mixed, axis=-1, keepdims=True) + EPS)
    vectors_ref[...] = (mixed * scale * out_gain_ref[...]).astype(BF)
    for save in saves:
        save.wait()


def arrange_kernel(users, near, near_ref, vectors_ref, spread_ref):
    total, width = spread_ref.shape
    block = near * users + 8
    pair = 2 * block
    at = iota((pair, near * 8), 0) % block
    source = jnp.where(at < near * users, at // users * 8 + at % users, -1)
    item_rows = dot(one_hot(iota((pair, near * 8), 1) == source), near_ref[...])
    at = iota((pair, PAD), 0) % block
    source = jnp.where((at >= near * users) & (at < (near + 1) * users), at - near * users, -1)
    user_rows = dot(one_hot(iota((pair, PAD), 1) == source), vectors_ref[...])
    rows = (item_rows + user_rows).astype(BF)
    for i in range(total // pair):
        spread_ref[i * pair : (i + 1) * pair, :] = rows


def softmax_kernel(
    users, near, scale, place_ref, gathered_ref, swapped_ref, *refs
):
    ahead, refs = refs[:3], refs[3:]
    d_user_ref, d_part_ref, loss_ref, refs = *refs[:3], refs[3:]
    copies = copies_of(zip(ahead, refs[:3]), refs[3])
    rows, width = gathered_ref.shape
    items = near * users
    block = items + 8
    blocks = rows // block
    mine, plane = place_ref[0], place_ref[1]
    own, other = gathered_ref[...], swapped_ref[...]

    def source_of_users(shape):
        line = iota(shape, 0)
        return line // users * block + items + line % users

    group = (blocks * users, rows)
    at_group = iota(group, 1) == source_of_users(group)
    line = (near * 8, rows)
    at_line = (iota(line, 0) % 8 < users) & (
        iota(line, 1) == mine * block + iota(line, 0) // 8 * users + iota(line, 0) % 8
    )
    self = (PAD, rows)
    at_self = (iota(self, 0) < users) & (iota(self, 1) == mine * block + items + iota(self, 0))
    picked = dot(jnp.concatenate([one_hot(at_group), one_hot(at_line), one_hot(at_self)], axis=0), own)
    own_users = picked[0 : blocks * users].astype(BF)
    line_items = picked[blocks * users : blocks * users + near * 8].astype(BF)
    self_users = picked[blocks * users + near * 8 :].astype(BF)
    other_users = dot(one_hot(at_group), other).astype(BF)
    group_users = jnp.concatenate([own_users, other_users], axis=0)
    total = 2 * blocks * users

    valid = iota((rows, total), 0) % block < items
    first = jnp.where(valid, scale * dot_nt(own, group_users), -jnp.inf)
    second = jnp.where(valid, scale * dot_nt(other, group_users), -jnp.inf)
    top = jnp.maximum(
        jnp.max(first, axis=0, keepdims=True), jnp.max(second, axis=0, keepdims=True)
    )
    count = jnp.sum(jnp.exp(first - top), axis=0, keepdims=True) + jnp.sum(
        jnp.exp(second - top), axis=0, keepdims=True
    )
    normalizer = top + jnp.log(count)
    shape = (near * 8, total)
    which = iota(shape, 0)
    target = (which // 8 == plane) & (iota(shape, 1) == mine * users + which % 8)
    slope = jnp.exp(scale * dot_nt(line_items, group_users) - normalizer)
    slope = jnp.where(which % 8 < users, slope - jnp.where(target, 1.0, 0.0), 0.0).astype(BF)
    d_part_ref[...] = (scale * dot(slope, group_users)).astype(BF)

    shape = (PAD, rows)
    lanes = iota(shape, 1)
    real = lanes % block < items
    valid = iota(shape, 0) < users
    target = lanes == mine * block + plane * users + iota(shape, 0)
    first = jnp.where(real, scale * dot_nt(self_users, own), -jnp.inf)
    second = jnp.where(real, scale * dot_nt(self_users, other), -jnp.inf)
    top = jnp.maximum(
        jnp.max(first, axis=1, keepdims=True), jnp.max(second, axis=1, keepdims=True)
    )
    count = jnp.sum(jnp.exp(first - top), axis=1, keepdims=True) + jnp.sum(
        jnp.exp(second - top), axis=1, keepdims=True
    )
    normalizer = top + jnp.log(count)
    slope = jnp.exp(first - normalizer) - jnp.where(target, 1.0, 0.0)
    d_user = dot(jnp.where(valid, slope, 0.0).astype(BF), own)
    slope = jnp.exp(second - normalizer)
    d_user = d_user + dot(jnp.where(valid, slope, 0.0).astype(BF), other)
    d_user_ref[...] = (scale * d_user).astype(BF).astype(F32)
    each = jnp.sum(jnp.where(valid & target, normalizer - first, 0.0), axis=1, keepdims=True)
    loss_ref[...] = jnp.broadcast_to(jnp.sum(each, axis=0, keepdims=True), loss_ref.shape)
    for copy in copies:
        copy.wait()


def norm_backward(values, cotangent, gain):
    inverse = lax.rsqrt(jnp.mean(values * values, axis=-1, keepdims=True) + EPS)
    pulled = cotangent * gain
    along = jnp.mean(pulled * values, axis=-1, keepdims=True)
    return inverse * pulled - values * (inverse * inverse * inverse * along)


def user_backward_kernel(users, d_user_ref, mixed_ref, out_gain_ref, w_out, *refs):
    sources, refs = refs[:15], refs[15:]
    d_rows_ref, ahead, refs = refs[0], refs[1:7], refs[7:]
    targets, (d_normed, sems) = refs[:9], refs[9:]
    w_value, normed_ref, weights_ref, qk_ref, w_key, w_query = targets[:6]
    hidden_ref, norm_gain_ref, in_proj = targets[6:]
    copies = copies_of(zip(sources, tuple(targets) + tuple(ahead)), sems)
    span, width = hidden_ref.shape
    hist = span // users
    heads = width // HEAD_DIM
    mask = head_mask(heads, width)
    d_mixed = norm_backward(mixed_ref[...], d_user_ref[...], out_gain_ref[...])
    d_attended = dot_nt(d_mixed.astype(BF), w_out[...])
    copies[0].wait()
    d_mixes = dot_nt(spread_heads(d_attended, mask, users), w_value[...]).astype(BF)
    for copy in copies[1:4]:
        copy.wait()
    d_qk = []
    for u in range(users):
        own = normed_ref[u * hist : (u + 1) * hist, :]
        weights = weights_ref[u * heads : (u + 1) * heads, :]
        pulled = d_mixes[u * heads : (u + 1) * heads]
        d_weights = dot_nt(pulled, own)
        d_scores = weights * (d_weights - jnp.sum(weights * d_weights, axis=1, keepdims=True))
        d_scores = (d_scores * (1.0 / math.sqrt(HEAD_DIM))).astype(BF)
        d_normed[u * hist : (u + 1) * hist, :] = dot_tn(weights.astype(BF), pulled) + dot_tn(
            d_scores, qk_ref[u * heads : (u + 1) * heads, :]
        )
        d_qk.append(dot(d_scores, own))
    d_qk = jnp.concatenate(d_qk, axis=0).astype(BF)
    copies[4].wait()
    d_query = join_heads(dot(d_qk, w_key[...]), mask, users).astype(BF)
    copies[5].wait()
    d_last = dot_nt(d_query, w_query[...])
    for u in range(users):
        at = slice((u + 1) * hist - 1, (u + 1) * hist)
        d_normed[at, :] = d_normed[at, :] + d_last[u : u + 1]
    copies[6].wait()
    copies[7].wait()
    d_normed[...] = norm_backward(hidden_ref[...], d_normed[...], norm_gain_ref[...])
    for u in range(users):
        at = slice((u + 1) * hist - 1, (u + 1) * hist)
        d_normed[at, :] = d_normed[at, :] + d_mixed[u : u + 1]
    copies[8].wait()
    d_rows_ref[...] = dot_nt(d_normed[...].astype(BF), in_proj[...]).astype(BF)
    for copy in copies[9:]:
        copy.wait()


def item_backward_kernel(users, parts_ref, d_rows_ref, *refs):
    row_ref, gain, outer_ref, inner_ref, item_w2, item_w1, outgoing = refs
    slots = outgoing.shape[0]
    span = d_rows_ref.shape[0]
    wide = row_ref.shape[1]
    peers = parts_ref.shape[0]
    shape = (PAD, peers)
    added = (iota(shape, 1) % 8 == iota(shape, 0)) & (iota(shape, 0) < users)
    d_item = dot(one_hot(added), parts_ref[...]).astype(BF).astype(F32)
    picks = one_hot(iota((slots, wide), 0) == row_ref[0:1, :])
    total = dot(picks[:, 0:span], d_rows_ref[...])
    d_outer = norm_backward(outer_ref[...], d_item, gain[...])
    inner = inner_ref[...]
    gate = jax.nn.sigmoid(inner)
    d_inner = dot_nt(d_outer.astype(BF), item_w2[...]) * (gate * (1.0 + inner * (1.0 - gate)))
    d_items = dot_nt(d_inner.astype(BF), item_w1[...])
    d_items = jnp.concatenate(
        [d_items, jnp.zeros((wide - span - PAD, d_items.shape[1]), F32)], axis=0
    ).astype(BF)
    outgoing[...] = (total + dot(picks[:, span:], d_items)).astype(BF)


def finish_kernel(total, sums_ref, other_ref, hot_ref, loss_ref):
    emb = hot_ref.shape[1]
    sums = sums_ref[...] + other_ref[...]
    hot_ref[...] = sums[:, 0:emb]
    loss_ref[...] = jnp.sum(sums[:, emb : emb + 1], axis=0, keepdims=True) / total


def scatter_kernel(returned_ref, row_ref, loss_ref, part_ref, hot_ref):
    rows, emb = part_ref.shape
    slots = returned_ref.shape[0]
    returned = returned_ref[...]
    picks = one_hot(iota((rows, slots), 0) == row_ref[0:1, :])
    part_ref[...] = dot(picks, returned).astype(BF)
    hot = dot(one_hot(iota((PAD, slots), 1) % SLOTS == HOT_SLOT), returned)
    hot_ref[:, 0:emb] = jnp.broadcast_to(hot[0:1], (hot_ref.shape[0], emb))
    hot_ref[:, emb:] = jnp.broadcast_to(loss_ref[0:1, :], (hot_ref.shape[0], 128))


def shards(
    history,
    item_ids,
    hot_table,
    rare_table,
    in_proj,
    pos_embed,
    norm_gain,
    w_query,
    w_key,
    w_value,
    w_out,
    out_gain,
    item_w1,
    item_w2,
    item_gain,
):
    users, hist = history.shape
    emb = hot_table.shape[1]
    rare_count = rare_table.shape[0]
    width = in_proj.shape[1]
    heads = width // HEAD_DIM
    scale = 4.0 / math.sqrt(width)
    owners = lax.axis_size(SHARD)
    towers = lax.axis_size("tower")
    near = lax.axis_size("z")
    total = users * towers * owners
    slots = owners * SLOTS
    span = users * hist
    wide = -(-(span + PAD) // 128) * 128
    swap = [(i, towers - 1 - i) for i in range(towers)]
    shape = jax.ShapeDtypeStruct
    sems = lambda n: pltpu.SemaphoreType.DMA((n,))
    vmem = lambda a: pltpu.VMEM(a.shape, a.dtype)
    hbm = lambda a: pltpu.HBM(a.shape, a.dtype)
    in_hbm = lambda a: pltpu.with_memory_space_constraint(a, pltpu.HBM)
    in_vmem = lambda a: pltpu.with_memory_space_constraint(a, pltpu.VMEM)
    like = lambda arrays: [pltpu.VMEM(a.shape, a.dtype) for a in arrays]
    exchange = functools.partial(lax.all_to_all, split_axis=0, concat_axis=0, tiled=True)

    places = (shape((8, wide), jnp.int32), shape((wide, 128), jnp.int32))
    loads = (history, item_ids.reshape(1, users), rare_table)
    request, known, row, column = pl.pallas_call(
        functools.partial(index_kernel, owners),
        out_shape=(
            shape((owners, 128), jnp.int32),
            pltpu.VMEM((rare_count, emb), BF),
            *map(hbm, places),
        ),
        in_specs=[HBM] * 3,
        out_specs=(VMEM, VMEM, HBM, HBM),
        scratch_shapes=like(loads + places) + [sems(5)],
        compiler_params=params(24),
        name="index",
    )(*map(in_hbm, loads))
    asked = exchange(request, SHARD)
    served, asked_row = pl.pallas_call(
        serve_kernel,
        out_shape=(shape((slots, emb), BF), pltpu.HBM((8, slots), jnp.int32)),
        in_specs=[VMEM, VMEM],
        out_specs=(VMEM, HBM),
        scratch_shapes=[pltpu.VMEM((8, slots), jnp.int32), pltpu.SemaphoreType.DMA],
        compiler_params=params(24),
        name="serve",
    )(asked, in_vmem(known))
    fetched = exchange(served, SHARD)

    norm_gain, out_gain, item_gain = (g.reshape(1, width) for g in (norm_gain, out_gain, item_gain))
    loads = (column, hot_table, item_w2)
    column_ready, hot_ready, item_w2_ready = pl.pallas_call(
        functools.partial(prefetch_kernel, len(loads)),
        out_shape=tuple(map(vmem, loads)),
        in_specs=[pl.BlockSpec(memory_space=pl.ANY)] + [HBM] * len(loads),
        out_specs=(VMEM,) * len(loads),
        scratch_shapes=[sems(len(loads))],
        compiler_params=params(24),
        name="prefetch",
    )(served, *map(in_hbm, loads))

    loads = (item_w1, item_gain)
    ahead = (in_proj, pos_embed)
    kept = (shape((PAD, width), F32), shape((PAD, width), F32))
    item_vec, inner, outer, in_proj_ready, pos_ready = pl.pallas_call(
        functools.partial(item_forward_kernel, users),
        out_shape=(shape((near * 8, width), BF), *map(hbm, kept), *map(vmem, ahead)),
        in_specs=[VMEM] * 4 + [HBM] * 4,
        out_specs=(VMEM, HBM, HBM, VMEM, VMEM),
        scratch_shapes=like(loads + kept) + [sems(4), sems(2)],
        compiler_params=params(24),
        name="item_forward",
    )(
        fetched,
        *map(in_vmem, (column_ready, hot_ready, item_w2_ready)),
        *map(in_hbm, loads + ahead),
    )
    near_items = exchange(item_vec, "z")

    loads = (norm_gain, w_query, w_key, w_value, w_out, out_gain)
    kept = (
        shape((span, width), F32),
        shape((span, width), BF),
        shape((users * heads, width), BF),
        shape((users * heads, hist), F32),
        shape((PAD, width), F32),
    )
    user_vec, hidden, normed, qk, weights, mixed = pl.pallas_call(
        functools.partial(user_forward_kernel, users),
        out_shape=(shape((PAD, width), BF), *map(hbm, kept)),
        in_specs=[VMEM] * 5 + [HBM] * len(loads),
        out_specs=(VMEM,) + (HBM,) * len(kept),
        scratch_shapes=like(loads + kept) + [sems(len(loads)), sems(len(kept))],
        compiler_params=params(40),
        name="user_forward",
    )(
        fetched,
        *map(in_vmem, (column_ready, hot_ready, in_proj_ready, pos_ready)),
        *map(in_hbm, loads),
    )

    rows = owners // near * (near * users + 8)
    spread = pl.pallas_call(
        functools.partial(arrange_kernel, users, near),
        out_shape=shape((rows, width), BF),
        in_specs=[VMEM, VMEM],
        out_specs=VMEM,
        compiler_params=params(24),
        name="arrange",
    )(near_items, user_vec)
    gathered = exchange(spread, ("x", "y"))
    swapped = lax.ppermute(gathered, "tower", swap)
    place = jnp.stack([lax.axis_index(("x", "y")), lax.axis_index("z")]).astype(jnp.int32)
    ahead = (mixed, out_gain, w_out)
    d_user, d_part, loss, *ready = pl.pallas_call(
        functools.partial(softmax_kernel, users, near, scale),
        out_shape=(
            shape((PAD, width), F32),
            shape((near * 8, width), BF),
            shape((8, 128), F32),
            *map(vmem, ahead),
        ),
        in_specs=[SMEM, VMEM, VMEM] + [HBM] * 3,
        out_specs=(VMEM,) * 6,
        scratch_shapes=[sems(3)],
        compiler_params=params(32),
        name="softmax",
    )(place, gathered, swapped, *map(in_hbm, ahead))
    parts = exchange(d_part, "z")

    loads = (w_value, normed, weights, qk, w_key, w_query, hidden, norm_gain, in_proj)
    ahead = (row, item_gain, outer, inner, item_w2, item_w1)
    d_rows, *item_ready = pl.pallas_call(
        functools.partial(user_backward_kernel, users),
        out_shape=(shape((span, emb), BF), *map(vmem, ahead)),
        in_specs=[VMEM] * 4 + [HBM] * 15,
        out_specs=(VMEM,) * 7,
        scratch_shapes=like(loads) + [pltpu.VMEM((span, width), F32), sems(15)],
        compiler_params=params(40),
        name="user_backward",
    )(d_user, *map(in_vmem, ready), *map(in_hbm, loads + ahead))
    outgoing = pl.pallas_call(
        functools.partial(item_backward_kernel, users),
        out_shape=shape((slots, emb), BF),
        in_specs=[VMEM] * 8,
        out_specs=VMEM,
        compiler_params=params(32),
        name="item_backward",
    )(parts, d_rows, *map(in_vmem, item_ready))

    returned = exchange(outgoing, SHARD)
    part, mine = pl.pallas_call(
        scatter_kernel,
        out_shape=(shape((rare_count, emb), BF), shape((owners, emb + 128), F32)),
        in_specs=[VMEM, VMEM, VMEM],
        out_specs=(VMEM, VMEM),
        compiler_params=params(24),
        name="scatter",
    )(returned, asked_row, loss)
    rare_grad = part.astype(F32) + lax.ppermute(part, "tower", swap).astype(F32)
    sums = exchange(mine, SHARD)
    other_sums = lax.ppermute(sums, "tower", swap)
    hot_total, loss_total = pl.pallas_call(
        functools.partial(finish_kernel, total),
        out_shape=(shape((owners, emb), F32), shape((1, 1), F32)),
        in_specs=[VMEM, VMEM],
        out_specs=(VMEM, VMEM),
        compiler_params=params(24),
        name="finish",
    )(sums, other_sums)
    return (hot_total, rare_grad, loss_total[0, 0])


def solution(mesh):
    sizes = (mesh.shape["tower"], 4, 4, mesh.shape["shard"] // 16)
    mesh = Mesh(mesh.devices.reshape(sizes), ("tower",) + SHARD)
    return jax.shard_map(
        shards,
        mesh=mesh,
        in_specs=(
            P(("tower",) + SHARD, None),
            P(("tower",) + SHARD),
            P(),
            P(SHARD, None),
            P(),
            P(),
            P(),
            P(),
            P(),
            P(),
            P(),
            P(),
            P(),
            P(),
            P(),
        ),
        out_specs=(P(), P(SHARD, None), P()),
        check_vma=False,
    )
```

```python
import functools
import math

import jax
import jax.numpy as jnp
from jax import lax
from jax.experimental import pallas as pl
from jax.experimental.pallas import tpu as pltpu
from jax.sharding import Mesh
from jax.sharding import PartitionSpec as P

HEAD_DIM = 64
EPS = 1e-06
SLOTS = 8
HOT_SLOT = 5
SHARD = ("x", "y", "z")
PAD = 16
BF = jnp.bfloat16
F32 = jnp.float32
VMEM = pl.BlockSpec(memory_space=pltpu.VMEM)
SMEM = pl.BlockSpec(memory_space=pltpu.SMEM)
HBM = pl.BlockSpec(memory_space=pltpu.HBM)
NT = (((1,), (1,)), ((), ()))
TN = (((0,), (0,)), ((), ()))


def dot(a, b):
    return jnp.dot(a, b, preferred_element_type=F32)


def dot_nt(a, b):
    return lax.dot_general(a, b, NT, preferred_element_type=F32)


def dot_tn(a, b):
    return lax.dot_general(a, b, TN, preferred_element_type=F32)


def iota(shape, axis):
    return lax.broadcasted_iota(jnp.int32, shape, axis)


def one_hot(mask):
    return jnp.where(mask, 1.0, 0.0).astype(BF)


def params(mib):
    return pltpu.CompilerParams(vmem_limit_bytes=mib * 1024 * 1024)


def copies_of(pairs, sems):
    copies = [pltpu.make_async_copy(a, b, sems.at[i]) for i, (a, b) in enumerate(pairs)]
    for copy in copies:
        copy.start()
    return copies


def index_kernel(
    owners,
    history_hbm,
    items_hbm,
    table_hbm,
    request_ref,
    known_ref,
    row_hbm,
    column_hbm,
    history_ref,
    items_ref,
    table,
    row,
    column,
    sems,
):
    loads = copies_of(
        [(history_hbm, history_ref), (items_hbm, items_ref), (table_hbm, table)], sems
    )
    loads[0].wait()
    loads[1].wait()
    hot_count = owners
    rare_count = table.shape[0]
    users = history_ref.shape[0]
    span = row.shape[1]
    parts = [history_ref[u : u + 1, :] for u in range(users)] + [items_ref[...]]
    filled = sum(p.shape[1] for p in parts)
    ids = jnp.concatenate(parts + [jnp.full((1, span - filled), -1, jnp.int32)], axis=1)
    is_rare = ids >= hot_count
    index = ids - hot_count
    owner = jnp.where(is_rare, index // rare_count, -1)
    value = jnp.where(is_rare, index % rare_count + 1, 0).astype(F32)
    hits = iota((owners, span), 0) == owner
    before = one_hot(iota((span, span), 0) < iota((span, span), 1))
    earlier = dot(one_hot(hits), before)
    position = jnp.sum(jnp.where(hits, earlier, 0.0), axis=0, keepdims=True).astype(jnp.int32)
    places = jnp.where(
        is_rare, owner * SLOTS + position, jnp.where(ids >= 0, ids * SLOTS + HOT_SLOT, -1)
    )
    row[...] = jnp.broadcast_to(places, row.shape)
    column[...] = jnp.transpose(jnp.broadcast_to(places.astype(F32), (128, span))).astype(jnp.int32)
    saves = copies_of([(row, row_hbm), (column, column_hbm)], sems.at[pl.ds(3, 2)])
    order = jnp.where(hits, earlier, -1.0)
    lanes = iota(request_ref.shape, 1)
    request = jnp.zeros(request_ref.shape, F32)
    for slot in range(HOT_SLOT):
        wanted = jnp.sum(jnp.where(order == float(slot), value, 0.0), axis=1, keepdims=True)
        request = jnp.where(lanes == slot, wanted, request)
    request_ref[...] = request.astype(jnp.int32)
    loads[2].wait()
    known_ref[...] = table[...].astype(BF)
    for save in saves:
        save.wait()


def serve_kernel(asked_ref, known_ref, served, row_hbm, row, sem):
    slots = served.shape[0]
    sources = asked_ref.shape[0]
    asked = asked_ref[...]
    high = (asked // 2).astype(F32).astype(BF)
    low = (asked % 2).astype(F32).astype(BF)
    expand = one_hot(iota((slots, sources), 0) // SLOTS == iota((slots, sources), 1))
    wide = 2.0 * dot(expand, high) + dot(expand, low)
    mine = iota(wide.shape, 1) == iota(wide.shape, 0) % SLOTS
    index = jnp.sum(jnp.where(mine, wide, 0.0), axis=1, keepdims=True) - 1.0
    index = jnp.broadcast_to(index, wide.shape)
    row[...] = jnp.transpose(index)[0:8].astype(jnp.int32)
    save = pltpu.make_async_copy(row, row_hbm, sem)
    save.start()
    index = index.astype(jnp.int32)
    lanes = iota(index.shape, 1)
    rows = known_ref.shape[0]
    picks = jnp.concatenate(
        [one_hot(index == lanes + 128 * j) for j in range(rows // 128)], axis=1
    )
    served[...] = dot(picks, known_ref[...]).astype(BF)
    save.wait()


def head_mask(heads, width):
    return iota((heads, width), 1) // HEAD_DIM == iota((heads, width), 0)


def spread_heads(values, mask, users):
    return jnp.concatenate(
        [jnp.where(mask, values[u : u + 1], 0.0) for u in range(users)], axis=0
    ).astype(BF)


def join_heads(full, mask, users):
    heads = mask.shape[0]
    parts = [
        jnp.sum(
            jnp.where(mask, full[u * heads : (u + 1) * heads], 0.0), axis=0, keepdims=True
        )
        for u in range(users)
    ]
    return jnp.concatenate(parts + [jnp.zeros((PAD - users, full.shape[1]), F32)], axis=0)


def look_up(column, fetched, hot):
    lanes = iota(column.shape, 1)
    slots = fetched.shape[0]
    picks = jnp.concatenate(
        [one_hot(column == lanes + 128 * j) for j in range(slots // 128)], axis=1
    )
    hot_picks = one_hot(column == lanes * SLOTS + HOT_SLOT)
    return (dot(picks, fetched[...]) + dot(hot_picks, hot[...].astype(BF))).astype(BF)


def item_forward_kernel(users, *refs):
    fetched_ref, sources, refs = refs[0], refs[1:6], refs[6:]
    vectors_ref, kept_hbm, refs = refs[0], refs[1:3], refs[3:]
    targets, kept, (in_sems, out_sems) = refs[:5], refs[5:7], refs[7:]
    column_of, hot, gain, item_w1, item_w2 = targets
    inner_ref, outer_ref = kept
    span = sources[0].shape[0]
    sources = (sources[0].at[pl.ds(span - 128, PAD)],) + tuple(sources[1:])
    copies = copies_of(zip(sources, targets), in_sems)
    copies[0].wait()
    copies[1].wait()
    rows = look_up(column_of[...], fetched_ref, hot)
    copies[2].wait()
    copies[3].wait()
    inner = dot(rows, item_w1[...])
    inner_ref[...] = inner
    gated = (inner * jax.nn.sigmoid(inner)).astype(BF)
    copies[4].wait()
    outer = dot(gated, item_w2[...])
    outer_ref[...] = outer
    saves = copies_of(zip(kept, kept_hbm), out_sems)
    scale = lax.rsqrt(jnp.mean(outer * outer, axis=-1, keepdims=True) + EPS)
    vectors = jnp.where(iota(outer.shape, 0) < users, outer * scale * gain[...], 0.0)
    peers = vectors_ref.shape[0] // 8
    vectors_ref[...] = jnp.concatenate([vectors[0:8]] * peers, axis=0).astype(BF)
    for save in saves:
        save.wait()


def user_forward_kernel(users, *refs):
    fetched_ref, sources, refs = refs[0], refs[1:11], refs[11:]
    vectors_ref, kept_hbm, refs = refs[0], refs[1:6], refs[6:]
    targets, kept, (in_sems, out_sems) = refs[:10], refs[10:15], refs[15:]
    column_of, hot, pos_of, norm_gain_ref, out_gain_ref = targets[:5]
    in_proj, w_query, w_key, w_value, w_out = targets[5:]
    hidden_ref, normed_ref, qk_ref, weights_ref, mixed_ref = kept
    copies = copies_of(zip(sources, targets), in_sems)
    saves = [
        pltpu.make_async_copy(a, b, out_sems.at[i]) for i, (a, b) in enumerate(zip(kept, kept_hbm))
    ]
    hist, width = pos_of.shape
    heads = width // HEAD_DIM
    span = users * hist
    copies[0].wait()
    copies[1].wait()
    rows = look_up(column_of[0:span, :], fetched_ref, hot)
    for copy in copies[2:6]:
        copy.wait()
    pos = pos_of[...].astype(F32)
    hidden = dot(rows, in_proj[...]) + jnp.concatenate([pos] * users, axis=0)
    hidden_ref[...] = hidden
    saves[0].start()
    scale = lax.rsqrt(jnp.mean(hidden * hidden, axis=-1, keepdims=True) + EPS)
    normed = (hidden * scale * norm_gain_ref[...]).astype(BF)
    normed_ref[...] = normed
    saves[1].start()
    last = jnp.concatenate(
        [normed[(u + 1) * hist - PAD : (u + 1) * hist].astype(F32)[PAD - 1 :] for u in range(users)]
        + [jnp.zeros((PAD - users, width), F32)],
        axis=0,
    ).astype(BF)
    mask = head_mask(heads, width)
    copies[6].wait()
    query = dot(last, w_query[...]).astype(BF).astype(F32)
    copies[7].wait()
    qk = dot_nt(spread_heads(query, mask, users), w_key[...]).astype(BF)
    qk_ref[...] = qk
    saves[2].start()
    shape = (users * heads, span)
    own = iota(shape, 0) // heads == iota(shape, 1) // hist
    scores = jnp.where(own, dot_nt(qk, normed) * (1.0 / math.sqrt(HEAD_DIM)), -jnp.inf)
    raised = jnp.exp(scores - jnp.max(scores, axis=1, keepdims=True))
    weights = raised / jnp.sum(raised, axis=1, keepdims=True)
    weights_ref[...] = weights
    saves[3].start()
    mixes = dot(weights.astype(BF), normed).astype(BF)
    copies[8].wait()
    attended = join_heads(dot(mixes, w_value[...]), mask, users).astype(BF)
    copies[9].wait()
    hidden_last = jnp.concatenate(
        [hidden[(u + 1) * hist - 1 : (u + 1) * hist] for u in range(users)]
        + [jnp.zeros((PAD - users, width), F32)],
        axis=0,
    )
    mixed = hidden_last + dot(attended, w_out[...])
    mixed_ref[...] = mixed
    saves[4].start()
    scale = lax.rsqrt(jnp.mean(mixed * mixed, axis=-1, keepdims=True) + EPS)
    vectors_ref[...] = (mixed * scale * out_gain_ref[...]).astype(BF)
    for save in saves:
        save.wait()


def arrange_kernel(users, near, near_ref, vectors_ref, spread_ref):
    total, width = spread_ref.shape
    block = near * users + 8
    pair = 2 * block
    at = iota((pair, near * 8), 0) % block
    source = jnp.where(at < near * users, at // users * 8 + at % users, -1)
    item_rows = dot(one_hot(iota((pair, near * 8), 1) == source), near_ref[...])
    at = iota((pair, PAD), 0) % block
    source = jnp.where((at >= near * users) & (at < (near + 1) * users), at - near * users, -1)
    user_rows = dot(one_hot(iota((pair, PAD), 1) == source), vectors_ref[...])
    rows = (item_rows + user_rows).astype(BF)
    for i in range(total // pair):
        spread_ref[i * pair : (i + 1) * pair, :] = rows


def softmax_kernel(
    users, near, scale, place_ref, gathered_ref, swapped_ref, d_user_ref, d_part_ref, loss_ref, raised_ref
):
    rows, width = gathered_ref.shape
    items = near * users
    block = items + 8
    blocks = rows // block
    mine, plane = place_ref[0], place_ref[1]
    own, other = gathered_ref[...], swapped_ref[...]
    shape = (blocks * users, rows)
    line = iota(shape, 0)
    picks = one_hot(iota(shape, 1) == line // users * block + items + line % users)
    group_users = jnp.concatenate([dot(picks, own), dot(picks, other)], axis=0).astype(BF)
    total = 2 * blocks * users

    shape = (rows, total)
    line = iota(shape, 0)
    valid = line % block < items
    first = jnp.where(valid, scale * dot_nt(own, group_users), -jnp.inf)
    second = jnp.where(valid, scale * dot_nt(other, group_users), -jnp.inf)
    top = jnp.maximum(
        jnp.max(first, axis=0, keepdims=True), jnp.max(second, axis=0, keepdims=True)
    )
    raised = jnp.exp(first - top)
    raised_ref[...] = raised
    other_raised = jnp.exp(second - top)
    count = jnp.sum(raised, axis=0, keepdims=True) + jnp.sum(other_raised, axis=0, keepdims=True)
    share = 1.0 / count

    line = (items, total)
    target = (iota(line, 0) // users == plane) & (
        iota(line, 1) == mine * users + iota(line, 0) % users
    )
    near_raised = raised_ref[pl.ds(pl.multiple_of(mine * block, 8), items), :]
    slope = (near_raised * share - jnp.where(target, 1.0, 0.0)).astype(BF)
    apart = (near * 8, items)
    at = iota(apart, 0)
    apart = one_hot((at % 8 < users) & (iota(apart, 1) == at // 8 * users + at % 8))
    d_part_ref[...] = (scale * dot(dot(apart, slope).astype(BF), group_users)).astype(BF)

    who = iota(shape, 1) - mine * users
    target = (who >= 0) & (who < users) & (iota(shape, 0) == mine * block + plane * users + who)
    slope = (raised * share - jnp.where(target, 1.0, 0.0)).astype(BF)
    other_slope = (other_raised * share).astype(BF)
    self = (PAD, total)
    self = one_hot((iota(self, 0) < users) & (iota(self, 1) == mine * users + iota(self, 0)))
    d_user = dot(dot_nt(self, slope).astype(BF), own)
    d_user = d_user + dot(dot_nt(self, other_slope).astype(BF), other)
    d_user_ref[...] = (scale * d_user).astype(BF).astype(F32)
    each = jnp.sum(jnp.where(target, top + jnp.log(count) - first, 0.0), axis=0, keepdims=True)
    loss_ref[...] = jnp.broadcast_to(jnp.sum(each, axis=1, keepdims=True), loss_ref.shape)


def norm_backward(values, cotangent, gain):
    inverse = lax.rsqrt(jnp.mean(values * values, axis=-1, keepdims=True) + EPS)
    pulled = cotangent * gain
    along = jnp.mean(pulled * values, axis=-1, keepdims=True)
    return inverse * pulled - values * (inverse * inverse * inverse * along)


def user_backward_kernel(users, d_user_ref, *refs):
    sources, refs = refs[:18], refs[18:]
    d_rows_ref, ahead, refs = refs[0], refs[1:7], refs[7:]
    targets, (d_normed, sems) = refs[:12], refs[12:]
    mixed_ref, out_gain_ref, w_out, w_value, normed_ref, weights_ref, qk_ref = targets[:7]
    w_key, w_query, hidden_ref, norm_gain_ref, in_proj = targets[7:]
    copies = copies_of(zip(sources, tuple(targets) + tuple(ahead)), sems)
    span, width = hidden_ref.shape
    hist = span // users
    heads = width // HEAD_DIM
    mask = head_mask(heads, width)
    for copy in copies[:3]:
        copy.wait()
    d_mixed = norm_backward(mixed_ref[...], d_user_ref[...], out_gain_ref[...])
    d_attended = dot_nt(d_mixed.astype(BF), w_out[...])
    copies[3].wait()
    d_mixes = dot_nt(spread_heads(d_attended, mask, users), w_value[...]).astype(BF)
    for copy in copies[4:7]:
        copy.wait()
    normed = normed_ref[...]
    weights = weights_ref[...]
    shape = weights.shape
    own = iota(shape, 0) // heads == iota(shape, 1) // hist
    d_weights = jnp.where(own, dot_nt(d_mixes, normed), 0.0)
    d_scores = weights * (d_weights - jnp.sum(weights * d_weights, axis=1, keepdims=True))
    d_scores = (d_scores * (1.0 / math.sqrt(HEAD_DIM))).astype(BF)
    d_normed[...] = dot_tn(
        jnp.concatenate([weights.astype(BF), d_scores], axis=0),
        jnp.concatenate([d_mixes, qk_ref[...]], axis=0),
    )
    d_qk = dot(d_scores, normed).astype(BF)
    copies[7].wait()
    d_query = join_heads(dot(d_qk, w_key[...]), mask, users).astype(BF)
    copies[8].wait()
    d_last = dot_nt(d_query, w_query[...])
    for u in range(users):
        at = slice((u + 1) * hist - 1, (u + 1) * hist)
        d_normed[at, :] = d_normed[at, :] + d_last[u : u + 1]
    copies[9].wait()
    copies[10].wait()
    d_normed[...] = norm_backward(hidden_ref[...], d_normed[...], norm_gain_ref[...])
    for u in range(users):
        at = slice((u + 1) * hist - 1, (u + 1) * hist)
        d_normed[at, :] = d_normed[at, :] + d_mixed[u : u + 1]
    copies[11].wait()
    d_rows_ref[...] = dot_nt(d_normed[...].astype(BF), in_proj[...]).astype(BF)
    for copy in copies[12:]:
        copy.wait()


def item_backward_kernel(users, parts_ref, d_rows_ref, *refs):
    row_ref, gain, outer_ref, inner_ref, item_w2, item_w1, outgoing = refs
    slots = outgoing.shape[0]
    span = d_rows_ref.shape[0]
    wide = row_ref.shape[1]
    peers = parts_ref.shape[0]
    shape = (PAD, peers)
    added = (iota(shape, 1) % 8 == iota(shape, 0)) & (iota(shape, 0) < users)
    d_item = dot(one_hot(added), parts_ref[...]).astype(BF).astype(F32)
    picks = one_hot(iota((slots, wide), 0) == row_ref[0:1, :])
    total = dot(picks[:, 0:span], d_rows_ref[...])
    d_outer = norm_backward(outer_ref[...], d_item, gain[...])
    inner = inner_ref[...]
    gate = jax.nn.sigmoid(inner)
    d_inner = dot_nt(d_outer.astype(BF), item_w2[...]) * (gate * (1.0 + inner * (1.0 - gate)))
    d_items = dot_nt(d_inner.astype(BF), item_w1[...])
    d_items = jnp.concatenate(
        [d_items, jnp.zeros((wide - span - PAD, d_items.shape[1]), F32)], axis=0
    ).astype(BF)
    outgoing[...] = (total + dot(picks[:, span:], d_items)).astype(BF)


def finish_kernel(total, sums_ref, other_ref, hot_ref, loss_ref):
    emb = hot_ref.shape[1]
    sums = sums_ref[:, 0, :] + other_ref[:, 0, :]
    hot_ref[...] = sums[:, 0:emb]
    loss_ref[...] = jnp.sum(sums[:, emb : emb + 1], axis=0, keepdims=True) / total


def scatter_kernel(returned_ref, row_ref, loss_ref, part_ref, hot_ref):
    rows, emb = part_ref.shape
    slots = returned_ref.shape[0]
    returned = returned_ref[...]
    picks = one_hot(iota((rows, slots), 0) == row_ref[0:1, :])
    part_ref[...] = dot(picks, returned).astype(BF)
    hot = dot(one_hot(iota((PAD, slots), 1) % SLOTS == HOT_SLOT), returned)
    line = jnp.concatenate([hot[0:1], loss_ref[0:1, :]], axis=1)
    hot_ref[...] = jnp.broadcast_to(line[None], hot_ref.shape)


def shards(
    history,
    item_ids,
    hot_table,
    rare_table,
    in_proj,
    pos_embed,
    norm_gain,
    w_query,
    w_key,
    w_value,
    w_out,
    out_gain,
    item_w1,
    item_w2,
    item_gain,
):
    users, hist = history.shape
    emb = hot_table.shape[1]
    rare_count = rare_table.shape[0]
    width = in_proj.shape[1]
    heads = width // HEAD_DIM
    scale = 4.0 / math.sqrt(width)
    owners = lax.axis_size(SHARD)
    towers = lax.axis_size("tower")
    near = lax.axis_size("z")
    total = users * towers * owners
    slots = owners * SLOTS
    span = users * hist
    wide = -(-(span + PAD) // 128) * 128
    swap = [(i, towers - 1 - i) for i in range(towers)]
    shape = jax.ShapeDtypeStruct
    sems = lambda n: pltpu.SemaphoreType.DMA((n,))
    vmem = lambda a: pltpu.VMEM(a.shape, a.dtype)
    hbm = lambda a: pltpu.HBM(a.shape, a.dtype)
    in_hbm = lambda a: pltpu.with_memory_space_constraint(a, pltpu.HBM)
    in_vmem = lambda a: pltpu.with_memory_space_constraint(a, pltpu.VMEM)
    like = lambda arrays: [pltpu.VMEM(a.shape, a.dtype) for a in arrays]
    exchange = functools.partial(lax.all_to_all, split_axis=0, concat_axis=0, tiled=True)

    places = (shape((8, wide), jnp.int32), shape((wide, 128), jnp.int32))
    loads = (history, item_ids.reshape(1, users), rare_table)
    request, known, row, column = pl.pallas_call(
        functools.partial(index_kernel, owners),
        out_shape=(
            shape((owners, 128), jnp.int32),
            pltpu.VMEM((rare_count, emb), BF),
            *map(hbm, places),
        ),
        in_specs=[HBM] * 3,
        out_specs=(VMEM, VMEM, HBM, HBM),
        scratch_shapes=like(loads + places) + [sems(5)],
        compiler_params=params(24),
        name="index",
    )(*map(in_hbm, loads))
    asked = exchange(request, SHARD)
    served, asked_row = pl.pallas_call(
        serve_kernel,
        out_shape=(shape((slots, emb), BF), pltpu.HBM((8, slots), jnp.int32)),
        in_specs=[VMEM, VMEM],
        out_specs=(VMEM, HBM),
        scratch_shapes=[pltpu.VMEM((8, slots), jnp.int32), pltpu.SemaphoreType.DMA],
        compiler_params=params(24),
        name="serve",
    )(asked, in_vmem(known))
    fetched = exchange(served, SHARD)

    norm_gain, out_gain, item_gain = (g.reshape(1, width) for g in (norm_gain, out_gain, item_gain))
    loads = (column, hot_table, item_gain, item_w1, item_w2)
    kept = (shape((PAD, width), F32), shape((PAD, width), F32))
    item_vec, inner, outer = pl.pallas_call(
        functools.partial(item_forward_kernel, users),
        out_shape=(shape((near * 8, width), BF), *map(hbm, kept)),
        in_specs=[VMEM] + [HBM] * 5,
        out_specs=(VMEM, HBM, HBM),
        scratch_shapes=[pltpu.VMEM((PAD, 128), jnp.int32)]
        + like(loads[1:] + kept)
        + [sems(5), sems(2)],
        compiler_params=params(24),
        name="item_forward",
    )(fetched, *map(in_hbm, loads))
    near_items = exchange(item_vec, "z")

    loads = (column, hot_table, pos_embed, norm_gain, out_gain)
    loads += (in_proj, w_query, w_key, w_value, w_out)
    kept = (
        shape((span, width), F32),
        shape((span, width), BF),
        shape((users * heads, width), BF),
        shape((users * heads, span), F32),
        shape((PAD, width), F32),
    )
    user_vec, hidden, normed, qk, weights, mixed = pl.pallas_call(
        functools.partial(user_forward_kernel, users),
        out_shape=(shape((PAD, width), BF), *map(hbm, kept)),
        in_specs=[VMEM] + [HBM] * len(loads),
        out_specs=(VMEM,) + (HBM,) * len(kept),
        scratch_shapes=like(loads + kept) + [sems(len(loads)), sems(len(kept))],
        compiler_params=params(40),
        name="user_forward",
    )(fetched, *map(in_hbm, loads))

    rows = owners // near * (near * users + 8)
    spread = pl.pallas_call(
        functools.partial(arrange_kernel, users, near),
        out_shape=shape((rows, width), BF),
        in_specs=[VMEM, VMEM],
        out_specs=VMEM,
        compiler_params=params(24),
        name="arrange",
    )(near_items, user_vec)
    gathered = exchange(spread, ("x", "y"))
    swapped = lax.ppermute(gathered, "tower", swap)
    place = jnp.stack([lax.axis_index(("x", "y")), lax.axis_index("z")]).astype(jnp.int32)
    d_user, d_part, loss = pl.pallas_call(
        functools.partial(softmax_kernel, users, near, scale),
        out_shape=(shape((PAD, width), F32), shape((near * 8, width), BF), shape((8, 128), F32)),
        in_specs=[SMEM, VMEM, VMEM],
        out_specs=(VMEM, VMEM, VMEM),
        scratch_shapes=[pltpu.VMEM((rows, 2 * owners // near * users), F32)],
        compiler_params=params(32),
        name="softmax",
    )(place, gathered, swapped)
    parts = exchange(d_part, "z")

    loads = (mixed, out_gain, w_out, w_value, normed, weights, qk)
    loads += (w_key, w_query, hidden, norm_gain, in_proj)
    ahead = (row, item_gain, outer, inner, item_w2, item_w1)
    d_rows, *item_ready = pl.pallas_call(
        functools.partial(user_backward_kernel, users),
        out_shape=(shape((span, emb), BF), *map(vmem, ahead)),
        in_specs=[VMEM] + [HBM] * 18,
        out_specs=(VMEM,) * 7,
        scratch_shapes=like(loads) + [pltpu.VMEM((span, width), F32), sems(18)],
        compiler_params=params(40),
        name="user_backward",
    )(d_user, *map(in_hbm, loads + ahead))
    outgoing = pl.pallas_call(
        functools.partial(item_backward_kernel, users),
        out_shape=shape((slots, emb), BF),
        in_specs=[VMEM] * 8,
        out_specs=VMEM,
        compiler_params=params(32),
        name="item_backward",
    )(parts, d_rows, *map(in_vmem, item_ready))

    returned = exchange(outgoing, SHARD)
    part, mine = pl.pallas_call(
        scatter_kernel,
        out_shape=(shape((rare_count, emb), BF), shape((owners, 1, emb + 128), F32)),
        in_specs=[VMEM, VMEM, VMEM],
        out_specs=(VMEM, VMEM),
        compiler_params=params(24),
        name="scatter",
    )(returned, asked_row, loss)
    rare_grad = part.astype(F32) + lax.ppermute(part, "tower", swap).astype(F32)
    sums = exchange(mine, SHARD)
    other_sums = lax.ppermute(sums, "tower", swap)
    hot_total, loss_total = pl.pallas_call(
        functools.partial(finish_kernel, total),
        out_shape=(shape((owners, emb), F32), shape((1, 1), F32)),
        in_specs=[VMEM, VMEM],
        out_specs=(VMEM, VMEM),
        compiler_params=params(24),
        name="finish",
    )(sums, other_sums)
    return (hot_total, rare_grad, loss_total[0, 0])


def solution(mesh):
    sizes = (mesh.shape["tower"], 4, 4, mesh.shape["shard"] // 16)
    mesh = Mesh(mesh.devices.reshape(sizes), ("tower",) + SHARD)
    return jax.shard_map(
        shards,
        mesh=mesh,
        in_specs=(
            P(("tower",) + SHARD, None),
            P(("tower",) + SHARD),
            P(),
            P(SHARD, None),
            P(),
            P(),
            P(),
            P(),
            P(),
            P(),
            P(),
            P(),
            P(),
            P(),
            P(),
        ),
        out_specs=(P(), P(SHARD, None), P()),
        check_vma=False,
    )
```

```python
import functools
import math

import jax
import jax.numpy as jnp
from jax import lax
from jax.experimental import pallas as pl
from jax.experimental.pallas import tpu as pltpu
from jax.sharding import Mesh
from jax.sharding import PartitionSpec as P

HEAD_DIM = 64
EPS = 1e-06
SLOTS = 8
HOT_SLOT = 5
HOT_CODE = 4096
GROUP = ("x", "y", "zh")
LINE = ("zh", "zl")
SHARD = GROUP + ("zl",)
PAD = 16
BF = jnp.bfloat16
F32 = jnp.float32
VMEM = pl.BlockSpec(memory_space=pltpu.VMEM)
SMEM = pl.BlockSpec(memory_space=pltpu.SMEM)
HBM = pl.BlockSpec(memory_space=pltpu.HBM)
NT = (((1,), (1,)), ((), ()))
TN = (((0,), (0,)), ((), ()))


def dot(a, b):
    return jnp.dot(a, b, preferred_element_type=F32)


def dot_nt(a, b):
    return lax.dot_general(a, b, NT, preferred_element_type=F32)


def dot_tn(a, b):
    return lax.dot_general(a, b, TN, preferred_element_type=F32)


def iota(shape, axis):
    return lax.broadcasted_iota(jnp.int32, shape, axis)


def one_hot(mask):
    return jnp.where(mask, 1.0, 0.0).astype(BF)


def params(mib):
    return pltpu.CompilerParams(vmem_limit_bytes=mib * 1024 * 1024)


def copies_of(pairs, sems):
    copies = [pltpu.make_async_copy(a, b, sems.at[i]) for i, (a, b) in enumerate(pairs)]
    for copy in copies:
        copy.start()
    return copies


def index_kernel(
    owners,
    history_hbm,
    items_hbm,
    table_hbm,
    request_ref,
    known_ref,
    row_hbm,
    column_hbm,
    history_ref,
    items_ref,
    table,
    row,
    column,
    sems,
):
    loads = copies_of(
        [(history_hbm, history_ref), (items_hbm, items_ref), (table_hbm, table)], sems
    )
    loads[0].wait()
    loads[1].wait()
    hot_count = owners
    rare_count = table.shape[0]
    users = history_ref.shape[0]
    span = row.shape[1]
    parts = [history_ref[u : u + 1, :] for u in range(users)] + [items_ref[...]]
    filled = sum(p.shape[1] for p in parts)
    ids = jnp.concatenate(parts + [jnp.full((1, span - filled), -1, jnp.int32)], axis=1)
    is_rare = ids >= hot_count
    index = ids - hot_count
    owner = jnp.where(is_rare, index // rare_count, -1)
    value = jnp.where(is_rare, index % rare_count + 1, 0).astype(F32)
    hits = iota((owners, span), 0) == owner
    before = one_hot(iota((span, span), 0) < iota((span, span), 1))
    earlier = dot(one_hot(hits), before)
    position = jnp.sum(jnp.where(hits, earlier, 0.0), axis=0, keepdims=True).astype(jnp.int32)
    places = jnp.where(
        is_rare, owner * SLOTS + position, jnp.where(ids >= 0, ids + HOT_CODE, -1)
    )
    row[...] = jnp.broadcast_to(places, row.shape)
    column[...] = jnp.transpose(jnp.broadcast_to(places.astype(F32), (128, span))).astype(jnp.int32)
    saves = copies_of([(row, row_hbm), (column, column_hbm)], sems.at[pl.ds(3, 2)])
    order = jnp.where(hits, earlier, -1.0)
    lanes = iota(request_ref.shape, 1)
    request = jnp.zeros(request_ref.shape, F32)
    for slot in range(HOT_SLOT):
        wanted = jnp.sum(jnp.where(order == float(slot), value, 0.0), axis=1, keepdims=True)
        request = jnp.where(lanes == slot, wanted, request)
    request_ref[...] = request.astype(jnp.int32)
    loads[2].wait()
    known_ref[...] = table[...].astype(BF)
    for save in saves:
        save.wait()


def serve_kernel(
    asked_ref, known_ref, hot_hbm, column_hbm, served, hot_ref, column_ref, row_hbm, hot, row, sems
):
    span = column_hbm.shape[0] - 128
    loads = copies_of(
        [(hot_hbm, hot), (column_hbm.at[pl.ds(span, PAD)], column_ref)], sems
    )
    slots = served.shape[0]
    sources = asked_ref.shape[0]
    asked = asked_ref[...]
    high = (asked // 2).astype(F32).astype(BF)
    low = (asked % 2).astype(F32).astype(BF)
    expand = one_hot(iota((slots, sources), 0) // SLOTS == iota((slots, sources), 1))
    wide = 2.0 * dot(expand, high) + dot(expand, low)
    mine = iota(wide.shape, 1) == iota(wide.shape, 0) % SLOTS
    index = jnp.sum(jnp.where(mine, wide, 0.0), axis=1, keepdims=True) - 1.0
    index = jnp.broadcast_to(index, wide.shape)
    row[...] = jnp.transpose(index)[0:8].astype(jnp.int32)
    save = pltpu.make_async_copy(row, row_hbm, sems.at[2])
    save.start()
    index = index.astype(jnp.int32)
    lanes = iota(index.shape, 1)
    rows = known_ref.shape[0]
    picks = jnp.concatenate(
        [one_hot(index == lanes + 128 * j) for j in range(rows // 128)], axis=1
    )
    served[...] = dot(picks, known_ref[...]).astype(BF)
    for load in loads:
        load.wait()
    hot_ref[...] = hot[...].astype(BF)
    save.wait()


def head_mask(heads, width):
    return iota((heads, width), 1) // HEAD_DIM == iota((heads, width), 0)


def spread_heads(values, mask, users):
    return jnp.concatenate(
        [jnp.where(mask, values[u : u + 1], 0.0) for u in range(users)], axis=0
    ).astype(BF)


def join_heads(full, mask, users):
    heads = mask.shape[0]
    parts = [
        jnp.sum(
            jnp.where(mask, full[u * heads : (u + 1) * heads], 0.0), axis=0, keepdims=True
        )
        for u in range(users)
    ]
    return jnp.concatenate(parts + [jnp.zeros((PAD - users, full.shape[1]), F32)], axis=0)


def look_up(column, fetched, hot):
    lanes = iota(column.shape, 1)
    slots = fetched.shape[0]
    picks = jnp.concatenate(
        [one_hot(column == lanes + 128 * j) for j in range(slots // 128)], axis=1
    )
    hot_picks = one_hot(column == lanes + HOT_CODE)
    return (dot(picks, fetched[...]) + dot(hot_picks, hot[...].astype(BF))).astype(BF)


def item_forward_kernel(users, fetched_ref, hot_ref, column_ref, *refs):
    sources, refs = refs[:3], refs[3:]
    vectors_ref, inner_hbm, refs = refs[0], refs[1], refs[2:]
    targets, (inner_ref, sems) = refs[:3], refs[3:]
    item_w1, item_w2, gain = targets
    copies = copies_of(zip(sources, targets), sems)
    rows = look_up(column_ref[...], fetched_ref, hot_ref)
    copies[0].wait()
    inner = dot(rows, item_w1[...])
    inner_ref[...] = inner
    save = pltpu.make_async_copy(inner_ref, inner_hbm, sems.at[3])
    save.start()
    gated = (inner * jax.nn.sigmoid(inner)).astype(BF)
    copies[1].wait()
    copies[2].wait()
    outer = dot(gated, item_w2[...])
    scale = lax.rsqrt(jnp.mean(outer * outer, axis=-1, keepdims=True) + EPS)
    vectors = jnp.where(iota(outer.shape, 0) < users, outer * scale * gain[...], 0.0)
    peers = vectors_ref.shape[0] // 8
    vectors_ref[...] = jnp.concatenate([vectors[0:8]] * peers, axis=0).astype(BF)
    save.wait()


def user_forward_kernel(users, *refs):
    fetched_ref, sources, refs = refs[0], refs[1:11], refs[11:]
    vectors_ref, kept_hbm, refs = refs[0], refs[1:6], refs[6:]
    targets, kept, (in_sems, out_sems) = refs[:10], refs[10:15], refs[15:]
    column_of, hot, pos_of, norm_gain_ref, out_gain_ref = targets[:5]
    in_proj, w_query, w_key, w_value, w_out = targets[5:]
    hidden_ref, normed_ref, qk_ref, weights_ref, mixed_ref = kept
    copies = copies_of(zip(sources, targets), in_sems)
    saves = [
        pltpu.make_async_copy(a, b, out_sems.at[i]) for i, (a, b) in enumerate(zip(kept, kept_hbm))
    ]
    hist, width = pos_of.shape
    heads = width // HEAD_DIM
    span = users * hist
    copies[0].wait()
    copies[1].wait()
    rows = look_up(column_of[0:span, :], fetched_ref, hot)
    for copy in copies[2:6]:
        copy.wait()
    pos = pos_of[...].astype(F32)
    hidden = dot(rows, in_proj[...]) + jnp.concatenate([pos] * users, axis=0)
    hidden_ref[...] = hidden
    saves[0].start()
    scale = lax.rsqrt(jnp.mean(hidden * hidden, axis=-1, keepdims=True) + EPS)
    normed = (hidden * scale * norm_gain_ref[...]).astype(BF)
    normed_ref[...] = normed
    saves[1].start()
    last = jnp.concatenate(
        [normed[(u + 1) * hist - PAD : (u + 1) * hist].astype(F32)[PAD - 1 :] for u in range(users)]
        + [jnp.zeros((PAD - users, width), F32)],
        axis=0,
    ).astype(BF)
    mask = head_mask(heads, width)
    copies[6].wait()
    query = dot(last, w_query[...]).astype(BF).astype(F32)
    copies[7].wait()
    qk = dot_nt(spread_heads(query, mask, users), w_key[...]).astype(BF)
    qk_ref[...] = qk
    saves[2].start()
    shape = (users * heads, span)
    own = iota(shape, 0) // heads == iota(shape, 1) // hist
    scores = jnp.where(own, dot_nt(qk, normed) * (1.0 / math.sqrt(HEAD_DIM)), -jnp.inf)
    raised = jnp.exp(scores - jnp.max(scores, axis=1, keepdims=True))
    weights = raised / jnp.sum(raised, axis=1, keepdims=True)
    weights_ref[...] = weights
    saves[3].start()
    mixes = dot(weights.astype(BF), normed).astype(BF)
    copies[8].wait()
    attended = join_heads(dot(mixes, w_value[...]), mask, users).astype(BF)
    copies[9].wait()
    hidden_last = jnp.concatenate(
        [hidden[(u + 1) * hist - 1 : (u + 1) * hist] for u in range(users)]
        + [jnp.zeros((PAD - users, width), F32)],
        axis=0,
    )
    mixed = hidden_last + dot(attended, w_out[...])
    mixed_ref[...] = mixed
    saves[4].start()
    scale = lax.rsqrt(jnp.mean(mixed * mixed, axis=-1, keepdims=True) + EPS)
    vectors_ref[...] = (mixed * scale * out_gain_ref[...]).astype(BF)
    for save in saves:
        save.wait()


def arrange_kernel(users, near, near_ref, vectors_ref, spread_ref):
    total, width = spread_ref.shape
    block = near * users + 8
    pair = 2 * block
    at = iota((pair, near * 8), 0) % block
    source = jnp.where(at < near * users, at // users * 8 + at % users, -1)
    item_rows = dot(one_hot(iota((pair, near * 8), 1) == source), near_ref[...])
    at = iota((pair, PAD), 0) % block
    source = jnp.where((at >= near * users) & (at < (near + 1) * users), at - near * users, -1)
    user_rows = dot(one_hot(iota((pair, PAD), 1) == source), vectors_ref[...])
    rows = (item_rows + user_rows).astype(BF)
    for i in range(total // pair):
        spread_ref[i * pair : (i + 1) * pair, :] = rows


def softmax_kernel(
    users, near, scale, place_ref, gathered_ref, swapped_ref, d_user_ref, d_part_ref, raised_ref
):
    rows, width = gathered_ref.shape
    items = near * users
    block = items + 8
    blocks = rows // block
    mine, plane = place_ref[0], place_ref[1]
    own, other = gathered_ref[...], swapped_ref[...]
    shape = (blocks * users, rows)
    line = iota(shape, 0)
    picks = one_hot(iota(shape, 1) == line // users * block + items + line % users)
    group_users = jnp.concatenate([dot(picks, own), dot(picks, other)], axis=0).astype(BF)
    total = 2 * blocks * users

    shape = (rows, total)
    line = iota(shape, 0)
    valid = line % block < items
    first = jnp.where(valid, scale * dot_nt(own, group_users), -jnp.inf)
    second = jnp.where(valid, scale * dot_nt(other, group_users), -jnp.inf)
    top = jnp.maximum(
        jnp.max(first, axis=0, keepdims=True), jnp.max(second, axis=0, keepdims=True)
    )
    raised = jnp.exp(first - top)
    raised_ref[...] = raised
    other_raised = jnp.exp(second - top)
    count = jnp.sum(raised, axis=0, keepdims=True) + jnp.sum(other_raised, axis=0, keepdims=True)
    share = 1.0 / count

    line = (items, total)
    target = (iota(line, 0) // users == plane) & (
        iota(line, 1) == mine * users + iota(line, 0) % users
    )
    near_raised = raised_ref[pl.ds(pl.multiple_of(mine * block, 8), items), :]
    slope = (near_raised * share - jnp.where(target, 1.0, 0.0)).astype(BF)
    apart = (near * 8, items)
    at = iota(apart, 0)
    apart = one_hot((at % 8 < users) & (iota(apart, 1) == at // 8 * users + at % 8))
    d_part = scale * dot(dot(apart, slope).astype(BF), group_users)

    who = iota(shape, 1) - mine * users
    target = (who >= 0) & (who < users) & (iota(shape, 0) == mine * block + plane * users + who)
    slope = (raised * share - jnp.where(target, 1.0, 0.0)).astype(BF)
    other_slope = (other_raised * share).astype(BF)
    self = (PAD, total)
    self = one_hot((iota(self, 0) < users) & (iota(self, 1) == mine * users + iota(self, 0)))
    d_user = dot(dot_nt(self, slope).astype(BF), own)
    d_user = d_user + dot(dot_nt(self, other_slope).astype(BF), other)
    d_user_ref[...] = (scale * d_user).astype(BF).astype(F32)
    each = jnp.sum(jnp.where(target, top + jnp.log(count) - first, 0.0), axis=0, keepdims=True)
    loss = jnp.sum(each, axis=1, keepdims=True)
    high = loss.astype(BF).astype(F32)
    middle = (loss - high).astype(BF).astype(F32)
    low = loss - high - middle
    shape = d_part.shape
    lanes = iota(shape, 1)
    loss = jnp.where(lanes == 0, high, jnp.where(lanes == 1, middle, jnp.where(lanes == 2, low, 0.0)))
    d_part_ref[...] = jnp.where(iota(shape, 0) % 8 == users, loss, d_part).astype(BF)


def norm_backward(values, cotangent, gain):
    inverse = lax.rsqrt(jnp.mean(values * values, axis=-1, keepdims=True) + EPS)
    pulled = cotangent * gain
    along = jnp.mean(pulled * values, axis=-1, keepdims=True)
    return inverse * pulled - values * (inverse * inverse * inverse * along)


def user_backward_kernel(users, d_user_ref, *refs):
    sources, refs = refs[:17], refs[17:]
    d_rows_ref, ahead, outer_ref, refs = refs[0], refs[1:6], refs[6], refs[7:]
    targets, (d_normed, sems) = refs[:12], refs[12:]
    mixed_ref, out_gain_ref, w_out, w_value, normed_ref, weights_ref, qk_ref = targets[:7]
    w_key, w_query, hidden_ref, norm_gain_ref, in_proj = targets[7:]
    copies = copies_of(zip(sources, tuple(targets) + tuple(ahead)), sems)
    span, width = hidden_ref.shape
    hist = span // users
    heads = width // HEAD_DIM
    mask = head_mask(heads, width)
    for copy in copies[:3]:
        copy.wait()
    d_mixed = norm_backward(mixed_ref[...], d_user_ref[...], out_gain_ref[...])
    d_attended = dot_nt(d_mixed.astype(BF), w_out[...])
    copies[3].wait()
    d_mixes = dot_nt(spread_heads(d_attended, mask, users), w_value[...]).astype(BF)
    for copy in copies[4:7]:
        copy.wait()
    normed = normed_ref[...]
    weights = weights_ref[...]
    shape = weights.shape
    own = iota(shape, 0) // heads == iota(shape, 1) // hist
    d_weights = jnp.where(own, dot_nt(d_mixes, normed), 0.0)
    d_scores = weights * (d_weights - jnp.sum(weights * d_weights, axis=1, keepdims=True))
    d_scores = (d_scores * (1.0 / math.sqrt(HEAD_DIM))).astype(BF)
    d_normed[...] = dot_tn(
        jnp.concatenate([weights.astype(BF), d_scores], axis=0),
        jnp.concatenate([d_mixes, qk_ref[...]], axis=0),
    )
    d_qk = dot(d_scores, normed).astype(BF)
    copies[7].wait()
    d_query = join_heads(dot(d_qk, w_key[...]), mask, users).astype(BF)
    copies[8].wait()
    d_last = dot_nt(d_query, w_query[...])
    for u in range(users):
        at = slice((u + 1) * hist - 1, (u + 1) * hist)
        d_normed[at, :] = d_normed[at, :] + d_last[u : u + 1]
    copies[9].wait()
    copies[10].wait()
    d_normed[...] = norm_backward(hidden_ref[...], d_normed[...], norm_gain_ref[...])
    for u in range(users):
        at = slice((u + 1) * hist - 1, (u + 1) * hist)
        d_normed[at, :] = d_normed[at, :] + d_mixed[u : u + 1]
    copies[11].wait()
    d_rows_ref[...] = dot_nt(d_normed[...].astype(BF), in_proj[...]).astype(BF)
    for copy in copies[12:]:
        copy.wait()
    inner = ahead[2][...]
    outer_ref[...] = dot((inner * jax.nn.sigmoid(inner)).astype(BF), ahead[3][...])


def item_backward_kernel(users, parts_ref, d_rows_ref, *refs):
    row_ref, gain, inner_ref, item_w2, item_w1, outer_ref, outgoing, loss_ref = refs
    slots = outgoing.shape[0]
    span = d_rows_ref.shape[0]
    wide = row_ref.shape[1]
    peers = parts_ref.shape[0]
    shape = (PAD, peers)
    sums = dot(one_hot(iota(shape, 1) % 8 == iota(shape, 0)), parts_ref[...])
    shape = (1, 128)
    loss = jnp.where(iota(shape, 1) < 3, sums[users : users + 1, 0:128], 0.0)
    loss_ref[...] = jnp.broadcast_to(jnp.sum(loss, axis=1, keepdims=True), loss_ref.shape)
    d_item = jnp.where(iota(sums.shape, 0) < users, sums, 0.0).astype(BF).astype(F32)
    line = iota((slots, 1), 0)
    slot = line % SLOTS
    hot = HOT_CODE + line // (2 * SLOTS) + (slot - HOT_SLOT) * (slots // (2 * SLOTS))
    code = jnp.where(slot < HOT_SLOT, line, jnp.where(slot < HOT_SLOT + 2, hot, -2))
    picks = one_hot(code == row_ref[0:1, :])
    total = dot(picks[:, 0:span], d_rows_ref[...])
    d_outer = norm_backward(outer_ref[...], d_item, gain[...])
    inner = inner_ref[...]
    gate = jax.nn.sigmoid(inner)
    d_inner = dot_nt(d_outer.astype(BF), item_w2[...]) * (gate * (1.0 + inner * (1.0 - gate)))
    d_items = dot_nt(d_inner.astype(BF), item_w1[...])
    d_items = jnp.concatenate(
        [d_items, jnp.zeros((wide - span - PAD, d_items.shape[1]), F32)], axis=0
    ).astype(BF)
    outgoing[...] = (total + dot(picks[:, span:], d_items)).astype(BF)


def scatter_kernel(returned_ref, row_ref, loss_ref, part_ref, sums_ref):
    rows, emb = part_ref.shape
    slots = returned_ref.shape[0]
    returned = returned_ref[...]
    picks = one_hot(iota((rows, slots), 0) == row_ref[0:1, :])
    part_ref[...] = dot(picks, returned).astype(BF)
    shape = (PAD, slots)
    hot = dot(one_hot((iota(shape, 0) < 2) & (iota(shape, 1) % SLOTS == iota(shape, 0) + HOT_SLOT)), returned)
    halves = [hot[i : i + 1, j : j + 128] for i in range(2) for j in range(0, emb, 128)]
    block = jnp.concatenate(halves + [loss_ref[0 : 8 - len(halves), :]], axis=0)
    sums_ref[...] = jnp.concatenate([block] * (sums_ref.shape[0] // 8), axis=0)


def finish_kernel(count, sums_ref, other_ref, hot_ref, loss_ref):
    emb = hot_ref.shape[1]
    groups = sums_ref.shape[0] // 8

    def of_row(row):
        at = pl.ds(row, groups, stride=8)
        return sums_ref[at, :] + other_ref[at, :]

    row = 0
    for i in range(2):
        for j in range(0, emb, 128):
            hot_ref[i * groups : (i + 1) * groups, j : j + 128] = of_row(row)
            row += 1
    loss_ref[...] = jnp.sum(of_row(row)[:, 0:1], axis=0, keepdims=True) / count


def shards(
    history,
    item_ids,
    hot_table,
    rare_table,
    in_proj,
    pos_embed,
    norm_gain,
    w_query,
    w_key,
    w_value,
    w_out,
    out_gain,
    item_w1,
    item_w2,
    item_gain,
):
    users, hist = history.shape
    emb = hot_table.shape[1]
    rare_count = rare_table.shape[0]
    width = in_proj.shape[1]
    heads = width // HEAD_DIM
    scale = 4.0 / math.sqrt(width)
    owners = lax.axis_size(SHARD)
    towers = lax.axis_size("tower")
    near = lax.axis_size(LINE)
    total = users * towers * owners
    slots = owners * SLOTS
    span = users * hist
    wide = -(-(span + PAD) // 128) * 128
    swap = [(i, towers - 1 - i) for i in range(towers)]
    shape = jax.ShapeDtypeStruct
    sems = lambda n: pltpu.SemaphoreType.DMA((n,))
    vmem = lambda a: pltpu.VMEM(a.shape, a.dtype)
    hbm = lambda a: pltpu.HBM(a.shape, a.dtype)
    in_hbm = lambda a: pltpu.with_memory_space_constraint(a, pltpu.HBM)
    in_vmem = lambda a: pltpu.with_memory_space_constraint(a, pltpu.VMEM)
    like = lambda arrays: [pltpu.VMEM(a.shape, a.dtype) for a in arrays]
    exchange = functools.partial(lax.all_to_all, split_axis=0, concat_axis=0, tiled=True)

    places = (shape((8, wide), jnp.int32), shape((wide, 128), jnp.int32))
    loads = (history, item_ids.reshape(1, users), rare_table)
    request, known, row, column = pl.pallas_call(
        functools.partial(index_kernel, owners),
        out_shape=(
            shape((owners, 128), jnp.int32),
            pltpu.VMEM((rare_count, emb), BF),
            *map(hbm, places),
        ),
        in_specs=[HBM] * 3,
        out_specs=(VMEM, VMEM, HBM, HBM),
        scratch_shapes=like(loads + places) + [sems(5)],
        compiler_params=params(24),
        name="index",
    )(*map(in_hbm, loads))
    asked = exchange(request, SHARD)
    served, hot_ready, item_column, asked_row = pl.pallas_call(
        serve_kernel,
        out_shape=(
            shape((slots, emb), BF),
            pltpu.VMEM(hot_table.shape, BF),
            pltpu.VMEM((PAD, 128), jnp.int32),
            pltpu.HBM((8, slots), jnp.int32),
        ),
        in_specs=[VMEM, VMEM, HBM, HBM],
        out_specs=(VMEM, VMEM, VMEM, HBM),
        scratch_shapes=[
            pltpu.VMEM(hot_table.shape, F32),
            pltpu.VMEM((8, slots), jnp.int32),
            sems(3),
        ],
        compiler_params=params(24),
        name="serve",
    )(asked, in_vmem(known), in_hbm(hot_table), in_hbm(column))
    fetched = exchange(served, SHARD)

    norm_gain, out_gain, item_gain = (g.reshape(1, width) for g in (norm_gain, out_gain, item_gain))
    loads = (item_w1, item_w2, item_gain)
    item_vec, inner = pl.pallas_call(
        functools.partial(item_forward_kernel, users),
        out_shape=(shape((near * 8, width), BF), pltpu.HBM((PAD, width), F32)),
        in_specs=[VMEM] * 3 + [HBM] * 3,
        out_specs=(VMEM, HBM),
        scratch_shapes=like(loads) + [pltpu.VMEM((PAD, width), F32), sems(4)],
        compiler_params=params(24),
        name="item_forward",
    )(fetched, in_vmem(hot_ready), in_vmem(item_column), *map(in_hbm, loads))
    near_items = exchange(item_vec, LINE)

    loads = (column, hot_table, pos_embed, norm_gain, out_gain)
    loads += (in_proj, w_query, w_key, w_value, w_out)
    kept = (
        shape((span, width), F32),
        shape((span, width), BF),
        shape((users * heads, width), BF),
        shape((users * heads, span), F32),
        shape((PAD, width), F32),
    )
    user_vec, hidden, normed, qk, weights, mixed = pl.pallas_call(
        functools.partial(user_forward_kernel, users),
        out_shape=(shape((PAD, width), BF), *map(hbm, kept)),
        in_specs=[VMEM] + [HBM] * len(loads),
        out_specs=(VMEM,) + (HBM,) * len(kept),
        scratch_shapes=like(loads + kept) + [sems(len(loads)), sems(len(kept))],
        compiler_params=params(40),
        name="user_forward",
    )(fetched, *map(in_hbm, loads))

    rows = owners // near * (near * users + 8)
    spread = pl.pallas_call(
        functools.partial(arrange_kernel, users, near),
        out_shape=shape((rows, width), BF),
        in_specs=[VMEM, VMEM],
        out_specs=VMEM,
        compiler_params=params(24),
        name="arrange",
    )(near_items, user_vec)
    gathered = exchange(spread, ("x", "y"))
    swapped = lax.ppermute(gathered, "tower", swap)
    place = jnp.stack([lax.axis_index(("x", "y")), lax.axis_index(LINE)]).astype(jnp.int32)
    d_user, d_part = pl.pallas_call(
        functools.partial(softmax_kernel, users, near, scale),
        out_shape=(shape((PAD, width), F32), shape((near * 8, width), BF)),
        in_specs=[SMEM, VMEM, VMEM],
        out_specs=(VMEM, VMEM),
        scratch_shapes=[pltpu.VMEM((rows, 2 * owners // near * users), F32)],
        compiler_params=params(32),
        name="softmax",
    )(place, gathered, swapped)
    parts = exchange(d_part, LINE)

    loads = (mixed, out_gain, w_out, w_value, normed, weights, qk)
    loads += (w_key, w_query, hidden, norm_gain, in_proj)
    ahead = (row, item_gain, inner, item_w2, item_w1)
    d_rows, *item_ready = pl.pallas_call(
        functools.partial(user_backward_kernel, users),
        out_shape=(shape((span, emb), BF), *map(vmem, ahead), pltpu.VMEM((PAD, width), F32)),
        in_specs=[VMEM] + [HBM] * 17,
        out_specs=(VMEM,) * 7,
        scratch_shapes=like(loads) + [pltpu.VMEM((span, width), F32), sems(17)],
        compiler_params=params(40),
        name="user_backward",
    )(d_user, *map(in_hbm, loads + ahead))
    outgoing, loss = pl.pallas_call(
        functools.partial(item_backward_kernel, users),
        out_shape=(shape((slots, emb), BF), shape((8, 128), F32)),
        in_specs=[VMEM] * 8,
        out_specs=(VMEM, VMEM),
        compiler_params=params(32),
        name="item_backward",
    )(parts, d_rows, *map(in_vmem, item_ready))

    returned = exchange(outgoing, SHARD)
    part, mine = pl.pallas_call(
        scatter_kernel,
        out_shape=(shape((rare_count, emb), BF), shape((owners // 2 * 8, 128), F32)),
        in_specs=[VMEM, VMEM, VMEM],
        out_specs=(VMEM, VMEM),
        compiler_params=params(24),
        name="scatter",
    )(returned, asked_row, loss)
    rare_grad = part.astype(F32) + lax.ppermute(part, "tower", swap).astype(F32)
    sums = exchange(mine, GROUP)
    other_sums = lax.ppermute(sums, "tower", swap)
    hot_total, loss_total = pl.pallas_call(
        functools.partial(finish_kernel, total * (near // 2)),
        out_shape=(shape((owners, emb), F32), shape((1, 1), F32)),
        in_specs=[VMEM, VMEM],
        out_specs=(VMEM, VMEM),
        compiler_params=params(24),
        name="finish",
    )(sums, other_sums)
    return (hot_total, rare_grad, loss_total[0, 0])


def solution(mesh):
    sizes = (mesh.shape["tower"], 4, 4, mesh.shape["shard"] // 32, 2)
    mesh = Mesh(mesh.devices.reshape(sizes), ("tower",) + SHARD)
    return jax.shard_map(
        shards,
        mesh=mesh,
        in_specs=(
            P(("tower",) + SHARD, None),
            P(("tower",) + SHARD),
            P(),
            P(SHARD, None),
            P(),
            P(),
            P(),
            P(),
            P(),
            P(),
            P(),
            P(),
            P(),
            P(),
            P(),
        ),
        out_specs=(P(), P(SHARD, None), P()),
        check_vma=False,
    )
```

```python
import functools
import math

import jax
import jax.numpy as jnp
from jax import lax
from jax.experimental import pallas as pl
from jax.experimental.pallas import tpu as pltpu
from jax.sharding import Mesh
from jax.sharding import PartitionSpec as P

HEAD_DIM = 64
EPS = 1e-06
SLOTS = 8
HOT_SLOT = 5
PIECES = 4
HOT_CODE = 4096
GROUP = ("x", "y", "zh")
LINE = ("zh", "zl")
SHARD = GROUP + ("zl",)
PAD = 16
BF = jnp.bfloat16
F32 = jnp.float32
VMEM = pl.BlockSpec(memory_space=pltpu.VMEM)
SMEM = pl.BlockSpec(memory_space=pltpu.SMEM)
HBM = pl.BlockSpec(memory_space=pltpu.HBM)
NT = (((1,), (1,)), ((), ()))
TN = (((0,), (0,)), ((), ()))


def dot(a, b):
    return jnp.dot(a, b, preferred_element_type=F32)


def dot_nt(a, b):
    return lax.dot_general(a, b, NT, preferred_element_type=F32)


def dot_tn(a, b):
    return lax.dot_general(a, b, TN, preferred_element_type=F32)


def iota(shape, axis):
    return lax.broadcasted_iota(jnp.int32, shape, axis)


def one_hot(mask):
    return jnp.where(mask, 1.0, 0.0).astype(BF)


def params(mib):
    return pltpu.CompilerParams(vmem_limit_bytes=mib * 1024 * 1024)


def copies_of(pairs, sems):
    copies = [pltpu.make_async_copy(a, b, sems.at[i]) for i, (a, b) in enumerate(pairs)]
    for copy in copies:
        copy.start()
    return copies


def index_kernel(
    owners,
    history_hbm,
    items_hbm,
    table_hbm,
    request_ref,
    known_ref,
    row_hbm,
    column_hbm,
    history_ref,
    items_ref,
    table,
    row,
    column,
    sems,
):
    loads = copies_of(
        [(history_hbm, history_ref), (items_hbm, items_ref), (table_hbm, table)], sems
    )
    loads[0].wait()
    loads[1].wait()
    hot_count = owners
    rare_count = table.shape[0]
    users = history_ref.shape[0]
    span = row.shape[1]
    parts = [history_ref[u : u + 1, :] for u in range(users)] + [items_ref[...]]
    filled = sum(p.shape[1] for p in parts)
    ids = jnp.concatenate(parts + [jnp.full((1, span - filled), -1, jnp.int32)], axis=1)
    is_rare = ids >= hot_count
    index = ids - hot_count
    owner = jnp.where(is_rare, index // rare_count, -1)
    value = jnp.where(is_rare, index % rare_count + 1, 0).astype(F32)
    hits = iota((owners, span), 0) == owner
    before = one_hot(iota((span, span), 0) < iota((span, span), 1))
    earlier = dot(one_hot(hits), before)
    position = jnp.sum(jnp.where(hits, earlier, 0.0), axis=0, keepdims=True).astype(jnp.int32)
    places = jnp.where(
        is_rare, owner * SLOTS + position, jnp.where(ids >= 0, ids + HOT_CODE, -1)
    )
    row[...] = jnp.broadcast_to(places, row.shape)
    column[...] = jnp.transpose(jnp.broadcast_to(places.astype(F32), (128, span))).astype(jnp.int32)
    saves = copies_of([(row, row_hbm), (column, column_hbm)], sems.at[pl.ds(3, 2)])
    order = jnp.where(hits, earlier, -1.0)
    lanes = iota(request_ref.shape, 1)
    request = jnp.zeros(request_ref.shape, F32)
    for slot in range(HOT_SLOT):
        wanted = jnp.sum(jnp.where(order == float(slot), value, 0.0), axis=1, keepdims=True)
        request = jnp.where(lanes == slot, wanted, request)
    request_ref[...] = request.astype(jnp.int32)
    loads[2].wait()
    known_ref[...] = table[...].astype(BF)
    for save in saves:
        save.wait()


def serve_kernel(
    asked_ref, known_ref, hot_hbm, column_hbm, served, hot_ref, column_ref, row_hbm, hot, row, sems
):
    span = column_hbm.shape[0] - 128
    loads = copies_of(
        [(hot_hbm, hot), (column_hbm.at[pl.ds(span, PAD)], column_ref)], sems
    )
    slots = served.shape[0]
    sources = asked_ref.shape[0]
    asked = asked_ref[...]
    high = (asked // 2).astype(F32).astype(BF)
    low = (asked % 2).astype(F32).astype(BF)
    expand = one_hot(iota((slots, sources), 0) // SLOTS == iota((slots, sources), 1))
    wide = 2.0 * dot(expand, high) + dot(expand, low)
    mine = iota(wide.shape, 1) == iota(wide.shape, 0) % SLOTS
    index = jnp.sum(jnp.where(mine, wide, 0.0), axis=1, keepdims=True) - 1.0
    index = jnp.broadcast_to(index, wide.shape)
    row[...] = jnp.transpose(index)[0:8].astype(jnp.int32)
    save = pltpu.make_async_copy(row, row_hbm, sems.at[2])
    save.start()
    index = index.astype(jnp.int32)
    lanes = iota(index.shape, 1)
    rows = known_ref.shape[0]
    picks = jnp.concatenate(
        [one_hot(index == lanes + 128 * j) for j in range(rows // 128)], axis=1
    )
    served[...] = dot(picks, known_ref[...]).astype(BF)
    for load in loads:
        load.wait()
    hot_ref[...] = hot[...].astype(BF)
    save.wait()


def head_mask(heads, width):
    return iota((heads, width), 1) // HEAD_DIM == iota((heads, width), 0)


def spread_heads(values, mask, users):
    return jnp.concatenate(
        [jnp.where(mask, values[u : u + 1], 0.0) for u in range(users)], axis=0
    ).astype(BF)


def join_heads(full, mask, users):
    heads = mask.shape[0]
    parts = [
        jnp.sum(
            jnp.where(mask, full[u * heads : (u + 1) * heads], 0.0), axis=0, keepdims=True
        )
        for u in range(users)
    ]
    return jnp.concatenate(parts + [jnp.zeros((PAD - users, full.shape[1]), F32)], axis=0)


def look_up(column, fetched, hot):
    lanes = iota(column.shape, 1)
    slots = fetched.shape[0]
    picks = jnp.concatenate(
        [one_hot(column == lanes + 128 * j) for j in range(slots // 128)], axis=1
    )
    hot_picks = one_hot(column == lanes + HOT_CODE)
    return (dot(picks, fetched[...]) + dot(hot_picks, hot[...].astype(BF))).astype(BF)


def item_forward_kernel(users, fetched_ref, hot_ref, column_ref, *refs):
    sources, refs = refs[:3], refs[3:]
    vectors_ref, inner_hbm, refs = refs[0], refs[1], refs[2:]
    targets, (inner_ref, sems) = refs[:3], refs[3:]
    item_w1, item_w2, gain = targets
    copies = copies_of(zip(sources, targets), sems)
    rows = look_up(column_ref[...], fetched_ref, hot_ref)
    copies[0].wait()
    inner = dot(rows, item_w1[...])
    inner_ref[...] = inner
    save = pltpu.make_async_copy(inner_ref, inner_hbm, sems.at[3])
    save.start()
    gated = (inner * jax.nn.sigmoid(inner)).astype(BF)
    copies[1].wait()
    copies[2].wait()
    outer = dot(gated, item_w2[...])
    scale = lax.rsqrt(jnp.mean(outer * outer, axis=-1, keepdims=True) + EPS)
    vectors = jnp.where(iota(outer.shape, 0) < users, outer * scale * gain[...], 0.0)
    peers = vectors_ref.shape[0] // 8
    vectors_ref[...] = jnp.concatenate([vectors[0:8]] * peers, axis=0).astype(BF)
    save.wait()


def user_forward_kernel(users, *refs):
    fetched_ref, sources, refs = refs[0], refs[1:11], refs[11:]
    vectors_ref, kept_hbm, refs = refs[0], refs[1:6], refs[6:]
    targets, kept, (in_sems, out_sems) = refs[:10], refs[10:15], refs[15:]
    column_of, hot, pos_of, norm_gain_ref, out_gain_ref = targets[:5]
    in_proj, w_query, w_key, w_value, w_out = targets[5:]
    hidden_ref, normed_ref, qk_ref, weights_ref, mixed_ref = kept
    copies = copies_of(zip(sources, targets), in_sems)
    saves = [
        pltpu.make_async_copy(a, b, out_sems.at[i]) for i, (a, b) in enumerate(zip(kept, kept_hbm))
    ]
    hist, width = pos_of.shape
    heads = width // HEAD_DIM
    span = users * hist
    copies[0].wait()
    copies[1].wait()
    rows = look_up(column_of[0:span, :], fetched_ref, hot)
    for copy in copies[2:6]:
        copy.wait()
    pos = pos_of[...].astype(F32)
    hidden = dot(rows, in_proj[...]) + jnp.concatenate([pos] * users, axis=0)
    hidden_ref[...] = hidden
    saves[0].start()
    scale = lax.rsqrt(jnp.mean(hidden * hidden, axis=-1, keepdims=True) + EPS)
    normed = (hidden * scale * norm_gain_ref[...]).astype(BF)
    normed_ref[...] = normed
    saves[1].start()
    last = jnp.concatenate(
        [normed[(u + 1) * hist - PAD : (u + 1) * hist].astype(F32)[PAD - 1 :] for u in range(users)]
        + [jnp.zeros((PAD - users, width), F32)],
        axis=0,
    ).astype(BF)
    mask = head_mask(heads, width)
    copies[6].wait()
    query = dot(last, w_query[...]).astype(BF).astype(F32)
    copies[7].wait()
    qk = dot_nt(spread_heads(query, mask, users), w_key[...]).astype(BF)
    qk_ref[...] = qk
    saves[2].start()
    shape = (users * heads, span)
    own = iota(shape, 0) // heads == iota(shape, 1) // hist
    scores = jnp.where(own, dot_nt(qk, normed) * (1.0 / math.sqrt(HEAD_DIM)), -jnp.inf)
    raised = jnp.exp(scores - jnp.max(scores, axis=1, keepdims=True))
    weights = raised / jnp.sum(raised, axis=1, keepdims=True)
    weights_ref[...] = weights
    saves[3].start()
    mixes = dot(weights.astype(BF), normed).astype(BF)
    copies[8].wait()
    attended = join_heads(dot(mixes, w_value[...]), mask, users).astype(BF)
    copies[9].wait()
    hidden_last = jnp.concatenate(
        [hidden[(u + 1) * hist - 1 : (u + 1) * hist] for u in range(users)]
        + [jnp.zeros((PAD - users, width), F32)],
        axis=0,
    )
    mixed = hidden_last + dot(attended, w_out[...])
    mixed_ref[...] = mixed
    saves[4].start()
    scale = lax.rsqrt(jnp.mean(mixed * mixed, axis=-1, keepdims=True) + EPS)
    vectors_ref[...] = (mixed * scale * out_gain_ref[...]).astype(BF)
    for save in saves:
        save.wait()


def arrange_kernel(users, near, near_ref, vectors_ref, spread_ref):
    total, width = spread_ref.shape
    block = near * users + 8
    pair = 2 * block
    at = iota((pair, near * 8), 0) % block
    source = jnp.where(at < near * users, at // users * 8 + at % users, -1)
    item_rows = dot(one_hot(iota((pair, near * 8), 1) == source), near_ref[...])
    at = iota((pair, PAD), 0) % block
    source = jnp.where((at >= near * users) & (at < (near + 1) * users), at - near * users, -1)
    user_rows = dot(one_hot(iota((pair, PAD), 1) == source), vectors_ref[...])
    rows = (item_rows + user_rows).astype(BF)
    for i in range(total // pair):
        spread_ref[i * pair : (i + 1) * pair, :] = rows


def softmax_kernel(
    users, near, scale, place_ref, gathered_ref, swapped_ref, d_user_ref, d_part_ref, raised_ref
):
    rows, width = gathered_ref.shape
    items = near * users
    block = items + 8
    blocks = rows // block
    mine, plane = place_ref[0], place_ref[1]
    own, other = gathered_ref[...], swapped_ref[...]
    shape = (blocks * users, rows)
    line = iota(shape, 0)
    picks = one_hot(iota(shape, 1) == line // users * block + items + line % users)
    group_users = jnp.concatenate([dot(picks, own), dot(picks, other)], axis=0).astype(BF)
    total = 2 * blocks * users

    shape = (rows, total)
    line = iota(shape, 0)
    valid = line % block < items
    first = jnp.where(valid, scale * dot_nt(own, group_users), -jnp.inf)
    second = jnp.where(valid, scale * dot_nt(other, group_users), -jnp.inf)
    top = jnp.maximum(
        jnp.max(first, axis=0, keepdims=True), jnp.max(second, axis=0, keepdims=True)
    )
    raised = jnp.exp(first - top)
    raised_ref[...] = raised
    other_raised = jnp.exp(second - top)
    count = jnp.sum(raised, axis=0, keepdims=True) + jnp.sum(other_raised, axis=0, keepdims=True)
    share = 1.0 / count

    line = (items, total)
    target = (iota(line, 0) // users == plane) & (
        iota(line, 1) == mine * users + iota(line, 0) % users
    )
    near_raised = raised_ref[pl.ds(pl.multiple_of(mine * block, 8), items), :]
    slope = (near_raised * share - jnp.where(target, 1.0, 0.0)).astype(BF)
    apart = (near * 8, items)
    at = iota(apart, 0)
    apart = one_hot((at % 8 < users) & (iota(apart, 1) == at // 8 * users + at % 8))
    d_part = scale * dot(dot(apart, slope).astype(BF), group_users)

    who = iota(shape, 1) - mine * users
    target = (who >= 0) & (who < users) & (iota(shape, 0) == mine * block + plane * users + who)
    slope = (raised * share - jnp.where(target, 1.0, 0.0)).astype(BF)
    other_slope = (other_raised * share).astype(BF)
    self = (PAD, total)
    self = one_hot((iota(self, 0) < users) & (iota(self, 1) == mine * users + iota(self, 0)))
    d_user = dot(dot_nt(self, slope).astype(BF), own)
    d_user = d_user + dot(dot_nt(self, other_slope).astype(BF), other)
    d_user_ref[...] = (scale * d_user).astype(BF).astype(F32)
    each = jnp.sum(jnp.where(target, top + jnp.log(count) - first, 0.0), axis=0, keepdims=True)
    loss = jnp.sum(each, axis=1, keepdims=True)
    high = loss.astype(BF).astype(F32)
    middle = (loss - high).astype(BF).astype(F32)
    low = loss - high - middle
    shape = d_part.shape
    lanes = iota(shape, 1)
    loss = jnp.where(lanes == 0, high, jnp.where(lanes == 1, middle, jnp.where(lanes == 2, low, 0.0)))
    d_part_ref[...] = jnp.where(iota(shape, 0) % 8 == users, loss, d_part).astype(BF)


def norm_backward(values, cotangent, gain):
    inverse = lax.rsqrt(jnp.mean(values * values, axis=-1, keepdims=True) + EPS)
    pulled = cotangent * gain
    along = jnp.mean(pulled * values, axis=-1, keepdims=True)
    return inverse * pulled - values * (inverse * inverse * inverse * along)


def user_backward_kernel(users, d_user_ref, *refs):
    sources, refs = refs[:17], refs[17:]
    d_rows_ref, ahead, outer_ref, refs = refs[0], refs[1:6], refs[6], refs[7:]
    targets, (d_normed, sems) = refs[:12], refs[12:]
    mixed_ref, out_gain_ref, w_out, w_value, normed_ref, weights_ref, qk_ref = targets[:7]
    w_key, w_query, hidden_ref, norm_gain_ref, in_proj = targets[7:]
    pairs = []
    for source, target in zip(sources, tuple(targets) + tuple(ahead)):
        pieces = PIECES if target is w_out or target is w_value else 1
        size = target.shape[0] // pieces
        for piece in range(pieces):
            at = pl.ds(piece * size, size)
            pairs.append((source.at[at], target.at[at]) if pieces > 1 else (source, target))
    copies = copies_of(pairs, sems)
    parts, copies = copies[2 : 2 + 2 * PIECES], copies[:2] + copies[2 + 2 * PIECES :]

    def times(values, weights, arrivals):
        size = weights.shape[0] // PIECES
        columns = []
        for piece, arrival in enumerate(arrivals):
            arrival.wait()
            columns.append(dot_nt(values, weights[piece * size : (piece + 1) * size, :]))
        return jnp.concatenate(columns, axis=1)

    span, width = hidden_ref.shape
    hist = span // users
    heads = width // HEAD_DIM
    mask = head_mask(heads, width)
    for copy in copies[:2]:
        copy.wait()
    d_mixed = norm_backward(mixed_ref[...], d_user_ref[...], out_gain_ref[...])
    d_attended = times(d_mixed.astype(BF), w_out, parts[:PIECES])
    d_mixes = times(spread_heads(d_attended, mask, users), w_value, parts[PIECES:]).astype(BF)
    for copy in copies[2:5]:
        copy.wait()
    normed = normed_ref[...]
    weights = weights_ref[...]
    shape = weights.shape
    own = iota(shape, 0) // heads == iota(shape, 1) // hist
    d_weights = jnp.where(own, dot_nt(d_mixes, normed), 0.0)
    d_scores = weights * (d_weights - jnp.sum(weights * d_weights, axis=1, keepdims=True))
    d_scores = (d_scores * (1.0 / math.sqrt(HEAD_DIM))).astype(BF)
    d_normed[...] = dot_tn(
        jnp.concatenate([weights.astype(BF), d_scores], axis=0),
        jnp.concatenate([d_mixes, qk_ref[...]], axis=0),
    )
    d_qk = dot(d_scores, normed).astype(BF)
    copies[5].wait()
    d_query = join_heads(dot(d_qk, w_key[...]), mask, users).astype(BF)
    copies[6].wait()
    d_last = dot_nt(d_query, w_query[...])
    for u in range(users):
        at = slice((u + 1) * hist - 1, (u + 1) * hist)
        d_normed[at, :] = d_normed[at, :] + d_last[u : u + 1]
    copies[7].wait()
    copies[8].wait()
    d_normed[...] = norm_backward(hidden_ref[...], d_normed[...], norm_gain_ref[...])
    for u in range(users):
        at = slice((u + 1) * hist - 1, (u + 1) * hist)
        d_normed[at, :] = d_normed[at, :] + d_mixed[u : u + 1]
    copies[9].wait()
    d_rows_ref[...] = dot_nt(d_normed[...].astype(BF), in_proj[...]).astype(BF)
    for copy in copies[10:]:
        copy.wait()
    inner = ahead[2][...]
    outer_ref[...] = dot((inner * jax.nn.sigmoid(inner)).astype(BF), ahead[3][...])


def item_backward_kernel(users, parts_ref, d_rows_ref, *refs):
    row_ref, gain, inner_ref, item_w2, item_w1, outer_ref, outgoing, loss_ref = refs
    slots = outgoing.shape[0]
    span = d_rows_ref.shape[0]
    wide = row_ref.shape[1]
    peers = parts_ref.shape[0]
    shape = (PAD, peers)
    sums = dot(one_hot(iota(shape, 1) % 8 == iota(shape, 0)), parts_ref[...])
    shape = (1, 128)
    loss = jnp.where(iota(shape, 1) < 3, sums[users : users + 1, 0:128], 0.0)
    loss_ref[...] = jnp.broadcast_to(jnp.sum(loss, axis=1, keepdims=True), loss_ref.shape)
    d_item = jnp.where(iota(sums.shape, 0) < users, sums, 0.0).astype(BF).astype(F32)
    line = iota((slots, 1), 0)
    slot = line % SLOTS
    hot = HOT_CODE + line // (2 * SLOTS) + (slot - HOT_SLOT) * (slots // (2 * SLOTS))
    code = jnp.where(slot < HOT_SLOT, line, jnp.where(slot < HOT_SLOT + 2, hot, -2))
    picks = one_hot(code == row_ref[0:1, :])
    total = dot(picks[:, 0:span], d_rows_ref[...])
    d_outer = norm_backward(outer_ref[...], d_item, gain[...])
    inner = inner_ref[...]
    gate = jax.nn.sigmoid(inner)
    d_inner = dot_nt(d_outer.astype(BF), item_w2[...]) * (gate * (1.0 + inner * (1.0 - gate)))
    d_items = dot_nt(d_inner.astype(BF), item_w1[...])
    d_items = jnp.concatenate(
        [d_items, jnp.zeros((wide - span - PAD, d_items.shape[1]), F32)], axis=0
    ).astype(BF)
    outgoing[...] = (total + dot(picks[:, span:], d_items)).astype(BF)


def scatter_kernel(returned_ref, row_ref, loss_ref, part_ref, sums_ref):
    rows, emb = part_ref.shape
    slots = returned_ref.shape[0]
    returned = returned_ref[...]
    picks = one_hot(iota((rows, slots), 0) == row_ref[0:1, :])
    part_ref[...] = dot(picks, returned).astype(BF)
    shape = (PAD, slots)
    hot = dot(one_hot((iota(shape, 0) < 2) & (iota(shape, 1) % SLOTS == iota(shape, 0) + HOT_SLOT)), returned)
    halves = [hot[i : i + 1, j : j + 128] for i in range(2) for j in range(0, emb, 128)]
    block = jnp.concatenate(halves + [loss_ref[0 : 8 - len(halves), :]], axis=0)
    sums_ref[...] = jnp.concatenate([block] * (sums_ref.shape[0] // 8), axis=0)


def finish_kernel(count, sums_ref, other_ref, hot_ref, loss_ref):
    emb = hot_ref.shape[1]
    groups = sums_ref.shape[0] // 8

    def of_row(row):
        at = pl.ds(row, groups, stride=8)
        return sums_ref[at, :] + other_ref[at, :]

    row = 0
    for i in range(2):
        for j in range(0, emb, 128):
            hot_ref[i * groups : (i + 1) * groups, j : j + 128] = of_row(row)
            row += 1
    loss_ref[...] = jnp.sum(of_row(row)[:, 0:1], axis=0, keepdims=True) / count


def shards(
    history,
    item_ids,
    hot_table,
    rare_table,
    in_proj,
    pos_embed,
    norm_gain,
    w_query,
    w_key,
    w_value,
    w_out,
    out_gain,
    item_w1,
    item_w2,
    item_gain,
):
    users, hist = history.shape
    emb = hot_table.shape[1]
    rare_count = rare_table.shape[0]
    width = in_proj.shape[1]
    heads = width // HEAD_DIM
    scale = 4.0 / math.sqrt(width)
    owners = lax.axis_size(SHARD)
    towers = lax.axis_size("tower")
    near = lax.axis_size(LINE)
    total = users * towers * owners
    slots = owners * SLOTS
    span = users * hist
    wide = -(-(span + PAD) // 128) * 128
    swap = [(i, towers - 1 - i) for i in range(towers)]
    shape = jax.ShapeDtypeStruct
    sems = lambda n: pltpu.SemaphoreType.DMA((n,))
    vmem = lambda a: pltpu.VMEM(a.shape, a.dtype)
    hbm = lambda a: pltpu.HBM(a.shape, a.dtype)
    in_hbm = lambda a: pltpu.with_memory_space_constraint(a, pltpu.HBM)
    in_vmem = lambda a: pltpu.with_memory_space_constraint(a, pltpu.VMEM)
    like = lambda arrays: [pltpu.VMEM(a.shape, a.dtype) for a in arrays]
    exchange = functools.partial(lax.all_to_all, split_axis=0, concat_axis=0, tiled=True)

    places = (shape((8, wide), jnp.int32), shape((wide, 128), jnp.int32))
    loads = (history, item_ids.reshape(1, users), rare_table)
    request, known, row, column = pl.pallas_call(
        functools.partial(index_kernel, owners),
        out_shape=(
            shape((owners, 128), jnp.int32),
            pltpu.VMEM((rare_count, emb), BF),
            *map(hbm, places),
        ),
        in_specs=[HBM] * 3,
        out_specs=(VMEM, VMEM, HBM, HBM),
        scratch_shapes=like(loads + places) + [sems(5)],
        compiler_params=params(24),
        name="index",
    )(*map(in_hbm, loads))
    asked = exchange(request, SHARD)
    served, hot_ready, item_column, asked_row = pl.pallas_call(
        serve_kernel,
        out_shape=(
            shape((slots, emb), BF),
            pltpu.VMEM(hot_table.shape, BF),
            pltpu.VMEM((PAD, 128), jnp.int32),
            pltpu.HBM((8, slots), jnp.int32),
        ),
        in_specs=[VMEM, VMEM, HBM, HBM],
        out_specs=(VMEM, VMEM, VMEM, HBM),
        scratch_shapes=[
            pltpu.VMEM(hot_table.shape, F32),
            pltpu.VMEM((8, slots), jnp.int32),
            sems(3),
        ],
        compiler_params=params(24),
        name="serve",
    )(asked, in_vmem(known), in_hbm(hot_table), in_hbm(column))
    fetched = exchange(served, SHARD)

    norm_gain, out_gain, item_gain = (g.reshape(1, width) for g in (norm_gain, out_gain, item_gain))
    loads = (item_w1, item_w2, item_gain)
    item_vec, inner = pl.pallas_call(
        functools.partial(item_forward_kernel, users),
        out_shape=(shape((near * 8, width), BF), pltpu.HBM((PAD, width), F32)),
        in_specs=[VMEM] * 3 + [HBM] * 3,
        out_specs=(VMEM, HBM),
        scratch_shapes=like(loads) + [pltpu.VMEM((PAD, width), F32), sems(4)],
        compiler_params=params(24),
        name="item_forward",
    )(fetched, in_vmem(hot_ready), in_vmem(item_column), *map(in_hbm, loads))
    near_items = exchange(item_vec, LINE)

    loads = (column, hot_table, pos_embed, norm_gain, out_gain)
    loads += (in_proj, w_query, w_key, w_value, w_out)
    kept = (
        shape((span, width), F32),
        shape((span, width), BF),
        shape((users * heads, width), BF),
        shape((users * heads, span), F32),
        shape((PAD, width), F32),
    )
    user_vec, hidden, normed, qk, weights, mixed = pl.pallas_call(
        functools.partial(user_forward_kernel, users),
        out_shape=(shape((PAD, width), BF), *map(hbm, kept)),
        in_specs=[VMEM] + [HBM] * len(loads),
        out_specs=(VMEM,) + (HBM,) * len(kept),
        scratch_shapes=like(loads + kept) + [sems(len(loads)), sems(len(kept))],
        compiler_params=params(40),
        name="user_forward",
    )(fetched, *map(in_hbm, loads))

    rows = owners // near * (near * users + 8)
    spread = pl.pallas_call(
        functools.partial(arrange_kernel, users, near),
        out_shape=shape((rows, width), BF),
        in_specs=[VMEM, VMEM],
        out_specs=VMEM,
        compiler_params=params(24),
        name="arrange",
    )(near_items, user_vec)
    gathered = exchange(spread, ("x", "y"))
    swapped = lax.ppermute(gathered, "tower", swap)
    place = jnp.stack([lax.axis_index(("x", "y")), lax.axis_index(LINE)]).astype(jnp.int32)
    d_user, d_part = pl.pallas_call(
        functools.partial(softmax_kernel, users, near, scale),
        out_shape=(shape((PAD, width), F32), shape((near * 8, width), BF)),
        in_specs=[SMEM, VMEM, VMEM],
        out_specs=(VMEM, VMEM),
        scratch_shapes=[pltpu.VMEM((rows, 2 * owners // near * users), F32)],
        compiler_params=params(32),
        name="softmax",
    )(place, gathered, swapped)
    parts = exchange(d_part, LINE)

    loads = (mixed, out_gain, w_out, w_value, normed, weights, qk)
    loads += (w_key, w_query, hidden, norm_gain, in_proj)
    ahead = (row, item_gain, inner, item_w2, item_w1)
    d_rows, *item_ready = pl.pallas_call(
        functools.partial(user_backward_kernel, users),
        out_shape=(shape((span, emb), BF), *map(vmem, ahead), pltpu.VMEM((PAD, width), F32)),
        in_specs=[VMEM] + [HBM] * 17,
        out_specs=(VMEM,) * 7,
        scratch_shapes=like(loads) + [pltpu.VMEM((span, width), F32), sems(15 + 2 * PIECES)],
        compiler_params=params(40),
        name="user_backward",
    )(d_user, *map(in_hbm, loads + ahead))
    outgoing, loss = pl.pallas_call(
        functools.partial(item_backward_kernel, users),
        out_shape=(shape((slots, emb), BF), shape((8, 128), F32)),
        in_specs=[VMEM] * 8,
        out_specs=(VMEM, VMEM),
        compiler_params=params(32),
        name="item_backward",
    )(parts, d_rows, *map(in_vmem, item_ready))

    returned = exchange(outgoing, SHARD)
    part, mine = pl.pallas_call(
        scatter_kernel,
        out_shape=(shape((rare_count, emb), BF), shape((owners // 2 * 8, 128), F32)),
        in_specs=[VMEM, VMEM, VMEM],
        out_specs=(VMEM, VMEM),
        compiler_params=params(24),
        name="scatter",
    )(returned, asked_row, loss)
    sums, part = lax.optimization_barrier((exchange(mine, GROUP), part))
    rare_grad = part.astype(F32) + lax.ppermute(part, "tower", swap).astype(F32)
    other_sums = lax.ppermute(sums, "tower", swap)
    hot_total, loss_total = pl.pallas_call(
        functools.partial(finish_kernel, total * (near // 2)),
        out_shape=(shape((owners, emb), F32), shape((1, 1), F32)),
        in_specs=[VMEM, VMEM],
        out_specs=(VMEM, VMEM),
        compiler_params=params(24),
        name="finish",
    )(sums, other_sums)
    return (hot_total, rare_grad, loss_total[0, 0])


def solution(mesh):
    sizes = (mesh.shape["tower"], 4, 4, mesh.shape["shard"] // 32, 2)
    mesh = Mesh(mesh.devices.reshape(sizes), ("tower",) + SHARD)
    return jax.shard_map(
        shards,
        mesh=mesh,
        in_specs=(
            P(("tower",) + SHARD, None),
            P(("tower",) + SHARD),
            P(),
            P(SHARD, None),
            P(),
            P(),
            P(),
            P(),
            P(),
            P(),
            P(),
            P(),
            P(),
            P(),
            P(),
        ),
        out_specs=(P(), P(SHARD, None), P()),
        check_vma=False,
    )
```

```python
import functools
import math

import jax
import jax.numpy as jnp
from jax import lax
from jax.experimental import pallas as pl
from jax.experimental.pallas import tpu as pltpu
from jax.sharding import Mesh
from jax.sharding import PartitionSpec as P

HEAD_DIM = 64
EPS = 1e-06
SLOTS = 8
USED = 5
HOT_CODE = 4096
LINE = ("zh", "zl")
SHARD = ("x", "y") + LINE
GROUP = ("x", "y", "zl")
PAD = 16
BF = jnp.bfloat16
F32 = jnp.float32
VMEM = pl.BlockSpec(memory_space=pltpu.VMEM)
SMEM = pl.BlockSpec(memory_space=pltpu.SMEM)
HBM = pl.BlockSpec(memory_space=pltpu.HBM)
NT = (((1,), (1,)), ((), ()))
TN = (((0,), (0,)), ((), ()))


def dot(a, b):
    return jnp.dot(a, b, preferred_element_type=F32)


def dot_nt(a, b):
    return lax.dot_general(a, b, NT, preferred_element_type=F32)


def dot_tn(a, b):
    return lax.dot_general(a, b, TN, preferred_element_type=F32)


def iota(shape, axis):
    return lax.broadcasted_iota(jnp.int32, shape, axis)


def one_hot(mask):
    return jnp.where(mask, 1.0, 0.0).astype(BF)


def params(mib):
    return pltpu.CompilerParams(vmem_limit_bytes=mib * 1024 * 1024)


def copies_of(pairs, sems):
    copies = [pltpu.make_async_copy(a, b, sems.at[i]) for i, (a, b) in enumerate(pairs)]
    for copy in copies:
        copy.start()
    return copies


def index_kernel(
    owners,
    history_hbm,
    items_hbm,
    table_hbm,
    request_ref,
    known_ref,
    row_hbm,
    column_hbm,
    history_ref,
    items_ref,
    table,
    row,
    column,
    sems,
):
    loads = copies_of(
        [(history_hbm, history_ref), (items_hbm, items_ref), (table_hbm, table)], sems
    )
    loads[0].wait()
    loads[1].wait()
    hot_count = owners
    rare_count = table.shape[0]
    users = history_ref.shape[0]
    span = row.shape[1]
    parts = [history_ref[u : u + 1, :] for u in range(users)] + [items_ref[...]]
    filled = sum(p.shape[1] for p in parts)
    ids = jnp.concatenate(parts + [jnp.full((1, span - filled), -1, jnp.int32)], axis=1)
    is_rare = ids >= hot_count
    index = ids - hot_count
    owner = jnp.where(is_rare, index // rare_count, -1)
    value = jnp.where(is_rare, index % rare_count + 1, 0).astype(F32)
    hits = iota((owners, span), 0) == owner
    before = one_hot(iota((span, span), 0) < iota((span, span), 1))
    earlier = dot(one_hot(hits), before)
    position = jnp.sum(jnp.where(hits, earlier, 0.0), axis=0, keepdims=True).astype(jnp.int32)
    places = jnp.where(
        is_rare, owner * SLOTS + position, jnp.where(ids >= 0, ids + HOT_CODE, -1)
    )
    row[...] = jnp.broadcast_to(places, row.shape)
    column[...] = jnp.transpose(jnp.broadcast_to(places.astype(F32), (128, span))).astype(jnp.int32)
    saves = copies_of([(row, row_hbm), (column, column_hbm)], sems.at[pl.ds(3, 2)])
    order = jnp.where(hits, earlier, -1.0)
    lanes = iota(request_ref.shape, 1)
    request = jnp.zeros(request_ref.shape, F32)
    for slot in range(USED):
        wanted = jnp.sum(jnp.where(order == float(slot), value, 0.0), axis=1, keepdims=True)
        request = jnp.where(lanes == slot, wanted, request)
    request_ref[...] = request.astype(jnp.int32)
    loads[2].wait()
    known_ref[...] = table[...].astype(BF)
    for save in saves:
        save.wait()


def serve_kernel(
    asked_ref, known_ref, hot_hbm, column_hbm, served, hot_ref, column_ref, row_hbm, hot, row, sems
):
    span = column_hbm.shape[0] - 128
    loads = copies_of(
        [(hot_hbm, hot), (column_hbm.at[pl.ds(span, PAD)], column_ref)], sems
    )
    slots = served.shape[0]
    sources = asked_ref.shape[0]
    asked = asked_ref[...]
    high = (asked // 2).astype(F32).astype(BF)
    low = (asked % 2).astype(F32).astype(BF)
    expand = one_hot(iota((slots, sources), 0) // SLOTS == iota((slots, sources), 1))
    wide = 2.0 * dot(expand, high) + dot(expand, low)
    mine = iota(wide.shape, 1) == iota(wide.shape, 0) % SLOTS
    index = jnp.sum(jnp.where(mine, wide, 0.0), axis=1, keepdims=True) - 1.0
    index = jnp.broadcast_to(index, wide.shape)
    row[...] = jnp.transpose(index)[0:8].astype(jnp.int32)
    save = pltpu.make_async_copy(row, row_hbm, sems.at[2])
    save.start()
    index = index.astype(jnp.int32)
    lanes = iota(index.shape, 1)
    rows = known_ref.shape[0]
    picks = jnp.concatenate(
        [one_hot(index == lanes + 128 * j) for j in range(rows // 128)], axis=1
    )
    served[...] = dot(picks, known_ref[...]).astype(BF)
    for load in loads:
        load.wait()
    hot_ref[...] = hot[...].astype(BF)
    save.wait()


def head_mask(heads, width):
    return iota((heads, width), 1) // HEAD_DIM == iota((heads, width), 0)


def spread_heads(values, mask, users):
    return jnp.concatenate(
        [jnp.where(mask, values[u : u + 1], 0.0) for u in range(users)], axis=0
    ).astype(BF)


def join_heads(full, mask, users):
    heads = mask.shape[0]
    parts = [
        jnp.sum(
            jnp.where(mask, full[u * heads : (u + 1) * heads], 0.0), axis=0, keepdims=True
        )
        for u in range(users)
    ]
    return jnp.concatenate(parts + [jnp.zeros((PAD - users, full.shape[1]), F32)], axis=0)


def look_up(column, fetched, hot):
    lanes = iota(column.shape, 1)
    slots = fetched.shape[0]
    picks = jnp.concatenate(
        [one_hot(column == lanes + 128 * j) for j in range(slots // 128)], axis=1
    )
    hot_picks = one_hot(column == lanes + HOT_CODE)
    return (dot(picks, fetched[...]) + dot(hot_picks, hot[...].astype(BF))).astype(BF)


def item_forward_kernel(users, fetched_ref, hot_ref, column_ref, *refs):
    sources, refs = refs[:3], refs[3:]
    vectors_ref, inner_hbm, refs = refs[0], refs[1], refs[2:]
    targets, (inner_ref, sems) = refs[:3], refs[3:]
    item_w1, item_w2, gain = targets
    copies = copies_of(zip(sources, targets), sems)
    rows = look_up(column_ref[...], fetched_ref, hot_ref)
    copies[0].wait()
    inner = dot(rows, item_w1[...])
    inner_ref[...] = inner
    save = pltpu.make_async_copy(inner_ref, inner_hbm, sems.at[3])
    save.start()
    gated = (inner * jax.nn.sigmoid(inner)).astype(BF)
    copies[1].wait()
    copies[2].wait()
    outer = dot(gated, item_w2[...])
    scale = lax.rsqrt(jnp.mean(outer * outer, axis=-1, keepdims=True) + EPS)
    vectors = jnp.where(iota(outer.shape, 0) < users, outer * scale * gain[...], 0.0)
    peers = vectors_ref.shape[0] // 8
    vectors_ref[...] = jnp.concatenate([vectors[0:8]] * peers, axis=0).astype(BF)
    save.wait()


def user_forward_kernel(users, *refs):
    fetched_ref, sources, refs = refs[0], refs[1:11], refs[11:]
    vectors_ref, kept_hbm, refs = refs[0], refs[1:6], refs[6:]
    targets, kept, (in_sems, out_sems) = refs[:10], refs[10:15], refs[15:]
    column_of, hot, pos_of, norm_gain_ref, out_gain_ref = targets[:5]
    in_proj, w_query, w_key, w_value, w_out = targets[5:]
    hidden_ref, normed_ref, qk_ref, weights_ref, mixed_ref = kept
    copies = copies_of(zip(sources, targets), in_sems)
    saves = [
        pltpu.make_async_copy(a, b, out_sems.at[i]) for i, (a, b) in enumerate(zip(kept, kept_hbm))
    ]
    hist, width = pos_of.shape
    heads = width // HEAD_DIM
    span = users * hist
    copies[0].wait()
    copies[1].wait()
    rows = look_up(column_of[0:span, :], fetched_ref, hot)
    for copy in copies[2:6]:
        copy.wait()
    pos = pos_of[...].astype(F32)
    hidden = dot(rows, in_proj[...]) + jnp.concatenate([pos] * users, axis=0)
    hidden_ref[...] = hidden
    saves[0].start()
    scale = lax.rsqrt(jnp.mean(hidden * hidden, axis=-1, keepdims=True) + EPS)
    normed = (hidden * scale * norm_gain_ref[...]).astype(BF)
    normed_ref[...] = normed
    saves[1].start()
    last = jnp.concatenate(
        [normed[(u + 1) * hist - PAD : (u + 1) * hist].astype(F32)[PAD - 1 :] for u in range(users)]
        + [jnp.zeros((PAD - users, width), F32)],
        axis=0,
    ).astype(BF)
    mask = head_mask(heads, width)
    copies[6].wait()
    query = dot(last, w_query[...]).astype(BF).astype(F32)
    copies[7].wait()
    qk = dot_nt(spread_heads(query, mask, users), w_key[...]).astype(BF)
    qk_ref[...] = qk
    saves[2].start()
    shape = (users * heads, span)
    own = iota(shape, 0) // heads == iota(shape, 1) // hist
    scores = jnp.where(own, dot_nt(qk, normed) * (1.0 / math.sqrt(HEAD_DIM)), -jnp.inf)
    raised = jnp.exp(scores - jnp.max(scores, axis=1, keepdims=True))
    weights = raised / jnp.sum(raised, axis=1, keepdims=True)
    weights_ref[...] = weights
    saves[3].start()
    mixes = dot(weights.astype(BF), normed).astype(BF)
    copies[8].wait()
    attended = join_heads(dot(mixes, w_value[...]), mask, users).astype(BF)
    copies[9].wait()
    hidden_last = jnp.concatenate(
        [hidden[(u + 1) * hist - 1 : (u + 1) * hist] for u in range(users)]
        + [jnp.zeros((PAD - users, width), F32)],
        axis=0,
    )
    mixed = hidden_last + dot(attended, w_out[...])
    mixed_ref[...] = mixed
    saves[4].start()
    scale = lax.rsqrt(jnp.mean(mixed * mixed, axis=-1, keepdims=True) + EPS)
    vectors_ref[...] = (mixed * scale * out_gain_ref[...]).astype(BF)
    for save in saves:
        save.wait()


def arrange_kernel(users, near, near_ref, vectors_ref, spread_ref):
    total, width = spread_ref.shape
    block = near * users + 8
    pair = 2 * block
    at = iota((pair, near * 8), 0) % block
    source = jnp.where(at < near * users, at // users * 8 + at % users, -1)
    item_rows = dot(one_hot(iota((pair, near * 8), 1) == source), near_ref[...])
    at = iota((pair, PAD), 0) % block
    source = jnp.where((at >= near * users) & (at < (near + 1) * users), at - near * users, -1)
    user_rows = dot(one_hot(iota((pair, PAD), 1) == source), vectors_ref[...])
    rows = (item_rows + user_rows).astype(BF)
    for i in range(total // pair):
        spread_ref[i * pair : (i + 1) * pair, :] = rows


def softmax_kernel(
    users, near, scale, place_ref, gathered_ref, swapped_ref, d_user_ref, d_part_ref, raised_ref
):
    rows, width = gathered_ref.shape
    items = near * users
    block = items + 8
    blocks = rows // block
    mine, plane = place_ref[0], place_ref[1]
    own, other = gathered_ref[...], swapped_ref[...]
    shape = (blocks * users, rows)
    line = iota(shape, 0)
    picks = one_hot(iota(shape, 1) == line // users * block + items + line % users)
    group_users = jnp.concatenate([dot(picks, own), dot(picks, other)], axis=0).astype(BF)
    total = 2 * blocks * users

    shape = (rows, total)
    line = iota(shape, 0)
    valid = line % block < items
    first = jnp.where(valid, scale * dot_nt(own, group_users), -jnp.inf)
    second = jnp.where(valid, scale * dot_nt(other, group_users), -jnp.inf)
    top = jnp.maximum(
        jnp.max(first, axis=0, keepdims=True), jnp.max(second, axis=0, keepdims=True)
    )
    raised = jnp.exp(first - top)
    raised_ref[...] = raised
    other_raised = jnp.exp(second - top)
    count = jnp.sum(raised, axis=0, keepdims=True) + jnp.sum(other_raised, axis=0, keepdims=True)
    share = 1.0 / count

    line = (items, total)
    target = (iota(line, 0) // users == plane) & (
        iota(line, 1) == mine * users + iota(line, 0) % users
    )
    near_raised = raised_ref[pl.ds(pl.multiple_of(mine * block, 8), items), :]
    slope = (near_raised * share - jnp.where(target, 1.0, 0.0)).astype(BF)
    apart = (near * 8, items)
    at = iota(apart, 0)
    apart = one_hot((at % 8 < users) & (iota(apart, 1) == at // 8 * users + at % 8))
    d_part = scale * dot(dot(apart, slope).astype(BF), group_users)

    who = iota(shape, 1) - mine * users
    target = (who >= 0) & (who < users) & (iota(shape, 0) == mine * block + plane * users + who)
    slope = (raised * share - jnp.where(target, 1.0, 0.0)).astype(BF)
    other_slope = (other_raised * share).astype(BF)
    self = (PAD, total)
    self = one_hot((iota(self, 0) < users) & (iota(self, 1) == mine * users + iota(self, 0)))
    d_user = dot(dot_nt(self, slope).astype(BF), own)
    d_user = d_user + dot(dot_nt(self, other_slope).astype(BF), other)
    d_user_ref[...] = (scale * d_user).astype(BF).astype(F32)
    each = jnp.sum(jnp.where(target, top + jnp.log(count) - first, 0.0), axis=0, keepdims=True)
    loss = jnp.sum(each, axis=1, keepdims=True)
    high = loss.astype(BF).astype(F32)
    middle = (loss - high).astype(BF).astype(F32)
    low = loss - high - middle
    shape = d_part.shape
    lanes = iota(shape, 1)
    loss = jnp.where(lanes == 0, high, jnp.where(lanes == 1, middle, jnp.where(lanes == 2, low, 0.0)))
    d_part_ref[...] = jnp.where(iota(shape, 0) % 8 == users, loss, d_part).astype(BF)


def norm_backward(values, cotangent, gain):
    inverse = lax.rsqrt(jnp.mean(values * values, axis=-1, keepdims=True) + EPS)
    pulled = cotangent * gain
    along = jnp.mean(pulled * values, axis=-1, keepdims=True)
    return inverse * pulled - values * (inverse * inverse * inverse * along)


def user_backward_kernel(users, d_user_ref, *refs):
    sources, refs = refs[:17], refs[17:]
    d_rows_ref, ahead, outer_ref, refs = refs[0], refs[1:6], refs[6], refs[7:]
    targets, (d_normed, sems) = refs[:12], refs[12:]
    mixed_ref, out_gain_ref, w_out, w_value, normed_ref, weights_ref, qk_ref = targets[:7]
    w_key, w_query, hidden_ref, norm_gain_ref, in_proj = targets[7:]
    copies = copies_of(zip(sources, tuple(targets) + tuple(ahead)), sems)
    span, width = hidden_ref.shape
    hist = span // users
    heads = width // HEAD_DIM
    mask = head_mask(heads, width)
    for copy in copies[:3]:
        copy.wait()
    d_mixed = norm_backward(mixed_ref[...], d_user_ref[...], out_gain_ref[...])
    d_attended = dot_nt(d_mixed.astype(BF), w_out[...])
    copies[3].wait()
    d_mixes = dot_nt(spread_heads(d_attended, mask, users), w_value[...]).astype(BF)
    for copy in copies[4:7]:
        copy.wait()
    normed = normed_ref[...]
    weights = weights_ref[...]
    shape = weights.shape
    own = iota(shape, 0) // heads == iota(shape, 1) // hist
    d_weights = jnp.where(own, dot_nt(d_mixes, normed), 0.0)
    d_scores = weights * (d_weights - jnp.sum(weights * d_weights, axis=1, keepdims=True))
    d_scores = (d_scores * (1.0 / math.sqrt(HEAD_DIM))).astype(BF)
    d_normed[...] = dot_tn(
        jnp.concatenate([weights.astype(BF), d_scores], axis=0),
        jnp.concatenate([d_mixes, qk_ref[...]], axis=0),
    )
    d_qk = dot(d_scores, normed).astype(BF)
    copies[7].wait()
    d_query = join_heads(dot(d_qk, w_key[...]), mask, users).astype(BF)
    copies[8].wait()
    d_last = dot_nt(d_query, w_query[...])
    for u in range(users):
        at = slice((u + 1) * hist - 1, (u + 1) * hist)
        d_normed[at, :] = d_normed[at, :] + d_last[u : u + 1]
    copies[9].wait()
    copies[10].wait()
    d_normed[...] = norm_backward(hidden_ref[...], d_normed[...], norm_gain_ref[...])
    for u in range(users):
        at = slice((u + 1) * hist - 1, (u + 1) * hist)
        d_normed[at, :] = d_normed[at, :] + d_mixed[u : u + 1]
    copies[11].wait()
    d_rows_ref[...] = dot_nt(d_normed[...].astype(BF), in_proj[...]).astype(BF)
    for copy in copies[12:]:
        copy.wait()
    inner = ahead[2][...]
    outer_ref[...] = dot((inner * jax.nn.sigmoid(inner)).astype(BF), ahead[3][...])


def item_backward_kernel(users, parts_ref, d_rows_ref, *refs):
    row_ref, gain, inner_ref, item_w2, item_w1, outer_ref, outgoing, loss_ref = refs
    slots = outgoing.shape[0]
    span = d_rows_ref.shape[0]
    wide = row_ref.shape[1]
    peers = parts_ref.shape[0]
    shape = (PAD, peers)
    sums = dot(one_hot(iota(shape, 1) % 8 == iota(shape, 0)), parts_ref[...])
    shape = (1, 128)
    loss = jnp.where(iota(shape, 1) < 3, sums[users : users + 1, 0:128], 0.0)
    loss_ref[...] = jnp.broadcast_to(jnp.sum(loss, axis=1, keepdims=True), loss_ref.shape)
    d_item = jnp.where(iota(sums.shape, 0) < users, sums, 0.0).astype(BF).astype(F32)
    emb = d_rows_ref.shape[1]
    picks = one_hot(iota((slots, wide), 0) == row_ref[0:1, :])
    total = dot(picks[:, 0:span], d_rows_ref[...])
    hot_count = slots // SLOTS
    hot_picks = one_hot(iota((hot_count, wide), 0) + HOT_CODE == row_ref[0:1, :])
    hot = dot(hot_picks[:, 0:span], d_rows_ref[...])
    shape = (slots, hot_count)
    line = iota(shape, 0)
    owner = line // SLOTS
    held = owner // 8 * 2 + owner % 2 + line % SLOTS // 2 * (hot_count // 4)
    held = one_hot(iota(shape, 1) == held)
    d_outer = norm_backward(outer_ref[...], d_item, gain[...])
    inner = inner_ref[...]
    gate = jax.nn.sigmoid(inner)
    d_inner = dot_nt(d_outer.astype(BF), item_w2[...]) * (gate * (1.0 + inner * (1.0 - gate)))
    d_items = dot_nt(d_inner.astype(BF), item_w1[...])
    d_items = jnp.concatenate(
        [d_items, jnp.zeros((wide - span - PAD, d_items.shape[1]), F32)], axis=0
    ).astype(BF)
    outgoing[:, 0:emb] = (total + dot(picks[:, span:], d_items)).astype(BF)
    hot = (hot + dot(hot_picks[:, span:], d_items)).astype(BF)
    hot = dot(held, hot)
    half = emb // 2
    odd = iota((slots, half), 0) % 2 == 1
    outgoing[:, emb:] = jnp.where(odd, hot[:, half:], hot[:, 0:half]).astype(BF)


def scatter_kernel(returned_ref, row_ref, loss_ref, part_ref, sums_ref):
    rows, emb = part_ref.shape
    slots = returned_ref.shape[0]
    picks = one_hot(iota((rows, slots), 0) == row_ref[0:1, :])
    part_ref[...] = dot(picks, returned_ref[:, 0:emb]).astype(BF)
    shape = (PAD, slots)
    hot = dot(one_hot(iota(shape, 1) % SLOTS == iota(shape, 0)), returned_ref[:, emb:])
    block = jnp.concatenate([hot[0:SLOTS], loss_ref[...]], axis=0)
    sums_ref[...] = jnp.concatenate([block] * (sums_ref.shape[0] // PAD), axis=0)


def finish_kernel(count, sums_ref, other_ref, hot_ref, loss_ref):
    emb = hot_ref.shape[1]
    groups = sums_ref.shape[0] // PAD

    def of_row(row):
        at = pl.ds(row, groups, stride=PAD)
        return sums_ref[at, :] + other_ref[at, :]

    for row in range(SLOTS):
        at = row // 2 * groups
        half = row % 2 * (emb // 2)
        hot_ref[at : at + groups, half : half + emb // 2] = of_row(row)
    loss_ref[...] = jnp.sum(of_row(SLOTS)[:, 0:1], axis=0, keepdims=True) / count


def shards(
    history,
    item_ids,
    hot_table,
    rare_table,
    in_proj,
    pos_embed,
    norm_gain,
    w_query,
    w_key,
    w_value,
    w_out,
    out_gain,
    item_w1,
    item_w2,
    item_gain,
):
    users, hist = history.shape
    emb = hot_table.shape[1]
    rare_count = rare_table.shape[0]
    width = in_proj.shape[1]
    heads = width // HEAD_DIM
    scale = 4.0 / math.sqrt(width)
    owners = lax.axis_size(SHARD)
    towers = lax.axis_size("tower")
    near = lax.axis_size(LINE)
    total = users * towers * owners
    slots = owners * SLOTS
    span = users * hist
    wide = -(-(span + PAD) // 128) * 128
    swap = [(i, towers - 1 - i) for i in range(towers)]
    shape = jax.ShapeDtypeStruct
    sems = lambda n: pltpu.SemaphoreType.DMA((n,))
    vmem = lambda a: pltpu.VMEM(a.shape, a.dtype)
    hbm = lambda a: pltpu.HBM(a.shape, a.dtype)
    in_hbm = lambda a: pltpu.with_memory_space_constraint(a, pltpu.HBM)
    in_vmem = lambda a: pltpu.with_memory_space_constraint(a, pltpu.VMEM)
    like = lambda arrays: [pltpu.VMEM(a.shape, a.dtype) for a in arrays]
    exchange = functools.partial(lax.all_to_all, split_axis=0, concat_axis=0, tiled=True)

    places = (shape((8, wide), jnp.int32), shape((wide, 128), jnp.int32))
    loads = (history, item_ids.reshape(1, users), rare_table)
    request, known, row, column = pl.pallas_call(
        functools.partial(index_kernel, owners),
        out_shape=(
            shape((owners, 128), jnp.int32),
            pltpu.VMEM((rare_count, emb), BF),
            *map(hbm, places),
        ),
        in_specs=[HBM] * 3,
        out_specs=(VMEM, VMEM, HBM, HBM),
        scratch_shapes=like(loads + places) + [sems(5)],
        compiler_params=params(24),
        name="index",
    )(*map(in_hbm, loads))
    asked = exchange(request, SHARD)
    served, hot_ready, item_column, asked_row = pl.pallas_call(
        serve_kernel,
        out_shape=(
            shape((slots, emb), BF),
            pltpu.VMEM(hot_table.shape, BF),
            pltpu.VMEM((PAD, 128), jnp.int32),
            pltpu.HBM((8, slots), jnp.int32),
        ),
        in_specs=[VMEM, VMEM, HBM, HBM],
        out_specs=(VMEM, VMEM, VMEM, HBM),
        scratch_shapes=[
            pltpu.VMEM(hot_table.shape, F32),
            pltpu.VMEM((8, slots), jnp.int32),
            sems(3),
        ],
        compiler_params=params(24),
        name="serve",
    )(asked, in_vmem(known), in_hbm(hot_table), in_hbm(column))
    fetched = exchange(served, SHARD)

    norm_gain, out_gain, item_gain = (g.reshape(1, width) for g in (norm_gain, out_gain, item_gain))
    loads = (item_w1, item_w2, item_gain)
    item_vec, inner = pl.pallas_call(
        functools.partial(item_forward_kernel, users),
        out_shape=(shape((near * 8, width), BF), pltpu.HBM((PAD, width), F32)),
        in_specs=[VMEM] * 3 + [HBM] * 3,
        out_specs=(VMEM, HBM),
        scratch_shapes=like(loads) + [pltpu.VMEM((PAD, width), F32), sems(4)],
        compiler_params=params(24),
        name="item_forward",
    )(fetched, in_vmem(hot_ready), in_vmem(item_column), *map(in_hbm, loads))
    near_items = exchange(item_vec, LINE)

    loads = (column, hot_table, pos_embed, norm_gain, out_gain)
    loads += (in_proj, w_query, w_key, w_value, w_out)
    kept = (
        shape((span, width), F32),
        shape((span, width), BF),
        shape((users * heads, width), BF),
        shape((users * heads, span), F32),
        shape((PAD, width), F32),
    )
    user_vec, hidden, normed, qk, weights, mixed = pl.pallas_call(
        functools.partial(user_forward_kernel, users),
        out_shape=(shape((PAD, width), BF), *map(hbm, kept)),
        in_specs=[VMEM] + [HBM] * len(loads),
        out_specs=(VMEM,) + (HBM,) * len(kept),
        scratch_shapes=like(loads + kept) + [sems(len(loads)), sems(len(kept))],
        compiler_params=params(40),
        name="user_forward",
    )(fetched, *map(in_hbm, loads))

    rows = owners // near * (near * users + 8)
    spread = pl.pallas_call(
        functools.partial(arrange_kernel, users, near),
        out_shape=shape((rows, width), BF),
        in_specs=[VMEM, VMEM],
        out_specs=VMEM,
        compiler_params=params(24),
        name="arrange",
    )(near_items, user_vec)
    gathered = exchange(spread, ("x", "y"))
    swapped = lax.ppermute(gathered, "tower", swap)
    place = jnp.stack([lax.axis_index(("x", "y")), lax.axis_index(LINE)]).astype(jnp.int32)
    d_user, d_part = pl.pallas_call(
        functools.partial(softmax_kernel, users, near, scale),
        out_shape=(shape((PAD, width), F32), shape((near * 8, width), BF)),
        in_specs=[SMEM, VMEM, VMEM],
        out_specs=(VMEM, VMEM),
        scratch_shapes=[pltpu.VMEM((rows, 2 * owners // near * users), F32)],
        compiler_params=params(32),
        name="softmax",
    )(place, gathered, swapped)
    parts = exchange(d_part, LINE)

    loads = (mixed, out_gain, w_out, w_value, normed, weights, qk)
    loads += (w_key, w_query, hidden, norm_gain, in_proj)
    ahead = (row, item_gain, inner, item_w2, item_w1)
    d_rows, *item_ready = pl.pallas_call(
        functools.partial(user_backward_kernel, users),
        out_shape=(shape((span, emb), BF), *map(vmem, ahead), pltpu.VMEM((PAD, width), F32)),
        in_specs=[VMEM] + [HBM] * 17,
        out_specs=(VMEM,) * 7,
        scratch_shapes=like(loads) + [pltpu.VMEM((span, width), F32), sems(17)],
        compiler_params=params(40),
        name="user_backward",
    )(d_user, *map(in_hbm, loads + ahead))
    outgoing, loss = pl.pallas_call(
        functools.partial(item_backward_kernel, users),
        out_shape=(shape((slots, emb + 128), BF), shape((8, 128), F32)),
        in_specs=[VMEM] * 8,
        out_specs=(VMEM, VMEM),
        compiler_params=params(32),
        name="item_backward",
    )(parts, d_rows, *map(in_vmem, item_ready))

    returned = exchange(outgoing, SHARD)
    part, mine = pl.pallas_call(
        scatter_kernel,
        out_shape=(shape((rare_count, emb), BF), shape((owners // 4 * PAD, 128), F32)),
        in_specs=[VMEM, VMEM, VMEM],
        out_specs=(VMEM, VMEM),
        compiler_params=params(24),
        name="scatter",
    )(returned, asked_row, loss)
    rare_grad = part.astype(F32) + lax.ppermute(part, "tower", swap).astype(F32)
    sums = exchange(mine, GROUP)
    other_sums = lax.ppermute(sums, "tower", swap)
    hot_total, loss_total = pl.pallas_call(
        functools.partial(finish_kernel, total * 2),
        out_shape=(shape((owners, emb), F32), shape((1, 1), F32)),
        in_specs=[VMEM, VMEM],
        out_specs=(VMEM, VMEM),
        compiler_params=params(24),
        name="finish",
    )(sums, other_sums)
    return (hot_total, rare_grad, loss_total[0, 0])


def solution(mesh):
    sizes = (mesh.shape["tower"], 4, 4, mesh.shape["shard"] // 32, 2)
    mesh = Mesh(mesh.devices.reshape(sizes), ("tower",) + SHARD)
    return jax.shard_map(
        shards,
        mesh=mesh,
        in_specs=(
            P(("tower",) + SHARD, None),
            P(("tower",) + SHARD),
            P(),
            P(SHARD, None),
            P(),
            P(),
            P(),
            P(),
            P(),
            P(),
            P(),
            P(),
            P(),
            P(),
            P(),
        ),
        out_specs=(P(), P(SHARD, None), P()),
        check_vma=False,
    )
```

```python
import functools
import math

import jax
import jax.numpy as jnp
from jax import lax
from jax.experimental import pallas as pl
from jax.experimental.pallas import tpu as pltpu
from jax.sharding import Mesh
from jax.sharding import PartitionSpec as P

HEAD_DIM = 64
EPS = 1e-06
SLOTS = 8
HOT_SLOT = 5
HOT_CODE = 4096
LINE = ("zh", "zl")
SHARD = ("x", "y") + LINE
GROUP = ("x", "y", "zl")
PAD = 16
BF = jnp.bfloat16
F32 = jnp.float32
VMEM = pl.BlockSpec(memory_space=pltpu.VMEM)
SMEM = pl.BlockSpec(memory_space=pltpu.SMEM)
HBM = pl.BlockSpec(memory_space=pltpu.HBM)
NT = (((1,), (1,)), ((), ()))
TN = (((0,), (0,)), ((), ()))


def dot(a, b):
    return jnp.dot(a, b, preferred_element_type=F32)


def dot_nt(a, b):
    return lax.dot_general(a, b, NT, preferred_element_type=F32)


def dot_tn(a, b):
    return lax.dot_general(a, b, TN, preferred_element_type=F32)


def iota(shape, axis):
    return lax.broadcasted_iota(jnp.int32, shape, axis)


def one_hot(mask):
    return jnp.where(mask, 1.0, 0.0).astype(BF)


def params(mib):
    return pltpu.CompilerParams(vmem_limit_bytes=mib * 1024 * 1024)


def copies_of(pairs, sems):
    copies = [pltpu.make_async_copy(a, b, sems.at[i]) for i, (a, b) in enumerate(pairs)]
    for copy in copies:
        copy.start()
    return copies


def index_kernel(
    owners,
    history_hbm,
    items_hbm,
    table_hbm,
    request_ref,
    known_ref,
    row_hbm,
    column_hbm,
    history_ref,
    items_ref,
    table,
    row,
    column,
    sems,
):
    loads = copies_of(
        [(history_hbm, history_ref), (items_hbm, items_ref), (table_hbm, table)], sems
    )
    loads[0].wait()
    loads[1].wait()
    hot_count = owners
    rare_count = table.shape[0]
    users = history_ref.shape[0]
    span = row.shape[1]
    parts = [history_ref[u : u + 1, :] for u in range(users)] + [items_ref[...]]
    filled = sum(p.shape[1] for p in parts)
    ids = jnp.concatenate(parts + [jnp.full((1, span - filled), -1, jnp.int32)], axis=1)
    is_rare = ids >= hot_count
    index = ids - hot_count
    owner = jnp.where(is_rare, index // rare_count, -1)
    value = jnp.where(is_rare, index % rare_count + 1, 0).astype(F32)
    hits = iota((owners, span), 0) == owner
    before = one_hot(iota((span, span), 0) < iota((span, span), 1))
    earlier = dot(one_hot(hits), before)
    position = jnp.sum(jnp.where(hits, earlier, 0.0), axis=0, keepdims=True).astype(jnp.int32)
    places = jnp.where(
        is_rare, owner * SLOTS + position, jnp.where(ids >= 0, ids + HOT_CODE, -1)
    )
    row[...] = jnp.broadcast_to(places, row.shape)
    column[...] = jnp.transpose(jnp.broadcast_to(places.astype(F32), (128, span))).astype(jnp.int32)
    saves = copies_of([(row, row_hbm), (column, column_hbm)], sems.at[pl.ds(3, 2)])
    order = jnp.where(hits, earlier, -1.0)
    lanes = iota(request_ref.shape, 1)
    request = jnp.zeros(request_ref.shape, F32)
    for slot in range(HOT_SLOT):
        wanted = jnp.sum(jnp.where(order == float(slot), value, 0.0), axis=1, keepdims=True)
        request = jnp.where(lanes == slot, wanted, request)
    request_ref[...] = request.astype(jnp.int32)
    loads[2].wait()
    known_ref[...] = table[...].astype(BF)
    for save in saves:
        save.wait()


def serve_kernel(
    asked_ref, known_ref, hot_hbm, column_hbm, served, hot_ref, column_ref, row_hbm, hot, row, sems
):
    span = column_hbm.shape[0] - 128
    loads = copies_of(
        [(hot_hbm, hot), (column_hbm.at[pl.ds(span, PAD)], column_ref)], sems
    )
    slots = served.shape[0]
    sources = asked_ref.shape[0]
    asked = asked_ref[...]
    high = (asked // 2).astype(F32).astype(BF)
    low = (asked % 2).astype(F32).astype(BF)
    expand = one_hot(iota((slots, sources), 0) // SLOTS == iota((slots, sources), 1))
    wide = 2.0 * dot(expand, high) + dot(expand, low)
    mine = iota(wide.shape, 1) == iota(wide.shape, 0) % SLOTS
    index = jnp.sum(jnp.where(mine, wide, 0.0), axis=1, keepdims=True) - 1.0
    index = jnp.broadcast_to(index, wide.shape)
    row[...] = jnp.transpose(index)[0:8].astype(jnp.int32)
    save = pltpu.make_async_copy(row, row_hbm, sems.at[2])
    save.start()
    index = index.astype(jnp.int32)
    lanes = iota(index.shape, 1)
    rows = known_ref.shape[0]
    picks = jnp.concatenate(
        [one_hot(index == lanes + 128 * j) for j in range(rows // 128)], axis=1
    )
    served[...] = dot(picks, known_ref[...]).astype(BF)
    for load in loads:
        load.wait()
    hot_ref[...] = hot[...].astype(BF)
    save.wait()


def head_mask(heads, width):
    return iota((heads, width), 1) // HEAD_DIM == iota((heads, width), 0)


def spread_heads(values, mask, users):
    return jnp.concatenate(
        [jnp.where(mask, values[u : u + 1], 0.0) for u in range(users)], axis=0
    ).astype(BF)


def join_heads(full, mask, users):
    heads = mask.shape[0]
    parts = [
        jnp.sum(
            jnp.where(mask, full[u * heads : (u + 1) * heads], 0.0), axis=0, keepdims=True
        )
        for u in range(users)
    ]
    return jnp.concatenate(parts + [jnp.zeros((PAD - users, full.shape[1]), F32)], axis=0)


def look_up(column, fetched, hot):
    lanes = iota(column.shape, 1)
    slots = fetched.shape[0]
    picks = jnp.concatenate(
        [one_hot(column == lanes + 128 * j) for j in range(slots // 128)], axis=1
    )
    hot_picks = one_hot(column == lanes + HOT_CODE)
    return (dot(picks, fetched[...]) + dot(hot_picks, hot[...].astype(BF))).astype(BF)


def item_forward_kernel(users, fetched_ref, hot_ref, column_ref, *refs):
    sources, refs = refs[:3], refs[3:]
    vectors_ref, inner_hbm, refs = refs[0], refs[1], refs[2:]
    targets, (inner_ref, sems) = refs[:3], refs[3:]
    item_w1, item_w2, gain = targets
    copies = copies_of(zip(sources, targets), sems)
    rows = look_up(column_ref[...], fetched_ref, hot_ref)
    copies[0].wait()
    inner = dot(rows, item_w1[...])
    inner_ref[...] = inner
    save = pltpu.make_async_copy(inner_ref, inner_hbm, sems.at[3])
    save.start()
    gated = (inner * jax.nn.sigmoid(inner)).astype(BF)
    copies[1].wait()
    copies[2].wait()
    outer = dot(gated, item_w2[...])
    scale = lax.rsqrt(jnp.mean(outer * outer, axis=-1, keepdims=True) + EPS)
    vectors = jnp.where(iota(outer.shape, 0) < users, outer * scale * gain[...], 0.0)
    peers = vectors_ref.shape[0] // 8
    vectors_ref[...] = jnp.concatenate([vectors[0:8]] * peers, axis=0).astype(BF)
    save.wait()


def user_forward_kernel(users, *refs):
    fetched_ref, sources, refs = refs[0], refs[1:11], refs[11:]
    vectors_ref, kept_hbm, refs = refs[0], refs[1:6], refs[6:]
    targets, kept, (in_sems, out_sems) = refs[:10], refs[10:15], refs[15:]
    column_of, hot, pos_of, norm_gain_ref, out_gain_ref = targets[:5]
    in_proj, w_query, w_key, w_value, w_out = targets[5:]
    hidden_ref, normed_ref, qk_ref, weights_ref, mixed_ref = kept
    copies = copies_of(zip(sources, targets), in_sems)
    saves = [
        pltpu.make_async_copy(a, b, out_sems.at[i]) for i, (a, b) in enumerate(zip(kept, kept_hbm))
    ]
    hist, width = pos_of.shape
    heads = width // HEAD_DIM
    span = users * hist
    copies[0].wait()
    copies[1].wait()
    rows = look_up(column_of[0:span, :], fetched_ref, hot)
    for copy in copies[2:6]:
        copy.wait()
    pos = pos_of[...].astype(F32)
    hidden = dot(rows, in_proj[...]) + jnp.concatenate([pos] * users, axis=0)
    hidden_ref[...] = hidden
    saves[0].start()
    scale = lax.rsqrt(jnp.mean(hidden * hidden, axis=-1, keepdims=True) + EPS)
    normed = (hidden * scale * norm_gain_ref[...]).astype(BF)
    normed_ref[...] = normed
    saves[1].start()
    last = jnp.concatenate(
        [normed[(u + 1) * hist - PAD : (u + 1) * hist].astype(F32)[PAD - 1 :] for u in range(users)]
        + [jnp.zeros((PAD - users, width), F32)],
        axis=0,
    ).astype(BF)
    mask = head_mask(heads, width)
    copies[6].wait()
    query = dot(last, w_query[...]).astype(BF).astype(F32)
    copies[7].wait()
    qk = dot_nt(spread_heads(query, mask, users), w_key[...]).astype(BF)
    qk_ref[...] = qk
    saves[2].start()
    shape = (users * heads, span)
    own = iota(shape, 0) // heads == iota(shape, 1) // hist
    scores = jnp.where(own, dot_nt(qk, normed) * (1.0 / math.sqrt(HEAD_DIM)), -jnp.inf)
    raised = jnp.exp(scores - jnp.max(scores, axis=1, keepdims=True))
    weights = raised / jnp.sum(raised, axis=1, keepdims=True)
    weights_ref[...] = weights
    saves[3].start()
    mixes = dot(weights.astype(BF), normed).astype(BF)
    copies[8].wait()
    attended = join_heads(dot(mixes, w_value[...]), mask, users).astype(BF)
    copies[9].wait()
    hidden_last = jnp.concatenate(
        [hidden[(u + 1) * hist - 1 : (u + 1) * hist] for u in range(users)]
        + [jnp.zeros((PAD - users, width), F32)],
        axis=0,
    )
    mixed = hidden_last + dot(attended, w_out[...])
    mixed_ref[...] = mixed
    saves[4].start()
    scale = lax.rsqrt(jnp.mean(mixed * mixed, axis=-1, keepdims=True) + EPS)
    vectors_ref[...] = (mixed * scale * out_gain_ref[...]).astype(BF)
    for save in saves:
        save.wait()


def arrange_kernel(users, near, near_ref, vectors_ref, spread_ref):
    total, width = spread_ref.shape
    block = near * users + 8
    pair = 2 * block
    at = iota((pair, near * 8), 0) % block
    source = jnp.where(at < near * users, at // users * 8 + at % users, -1)
    item_rows = dot(one_hot(iota((pair, near * 8), 1) == source), near_ref[...])
    at = iota((pair, PAD), 0) % block
    source = jnp.where((at >= near * users) & (at < (near + 1) * users), at - near * users, -1)
    user_rows = dot(one_hot(iota((pair, PAD), 1) == source), vectors_ref[...])
    rows = (item_rows + user_rows).astype(BF)
    for i in range(total // pair):
        spread_ref[i * pair : (i + 1) * pair, :] = rows


def softmax_kernel(
    users, near, scale, place_ref, gathered_ref, swapped_ref, d_user_ref, d_part_ref, raised_ref
):
    rows, width = gathered_ref.shape
    items = near * users
    block = items + 8
    blocks = rows // block
    mine, plane = place_ref[0], place_ref[1]
    own, other = gathered_ref[...], swapped_ref[...]
    shape = (blocks * users, rows)
    line = iota(shape, 0)
    picks = one_hot(iota(shape, 1) == line // users * block + items + line % users)
    group_users = jnp.concatenate([dot(picks, own), dot(picks, other)], axis=0).astype(BF)
    total = 2 * blocks * users

    shape = (rows, total)
    line = iota(shape, 0)
    valid = line % block < items
    first = jnp.where(valid, scale * dot_nt(own, group_users), -jnp.inf)
    second = jnp.where(valid, scale * dot_nt(other, group_users), -jnp.inf)
    top = jnp.maximum(
        jnp.max(first, axis=0, keepdims=True), jnp.max(second, axis=0, keepdims=True)
    )
    raised = jnp.exp(first - top)
    raised_ref[...] = raised
    other_raised = jnp.exp(second - top)
    count = jnp.sum(raised, axis=0, keepdims=True) + jnp.sum(other_raised, axis=0, keepdims=True)
    share = 1.0 / count

    line = (items, total)
    target = (iota(line, 0) // users == plane) & (
        iota(line, 1) == mine * users + iota(line, 0) % users
    )
    near_raised = raised_ref[pl.ds(pl.multiple_of(mine * block, 8), items), :]
    slope = (near_raised * share - jnp.where(target, 1.0, 0.0)).astype(BF)
    apart = (near * 8, items)
    at = iota(apart, 0)
    apart = one_hot((at % 8 < users) & (iota(apart, 1) == at // 8 * users + at % 8))
    d_part = scale * dot(dot(apart, slope).astype(BF), group_users)

    who = iota(shape, 1) - mine * users
    target = (who >= 0) & (who < users) & (iota(shape, 0) == mine * block + plane * users + who)
    slope = (raised * share - jnp.where(target, 1.0, 0.0)).astype(BF)
    other_slope = (other_raised * share).astype(BF)
    self = (PAD, total)
    self = one_hot((iota(self, 0) < users) & (iota(self, 1) == mine * users + iota(self, 0)))
    d_user = dot(dot_nt(self, slope).astype(BF), own)
    d_user = d_user + dot(dot_nt(self, other_slope).astype(BF), other)
    d_user_ref[...] = (scale * d_user).astype(BF).astype(F32)
    each = jnp.sum(jnp.where(target, top + jnp.log(count) - first, 0.0), axis=0, keepdims=True)
    loss = jnp.sum(each, axis=1, keepdims=True)
    high = loss.astype(BF).astype(F32)
    middle = (loss - high).astype(BF).astype(F32)
    low = loss - high - middle
    shape = d_part.shape
    lanes = iota(shape, 1)
    loss = jnp.where(lanes == 0, high, jnp.where(lanes == 1, middle, jnp.where(lanes == 2, low, 0.0)))
    d_part_ref[...] = jnp.where(iota(shape, 0) % 8 == users, loss, d_part).astype(BF)


def norm_backward(values, cotangent, gain):
    inverse = lax.rsqrt(jnp.mean(values * values, axis=-1, keepdims=True) + EPS)
    pulled = cotangent * gain
    along = jnp.mean(pulled * values, axis=-1, keepdims=True)
    return inverse * pulled - values * (inverse * inverse * inverse * along)


def user_backward_kernel(users, d_user_ref, *refs):
    sources, refs = refs[:17], refs[17:]
    d_rows_ref, ahead, outer_ref, refs = refs[0], refs[1:6], refs[6], refs[7:]
    targets, (d_normed, sems) = refs[:12], refs[12:]
    mixed_ref, out_gain_ref, w_out, w_value, normed_ref, weights_ref, qk_ref = targets[:7]
    w_key, w_query, hidden_ref, norm_gain_ref, in_proj = targets[7:]
    copies = copies_of(zip(sources, tuple(targets) + tuple(ahead)), sems)
    span, width = hidden_ref.shape
    hist = span // users
    heads = width // HEAD_DIM
    mask = head_mask(heads, width)
    for copy in copies[:3]:
        copy.wait()
    d_mixed = norm_backward(mixed_ref[...], d_user_ref[...], out_gain_ref[...])
    d_attended = dot_nt(d_mixed.astype(BF), w_out[...])
    copies[3].wait()
    d_mixes = dot_nt(spread_heads(d_attended, mask, users), w_value[...]).astype(BF)
    for copy in copies[4:7]:
        copy.wait()
    normed = normed_ref[...]
    weights = weights_ref[...]
    shape = weights.shape
    own = iota(shape, 0) // heads == iota(shape, 1) // hist
    d_weights = jnp.where(own, dot_nt(d_mixes, normed), 0.0)
    d_scores = weights * (d_weights - jnp.sum(weights * d_weights, axis=1, keepdims=True))
    d_scores = (d_scores * (1.0 / math.sqrt(HEAD_DIM))).astype(BF)
    d_normed[...] = dot_tn(
        jnp.concatenate([weights.astype(BF), d_scores], axis=0),
        jnp.concatenate([d_mixes, qk_ref[...]], axis=0),
    )
    d_qk = dot(d_scores, normed).astype(BF)
    copies[7].wait()
    d_query = join_heads(dot(d_qk, w_key[...]), mask, users).astype(BF)
    copies[8].wait()
    d_last = dot_nt(d_query, w_query[...])
    for u in range(users):
        at = slice((u + 1) * hist - 1, (u + 1) * hist)
        d_normed[at, :] = d_normed[at, :] + d_last[u : u + 1]
    copies[9].wait()
    copies[10].wait()
    d_normed[...] = norm_backward(hidden_ref[...], d_normed[...], norm_gain_ref[...])
    for u in range(users):
        at = slice((u + 1) * hist - 1, (u + 1) * hist)
        d_normed[at, :] = d_normed[at, :] + d_mixed[u : u + 1]
    copies[11].wait()
    d_rows_ref[...] = dot_nt(d_normed[...].astype(BF), in_proj[...]).astype(BF)
    for copy in copies[12:]:
        copy.wait()
    inner = ahead[2][...]
    outer_ref[...] = dot((inner * jax.nn.sigmoid(inner)).astype(BF), ahead[3][...])


def item_backward_kernel(users, core_ref, parts_ref, d_rows_ref, *refs):
    row_ref, gain, inner_ref, item_w2, item_w1, outer_ref, refs = *refs[:6], refs[6:]
    d_all_ref, send_ref, keep_ref, loss_ref = refs
    span, emb = d_rows_ref.shape
    wide = row_ref.shape[1]
    peers = parts_ref.shape[0]
    shape = (PAD, peers)
    sums = dot(one_hot(iota(shape, 1) % 8 == iota(shape, 0)), parts_ref[...])
    shape = (1, 128)
    loss = jnp.where(iota(shape, 1) < 3, sums[users : users + 1, 0:128], 0.0)
    loss_ref[...] = jnp.broadcast_to(jnp.sum(loss, axis=1, keepdims=True), loss_ref.shape)
    d_item = jnp.where(iota(sums.shape, 0) < users, sums, 0.0).astype(BF).astype(F32)
    d_all_ref[0:span, :] = d_rows_ref[...]
    half = keep_ref.shape[0]
    first = HOT_CODE + core_ref[0] * half
    picks = one_hot(iota((half, wide), 0) + first == row_ref[0:1, :])
    keep = dot(picks[:, 0:span], d_rows_ref[...])
    first = HOT_CODE + (1 - core_ref[0]) * half
    other_picks = one_hot(iota((half, wide), 0) + first == row_ref[0:1, :])
    send = dot(other_picks[:, 0:span], d_rows_ref[...])
    d_outer = norm_backward(outer_ref[...], d_item, gain[...])
    inner = inner_ref[...]
    gate = jax.nn.sigmoid(inner)
    d_inner = dot_nt(d_outer.astype(BF), item_w2[...]) * (gate * (1.0 + inner * (1.0 - gate)))
    d_items = dot_nt(d_inner.astype(BF), item_w1[...])
    d_items = jnp.concatenate([d_items, jnp.zeros((wide - span - PAD, emb), F32)], axis=0).astype(BF)
    d_all_ref[span:, :] = d_items
    keep_ref[...] = keep + dot(picks[:, span:], d_items)
    send_ref[...] = send + dot(other_picks[:, span:], d_items)


def rare_kernel(d_all_ref, row_ref, rare_ref):
    shape = (rare_ref.shape[0], row_ref.shape[1])
    rare_ref[...] = dot(one_hot(iota(shape, 0) == row_ref[0:1, :]), d_all_ref[...]).astype(BF)


def outgoing_kernel(rare_ref, keep_ref, got_ref, outgoing_ref):
    half = keep_ref.shape[0]
    slots = rare_ref.shape[0]
    shape = (slots, half)
    line = iota(shape, 0)
    owner, slot = line // SLOTS, line % SLOTS - HOT_SLOT
    held = owner // 8 * 2 + owner % 2 + slot * (half // 2)
    held = one_hot((slot >= 0) & (slot < 2) & (iota(shape, 1) == held))
    hot = dot(held, (keep_ref[...] + got_ref[...]).astype(BF))
    outgoing_ref[...] = (rare_ref[...].astype(F32) + hot).astype(BF)


def scatter_kernel(returned_ref, row_ref, loss_ref, part_ref, sums_ref):
    rows, emb = part_ref.shape
    slots = returned_ref.shape[0]
    returned = returned_ref[...]
    picks = one_hot(iota((rows, slots), 0) == row_ref[0:1, :])
    part_ref[...] = dot(picks, returned).astype(BF)
    shape = (PAD, slots)
    hot = dot(one_hot((iota(shape, 0) < 2) & (iota(shape, 1) % SLOTS == iota(shape, 0) + HOT_SLOT)), returned)
    halves = [hot[i : i + 1, j : j + 128] for i in range(2) for j in range(0, emb, 128)]
    block = jnp.concatenate(halves + [loss_ref[0 : 8 - len(halves), :]], axis=0)
    sums_ref[...] = jnp.concatenate([block] * (sums_ref.shape[0] // 8), axis=0)


def finish_kernel(count, core_ref, sums_ref, other_ref, hot_ref, loss_ref):
    rows, emb = hot_ref.shape
    groups = sums_ref.shape[0] // 8
    for core, ref in ((core_ref[0], sums_ref), (1 - core_ref[0], other_ref)):
        row = 0
        for i in range(2):
            at = pl.ds(pl.multiple_of(core * (rows // 2) + i * groups, groups), groups)
            for j in range(0, emb, 128):
                hot_ref[at, j : j + 128] = ref[pl.ds(row, groups, stride=8), :]
                row += 1
    at = pl.ds(row, groups, stride=8)
    losses = sums_ref[at, :] + other_ref[at, :]
    loss_ref[...] = jnp.sum(losses[:, 0:1], axis=0, keepdims=True) / count


def shards(
    history,
    item_ids,
    hot_table,
    rare_table,
    in_proj,
    pos_embed,
    norm_gain,
    w_query,
    w_key,
    w_value,
    w_out,
    out_gain,
    item_w1,
    item_w2,
    item_gain,
):
    users, hist = history.shape
    emb = hot_table.shape[1]
    rare_count = rare_table.shape[0]
    width = in_proj.shape[1]
    heads = width // HEAD_DIM
    scale = 4.0 / math.sqrt(width)
    owners = lax.axis_size(SHARD)
    towers = lax.axis_size("tower")
    near = lax.axis_size(LINE)
    total = users * towers * owners
    slots = owners * SLOTS
    span = users * hist
    wide = -(-(span + PAD) // 128) * 128
    swap = [(i, towers - 1 - i) for i in range(towers)]
    shape = jax.ShapeDtypeStruct
    sems = lambda n: pltpu.SemaphoreType.DMA((n,))
    vmem = lambda a: pltpu.VMEM(a.shape, a.dtype)
    hbm = lambda a: pltpu.HBM(a.shape, a.dtype)
    in_hbm = lambda a: pltpu.with_memory_space_constraint(a, pltpu.HBM)
    in_vmem = lambda a: pltpu.with_memory_space_constraint(a, pltpu.VMEM)
    like = lambda arrays: [pltpu.VMEM(a.shape, a.dtype) for a in arrays]
    exchange = functools.partial(lax.all_to_all, split_axis=0, concat_axis=0, tiled=True)

    places = (shape((8, wide), jnp.int32), shape((wide, 128), jnp.int32))
    loads = (history, item_ids.reshape(1, users), rare_table)
    request, known, row, column = pl.pallas_call(
        functools.partial(index_kernel, owners),
        out_shape=(
            shape((owners, 128), jnp.int32),
            pltpu.VMEM((rare_count, emb), BF),
            *map(hbm, places),
        ),
        in_specs=[HBM] * 3,
        out_specs=(VMEM, VMEM, HBM, HBM),
        scratch_shapes=like(loads + places) + [sems(5)],
        compiler_params=params(24),
        name="index",
    )(*map(in_hbm, loads))
    asked = exchange(request, SHARD)
    served, hot_ready, item_column, asked_row = pl.pallas_call(
        serve_kernel,
        out_shape=(
            shape((slots, emb), BF),
            pltpu.VMEM(hot_table.shape, BF),
            pltpu.VMEM((PAD, 128), jnp.int32),
            pltpu.HBM((8, slots), jnp.int32),
        ),
        in_specs=[VMEM, VMEM, HBM, HBM],
        out_specs=(VMEM, VMEM, VMEM, HBM),
        scratch_shapes=[
            pltpu.VMEM(hot_table.shape, F32),
            pltpu.VMEM((8, slots), jnp.int32),
            sems(3),
        ],
        compiler_params=params(24),
        name="serve",
    )(asked, in_vmem(known), in_hbm(hot_table), in_hbm(column))
    fetched = exchange(served, SHARD)

    norm_gain, out_gain, item_gain = (g.reshape(1, width) for g in (norm_gain, out_gain, item_gain))
    loads = (item_w1, item_w2, item_gain)
    item_vec, inner = pl.pallas_call(
        functools.partial(item_forward_kernel, users),
        out_shape=(shape((near * 8, width), BF), pltpu.HBM((PAD, width), F32)),
        in_specs=[VMEM] * 3 + [HBM] * 3,
        out_specs=(VMEM, HBM),
        scratch_shapes=like(loads) + [pltpu.VMEM((PAD, width), F32), sems(4)],
        compiler_params=params(24),
        name="item_forward",
    )(fetched, in_vmem(hot_ready), in_vmem(item_column), *map(in_hbm, loads))
    near_items = exchange(item_vec, LINE)

    loads = (column, hot_table, pos_embed, norm_gain, out_gain)
    loads += (in_proj, w_query, w_key, w_value, w_out)
    kept = (
        shape((span, width), F32),
        shape((span, width), BF),
        shape((users * heads, width), BF),
        shape((users * heads, span), F32),
        shape((PAD, width), F32),
    )
    user_vec, hidden, normed, qk, weights, mixed = pl.pallas_call(
        functools.partial(user_forward_kernel, users),
        out_shape=(shape((PAD, width), BF), *map(hbm, kept)),
        in_specs=[VMEM] + [HBM] * len(loads),
        out_specs=(VMEM,) + (HBM,) * len(kept),
        scratch_shapes=like(loads + kept) + [sems(len(loads)), sems(len(kept))],
        compiler_params=params(40),
        name="user_forward",
    )(fetched, *map(in_hbm, loads))

    rows = owners // near * (near * users + 8)
    spread = pl.pallas_call(
        functools.partial(arrange_kernel, users, near),
        out_shape=shape((rows, width), BF),
        in_specs=[VMEM, VMEM],
        out_specs=VMEM,
        compiler_params=params(24),
        name="arrange",
    )(near_items, user_vec)
    gathered = exchange(spread, ("x", "y"))
    swapped = lax.ppermute(gathered, "tower", swap)
    place = jnp.stack([lax.axis_index(("x", "y")), lax.axis_index(LINE)]).astype(jnp.int32)
    d_user, d_part = pl.pallas_call(
        functools.partial(softmax_kernel, users, near, scale),
        out_shape=(shape((PAD, width), F32), shape((near * 8, width), BF)),
        in_specs=[SMEM, VMEM, VMEM],
        out_specs=(VMEM, VMEM),
        scratch_shapes=[pltpu.VMEM((rows, 2 * owners // near * users), F32)],
        compiler_params=params(32),
        name="softmax",
    )(place, gathered, swapped)
    parts = exchange(d_part, LINE)

    loads = (mixed, out_gain, w_out, w_value, normed, weights, qk)
    loads += (w_key, w_query, hidden, norm_gain, in_proj)
    ahead = (row, item_gain, inner, item_w2, item_w1)
    d_rows, *item_ready = pl.pallas_call(
        functools.partial(user_backward_kernel, users),
        out_shape=(shape((span, emb), BF), *map(vmem, ahead), pltpu.VMEM((PAD, width), F32)),
        in_specs=[VMEM] + [HBM] * 17,
        out_specs=(VMEM,) * 7,
        scratch_shapes=like(loads) + [pltpu.VMEM((span, width), F32), sems(17)],
        compiler_params=params(40),
        name="user_backward",
    )(d_user, *map(in_hbm, loads + ahead))
    core = lax.axis_index("tower").astype(jnp.int32).reshape(1)
    row_ready = item_ready[0]
    d_all, send, keep, loss = pl.pallas_call(
        functools.partial(item_backward_kernel, users),
        out_shape=(
            shape((wide, emb), BF),
            shape((owners // 2, emb), F32),
            shape((owners // 2, emb), F32),
            shape((8, 128), F32),
        ),
        in_specs=[SMEM] + [VMEM] * 8,
        out_specs=(VMEM,) * 4,
        compiler_params=params(32),
        name="item_backward",
    )(core, parts, d_rows, *map(in_vmem, item_ready))
    got = lax.ppermute(send, "tower", swap)
    rare = pl.pallas_call(
        rare_kernel,
        out_shape=shape((slots, emb), BF),
        in_specs=[VMEM, VMEM],
        out_specs=VMEM,
        compiler_params=params(32),
        name="rare",
    )(d_all, in_vmem(row_ready))
    outgoing = pl.pallas_call(
        outgoing_kernel,
        out_shape=shape((slots, emb), BF),
        in_specs=[VMEM] * 3,
        out_specs=VMEM,
        compiler_params=params(32),
        name="outgoing",
    )(rare, keep, got)

    returned = exchange(outgoing, SHARD)
    part, mine = pl.pallas_call(
        scatter_kernel,
        out_shape=(shape((rare_count, emb), BF), shape((owners // 4 * 8, 128), F32)),
        in_specs=[VMEM, VMEM, VMEM],
        out_specs=(VMEM, VMEM),
        compiler_params=params(24),
        name="scatter",
    )(returned, asked_row, loss)
    rare_grad = part.astype(F32) + lax.ppermute(part, "tower", swap).astype(F32)
    sums = exchange(mine, GROUP)
    other_sums = lax.ppermute(sums, "tower", swap)
    hot_total, loss_total = pl.pallas_call(
        functools.partial(finish_kernel, total * 2),
        out_shape=(shape((owners, emb), F32), shape((1, 1), F32)),
        in_specs=[SMEM, VMEM, VMEM],
        out_specs=(VMEM, VMEM),
        compiler_params=params(24),
        name="finish",
    )(core, sums, other_sums)
    return (hot_total, rare_grad, loss_total[0, 0])


def solution(mesh):
    sizes = (mesh.shape["tower"], 4, 4, mesh.shape["shard"] // 32, 2)
    mesh = Mesh(mesh.devices.reshape(sizes), ("tower",) + SHARD)
    return jax.shard_map(
        shards,
        mesh=mesh,
        in_specs=(
            P(("tower",) + SHARD, None),
            P(("tower",) + SHARD),
            P(),
            P(SHARD, None),
            P(),
            P(),
            P(),
            P(),
            P(),
            P(),
            P(),
            P(),
            P(),
            P(),
            P(),
        ),
        out_specs=(P(), P(SHARD, None), P()),
        check_vma=False,
    )
```

```python
import functools
import math

import jax
import jax.numpy as jnp
from jax import lax
from jax.experimental import pallas as pl
from jax.experimental.pallas import tpu as pltpu
from jax.sharding import Mesh
from jax.sharding import PartitionSpec as P

HEAD_DIM = 64
EPS = 1e-06
SLOTS = 8
HOT_SLOT = 5
HOT_CODE = 4096
LINE = ("zh", "zl")
SHARD = ("x", "y") + LINE
GROUP = ("x", "y", "zl")
PAD = 16
BF = jnp.bfloat16
F32 = jnp.float32
VMEM = pl.BlockSpec(memory_space=pltpu.VMEM)
SMEM = pl.BlockSpec(memory_space=pltpu.SMEM)
HBM = pl.BlockSpec(memory_space=pltpu.HBM)
NT = (((1,), (1,)), ((), ()))
TN = (((0,), (0,)), ((), ()))


def dot(a, b):
    return jnp.dot(a, b, preferred_element_type=F32)


def dot_nt(a, b):
    return lax.dot_general(a, b, NT, preferred_element_type=F32)


def dot_tn(a, b):
    return lax.dot_general(a, b, TN, preferred_element_type=F32)


def iota(shape, axis):
    return lax.broadcasted_iota(jnp.int32, shape, axis)


def one_hot(mask):
    return jnp.where(mask, 1.0, 0.0).astype(BF)


def params(mib):
    return pltpu.CompilerParams(vmem_limit_bytes=mib * 1024 * 1024)


def copies_of(pairs, sems):
    copies = [pltpu.make_async_copy(a, b, sems.at[i]) for i, (a, b) in enumerate(pairs)]
    for copy in copies:
        copy.start()
    return copies


def index_kernel(
    owners,
    history_hbm,
    items_hbm,
    table_hbm,
    request_ref,
    known_ref,
    row,
    column,
    history_ref,
    items_ref,
    table,
    sems,
):
    loads = copies_of(
        [(history_hbm, history_ref), (items_hbm, items_ref), (table_hbm, table)], sems
    )
    loads[0].wait()
    loads[1].wait()
    hot_count = owners
    rare_count = table.shape[0]
    users = history_ref.shape[0]
    span = row.shape[1]
    parts = [history_ref[u : u + 1, :] for u in range(users)] + [items_ref[...]]
    filled = sum(p.shape[1] for p in parts)
    ids = jnp.concatenate(parts + [jnp.full((1, span - filled), -1, jnp.int32)], axis=1)
    is_rare = ids >= hot_count
    index = ids - hot_count
    owner = jnp.where(is_rare, index // rare_count, -1)
    value = jnp.where(is_rare, index % rare_count + 1, 0).astype(F32)
    hits = iota((owners, span), 0) == owner
    before = one_hot(iota((span, span), 0) < iota((span, span), 1))
    earlier = dot(one_hot(hits), before)
    position = jnp.sum(jnp.where(hits, earlier, 0.0), axis=0, keepdims=True).astype(jnp.int32)
    places = jnp.where(
        is_rare, owner * SLOTS + position, jnp.where(ids >= 0, ids + HOT_CODE, -1)
    )
    row[...] = jnp.broadcast_to(places, row.shape)
    column[...] = jnp.transpose(jnp.broadcast_to(places.astype(F32), (128, span))).astype(jnp.int32)
    order = jnp.where(hits, earlier, -1.0)
    lanes = iota(request_ref.shape, 1)
    request = jnp.zeros(request_ref.shape, F32)
    for slot in range(HOT_SLOT):
        wanted = jnp.sum(jnp.where(order == float(slot), value, 0.0), axis=1, keepdims=True)
        request = jnp.where(lanes == slot, wanted, request)
    request_ref[...] = request.astype(jnp.int32)
    loads[2].wait()
    known_ref[...] = table[...].astype(BF)


def serve_kernel(
    asked_ref,
    known_ref,
    row_ref,
    column_ref,
    hot_hbm,
    served,
    hot_ref,
    item_column_ref,
    asked_row_hbm,
    row_hbm,
    column_hbm,
    hot,
    row,
    sems,
):
    copies = copies_of([(hot_hbm, hot), (row_ref, row_hbm), (column_ref, column_hbm)], sems)
    span = column_ref.shape[0] - 128
    item_column_ref[...] = column_ref[span : span + PAD, :]
    slots = served.shape[0]
    sources = asked_ref.shape[0]
    asked = asked_ref[...]
    high = (asked // 2).astype(F32).astype(BF)
    low = (asked % 2).astype(F32).astype(BF)
    expand = one_hot(iota((slots, sources), 0) // SLOTS == iota((slots, sources), 1))
    wide = 2.0 * dot(expand, high) + dot(expand, low)
    mine = iota(wide.shape, 1) == iota(wide.shape, 0) % SLOTS
    index = jnp.sum(jnp.where(mine, wide, 0.0), axis=1, keepdims=True) - 1.0
    index = jnp.broadcast_to(index, wide.shape)
    row[...] = jnp.transpose(index)[0:8].astype(jnp.int32)
    save = pltpu.make_async_copy(row, asked_row_hbm, sems.at[3])
    save.start()
    index = index.astype(jnp.int32)
    lanes = iota(index.shape, 1)
    rows = known_ref.shape[0]
    picks = jnp.concatenate(
        [one_hot(index == lanes + 128 * j) for j in range(rows // 128)], axis=1
    )
    served[...] = dot(picks, known_ref[...]).astype(BF)
    copies[0].wait()
    hot_ref[...] = hot[...].astype(BF)
    for copy in copies[1:] + [save]:
        copy.wait()


def head_mask(heads, width):
    return iota((heads, width), 1) // HEAD_DIM == iota((heads, width), 0)


def spread_heads(values, mask, users):
    return jnp.concatenate(
        [jnp.where(mask, values[u : u + 1], 0.0) for u in range(users)], axis=0
    ).astype(BF)


def join_heads(full, mask, users):
    heads = mask.shape[0]
    parts = [
        jnp.sum(
            jnp.where(mask, full[u * heads : (u + 1) * heads], 0.0), axis=0, keepdims=True
        )
        for u in range(users)
    ]
    return jnp.concatenate(parts + [jnp.zeros((PAD - users, full.shape[1]), F32)], axis=0)


def look_up(column, fetched, hot):
    lanes = iota(column.shape, 1)
    slots = fetched.shape[0]
    picks = jnp.concatenate(
        [one_hot(column == lanes + 128 * j) for j in range(slots // 128)], axis=1
    )
    hot_picks = one_hot(column == lanes + HOT_CODE)
    return (dot(picks, fetched[...]) + dot(hot_picks, hot[...].astype(BF))).astype(BF)


def item_forward_kernel(users, fetched_ref, hot_ref, column_ref, *refs):
    sources, (vectors_ref, inner_ref, outer_ref), refs = refs[:3], refs[3:6], refs[6:]
    targets, sems = refs[:3], refs[3]
    item_w1, item_w2, gain = targets
    copies = copies_of(zip(sources, targets), sems)
    rows = look_up(column_ref[...], fetched_ref, hot_ref)
    copies[0].wait()
    inner = dot(rows, item_w1[...])
    inner_ref[...] = inner
    gated = (inner * jax.nn.sigmoid(inner)).astype(BF)
    copies[1].wait()
    copies[2].wait()
    outer = dot(gated, item_w2[...])
    outer_ref[...] = outer
    scale = lax.rsqrt(jnp.mean(outer * outer, axis=-1, keepdims=True) + EPS)
    vectors = jnp.where(iota(outer.shape, 0) < users, outer * scale * gain[...], 0.0)
    peers = vectors_ref.shape[0] // 8
    vectors_ref[...] = jnp.concatenate([vectors[0:8]] * peers, axis=0).astype(BF)


def user_forward_kernel(users, *refs):
    fetched_ref, item_kept, sources, refs = refs[0], refs[1:3], refs[3:13], refs[13:]
    vectors_ref, kept_hbm, item_kept_hbm, refs = refs[0], refs[1:6], refs[6:8], refs[8:]
    targets, kept, (in_sems, out_sems) = refs[:10], refs[10:15], refs[15:]
    column_of, hot, pos_of, norm_gain_ref, out_gain_ref = targets[:5]
    in_proj, w_query, w_key, w_value, w_out = targets[5:]
    hidden_ref, normed_ref, qk_ref, weights_ref, mixed_ref = kept
    copies = copies_of(zip(sources, targets), in_sems)
    saves = [
        pltpu.make_async_copy(a, b, out_sems.at[i])
        for i, (a, b) in enumerate(zip(kept + item_kept, kept_hbm + item_kept_hbm))
    ]
    saves[5].start()
    saves[6].start()
    hist, width = pos_of.shape
    heads = width // HEAD_DIM
    span = users * hist
    copies[0].wait()
    copies[1].wait()
    rows = look_up(column_of[0:span, :], fetched_ref, hot)
    for copy in copies[2:6]:
        copy.wait()
    pos = pos_of[...].astype(F32)
    hidden = dot(rows, in_proj[...]) + jnp.concatenate([pos] * users, axis=0)
    hidden_ref[...] = hidden
    saves[0].start()
    scale = lax.rsqrt(jnp.mean(hidden * hidden, axis=-1, keepdims=True) + EPS)
    normed = (hidden * scale * norm_gain_ref[...]).astype(BF)
    normed_ref[...] = normed
    saves[1].start()
    last = jnp.concatenate(
        [normed[(u + 1) * hist - PAD : (u + 1) * hist].astype(F32)[PAD - 1 :] for u in range(users)]
        + [jnp.zeros((PAD - users, width), F32)],
        axis=0,
    ).astype(BF)
    mask = head_mask(heads, width)
    copies[6].wait()
    query = dot(last, w_query[...]).astype(BF).astype(F32)
    copies[7].wait()
    qk = dot_nt(spread_heads(query, mask, users), w_key[...]).astype(BF)
    qk_ref[...] = qk
    saves[2].start()
    shape = (users * heads, span)
    own = iota(shape, 0) // heads == iota(shape, 1) // hist
    scores = jnp.where(own, dot_nt(qk, normed) * (1.0 / math.sqrt(HEAD_DIM)), -jnp.inf)
    raised = jnp.exp(scores - jnp.max(scores, axis=1, keepdims=True))
    weights = raised / jnp.sum(raised, axis=1, keepdims=True)
    weights_ref[...] = weights
    saves[3].start()
    mixes = dot(weights.astype(BF), normed).astype(BF)
    copies[8].wait()
    attended = join_heads(dot(mixes, w_value[...]), mask, users).astype(BF)
    copies[9].wait()
    hidden_last = jnp.concatenate(
        [hidden[(u + 1) * hist - 1 : (u + 1) * hist] for u in range(users)]
        + [jnp.zeros((PAD - users, width), F32)],
        axis=0,
    )
    mixed = hidden_last + dot(attended, w_out[...])
    mixed_ref[...] = mixed
    saves[4].start()
    scale = lax.rsqrt(jnp.mean(mixed * mixed, axis=-1, keepdims=True) + EPS)
    vectors_ref[...] = (mixed * scale * out_gain_ref[...]).astype(BF)
    for save in saves:
        save.wait()


def arrange_kernel(users, near, near_ref, vectors_ref, spread_ref):
    total, width = spread_ref.shape
    block = near * users + 8
    pair = 2 * block
    at = iota((pair, near * 8), 0) % block
    source = jnp.where(at < near * users, at // users * 8 + at % users, -1)
    item_rows = dot(one_hot(iota((pair, near * 8), 1) == source), near_ref[...])
    at = iota((pair, PAD), 0) % block
    source = jnp.where((at >= near * users) & (at < (near + 1) * users), at - near * users, -1)
    user_rows = dot(one_hot(iota((pair, PAD), 1) == source), vectors_ref[...])
    rows = (item_rows + user_rows).astype(BF)
    for i in range(total // pair):
        spread_ref[i * pair : (i + 1) * pair, :] = rows


def softmax_kernel(
    users, near, scale, place_ref, gathered_ref, swapped_ref, d_user_ref, d_part_ref, raised_ref
):
    rows, width = gathered_ref.shape
    items = near * users
    block = items + 8
    blocks = rows // block
    mine, plane = place_ref[0], place_ref[1]
    own, other = gathered_ref[...], swapped_ref[...]
    shape = (blocks * users, rows)
    line = iota(shape, 0)
    picks = one_hot(iota(shape, 1) == line // users * block + items + line % users)
    group_users = jnp.concatenate([dot(picks, own), dot(picks, other)], axis=0).astype(BF)
    total = 2 * blocks * users

    shape = (rows, total)
    line = iota(shape, 0)
    valid = line % block < items
    first = jnp.where(valid, scale * dot_nt(own, group_users), -jnp.inf)
    second = jnp.where(valid, scale * dot_nt(other, group_users), -jnp.inf)
    top = jnp.maximum(
        jnp.max(first, axis=0, keepdims=True), jnp.max(second, axis=0, keepdims=True)
    )
    raised = jnp.exp(first - top)
    raised_ref[...] = raised
    other_raised = jnp.exp(second - top)
    count = jnp.sum(raised, axis=0, keepdims=True) + jnp.sum(other_raised, axis=0, keepdims=True)
    share = 1.0 / count

    line = (items, total)
    target = (iota(line, 0) // users == plane) & (
        iota(line, 1) == mine * users + iota(line, 0) % users
    )
    near_raised = raised_ref[pl.ds(pl.multiple_of(mine * block, 8), items), :]
    slope = (near_raised * share - jnp.where(target, 1.0, 0.0)).astype(BF)
    apart = (near * 8, items)
    at = iota(apart, 0)
    apart = one_hot((at % 8 < users) & (iota(apart, 1) == at // 8 * users + at % 8))
    d_part = scale * dot(dot(apart, slope).astype(BF), group_users)

    who = iota(shape, 1) - mine * users
    target = (who >= 0) & (who < users) & (iota(shape, 0) == mine * block + plane * users + who)
    slope = (raised * share - jnp.where(target, 1.0, 0.0)).astype(BF)
    other_slope = (other_raised * share).astype(BF)
    self = (PAD, total)
    self = one_hot((iota(self, 0) < users) & (iota(self, 1) == mine * users + iota(self, 0)))
    d_user = dot(dot_nt(self, slope).astype(BF), own)
    d_user = d_user + dot(dot_nt(self, other_slope).astype(BF), other)
    d_user_ref[...] = (scale * d_user).astype(BF).astype(F32)
    each = jnp.sum(jnp.where(target, top + jnp.log(count) - first, 0.0), axis=0, keepdims=True)
    loss = jnp.sum(each, axis=1, keepdims=True)
    high = loss.astype(BF).astype(F32)
    middle = (loss - high).astype(BF).astype(F32)
    low = loss - high - middle
    shape = d_part.shape
    lanes = iota(shape, 1)
    loss = jnp.where(lanes == 0, high, jnp.where(lanes == 1, middle, jnp.where(lanes == 2, low, 0.0)))
    d_part_ref[...] = jnp.where(iota(shape, 0) % 8 == users, loss, d_part).astype(BF)


def norm_backward(values, cotangent, gain):
    inverse = lax.rsqrt(jnp.mean(values * values, axis=-1, keepdims=True) + EPS)
    pulled = cotangent * gain
    along = jnp.mean(pulled * values, axis=-1, keepdims=True)
    return inverse * pulled - values * (inverse * inverse * inverse * along)


def user_backward_kernel(users, d_user_ref, *refs):
    sources, refs = refs[:18], refs[18:]
    d_rows_ref, ahead, refs = refs[0], refs[1:7], refs[7:]
    targets, (d_normed, sems) = refs[:12], refs[12:]
    mixed_ref, out_gain_ref, w_out, w_value, normed_ref, weights_ref, qk_ref = targets[:7]
    w_key, w_query, hidden_ref, norm_gain_ref, in_proj = targets[7:]
    copies = copies_of(zip(sources, tuple(targets) + tuple(ahead)), sems)
    span, width = hidden_ref.shape
    hist = span // users
    heads = width // HEAD_DIM
    mask = head_mask(heads, width)
    for copy in copies[:3]:
        copy.wait()
    d_mixed = norm_backward(mixed_ref[...], d_user_ref[...], out_gain_ref[...])
    d_attended = dot_nt(d_mixed.astype(BF), w_out[...])
    copies[3].wait()
    d_mixes = dot_nt(spread_heads(d_attended, mask, users), w_value[...]).astype(BF)
    for copy in copies[4:7]:
        copy.wait()
    normed = normed_ref[...]
    weights = weights_ref[...]
    shape = weights.shape
    own = iota(shape, 0) // heads == iota(shape, 1) // hist
    d_weights = jnp.where(own, dot_nt(d_mixes, normed), 0.0)
    d_scores = weights * (d_weights - jnp.sum(weights * d_weights, axis=1, keepdims=True))
    d_scores = (d_scores * (1.0 / math.sqrt(HEAD_DIM))).astype(BF)
    d_normed[...] = dot_tn(
        jnp.concatenate([weights.astype(BF), d_scores], axis=0),
        jnp.concatenate([d_mixes, qk_ref[...]], axis=0),
    )
    d_qk = dot(d_scores, normed).astype(BF)
    copies[7].wait()
    d_query = join_heads(dot(d_qk, w_key[...]), mask, users).astype(BF)
    copies[8].wait()
    d_last = dot_nt(d_query, w_query[...])
    for u in range(users):
        at = slice((u + 1) * hist - 1, (u + 1) * hist)
        d_normed[at, :] = d_normed[at, :] + d_last[u : u + 1]
    copies[9].wait()
    copies[10].wait()
    d_normed[...] = norm_backward(hidden_ref[...], d_normed[...], norm_gain_ref[...])
    for u in range(users):
        at = slice((u + 1) * hist - 1, (u + 1) * hist)
        d_normed[at, :] = d_normed[at, :] + d_mixed[u : u + 1]
    copies[11].wait()
    d_rows_ref[...] = dot_nt(d_normed[...].astype(BF), in_proj[...]).astype(BF)
    for copy in copies[12:]:
        copy.wait()


def item_backward_kernel(users, core_ref, parts_ref, d_rows_ref, *refs):
    row_ref, gain, inner_ref, item_w2, item_w1, outer_ref, refs = *refs[:6], refs[6:]
    d_all_ref, send_ref, keep_ref, loss_ref = refs
    span, emb = d_rows_ref.shape
    wide = row_ref.shape[1]
    peers = parts_ref.shape[0]
    shape = (PAD, peers)
    sums = dot(one_hot(iota(shape, 1) % 8 == iota(shape, 0)), parts_ref[...])
    shape = (1, 128)
    loss = jnp.where(iota(shape, 1) < 3, sums[users : users + 1, 0:128], 0.0)
    loss_ref[...] = jnp.broadcast_to(jnp.sum(loss, axis=1, keepdims=True), loss_ref.shape)
    d_item = jnp.where(iota(sums.shape, 0) < users, sums, 0.0).astype(BF).astype(F32)
    d_all_ref[0:span, :] = d_rows_ref[...]
    half = keep_ref.shape[0]
    first = HOT_CODE + core_ref[0] * half
    picks = one_hot(iota((half, wide), 0) + first == row_ref[0:1, :])
    keep = dot(picks[:, 0:span], d_rows_ref[...])
    first = HOT_CODE + (1 - core_ref[0]) * half
    other_picks = one_hot(iota((half, wide), 0) + first == row_ref[0:1, :])
    send = dot(other_picks[:, 0:span], d_rows_ref[...])
    d_outer = norm_backward(outer_ref[...], d_item, gain[...])
    inner = inner_ref[...]
    gate = jax.nn.sigmoid(inner)
    d_inner = dot_nt(d_outer.astype(BF), item_w2[...]) * (gate * (1.0 + inner * (1.0 - gate)))
    d_items = dot_nt(d_inner.astype(BF), item_w1[...])
    d_items = jnp.concatenate([d_items, jnp.zeros((wide - span - PAD, emb), F32)], axis=0).astype(BF)
    d_all_ref[span:, :] = d_items
    keep_ref[...] = keep + dot(picks[:, span:], d_items)
    send_ref[...] = send + dot(other_picks[:, span:], d_items)


def rare_kernel(d_all_ref, row_ref, rare_ref):
    shape = (rare_ref.shape[0], row_ref.shape[1])
    rare_ref[...] = dot(one_hot(iota(shape, 0) == row_ref[0:1, :]), d_all_ref[...]).astype(BF)


def outgoing_kernel(rare_ref, keep_ref, got_ref, outgoing_ref):
    half = keep_ref.shape[0]
    slots = rare_ref.shape[0]
    shape = (slots, half)
    line = iota(shape, 0)
    owner, slot = line // SLOTS, line % SLOTS - HOT_SLOT
    held = owner // 8 * 2 + owner % 2 + slot * (half // 2)
    held = one_hot((slot >= 0) & (slot < 2) & (iota(shape, 1) == held))
    hot = dot(held, (keep_ref[...] + got_ref[...]).astype(BF))
    outgoing_ref[...] = (rare_ref[...].astype(F32) + hot).astype(BF)


def scatter_kernel(returned_ref, row_ref, loss_ref, part_ref, sums_ref):
    rows, emb = part_ref.shape
    slots = returned_ref.shape[0]
    returned = returned_ref[...]
    picks = one_hot(iota((rows, slots), 0) == row_ref[0:1, :])
    part_ref[...] = dot(picks, returned).astype(BF)
    shape = (PAD, slots)
    hot = dot(one_hot((iota(shape, 0) < 2) & (iota(shape, 1) % SLOTS == iota(shape, 0) + HOT_SLOT)), returned)
    halves = [hot[i : i + 1, j : j + 128] for i in range(2) for j in range(0, emb, 128)]
    block = jnp.concatenate(halves + [loss_ref[0 : 8 - len(halves), :]], axis=0)
    sums_ref[...] = jnp.concatenate([block] * (sums_ref.shape[0] // 8), axis=0)


def finish_kernel(count, core_ref, sums_ref, other_ref, hot_ref, loss_ref):
    rows, emb = hot_ref.shape
    groups = sums_ref.shape[0] // 8
    for core, ref in ((core_ref[0], sums_ref), (1 - core_ref[0], other_ref)):
        row = 0
        for i in range(2):
            at = pl.ds(pl.multiple_of(core * (rows // 2) + i * groups, groups), groups)
            for j in range(0, emb, 128):
                hot_ref[at, j : j + 128] = ref[pl.ds(row, groups, stride=8), :]
                row += 1
    at = pl.ds(row, groups, stride=8)
    losses = sums_ref[at, :] + other_ref[at, :]
    loss_ref[...] = jnp.sum(losses[:, 0:1], axis=0, keepdims=True) / count


def shards(
    history,
    item_ids,
    hot_table,
    rare_table,
    in_proj,
    pos_embed,
    norm_gain,
    w_query,
    w_key,
    w_value,
    w_out,
    out_gain,
    item_w1,
    item_w2,
    item_gain,
):
    users, hist = history.shape
    emb = hot_table.shape[1]
    rare_count = rare_table.shape[0]
    width = in_proj.shape[1]
    heads = width // HEAD_DIM
    scale = 4.0 / math.sqrt(width)
    owners = lax.axis_size(SHARD)
    towers = lax.axis_size("tower")
    near = lax.axis_size(LINE)
    total = users * towers * owners
    slots = owners * SLOTS
    span = users * hist
    wide = -(-(span + PAD) // 128) * 128
    swap = [(i, towers - 1 - i) for i in range(towers)]
    shape = jax.ShapeDtypeStruct
    sems = lambda n: pltpu.SemaphoreType.DMA((n,))
    vmem = lambda a: pltpu.VMEM(a.shape, a.dtype)
    hbm = lambda a: pltpu.HBM(a.shape, a.dtype)
    in_hbm = lambda a: pltpu.with_memory_space_constraint(a, pltpu.HBM)
    in_vmem = lambda a: pltpu.with_memory_space_constraint(a, pltpu.VMEM)
    like = lambda arrays: [pltpu.VMEM(a.shape, a.dtype) for a in arrays]
    exchange = functools.partial(lax.all_to_all, split_axis=0, concat_axis=0, tiled=True)

    places = (shape((8, wide), jnp.int32), shape((wide, 128), jnp.int32))
    loads = (history, item_ids.reshape(1, users), rare_table)
    request, known, row, column = pl.pallas_call(
        functools.partial(index_kernel, owners),
        out_shape=(
            shape((owners, 128), jnp.int32),
            pltpu.VMEM((rare_count, emb), BF),
            *map(vmem, places),
        ),
        in_specs=[HBM] * 3,
        out_specs=(VMEM,) * 4,
        scratch_shapes=like(loads) + [sems(3)],
        compiler_params=params(24),
        name="index",
    )(*map(in_hbm, loads))
    asked = exchange(request, SHARD)
    served, hot_ready, item_column, asked_row, row, column = pl.pallas_call(
        serve_kernel,
        out_shape=(
            shape((slots, emb), BF),
            pltpu.VMEM(hot_table.shape, BF),
            pltpu.VMEM((PAD, 128), jnp.int32),
            pltpu.HBM((8, slots), jnp.int32),
            *map(hbm, places),
        ),
        in_specs=[VMEM] * 4 + [HBM],
        out_specs=(VMEM, VMEM, VMEM, HBM, HBM, HBM),
        scratch_shapes=[
            pltpu.VMEM(hot_table.shape, F32),
            pltpu.VMEM((8, slots), jnp.int32),
            sems(4),
        ],
        compiler_params=params(24),
        name="serve",
    )(asked, *map(in_vmem, (known, row, column)), in_hbm(hot_table))
    fetched = exchange(served, SHARD)

    norm_gain, out_gain, item_gain = (g.reshape(1, width) for g in (norm_gain, out_gain, item_gain))
    loads = (item_w1, item_w2, item_gain)
    item_kept = (shape((PAD, width), F32), shape((PAD, width), F32))
    item_vec, inner, outer = pl.pallas_call(
        functools.partial(item_forward_kernel, users),
        out_shape=(shape((near * 8, width), BF), *map(vmem, item_kept)),
        in_specs=[VMEM] * 3 + [HBM] * 3,
        out_specs=(VMEM,) * 3,
        scratch_shapes=like(loads) + [sems(3)],
        compiler_params=params(24),
        name="item_forward",
    )(fetched, in_vmem(hot_ready), in_vmem(item_column), *map(in_hbm, loads))
    near_items = exchange(item_vec, LINE)

    loads = (column, hot_table, pos_embed, norm_gain, out_gain)
    loads += (in_proj, w_query, w_key, w_value, w_out)
    kept = (
        shape((span, width), F32),
        shape((span, width), BF),
        shape((users * heads, width), BF),
        shape((users * heads, span), F32),
        shape((PAD, width), F32),
    )
    user_vec, hidden, normed, qk, weights, mixed, inner, outer = pl.pallas_call(
        functools.partial(user_forward_kernel, users),
        out_shape=(shape((PAD, width), BF), *map(hbm, kept + item_kept)),
        in_specs=[VMEM] * 3 + [HBM] * len(loads),
        out_specs=(VMEM,) + (HBM,) * (len(kept) + 2),
        scratch_shapes=like(loads + kept) + [sems(len(loads)), sems(len(kept) + 2)],
        compiler_params=params(40),
        name="user_forward",
    )(fetched, in_vmem(inner), in_vmem(outer), *map(in_hbm, loads))

    rows = owners // near * (near * users + 8)
    spread = pl.pallas_call(
        functools.partial(arrange_kernel, users, near),
        out_shape=shape((rows, width), BF),
        in_specs=[VMEM, VMEM],
        out_specs=VMEM,
        compiler_params=params(24),
        name="arrange",
    )(near_items, user_vec)
    gathered = exchange(spread, ("x", "y"))
    swapped = lax.ppermute(gathered, "tower", swap)
    place = jnp.stack([lax.axis_index(("x", "y")), lax.axis_index(LINE)]).astype(jnp.int32)
    d_user, d_part = pl.pallas_call(
        functools.partial(softmax_kernel, users, near, scale),
        out_shape=(shape((PAD, width), F32), shape((near * 8, width), BF)),
        in_specs=[SMEM, VMEM, VMEM],
        out_specs=(VMEM, VMEM),
        scratch_shapes=[pltpu.VMEM((rows, 2 * owners // near * users), F32)],
        compiler_params=params(32),
        name="softmax",
    )(place, gathered, swapped)
    parts = exchange(d_part, LINE)

    loads = (mixed, out_gain, w_out, w_value, normed, weights, qk)
    loads += (w_key, w_query, hidden, norm_gain, in_proj)
    ahead = (row, item_gain, inner, item_w2, item_w1, outer)
    d_rows, *item_ready = pl.pallas_call(
        functools.partial(user_backward_kernel, users),
        out_shape=(shape((span, emb), BF), *map(vmem, ahead)),
        in_specs=[VMEM] + [HBM] * 18,
        out_specs=(VMEM,) * 7,
        scratch_shapes=like(loads) + [pltpu.VMEM((span, width), F32), sems(18)],
        compiler_params=params(40),
        name="user_backward",
    )(d_user, *map(in_hbm, loads + ahead))
    core = lax.axis_index("tower").astype(jnp.int32).reshape(1)
    row_ready = item_ready[0]
    d_all, send, keep, loss = pl.pallas_call(
        functools.partial(item_backward_kernel, users),
        out_shape=(
            shape((wide, emb), BF),
            shape((owners // 2, emb), F32),
            shape((owners // 2, emb), F32),
            shape((8, 128), F32),
        ),
        in_specs=[SMEM] + [VMEM] * 8,
        out_specs=(VMEM,) * 4,
        compiler_params=params(32),
        name="item_backward",
    )(core, parts, d_rows, *map(in_vmem, item_ready))
    got = lax.ppermute(send, "tower", swap)
    rare = pl.pallas_call(
        rare_kernel,
        out_shape=shape((slots, emb), BF),
        in_specs=[VMEM, VMEM],
        out_specs=VMEM,
        compiler_params=params(32),
        name="rare",
    )(d_all, in_vmem(row_ready))
    outgoing = pl.pallas_call(
        outgoing_kernel,
        out_shape=shape((slots, emb), BF),
        in_specs=[VMEM] * 3,
        out_specs=VMEM,
        compiler_params=params(32),
        name="outgoing",
    )(rare, keep, got)

    returned = exchange(outgoing, SHARD)
    part, mine = pl.pallas_call(
        scatter_kernel,
        out_shape=(shape((rare_count, emb), BF), shape((owners // 4 * 8, 128), F32)),
        in_specs=[VMEM, VMEM, VMEM],
        out_specs=(VMEM, VMEM),
        compiler_params=params(24),
        name="scatter",
    )(returned, asked_row, loss)
    rare_grad = part.astype(F32) + lax.ppermute(part, "tower", swap).astype(F32)
    sums = exchange(mine, GROUP)
    other_sums = lax.ppermute(sums, "tower", swap)
    hot_total, loss_total = pl.pallas_call(
        functools.partial(finish_kernel, total * 2),
        out_shape=(shape((owners, emb), F32), shape((1, 1), F32)),
        in_specs=[SMEM, VMEM, VMEM],
        out_specs=(VMEM, VMEM),
        compiler_params=params(24),
        name="finish",
    )(core, sums, other_sums)
    return (hot_total, rare_grad, loss_total[0, 0])


def solution(mesh):
    sizes = (mesh.shape["tower"], 4, 4, mesh.shape["shard"] // 32, 2)
    mesh = Mesh(mesh.devices.reshape(sizes), ("tower",) + SHARD)
    return jax.shard_map(
        shards,
        mesh=mesh,
        in_specs=(
            P(("tower",) + SHARD, None),
            P(("tower",) + SHARD),
            P(),
            P(SHARD, None),
            P(),
            P(),
            P(),
            P(),
            P(),
            P(),
            P(),
            P(),
            P(),
            P(),
            P(),
        ),
        out_specs=(P(), P(SHARD, None), P()),
        check_vma=False,
    )
```

```python
import functools
import math

import jax
import jax.numpy as jnp
from jax import lax
from jax.experimental import pallas as pl
from jax.experimental.pallas import tpu as pltpu
from jax.sharding import Mesh
from jax.sharding import PartitionSpec as P

HEAD_DIM = 64
EPS = 1e-06
SLOTS = 8
HOT_SLOT = 5
HOT_CODE = 4096
LINE = ("zh", "zl")
SHARD = ("x", "y") + LINE
GROUP = ("x", "y", "zl")
PAD = 16
BF = jnp.bfloat16
F32 = jnp.float32
VMEM = pl.BlockSpec(memory_space=pltpu.VMEM)
SMEM = pl.BlockSpec(memory_space=pltpu.SMEM)
HBM = pl.BlockSpec(memory_space=pltpu.HBM)
NT = (((1,), (1,)), ((), ()))
TN = (((0,), (0,)), ((), ()))


def dot(a, b):
    return jnp.dot(a, b, preferred_element_type=F32)


def dot_nt(a, b):
    return lax.dot_general(a, b, NT, preferred_element_type=F32)


def dot_tn(a, b):
    return lax.dot_general(a, b, TN, preferred_element_type=F32)


def iota(shape, axis):
    return lax.broadcasted_iota(jnp.int32, shape, axis)


def one_hot(mask):
    return jnp.where(mask, 1.0, 0.0).astype(BF)


def params(mib):
    return pltpu.CompilerParams(vmem_limit_bytes=mib * 1024 * 1024)


def copies_of(pairs, sems):
    copies = [pltpu.make_async_copy(a, b, sems.at[i]) for i, (a, b) in enumerate(pairs)]
    for copy in copies:
        copy.start()
    return copies


def index_kernel(
    owners,
    history_hbm,
    items_hbm,
    table_hbm,
    request_ref,
    known_ref,
    row,
    column,
    history_ref,
    items_ref,
    table,
    sems,
):
    loads = copies_of(
        [(history_hbm, history_ref), (items_hbm, items_ref), (table_hbm, table)], sems
    )
    loads[0].wait()
    loads[1].wait()
    hot_count = owners
    rare_count = table.shape[0]
    users = history_ref.shape[0]
    span = row.shape[1]
    parts = [history_ref[u : u + 1, :] for u in range(users)] + [items_ref[...]]
    filled = sum(p.shape[1] for p in parts)
    ids = jnp.concatenate(parts + [jnp.full((1, span - filled), -1, jnp.int32)], axis=1)
    is_rare = ids >= hot_count
    index = ids - hot_count
    owner = jnp.where(is_rare, index // rare_count, -1)
    value = jnp.where(is_rare, index % rare_count + 1, 0).astype(F32)
    hits = iota((owners, span), 0) == owner
    before = one_hot(iota((span, span), 0) < iota((span, span), 1))
    earlier = dot(one_hot(hits), before)
    position = jnp.sum(jnp.where(hits, earlier, 0.0), axis=0, keepdims=True).astype(jnp.int32)
    places = jnp.where(
        is_rare, owner * SLOTS + position, jnp.where(ids >= 0, ids + HOT_CODE, -1)
    )
    row[...] = jnp.broadcast_to(places, row.shape)
    column[...] = jnp.transpose(jnp.broadcast_to(places.astype(F32), (128, span))).astype(jnp.int32)
    order = jnp.where(hits, earlier, -1.0)
    lanes = iota(request_ref.shape, 1)
    request = jnp.zeros(request_ref.shape, F32)
    for slot in range(HOT_SLOT):
        wanted = jnp.sum(jnp.where(order == float(slot), value, 0.0), axis=1, keepdims=True)
        request = jnp.where(lanes == slot, wanted, request)
    request_ref[...] = request.astype(jnp.int32)
    loads[2].wait()
    known_ref[...] = table[...].astype(BF)


def serve_kernel(
    asked_ref,
    known_ref,
    row_ref,
    column_ref,
    hot_hbm,
    served,
    hot_ref,
    item_column_ref,
    asked_row_hbm,
    row_hbm,
    column_hbm,
    hot,
    row,
    sems,
):
    copies = copies_of([(hot_hbm, hot), (row_ref, row_hbm), (column_ref, column_hbm)], sems)
    span = column_ref.shape[0] - 128
    item_column_ref[...] = column_ref[span : span + PAD, :]
    slots = served.shape[0]
    sources = asked_ref.shape[0]
    asked = asked_ref[...]
    high = (asked // 2).astype(F32).astype(BF)
    low = (asked % 2).astype(F32).astype(BF)
    expand = one_hot(iota((slots, sources), 0) // SLOTS == iota((slots, sources), 1))
    wide = 2.0 * dot(expand, high) + dot(expand, low)
    mine = iota(wide.shape, 1) == iota(wide.shape, 0) % SLOTS
    index = jnp.sum(jnp.where(mine, wide, 0.0), axis=1, keepdims=True) - 1.0
    index = jnp.broadcast_to(index, wide.shape)
    row[...] = jnp.transpose(index)[0:8].astype(jnp.int32)
    save = pltpu.make_async_copy(row, asked_row_hbm, sems.at[3])
    save.start()
    index = index.astype(jnp.int32)
    lanes = iota(index.shape, 1)
    rows = known_ref.shape[0]
    picks = jnp.concatenate(
        [one_hot(index == lanes + 128 * j) for j in range(rows // 128)], axis=1
    )
    served[...] = dot(picks, known_ref[...]).astype(BF)
    copies[0].wait()
    hot_ref[...] = hot[...].astype(BF)
    for copy in copies[1:] + [save]:
        copy.wait()


def head_mask(heads, width):
    return iota((heads, width), 1) // HEAD_DIM == iota((heads, width), 0)


def spread_heads(values, mask, users):
    return jnp.concatenate(
        [jnp.where(mask, values[u : u + 1], 0.0) for u in range(users)], axis=0
    ).astype(BF)


def join_heads(full, mask, users):
    heads = mask.shape[0]
    parts = [
        jnp.sum(
            jnp.where(mask, full[u * heads : (u + 1) * heads], 0.0), axis=0, keepdims=True
        )
        for u in range(users)
    ]
    return jnp.concatenate(parts + [jnp.zeros((PAD - users, full.shape[1]), F32)], axis=0)


def look_up(column, fetched, hot):
    lanes = iota(column.shape, 1)
    slots = fetched.shape[0]
    picks = jnp.concatenate(
        [one_hot(column == lanes + 128 * j) for j in range(slots // 128)], axis=1
    )
    hot_picks = one_hot(column == lanes + HOT_CODE)
    return (dot(picks, fetched[...]) + dot(hot_picks, hot[...].astype(BF))).astype(BF)


def item_forward_kernel(
    users,
    fetched_ref,
    hot_ref,
    column_ref,
    item_w2,
    item_w1_hbm,
    gain_hbm,
    vectors_ref,
    inner_ref,
    outer_ref,
    item_w1,
    gain,
    sems,
):
    loads = copies_of([(item_w1_hbm, item_w1), (gain_hbm, gain)], sems)
    rows = look_up(column_ref[...], fetched_ref, hot_ref)
    loads[0].wait()
    inner = dot(rows, item_w1[...])
    inner_ref[...] = inner
    gated = (inner * jax.nn.sigmoid(inner)).astype(BF)
    loads[1].wait()
    outer = dot(gated, item_w2[...])
    outer_ref[...] = outer
    scale = lax.rsqrt(jnp.mean(outer * outer, axis=-1, keepdims=True) + EPS)
    vectors = jnp.where(iota(outer.shape, 0) < users, outer * scale * gain[...], 0.0)
    peers = vectors_ref.shape[0] // 8
    vectors_ref[...] = jnp.concatenate([vectors[0:8]] * peers, axis=0).astype(BF)


def user_forward_kernel(users, *refs):
    fetched_ref, item_kept, sources, refs = refs[0], refs[1:3], refs[3:13], refs[13:]
    vectors_ref, kept_hbm, item_kept_hbm, refs = refs[0], refs[1:6], refs[6:8], refs[8:]
    targets, kept, (in_sems, out_sems) = refs[:10], refs[10:15], refs[15:]
    column_of, hot, pos_of, norm_gain_ref, out_gain_ref = targets[:5]
    in_proj, w_query, w_key, w_value, w_out = targets[5:]
    hidden_ref, normed_ref, qk_ref, weights_ref, mixed_ref = kept
    copies = copies_of(zip(sources, targets), in_sems)
    saves = [
        pltpu.make_async_copy(a, b, out_sems.at[i])
        for i, (a, b) in enumerate(zip(kept + item_kept, kept_hbm + item_kept_hbm))
    ]
    saves[5].start()
    saves[6].start()
    hist, width = pos_of.shape
    heads = width // HEAD_DIM
    span = users * hist
    copies[0].wait()
    copies[1].wait()
    rows = look_up(column_of[0:span, :], fetched_ref, hot)
    for copy in copies[2:6]:
        copy.wait()
    pos = pos_of[...].astype(F32)
    hidden = dot(rows, in_proj[...]) + jnp.concatenate([pos] * users, axis=0)
    hidden_ref[...] = hidden
    saves[0].start()
    scale = lax.rsqrt(jnp.mean(hidden * hidden, axis=-1, keepdims=True) + EPS)
    normed = (hidden * scale * norm_gain_ref[...]).astype(BF)
    normed_ref[...] = normed
    saves[1].start()
    last = jnp.concatenate(
        [normed[(u + 1) * hist - PAD : (u + 1) * hist].astype(F32)[PAD - 1 :] for u in range(users)]
        + [jnp.zeros((PAD - users, width), F32)],
        axis=0,
    ).astype(BF)
    mask = head_mask(heads, width)
    copies[6].wait()
    query = dot(last, w_query[...]).astype(BF).astype(F32)
    copies[7].wait()
    qk = dot_nt(spread_heads(query, mask, users), w_key[...]).astype(BF)
    qk_ref[...] = qk
    saves[2].start()
    shape = (users * heads, span)
    own = iota(shape, 0) // heads == iota(shape, 1) // hist
    scores = jnp.where(own, dot_nt(qk, normed) * (1.0 / math.sqrt(HEAD_DIM)), -jnp.inf)
    raised = jnp.exp(scores - jnp.max(scores, axis=1, keepdims=True))
    weights = raised / jnp.sum(raised, axis=1, keepdims=True)
    weights_ref[...] = weights
    saves[3].start()
    mixes = dot(weights.astype(BF), normed).astype(BF)
    copies[8].wait()
    attended = join_heads(dot(mixes, w_value[...]), mask, users).astype(BF)
    copies[9].wait()
    hidden_last = jnp.concatenate(
        [hidden[(u + 1) * hist - 1 : (u + 1) * hist] for u in range(users)]
        + [jnp.zeros((PAD - users, width), F32)],
        axis=0,
    )
    mixed = hidden_last + dot(attended, w_out[...])
    mixed_ref[...] = mixed
    saves[4].start()
    scale = lax.rsqrt(jnp.mean(mixed * mixed, axis=-1, keepdims=True) + EPS)
    vectors_ref[...] = (mixed * scale * out_gain_ref[...]).astype(BF)
    for save in saves:
        save.wait()


def arrange_kernel(users, near, near_ref, vectors_ref, spread_ref):
    total, width = spread_ref.shape
    block = near * users + 8
    pair = 2 * block
    at = iota((pair, near * 8), 0) % block
    source = jnp.where(at < near * users, at // users * 8 + at % users, -1)
    item_rows = dot(one_hot(iota((pair, near * 8), 1) == source), near_ref[...])
    at = iota((pair, PAD), 0) % block
    source = jnp.where((at >= near * users) & (at < (near + 1) * users), at - near * users, -1)
    user_rows = dot(one_hot(iota((pair, PAD), 1) == source), vectors_ref[...])
    rows = (item_rows + user_rows).astype(BF)
    for i in range(total // pair):
        spread_ref[i * pair : (i + 1) * pair, :] = rows


def softmax_kernel(
    users, near, scale, place_ref, gathered_ref, swapped_ref, d_user_ref, d_part_ref, raised_ref
):
    rows, width = gathered_ref.shape
    items = near * users
    block = items + 8
    blocks = rows // block
    mine, plane = place_ref[0], place_ref[1]
    own, other = gathered_ref[...], swapped_ref[...]
    shape = (blocks * users, rows)
    line = iota(shape, 0)
    picks = one_hot(iota(shape, 1) == line // users * block + items + line % users)
    group_users = jnp.concatenate([dot(picks, own), dot(picks, other)], axis=0).astype(BF)
    total = 2 * blocks * users

    shape = (rows, total)
    line = iota(shape, 0)
    valid = line % block < items
    first = jnp.where(valid, scale * dot_nt(own, group_users), -jnp.inf)
    second = jnp.where(valid, scale * dot_nt(other, group_users), -jnp.inf)
    top = jnp.maximum(
        jnp.max(first, axis=0, keepdims=True), jnp.max(second, axis=0, keepdims=True)
    )
    raised = jnp.exp(first - top)
    raised_ref[...] = raised
    other_raised = jnp.exp(second - top)
    count = jnp.sum(raised, axis=0, keepdims=True) + jnp.sum(other_raised, axis=0, keepdims=True)
    share = 1.0 / count

    line = (items, total)
    target = (iota(line, 0) // users == plane) & (
        iota(line, 1) == mine * users + iota(line, 0) % users
    )
    near_raised = raised_ref[pl.ds(pl.multiple_of(mine * block, 8), items), :]
    slope = (near_raised * share - jnp.where(target, 1.0, 0.0)).astype(BF)
    apart = (near * 8, items)
    at = iota(apart, 0)
    apart = one_hot((at % 8 < users) & (iota(apart, 1) == at // 8 * users + at % 8))
    d_part = scale * dot(dot(apart, slope).astype(BF), group_users)

    who = iota(shape, 1) - mine * users
    target = (who >= 0) & (who < users) & (iota(shape, 0) == mine * block + plane * users + who)
    slope = (raised * share - jnp.where(target, 1.0, 0.0)).astype(BF)
    other_slope = (other_raised * share).astype(BF)
    self = (PAD, total)
    self = one_hot((iota(self, 0) < users) & (iota(self, 1) == mine * users + iota(self, 0)))
    d_user = dot(dot_nt(self, slope).astype(BF), own)
    d_user = d_user + dot(dot_nt(self, other_slope).astype(BF), other)
    d_user_ref[...] = (scale * d_user).astype(BF).astype(F32)
    each = jnp.sum(jnp.where(target, top + jnp.log(count) - first, 0.0), axis=0, keepdims=True)
    loss = jnp.sum(each, axis=1, keepdims=True)
    high = loss.astype(BF).astype(F32)
    middle = (loss - high).astype(BF).astype(F32)
    low = loss - high - middle
    shape = d_part.shape
    lanes = iota(shape, 1)
    loss = jnp.where(lanes == 0, high, jnp.where(lanes == 1, middle, jnp.where(lanes == 2, low, 0.0)))
    d_part_ref[...] = jnp.where(iota(shape, 0) % 8 == users, loss, d_part).astype(BF)


def norm_backward(values, cotangent, gain):
    inverse = lax.rsqrt(jnp.mean(values * values, axis=-1, keepdims=True) + EPS)
    pulled = cotangent * gain
    along = jnp.mean(pulled * values, axis=-1, keepdims=True)
    return inverse * pulled - values * (inverse * inverse * inverse * along)


def user_backward_kernel(users, d_user_ref, w_out, *refs):
    sources, refs = refs[:17], refs[17:]
    d_rows_ref, ahead, refs = refs[0], refs[1:7], refs[7:]
    targets, (d_normed, sems) = refs[:11], refs[11:]
    mixed_ref, out_gain_ref, w_value, normed_ref, weights_ref, qk_ref = targets[:6]
    w_key, w_query, hidden_ref, norm_gain_ref, in_proj = targets[6:]
    copies = copies_of(zip(sources, tuple(targets) + tuple(ahead)), sems)
    span, width = hidden_ref.shape
    hist = span // users
    heads = width // HEAD_DIM
    mask = head_mask(heads, width)
    for copy in copies[:2]:
        copy.wait()
    d_mixed = norm_backward(mixed_ref[...], d_user_ref[...], out_gain_ref[...])
    d_attended = dot_nt(d_mixed.astype(BF), w_out[...])
    copies[2].wait()
    d_mixes = dot_nt(spread_heads(d_attended, mask, users), w_value[...]).astype(BF)
    for copy in copies[3:6]:
        copy.wait()
    normed = normed_ref[...]
    weights = weights_ref[...]
    shape = weights.shape
    own = iota(shape, 0) // heads == iota(shape, 1) // hist
    d_weights = jnp.where(own, dot_nt(d_mixes, normed), 0.0)
    d_scores = weights * (d_weights - jnp.sum(weights * d_weights, axis=1, keepdims=True))
    d_scores = (d_scores * (1.0 / math.sqrt(HEAD_DIM))).astype(BF)
    d_normed[...] = dot_tn(
        jnp.concatenate([weights.astype(BF), d_scores], axis=0),
        jnp.concatenate([d_mixes, qk_ref[...]], axis=0),
    )
    d_qk = dot(d_scores, normed).astype(BF)
    copies[6].wait()
    d_query = join_heads(dot(d_qk, w_key[...]), mask, users).astype(BF)
    copies[7].wait()
    d_last = dot_nt(d_query, w_query[...])
    for u in range(users):
        at = slice((u + 1) * hist - 1, (u + 1) * hist)
        d_normed[at, :] = d_normed[at, :] + d_last[u : u + 1]
    copies[8].wait()
    copies[9].wait()
    d_normed[...] = norm_backward(hidden_ref[...], d_normed[...], norm_gain_ref[...])
    for u in range(users):
        at = slice((u + 1) * hist - 1, (u + 1) * hist)
        d_normed[at, :] = d_normed[at, :] + d_mixed[u : u + 1]
    copies[10].wait()
    d_rows_ref[...] = dot_nt(d_normed[...].astype(BF), in_proj[...]).astype(BF)
    for copy in copies[11:]:
        copy.wait()


def item_backward_kernel(users, core_ref, parts_ref, d_rows_ref, *refs):
    row_ref, gain, inner_ref, item_w2, item_w1, outer_ref, refs = *refs[:6], refs[6:]
    d_all_ref, send_ref, keep_ref, loss_ref = refs
    span, emb = d_rows_ref.shape
    wide = row_ref.shape[1]
    peers = parts_ref.shape[0]
    shape = (PAD, peers)
    sums = dot(one_hot(iota(shape, 1) % 8 == iota(shape, 0)), parts_ref[...])
    shape = (1, 128)
    loss = jnp.where(iota(shape, 1) < 3, sums[users : users + 1, 0:128], 0.0)
    loss_ref[...] = jnp.broadcast_to(jnp.sum(loss, axis=1, keepdims=True), loss_ref.shape)
    d_item = jnp.where(iota(sums.shape, 0) < users, sums, 0.0).astype(BF).astype(F32)
    d_all_ref[0:span, :] = d_rows_ref[...]
    half = keep_ref.shape[0]
    first = HOT_CODE + core_ref[0] * half
    picks = one_hot(iota((half, wide), 0) + first == row_ref[0:1, :])
    keep = dot(picks[:, 0:span], d_rows_ref[...])
    first = HOT_CODE + (1 - core_ref[0]) * half
    other_picks = one_hot(iota((half, wide), 0) + first == row_ref[0:1, :])
    send = dot(other_picks[:, 0:span], d_rows_ref[...])
    d_outer = norm_backward(outer_ref[...], d_item, gain[...])
    inner = inner_ref[...]
    gate = jax.nn.sigmoid(inner)
    d_inner = dot_nt(d_outer.astype(BF), item_w2[...]) * (gate * (1.0 + inner * (1.0 - gate)))
    d_items = dot_nt(d_inner.astype(BF), item_w1[...])
    d_items = jnp.concatenate([d_items, jnp.zeros((wide - span - PAD, emb), F32)], axis=0).astype(BF)
    d_all_ref[span:, :] = d_items
    keep_ref[...] = keep + dot(picks[:, span:], d_items)
    send_ref[...] = send + dot(other_picks[:, span:], d_items)


def rare_kernel(d_all_ref, row_ref, rare_ref):
    shape = (rare_ref.shape[0], row_ref.shape[1])
    rare_ref[...] = dot(one_hot(iota(shape, 0) == row_ref[0:1, :]), d_all_ref[...]).astype(BF)


def outgoing_kernel(rare_ref, keep_ref, got_ref, outgoing_ref):
    half = keep_ref.shape[0]
    slots = rare_ref.shape[0]
    shape = (slots, half)
    line = iota(shape, 0)
    owner, slot = line // SLOTS, line % SLOTS - HOT_SLOT
    held = owner // 8 * 2 + owner % 2 + slot * (half // 2)
    held = one_hot((slot >= 0) & (slot < 2) & (iota(shape, 1) == held))
    hot = dot(held, (keep_ref[...] + got_ref[...]).astype(BF))
    outgoing_ref[...] = (rare_ref[...].astype(F32) + hot).astype(BF)


def scatter_kernel(returned_ref, row_ref, loss_ref, part_ref, sums_ref):
    rows, emb = part_ref.shape
    slots = returned_ref.shape[0]
    returned = returned_ref[...]
    picks = one_hot(iota((rows, slots), 0) == row_ref[0:1, :])
    part_ref[...] = dot(picks, returned).astype(BF)
    shape = (PAD, slots)
    hot = dot(one_hot((iota(shape, 0) < 2) & (iota(shape, 1) % SLOTS == iota(shape, 0) + HOT_SLOT)), returned)
    halves = [hot[i : i + 1, j : j + 128] for i in range(2) for j in range(0, emb, 128)]
    block = jnp.concatenate(halves + [loss_ref[0 : 8 - len(halves), :]], axis=0)
    sums_ref[...] = jnp.concatenate([block] * (sums_ref.shape[0] // 8), axis=0)


def finish_kernel(count, core_ref, sums_ref, other_ref, hot_ref, loss_ref):
    rows, emb = hot_ref.shape
    groups = sums_ref.shape[0] // 8
    for core, ref in ((core_ref[0], sums_ref), (1 - core_ref[0], other_ref)):
        row = 0
        for i in range(2):
            at = pl.ds(pl.multiple_of(core * (rows // 2) + i * groups, groups), groups)
            for j in range(0, emb, 128):
                hot_ref[at, j : j + 128] = ref[pl.ds(row, groups, stride=8), :]
                row += 1
    at = pl.ds(row, groups, stride=8)
    losses = sums_ref[at, :] + other_ref[at, :]
    loss_ref[...] = jnp.sum(losses[:, 0:1], axis=0, keepdims=True) / count


def shards(
    history,
    item_ids,
    hot_table,
    rare_table,
    in_proj,
    pos_embed,
    norm_gain,
    w_query,
    w_key,
    w_value,
    w_out,
    out_gain,
    item_w1,
    item_w2,
    item_gain,
):
    users, hist = history.shape
    emb = hot_table.shape[1]
    rare_count = rare_table.shape[0]
    width = in_proj.shape[1]
    heads = width // HEAD_DIM
    scale = 4.0 / math.sqrt(width)
    owners = lax.axis_size(SHARD)
    towers = lax.axis_size("tower")
    near = lax.axis_size(LINE)
    total = users * towers * owners
    slots = owners * SLOTS
    span = users * hist
    wide = -(-(span + PAD) // 128) * 128
    swap = [(i, towers - 1 - i) for i in range(towers)]
    shape = jax.ShapeDtypeStruct
    sems = lambda n: pltpu.SemaphoreType.DMA((n,))
    vmem = lambda a: pltpu.VMEM(a.shape, a.dtype)
    hbm = lambda a: pltpu.HBM(a.shape, a.dtype)
    in_hbm = lambda a: pltpu.with_memory_space_constraint(a, pltpu.HBM)
    in_vmem = lambda a: pltpu.with_memory_space_constraint(a, pltpu.VMEM)
    like = lambda arrays: [pltpu.VMEM(a.shape, a.dtype) for a in arrays]
    exchange = functools.partial(lax.all_to_all, split_axis=0, concat_axis=0, tiled=True)

    places = (shape((8, wide), jnp.int32), shape((wide, 128), jnp.int32))
    loads = (history, item_ids.reshape(1, users), rare_table)
    request, known, row, column = pl.pallas_call(
        functools.partial(index_kernel, owners),
        out_shape=(
            shape((owners, 128), jnp.int32),
            pltpu.VMEM((rare_count, emb), BF),
            *map(vmem, places),
        ),
        in_specs=[HBM] * 3,
        out_specs=(VMEM,) * 4,
        scratch_shapes=like(loads) + [sems(3)],
        compiler_params=params(24),
        name="index",
    )(*map(in_hbm, loads))
    asked = exchange(request, SHARD)
    served, hot_ready, item_column, asked_row, row, column = pl.pallas_call(
        serve_kernel,
        out_shape=(
            shape((slots, emb), BF),
            pltpu.VMEM(hot_table.shape, BF),
            pltpu.VMEM((PAD, 128), jnp.int32),
            pltpu.HBM((8, slots), jnp.int32),
            *map(hbm, places),
        ),
        in_specs=[VMEM] * 4 + [HBM],
        out_specs=(VMEM, VMEM, VMEM, HBM, HBM, HBM),
        scratch_shapes=[
            pltpu.VMEM(hot_table.shape, F32),
            pltpu.VMEM((8, slots), jnp.int32),
            sems(4),
        ],
        compiler_params=params(24),
        name="serve",
    )(asked, *map(in_vmem, (known, row, column)), in_hbm(hot_table))
    fetched = exchange(served, SHARD)

    norm_gain, out_gain, item_gain = (g.reshape(1, width) for g in (norm_gain, out_gain, item_gain))
    item_kept = (shape((PAD, width), F32), shape((PAD, width), F32))
    item_vec, inner, outer = pl.pallas_call(
        functools.partial(item_forward_kernel, users),
        out_shape=(shape((near * 8, width), BF), *map(vmem, item_kept)),
        in_specs=[VMEM] * 4 + [HBM] * 2,
        out_specs=(VMEM,) * 3,
        scratch_shapes=like((item_w1, item_gain)) + [sems(2)],
        compiler_params=params(24),
        name="item_forward",
    )(
        fetched,
        *map(in_vmem, (hot_ready, item_column, item_w2)),
        *map(in_hbm, (item_w1, item_gain)),
    )
    near_items = exchange(item_vec, LINE)

    loads = (column, hot_table, pos_embed, norm_gain, out_gain)
    loads += (in_proj, w_query, w_key, w_value, w_out)
    kept = (
        shape((span, width), F32),
        shape((span, width), BF),
        shape((users * heads, width), BF),
        shape((users * heads, span), F32),
        shape((PAD, width), F32),
    )
    user_vec, hidden, normed, qk, weights, mixed, inner, outer = pl.pallas_call(
        functools.partial(user_forward_kernel, users),
        out_shape=(shape((PAD, width), BF), *map(hbm, kept + item_kept)),
        in_specs=[VMEM] * 3 + [HBM] * len(loads),
        out_specs=(VMEM,) + (HBM,) * (len(kept) + 2),
        scratch_shapes=like(loads + kept) + [sems(len(loads)), sems(len(kept) + 2)],
        compiler_params=params(40),
        name="user_forward",
    )(fetched, in_vmem(inner), in_vmem(outer), *map(in_hbm, loads))

    rows = owners // near * (near * users + 8)
    spread = pl.pallas_call(
        functools.partial(arrange_kernel, users, near),
        out_shape=shape((rows, width), BF),
        in_specs=[VMEM, VMEM],
        out_specs=VMEM,
        compiler_params=params(24),
        name="arrange",
    )(near_items, user_vec)
    gathered = exchange(spread, ("x", "y"))
    swapped = lax.ppermute(gathered, "tower", swap)
    place = jnp.stack([lax.axis_index(("x", "y")), lax.axis_index(LINE)]).astype(jnp.int32)
    d_user, d_part = pl.pallas_call(
        functools.partial(softmax_kernel, users, near, scale),
        out_shape=(shape((PAD, width), F32), shape((near * 8, width), BF)),
        in_specs=[SMEM, VMEM, VMEM],
        out_specs=(VMEM, VMEM),
        scratch_shapes=[pltpu.VMEM((rows, 2 * owners // near * users), F32)],
        compiler_params=params(32),
        name="softmax",
    )(place, gathered, swapped)
    parts = exchange(d_part, LINE)

    loads = (mixed, out_gain, w_value, normed, weights, qk)
    loads += (w_key, w_query, hidden, norm_gain, in_proj)
    ahead = (row, item_gain, inner, item_w2, item_w1, outer)
    d_rows, *item_ready = pl.pallas_call(
        functools.partial(user_backward_kernel, users),
        out_shape=(shape((span, emb), BF), *map(vmem, ahead)),
        in_specs=[VMEM] * 2 + [HBM] * 17,
        out_specs=(VMEM,) * 7,
        scratch_shapes=like(loads) + [pltpu.VMEM((span, width), F32), sems(17)],
        compiler_params=params(40),
        name="user_backward",
    )(d_user, in_vmem(w_out), *map(in_hbm, loads + ahead))
    core = lax.axis_index("tower").astype(jnp.int32).reshape(1)
    row_ready = item_ready[0]
    d_all, send, keep, loss = pl.pallas_call(
        functools.partial(item_backward_kernel, users),
        out_shape=(
            shape((wide, emb), BF),
            shape((owners // 2, emb), F32),
            shape((owners // 2, emb), F32),
            shape((8, 128), F32),
        ),
        in_specs=[SMEM] + [VMEM] * 8,
        out_specs=(VMEM,) * 4,
        compiler_params=params(32),
        name="item_backward",
    )(core, parts, d_rows, *map(in_vmem, item_ready))
    got = lax.ppermute(send, "tower", swap)
    rare = pl.pallas_call(
        rare_kernel,
        out_shape=shape((slots, emb), BF),
        in_specs=[VMEM, VMEM],
        out_specs=VMEM,
        compiler_params=params(32),
        name="rare",
    )(d_all, in_vmem(row_ready))
    outgoing = pl.pallas_call(
        outgoing_kernel,
        out_shape=shape((slots, emb), BF),
        in_specs=[VMEM] * 3,
        out_specs=VMEM,
        compiler_params=params(32),
        name="outgoing",
    )(rare, keep, got)

    returned = exchange(outgoing, SHARD)
    part, mine = pl.pallas_call(
        scatter_kernel,
        out_shape=(shape((rare_count, emb), BF), shape((owners // 4 * 8, 128), F32)),
        in_specs=[VMEM, VMEM, VMEM],
        out_specs=(VMEM, VMEM),
        compiler_params=params(24),
        name="scatter",
    )(returned, asked_row, loss)
    rare_grad = part.astype(F32) + lax.ppermute(part, "tower", swap).astype(F32)
    sums = exchange(mine, GROUP)
    other_sums = lax.ppermute(sums, "tower", swap)
    hot_total, loss_total = pl.pallas_call(
        functools.partial(finish_kernel, total * 2),
        out_shape=(shape((owners, emb), F32), shape((1, 1), F32)),
        in_specs=[SMEM, VMEM, VMEM],
        out_specs=(VMEM, VMEM),
        compiler_params=params(24),
        name="finish",
    )(core, sums, other_sums)
    return (hot_total, rare_grad, loss_total[0, 0])


def solution(mesh):
    sizes = (mesh.shape["tower"], 4, 4, mesh.shape["shard"] // 32, 2)
    mesh = Mesh(mesh.devices.reshape(sizes), ("tower",) + SHARD)
    return jax.shard_map(
        shards,
        mesh=mesh,
        in_specs=(
            P(("tower",) + SHARD, None),
            P(("tower",) + SHARD),
            P(),
            P(SHARD, None),
            P(),
            P(),
            P(),
            P(),
            P(),
            P(),
            P(),
            P(),
            P(),
            P(),
            P(),
        ),
        out_specs=(P(), P(SHARD, None), P()),
        check_vma=False,
    )
```

```python
import functools
import math

import jax
import jax.numpy as jnp
from jax import lax
from jax.experimental import pallas as pl
from jax.experimental.pallas import tpu as pltpu
from jax.sharding import Mesh
from jax.sharding import PartitionSpec as P

HEAD_DIM = 64
EPS = 1e-06
SLOTS = 8
HOT_SLOT = 5
HOT_CODE = 4096
LINE = ("zh", "zl")
SHARD = ("x", "y") + LINE
GROUP = ("x", "y", "zl")
PAD = 16
BF = jnp.bfloat16
F32 = jnp.float32
VMEM = pl.BlockSpec(memory_space=pltpu.VMEM)
SMEM = pl.BlockSpec(memory_space=pltpu.SMEM)
HBM = pl.BlockSpec(memory_space=pltpu.HBM)
NT = (((1,), (1,)), ((), ()))
TN = (((0,), (0,)), ((), ()))


def dot(a, b):
    return jnp.dot(a, b, preferred_element_type=F32)


def dot_nt(a, b):
    return lax.dot_general(a, b, NT, preferred_element_type=F32)


def dot_tn(a, b):
    return lax.dot_general(a, b, TN, preferred_element_type=F32)


def iota(shape, axis):
    return lax.broadcasted_iota(jnp.int32, shape, axis)


def one_hot(mask):
    return jnp.where(mask, 1.0, 0.0).astype(BF)


def params(mib):
    return pltpu.CompilerParams(vmem_limit_bytes=mib * 1024 * 1024)


def copies_of(pairs, sems):
    copies = [pltpu.make_async_copy(a, b, sems.at[i]) for i, (a, b) in enumerate(pairs)]
    for copy in copies:
        copy.start()
    return copies


def index_kernel(
    owners,
    history_hbm,
    items_hbm,
    table_hbm,
    request_ref,
    known_ref,
    row,
    column,
    history_ref,
    items_ref,
    table,
    sems,
):
    loads = copies_of(
        [(history_hbm, history_ref), (items_hbm, items_ref), (table_hbm, table)], sems
    )
    loads[0].wait()
    loads[1].wait()
    hot_count = owners
    rare_count = table.shape[0]
    users = history_ref.shape[0]
    span = row.shape[1]
    parts = [history_ref[u : u + 1, :] for u in range(users)] + [items_ref[...]]
    filled = sum(p.shape[1] for p in parts)
    ids = jnp.concatenate(parts + [jnp.full((1, span - filled), -1, jnp.int32)], axis=1)
    is_rare = ids >= hot_count
    index = ids - hot_count
    owner = jnp.where(is_rare, index // rare_count, -1)
    value = jnp.where(is_rare, index % rare_count + 1, 0).astype(F32)
    hits = iota((owners, span), 0) == owner
    before = one_hot(iota((span, span), 0) < iota((span, span), 1))
    earlier = dot(one_hot(hits), before)
    position = jnp.sum(jnp.where(hits, earlier, 0.0), axis=0, keepdims=True).astype(jnp.int32)
    places = jnp.where(
        is_rare, owner * SLOTS + position, jnp.where(ids >= 0, ids + HOT_CODE, -1)
    )
    row[...] = jnp.broadcast_to(places, row.shape)
    column[...] = jnp.transpose(jnp.broadcast_to(places.astype(F32), (128, span))).astype(jnp.int32)
    order = jnp.where(hits, earlier, -1.0)
    lanes = iota(request_ref.shape, 1)
    request = jnp.zeros(request_ref.shape, F32)
    for slot in range(HOT_SLOT):
        wanted = jnp.sum(jnp.where(order == float(slot), value, 0.0), axis=1, keepdims=True)
        request = jnp.where(lanes == slot, wanted, request)
    request_ref[...] = request.astype(jnp.int32)
    loads[2].wait()
    known_ref[...] = table[...].astype(BF)


def serve_kernel(
    asked_ref,
    known_ref,
    row_ref,
    column_ref,
    hot_hbm,
    served,
    hot_ref,
    item_column_ref,
    asked_row_hbm,
    row_hbm,
    column_hbm,
    hot,
    row,
    sems,
):
    copies = copies_of([(hot_hbm, hot), (row_ref, row_hbm), (column_ref, column_hbm)], sems)
    span = column_ref.shape[0] - 128
    item_column_ref[...] = column_ref[span : span + PAD, :]
    slots = served.shape[0]
    sources = asked_ref.shape[0]
    asked = asked_ref[...]
    high = (asked // 2).astype(F32).astype(BF)
    low = (asked % 2).astype(F32).astype(BF)
    expand = one_hot(iota((slots, sources), 0) // SLOTS == iota((slots, sources), 1))
    wide = 2.0 * dot(expand, high) + dot(expand, low)
    mine = iota(wide.shape, 1) == iota(wide.shape, 0) % SLOTS
    index = jnp.sum(jnp.where(mine, wide, 0.0), axis=1, keepdims=True) - 1.0
    index = jnp.broadcast_to(index, wide.shape)
    row[...] = jnp.transpose(index)[0:8].astype(jnp.int32)
    save = pltpu.make_async_copy(row, asked_row_hbm, sems.at[3])
    save.start()
    index = index.astype(jnp.int32)
    lanes = iota(index.shape, 1)
    rows = known_ref.shape[0]
    picks = jnp.concatenate(
        [one_hot(index == lanes + 128 * j) for j in range(rows // 128)], axis=1
    )
    served[...] = dot(picks, known_ref[...]).astype(BF)
    copies[0].wait()
    hot_ref[...] = hot[...].astype(BF)
    for copy in copies[1:] + [save]:
        copy.wait()


def head_mask(heads, width):
    return iota((heads, width), 1) // HEAD_DIM == iota((heads, width), 0)


def spread_heads(values, mask, users):
    return jnp.concatenate(
        [jnp.where(mask, values[u : u + 1], 0.0) for u in range(users)], axis=0
    ).astype(BF)


def join_heads(full, mask, users):
    heads = mask.shape[0]
    parts = [
        jnp.sum(
            jnp.where(mask, full[u * heads : (u + 1) * heads], 0.0), axis=0, keepdims=True
        )
        for u in range(users)
    ]
    return jnp.concatenate(parts + [jnp.zeros((PAD - users, full.shape[1]), F32)], axis=0)


def look_up(column, fetched, hot):
    lanes = iota(column.shape, 1)
    slots = fetched.shape[0]
    picks = jnp.concatenate(
        [one_hot(column == lanes + 128 * j) for j in range(slots // 128)], axis=1
    )
    hot_picks = one_hot(column == lanes + HOT_CODE)
    return (dot(picks, fetched[...]) + dot(hot_picks, hot[...].astype(BF))).astype(BF)


def item_forward_kernel(
    users,
    fetched_ref,
    hot_ref,
    column_ref,
    item_w2,
    item_w1_hbm,
    gain_hbm,
    vectors_ref,
    inner_ref,
    outer_ref,
    item_w1,
    gain,
    sems,
):
    loads = copies_of([(item_w1_hbm, item_w1), (gain_hbm, gain)], sems)
    rows = look_up(column_ref[...], fetched_ref, hot_ref)
    loads[0].wait()
    inner = dot(rows, item_w1[...])
    inner_ref[...] = inner
    gated = (inner * jax.nn.sigmoid(inner)).astype(BF)
    loads[1].wait()
    outer = dot(gated, item_w2[...])
    outer_ref[...] = outer
    scale = lax.rsqrt(jnp.mean(outer * outer, axis=-1, keepdims=True) + EPS)
    vectors = jnp.where(iota(outer.shape, 0) < users, outer * scale * gain[...], 0.0)
    peers = vectors_ref.shape[0] // 8
    vectors_ref[...] = jnp.concatenate([vectors[0:8]] * peers, axis=0).astype(BF)


def user_forward_kernel(users, *refs):
    fetched_ref, item_kept, sources, refs = refs[0], refs[1:3], refs[3:13], refs[13:]
    vectors_ref, kept_hbm, item_kept_hbm, refs = refs[0], refs[1:6], refs[6:8], refs[8:]
    targets, kept, (in_sems, out_sems) = refs[:10], refs[10:15], refs[15:]
    column_of, hot, pos_of, norm_gain_ref, out_gain_ref = targets[:5]
    in_proj, w_query, w_key, w_value, w_out = targets[5:]
    hidden_ref, normed_ref, qk_ref, weights_ref, mixed_ref = kept
    copies = copies_of(zip(sources, targets), in_sems)
    saves = [
        pltpu.make_async_copy(a, b, out_sems.at[i])
        for i, (a, b) in enumerate(zip(kept + item_kept, kept_hbm + item_kept_hbm))
    ]
    saves[5].start()
    saves[6].start()
    hist, width = pos_of.shape
    heads = width // HEAD_DIM
    span = users * hist
    copies[0].wait()
    copies[1].wait()
    rows = look_up(column_of[0:span, :], fetched_ref, hot)
    for copy in copies[2:6]:
        copy.wait()
    pos = pos_of[...].astype(F32)
    hidden = dot(rows, in_proj[...]) + jnp.concatenate([pos] * users, axis=0)
    hidden_ref[...] = hidden
    saves[0].start()
    scale = lax.rsqrt(jnp.mean(hidden * hidden, axis=-1, keepdims=True) + EPS)
    normed = (hidden * scale * norm_gain_ref[...]).astype(BF)
    normed_ref[...] = normed
    saves[1].start()
    last = jnp.concatenate(
        [normed[(u + 1) * hist - PAD : (u + 1) * hist].astype(F32)[PAD - 1 :] for u in range(users)]
        + [jnp.zeros((PAD - users, width), F32)],
        axis=0,
    ).astype(BF)
    mask = head_mask(heads, width)
    copies[6].wait()
    query = dot(last, w_query[...]).astype(BF).astype(F32)
    copies[7].wait()
    qk = dot_nt(spread_heads(query, mask, users), w_key[...]).astype(BF)
    qk_ref[...] = qk
    saves[2].start()
    shape = (users * heads, span)
    own = iota(shape, 0) // heads == iota(shape, 1) // hist
    scores = jnp.where(own, dot_nt(qk, normed) * (1.0 / math.sqrt(HEAD_DIM)), -jnp.inf)
    raised = jnp.exp(scores - jnp.max(scores, axis=1, keepdims=True))
    weights = raised / jnp.sum(raised, axis=1, keepdims=True)
    weights_ref[...] = weights
    saves[3].start()
    mixes = dot(weights.astype(BF), normed).astype(BF)
    copies[8].wait()
    attended = join_heads(dot(mixes, w_value[...]), mask, users).astype(BF)
    copies[9].wait()
    hidden_last = jnp.concatenate(
        [hidden[(u + 1) * hist - 1 : (u + 1) * hist] for u in range(users)]
        + [jnp.zeros((PAD - users, width), F32)],
        axis=0,
    )
    mixed = hidden_last + dot(attended, w_out[...])
    mixed_ref[...] = mixed
    saves[4].start()
    scale = lax.rsqrt(jnp.mean(mixed * mixed, axis=-1, keepdims=True) + EPS)
    vectors_ref[...] = (mixed * scale * out_gain_ref[...]).astype(BF)
    for save in saves:
        save.wait()


def arrange_kernel(users, near, near_ref, vectors_ref, spread_ref):
    width = near_ref.shape[1]
    block = near * users
    part = spread_ref.shape[1] - width
    shape = (block, near * 8)
    at = iota(shape, 0)
    source = at // users * 8 + at % users
    items = dot(one_hot(iota(shape, 1) == source), near_ref[...])
    shape = (block, PAD)
    at = iota(shape, 0)
    mine = jnp.zeros((block, part), F32)
    for c in range(near):
        picks = one_hot((at % near == c) & (iota(shape, 1) == at // near))
        mine = mine + dot(picks, vectors_ref[:, c * part : (c + 1) * part])
    rows = jnp.concatenate([items, mine], axis=1).astype(BF)
    for i in range(spread_ref.shape[0] // block):
        spread_ref[i * block : (i + 1) * block, :] = rows


def softmax_kernel(
    users, near, scale, place_ref, gathered_ref, swapped_ref, d_user_ref, d_part_ref, raised_ref
):
    rows = gathered_ref.shape[0]
    width = d_user_ref.shape[1]
    items = near * users
    group = rows // near
    mine, plane = place_ref[0], place_ref[1]
    own, other = gathered_ref[:, 0:width], swapped_ref[:, 0:width]
    shape = (rows, rows)
    line = iota(shape, 0)
    picks = one_hot(iota(shape, 1) == line % group * near + line // group)

    def users_of(ref):
        parts = dot(picks, ref[:, width:])
        return jnp.concatenate([parts[c * group : (c + 1) * group] for c in range(near)], axis=1)

    group_users = jnp.concatenate([users_of(gathered_ref), users_of(swapped_ref)], axis=0).astype(BF)
    total = 2 * group

    shape = (rows, total)
    first = scale * dot_nt(own, group_users)
    second = scale * dot_nt(other, group_users)
    top = jnp.maximum(
        jnp.max(first, axis=0, keepdims=True), jnp.max(second, axis=0, keepdims=True)
    )
    raised = jnp.exp(first - top)
    raised_ref[...] = raised
    other_raised = jnp.exp(second - top)
    count = jnp.sum(raised, axis=0, keepdims=True) + jnp.sum(other_raised, axis=0, keepdims=True)
    share = 1.0 / count

    line = (items, total)
    target = (iota(line, 0) // users == plane) & (
        iota(line, 1) == mine * users + iota(line, 0) % users
    )
    near_raised = raised_ref[pl.ds(pl.multiple_of(mine * items, 8), items), :]
    slope = (near_raised * share - jnp.where(target, 1.0, 0.0)).astype(BF)
    apart = (near * 8, items)
    at = iota(apart, 0)
    apart = one_hot((at % 8 < users) & (iota(apart, 1) == at // 8 * users + at % 8))
    d_part = scale * dot(dot(apart, slope).astype(BF), group_users)

    who = iota(shape, 1) - mine * users
    target = (who >= 0) & (who < users) & (iota(shape, 0) == mine * items + plane * users + who)
    slope = (raised * share - jnp.where(target, 1.0, 0.0)).astype(BF)
    other_slope = (other_raised * share).astype(BF)
    self = (PAD, total)
    self = one_hot((iota(self, 0) < users) & (iota(self, 1) == mine * users + iota(self, 0)))
    d_user = dot(dot_nt(self, slope).astype(BF), own)
    d_user = d_user + dot(dot_nt(self, other_slope).astype(BF), other)
    d_user_ref[...] = (scale * d_user).astype(BF).astype(F32)
    each = jnp.sum(jnp.where(target, top + jnp.log(count) - first, 0.0), axis=0, keepdims=True)
    loss = jnp.sum(each, axis=1, keepdims=True)
    high = loss.astype(BF).astype(F32)
    middle = (loss - high).astype(BF).astype(F32)
    low = loss - high - middle
    shape = d_part.shape
    lanes = iota(shape, 1)
    loss = jnp.where(lanes == 0, high, jnp.where(lanes == 1, middle, jnp.where(lanes == 2, low, 0.0)))
    d_part_ref[...] = jnp.where(iota(shape, 0) % 8 == users, loss, d_part).astype(BF)


def norm_backward(values, cotangent, gain):
    inverse = lax.rsqrt(jnp.mean(values * values, axis=-1, keepdims=True) + EPS)
    pulled = cotangent * gain
    along = jnp.mean(pulled * values, axis=-1, keepdims=True)
    return inverse * pulled - values * (inverse * inverse * inverse * along)


def user_backward_kernel(users, d_user_ref, *refs):
    sources, refs = refs[:18], refs[18:]
    d_rows_ref, ahead, refs = refs[0], refs[1:7], refs[7:]
    targets, (d_normed, sems) = refs[:12], refs[12:]
    mixed_ref, out_gain_ref, w_out, w_value, normed_ref, weights_ref, qk_ref = targets[:7]
    w_key, w_query, hidden_ref, norm_gain_ref, in_proj = targets[7:]
    copies = copies_of(zip(sources, tuple(targets) + tuple(ahead)), sems)
    span, width = hidden_ref.shape
    hist = span // users
    heads = width // HEAD_DIM
    mask = head_mask(heads, width)
    for copy in copies[:3]:
        copy.wait()
    d_mixed = norm_backward(mixed_ref[...], d_user_ref[...], out_gain_ref[...])
    d_attended = dot_nt(d_mixed.astype(BF), w_out[...])
    copies[3].wait()
    d_mixes = dot_nt(spread_heads(d_attended, mask, users), w_value[...]).astype(BF)
    for copy in copies[4:7]:
        copy.wait()
    normed = normed_ref[...]
    weights = weights_ref[...]
    shape = weights.shape
    own = iota(shape, 0) // heads == iota(shape, 1) // hist
    d_weights = jnp.where(own, dot_nt(d_mixes, normed), 0.0)
    d_scores = weights * (d_weights - jnp.sum(weights * d_weights, axis=1, keepdims=True))
    d_scores = (d_scores * (1.0 / math.sqrt(HEAD_DIM))).astype(BF)
    d_normed[...] = dot_tn(
        jnp.concatenate([weights.astype(BF), d_scores], axis=0),
        jnp.concatenate([d_mixes, qk_ref[...]], axis=0),
    )
    d_qk = dot(d_scores, normed).astype(BF)
    copies[7].wait()
    d_query = join_heads(dot(d_qk, w_key[...]), mask, users).astype(BF)
    copies[8].wait()
    d_last = dot_nt(d_query, w_query[...])
    for u in range(users):
        at = slice((u + 1) * hist - 1, (u + 1) * hist)
        d_normed[at, :] = d_normed[at, :] + d_last[u : u + 1]
    copies[9].wait()
    copies[10].wait()
    d_normed[...] = norm_backward(hidden_ref[...], d_normed[...], norm_gain_ref[...])
    for u in range(users):
        at = slice((u + 1) * hist - 1, (u + 1) * hist)
        d_normed[at, :] = d_normed[at, :] + d_mixed[u : u + 1]
    copies[11].wait()
    d_rows_ref[...] = dot_nt(d_normed[...].astype(BF), in_proj[...]).astype(BF)
    for copy in copies[12:]:
        copy.wait()


def item_backward_kernel(users, core_ref, parts_ref, d_rows_ref, *refs):
    row_ref, gain, inner_ref, item_w2, item_w1, outer_ref, refs = *refs[:6], refs[6:]
    d_all_ref, send_ref, keep_ref, loss_ref = refs
    span, emb = d_rows_ref.shape
    wide = row_ref.shape[1]
    peers = parts_ref.shape[0]
    shape = (PAD, peers)
    sums = dot(one_hot(iota(shape, 1) % 8 == iota(shape, 0)), parts_ref[...])
    shape = (1, 128)
    loss = jnp.where(iota(shape, 1) < 3, sums[users : users + 1, 0:128], 0.0)
    loss_ref[...] = jnp.broadcast_to(jnp.sum(loss, axis=1, keepdims=True), loss_ref.shape)
    d_item = jnp.where(iota(sums.shape, 0) < users, sums, 0.0).astype(BF).astype(F32)
    d_all_ref[0:span, :] = d_rows_ref[...]
    half = keep_ref.shape[0]
    first = HOT_CODE + core_ref[0] * half
    picks = one_hot(iota((half, wide), 0) + first == row_ref[0:1, :])
    keep = dot(picks[:, 0:span], d_rows_ref[...])
    first = HOT_CODE + (1 - core_ref[0]) * half
    other_picks = one_hot(iota((half, wide), 0) + first == row_ref[0:1, :])
    send = dot(other_picks[:, 0:span], d_rows_ref[...])
    d_outer = norm_backward(outer_ref[...], d_item, gain[...])
    inner = inner_ref[...]
    gate = jax.nn.sigmoid(inner)
    d_inner = dot_nt(d_outer.astype(BF), item_w2[...]) * (gate * (1.0 + inner * (1.0 - gate)))
    d_items = dot_nt(d_inner.astype(BF), item_w1[...])
    d_items = jnp.concatenate([d_items, jnp.zeros((wide - span - PAD, emb), F32)], axis=0).astype(BF)
    d_all_ref[span:, :] = d_items
    keep_ref[...] = keep + dot(picks[:, span:], d_items)
    send_ref[...] = send + dot(other_picks[:, span:], d_items)


def rare_kernel(d_all_ref, row_ref, rare_ref):
    shape = (rare_ref.shape[0], row_ref.shape[1])
    rare_ref[...] = dot(one_hot(iota(shape, 0) == row_ref[0:1, :]), d_all_ref[...]).astype(BF)


def outgoing_kernel(rare_ref, keep_ref, got_ref, outgoing_ref):
    half = keep_ref.shape[0]
    slots = rare_ref.shape[0]
    shape = (slots, half)
    line = iota(shape, 0)
    owner, slot = line // SLOTS, line % SLOTS - HOT_SLOT
    held = owner // 8 * 2 + owner % 2 + slot * (half // 2)
    held = one_hot((slot >= 0) & (slot < 2) & (iota(shape, 1) == held))
    hot = dot(held, (keep_ref[...] + got_ref[...]).astype(BF))
    outgoing_ref[...] = (rare_ref[...].astype(F32) + hot).astype(BF)


def scatter_kernel(returned_ref, row_ref, loss_ref, part_ref, sums_ref):
    rows, emb = part_ref.shape
    slots = returned_ref.shape[0]
    returned = returned_ref[...]
    picks = one_hot(iota((rows, slots), 0) == row_ref[0:1, :])
    part_ref[...] = dot(picks, returned).astype(BF)
    shape = (PAD, slots)
    hot = dot(one_hot((iota(shape, 0) < 2) & (iota(shape, 1) % SLOTS == iota(shape, 0) + HOT_SLOT)), returned)
    halves = [hot[i : i + 1, j : j + 128] for i in range(2) for j in range(0, emb, 128)]
    block = jnp.concatenate(halves + [loss_ref[0 : 8 - len(halves), :]], axis=0)
    sums_ref[...] = jnp.concatenate([block] * (sums_ref.shape[0] // 8), axis=0)


def finish_kernel(count, core_ref, sums_ref, other_ref, hot_ref, loss_ref):
    rows, emb = hot_ref.shape
    groups = sums_ref.shape[0] // 8
    for core, ref in ((core_ref[0], sums_ref), (1 - core_ref[0], other_ref)):
        row = 0
        for i in range(2):
            at = pl.ds(pl.multiple_of(core * (rows // 2) + i * groups, groups), groups)
            for j in range(0, emb, 128):
                hot_ref[at, j : j + 128] = ref[pl.ds(row, groups, stride=8), :]
                row += 1
    at = pl.ds(row, groups, stride=8)
    losses = sums_ref[at, :] + other_ref[at, :]
    loss_ref[...] = jnp.sum(losses[:, 0:1], axis=0, keepdims=True) / count


def shards(
    history,
    item_ids,
    hot_table,
    rare_table,
    in_proj,
    pos_embed,
    norm_gain,
    w_query,
    w_key,
    w_value,
    w_out,
    out_gain,
    item_w1,
    item_w2,
    item_gain,
):
    users, hist = history.shape
    emb = hot_table.shape[1]
    rare_count = rare_table.shape[0]
    width = in_proj.shape[1]
    heads = width // HEAD_DIM
    scale = 4.0 / math.sqrt(width)
    owners = lax.axis_size(SHARD)
    towers = lax.axis_size("tower")
    near = lax.axis_size(LINE)
    total = users * towers * owners
    slots = owners * SLOTS
    span = users * hist
    wide = -(-(span + PAD) // 128) * 128
    swap = [(i, towers - 1 - i) for i in range(towers)]
    shape = jax.ShapeDtypeStruct
    sems = lambda n: pltpu.SemaphoreType.DMA((n,))
    vmem = lambda a: pltpu.VMEM(a.shape, a.dtype)
    hbm = lambda a: pltpu.HBM(a.shape, a.dtype)
    in_hbm = lambda a: pltpu.with_memory_space_constraint(a, pltpu.HBM)
    in_vmem = lambda a: pltpu.with_memory_space_constraint(a, pltpu.VMEM)
    like = lambda arrays: [pltpu.VMEM(a.shape, a.dtype) for a in arrays]
    exchange = functools.partial(lax.all_to_all, split_axis=0, concat_axis=0, tiled=True)

    places = (shape((8, wide), jnp.int32), shape((wide, 128), jnp.int32))
    loads = (history, item_ids.reshape(1, users), rare_table)
    request, known, row, column = pl.pallas_call(
        functools.partial(index_kernel, owners),
        out_shape=(
            shape((owners, 128), jnp.int32),
            pltpu.VMEM((rare_count, emb), BF),
            *map(vmem, places),
        ),
        in_specs=[HBM] * 3,
        out_specs=(VMEM,) * 4,
        scratch_shapes=like(loads) + [sems(3)],
        compiler_params=params(24),
        name="index",
    )(*map(in_hbm, loads))
    asked = exchange(request, SHARD)
    served, hot_ready, item_column, asked_row, row, column = pl.pallas_call(
        serve_kernel,
        out_shape=(
            shape((slots, emb), BF),
            pltpu.VMEM(hot_table.shape, BF),
            pltpu.VMEM((PAD, 128), jnp.int32),
            pltpu.HBM((8, slots), jnp.int32),
            *map(hbm, places),
        ),
        in_specs=[VMEM] * 4 + [HBM],
        out_specs=(VMEM, VMEM, VMEM, HBM, HBM, HBM),
        scratch_shapes=[
            pltpu.VMEM(hot_table.shape, F32),
            pltpu.VMEM((8, slots), jnp.int32),
            sems(4),
        ],
        compiler_params=params(24),
        name="serve",
    )(asked, *map(in_vmem, (known, row, column)), in_hbm(hot_table))
    fetched = exchange(served, SHARD)

    norm_gain, out_gain, item_gain = (g.reshape(1, width) for g in (norm_gain, out_gain, item_gain))
    item_kept = (shape((PAD, width), F32), shape((PAD, width), F32))
    item_vec, inner, outer = pl.pallas_call(
        functools.partial(item_forward_kernel, users),
        out_shape=(shape((near * 8, width), BF), *map(vmem, item_kept)),
        in_specs=[VMEM] * 4 + [HBM] * 2,
        out_specs=(VMEM,) * 3,
        scratch_shapes=like((item_w1, item_gain)) + [sems(2)],
        compiler_params=params(24),
        name="item_forward",
    )(
        fetched,
        *map(in_vmem, (hot_ready, item_column, item_w2)),
        *map(in_hbm, (item_w1, item_gain)),
    )
    near_items = exchange(item_vec, LINE)

    loads = (column, hot_table, pos_embed, norm_gain, out_gain)
    loads += (in_proj, w_query, w_key, w_value, w_out)
    kept = (
        shape((span, width), F32),
        shape((span, width), BF),
        shape((users * heads, width), BF),
        shape((users * heads, span), F32),
        shape((PAD, width), F32),
    )
    user_vec, hidden, normed, qk, weights, mixed, inner, outer = pl.pallas_call(
        functools.partial(user_forward_kernel, users),
        out_shape=(shape((PAD, width), BF), *map(hbm, kept + item_kept)),
        in_specs=[VMEM] * 3 + [HBM] * len(loads),
        out_specs=(VMEM,) + (HBM,) * (len(kept) + 2),
        scratch_shapes=like(loads + kept) + [sems(len(loads)), sems(len(kept) + 2)],
        compiler_params=params(40),
        name="user_forward",
    )(fetched, in_vmem(inner), in_vmem(outer), *map(in_hbm, loads))

    rows = owners * users
    spread = pl.pallas_call(
        functools.partial(arrange_kernel, users, near),
        out_shape=shape((rows, width + width // near), BF),
        in_specs=[VMEM, VMEM],
        out_specs=VMEM,
        compiler_params=params(24),
        name="arrange",
    )(near_items, user_vec)
    gathered = exchange(spread, ("x", "y"))
    swapped = lax.ppermute(gathered, "tower", swap)
    place = jnp.stack([lax.axis_index(("x", "y")), lax.axis_index(LINE)]).astype(jnp.int32)
    d_user, d_part = pl.pallas_call(
        functools.partial(softmax_kernel, users, near, scale),
        out_shape=(shape((PAD, width), F32), shape((near * 8, width), BF)),
        in_specs=[SMEM, VMEM, VMEM],
        out_specs=(VMEM, VMEM),
        scratch_shapes=[pltpu.VMEM((rows, 2 * owners // near * users), F32)],
        compiler_params=params(32),
        name="softmax",
    )(place, gathered, swapped)
    parts = exchange(d_part, LINE)

    loads = (mixed, out_gain, w_out, w_value, normed, weights, qk)
    loads += (w_key, w_query, hidden, norm_gain, in_proj)
    ahead = (row, item_gain, inner, item_w2, item_w1, outer)
    d_rows, *item_ready = pl.pallas_call(
        functools.partial(user_backward_kernel, users),
        out_shape=(shape((span, emb), BF), *map(vmem, ahead)),
        in_specs=[VMEM] + [HBM] * 18,
        out_specs=(VMEM,) * 7,
        scratch_shapes=like(loads) + [pltpu.VMEM((span, width), F32), sems(18)],
        compiler_params=params(40),
        name="user_backward",
    )(d_user, *map(in_hbm, loads + ahead))
    core = lax.axis_index("tower").astype(jnp.int32).reshape(1)
    row_ready = item_ready[0]
    d_all, send, keep, loss = pl.pallas_call(
        functools.partial(item_backward_kernel, users),
        out_shape=(
            shape((wide, emb), BF),
            shape((owners // 2, emb), F32),
            shape((owners // 2, emb), F32),
            shape((8, 128), F32),
        ),
        in_specs=[SMEM] + [VMEM] * 8,
        out_specs=(VMEM,) * 4,
        compiler_params=params(32),
        name="item_backward",
    )(core, parts, d_rows, *map(in_vmem, item_ready))
    got = lax.ppermute(send, "tower", swap)
    rare = pl.pallas_call(
        rare_kernel,
        out_shape=shape((slots, emb), BF),
        in_specs=[VMEM, VMEM],
        out_specs=VMEM,
        compiler_params=params(32),
        name="rare",
    )(d_all, in_vmem(row_ready))
    outgoing = pl.pallas_call(
        outgoing_kernel,
        out_shape=shape((slots, emb), BF),
        in_specs=[VMEM] * 3,
        out_specs=VMEM,
        compiler_params=params(32),
        name="outgoing",
    )(rare, keep, got)

    returned = exchange(outgoing, SHARD)
    part, mine = pl.pallas_call(
        scatter_kernel,
        out_shape=(shape((rare_count, emb), BF), shape((owners // 4 * 8, 128), F32)),
        in_specs=[VMEM, VMEM, VMEM],
        out_specs=(VMEM, VMEM),
        compiler_params=params(24),
        name="scatter",
    )(returned, asked_row, loss)
    rare_grad = part.astype(F32) + lax.ppermute(part, "tower", swap).astype(F32)
    sums = exchange(mine, GROUP)
    other_sums = lax.ppermute(sums, "tower", swap)
    hot_total, loss_total = pl.pallas_call(
        functools.partial(finish_kernel, total * 2),
        out_shape=(shape((owners, emb), F32), shape((1, 1), F32)),
        in_specs=[SMEM, VMEM, VMEM],
        out_specs=(VMEM, VMEM),
        compiler_params=params(24),
        name="finish",
    )(core, sums, other_sums)
    return (hot_total, rare_grad, loss_total[0, 0])


def solution(mesh):
    sizes = (mesh.shape["tower"], 4, 4, mesh.shape["shard"] // 32, 2)
    mesh = Mesh(mesh.devices.reshape(sizes), ("tower",) + SHARD)
    return jax.shard_map(
        shards,
        mesh=mesh,
        in_specs=(
            P(("tower",) + SHARD, None),
            P(("tower",) + SHARD),
            P(),
            P(SHARD, None),
            P(),
            P(),
            P(),
            P(),
            P(),
            P(),
            P(),
            P(),
            P(),
            P(),
            P(),
        ),
        out_specs=(P(), P(SHARD, None), P()),
        check_vma=False,
    )
```

```python
import functools
import math

import jax
import jax.numpy as jnp
from jax import lax
from jax.experimental import pallas as pl
from jax.experimental.pallas import tpu as pltpu
from jax.sharding import Mesh
from jax.sharding import PartitionSpec as P

HEAD_DIM = 64
EPS = 1e-06
SLOTS = 8
HOT_SLOT = 5
HOT_CODE = 4096
LINE = ("zh", "zl")
SHARD = ("x", "y") + LINE
GROUP = ("x", "y", "zl")
PAD = 16
BF = jnp.bfloat16
F32 = jnp.float32
VMEM = pl.BlockSpec(memory_space=pltpu.VMEM)
SMEM = pl.BlockSpec(memory_space=pltpu.SMEM)
HBM = pl.BlockSpec(memory_space=pltpu.HBM)
NT = (((1,), (1,)), ((), ()))
TN = (((0,), (0,)), ((), ()))


def dot(a, b):
    return jnp.dot(a, b, preferred_element_type=F32)


def dot_nt(a, b):
    return lax.dot_general(a, b, NT, preferred_element_type=F32)


def dot_tn(a, b):
    return lax.dot_general(a, b, TN, preferred_element_type=F32)


def iota(shape, axis):
    return lax.broadcasted_iota(jnp.int32, shape, axis)


def one_hot(mask):
    return jnp.where(mask, 1.0, 0.0).astype(BF)


def params(mib):
    return pltpu.CompilerParams(vmem_limit_bytes=mib * 1024 * 1024)


def copies_of(pairs, sems):
    copies = [pltpu.make_async_copy(a, b, sems.at[i]) for i, (a, b) in enumerate(pairs)]
    for copy in copies:
        copy.start()
    return copies


def index_kernel(
    owners,
    history_hbm,
    items_hbm,
    table_hbm,
    request_ref,
    known_ref,
    row,
    column,
    history_ref,
    items_ref,
    table,
    sems,
):
    loads = copies_of(
        [(history_hbm, history_ref), (items_hbm, items_ref), (table_hbm, table)], sems
    )
    loads[0].wait()
    loads[1].wait()
    hot_count = owners
    rare_count = table.shape[0]
    users = history_ref.shape[0]
    span = row.shape[1]
    parts = [history_ref[u : u + 1, :] for u in range(users)] + [items_ref[...]]
    filled = sum(p.shape[1] for p in parts)
    ids = jnp.concatenate(parts + [jnp.full((1, span - filled), -1, jnp.int32)], axis=1)
    is_rare = ids >= hot_count
    index = ids - hot_count
    owner = jnp.where(is_rare, index // rare_count, -1)
    value = jnp.where(is_rare, index % rare_count + 1, 0).astype(F32)
    hits = iota((owners, span), 0) == owner
    before = one_hot(iota((span, span), 0) < iota((span, span), 1))
    earlier = dot(one_hot(hits), before)
    position = jnp.sum(jnp.where(hits, earlier, 0.0), axis=0, keepdims=True).astype(jnp.int32)
    places = jnp.where(
        is_rare, owner * SLOTS + position, jnp.where(ids >= 0, ids + HOT_CODE, -1)
    )
    row[...] = jnp.broadcast_to(places, row.shape)
    column[...] = jnp.transpose(jnp.broadcast_to(places.astype(F32), (128, span))).astype(jnp.int32)
    order = jnp.where(hits, earlier, -1.0)
    lanes = iota(request_ref.shape, 1)
    request = jnp.zeros(request_ref.shape, F32)
    for slot in range(HOT_SLOT):
        wanted = jnp.sum(jnp.where(order == float(slot), value, 0.0), axis=1, keepdims=True)
        request = jnp.where(lanes == slot, wanted, request)
    request_ref[...] = request.astype(jnp.int32)
    loads[2].wait()
    known_ref[...] = table[...].astype(BF)


def serve_kernel(
    asked_ref,
    known_ref,
    row_ref,
    column_ref,
    hot_hbm,
    served,
    hot_ref,
    item_column_ref,
    asked_row_hbm,
    row_hbm,
    column_hbm,
    hot,
    row,
    sems,
):
    copies = copies_of([(hot_hbm, hot), (row_ref, row_hbm), (column_ref, column_hbm)], sems)
    span = column_ref.shape[0] - 128
    item_column_ref[...] = column_ref[span : span + PAD, :]
    slots = served.shape[0]
    sources = asked_ref.shape[0]
    asked = asked_ref[...]
    high = (asked // 2).astype(F32).astype(BF)
    low = (asked % 2).astype(F32).astype(BF)
    expand = one_hot(iota((slots, sources), 0) // SLOTS == iota((slots, sources), 1))
    wide = 2.0 * dot(expand, high) + dot(expand, low)
    mine = iota(wide.shape, 1) == iota(wide.shape, 0) % SLOTS
    index = jnp.sum(jnp.where(mine, wide, 0.0), axis=1, keepdims=True) - 1.0
    index = jnp.broadcast_to(index, wide.shape)
    row[...] = jnp.transpose(index)[0:8].astype(jnp.int32)
    save = pltpu.make_async_copy(row, asked_row_hbm, sems.at[3])
    save.start()
    index = index.astype(jnp.int32)
    lanes = iota(index.shape, 1)
    rows = known_ref.shape[0]
    picks = jnp.concatenate(
        [one_hot(index == lanes + 128 * j) for j in range(rows // 128)], axis=1
    )
    served[...] = dot(picks, known_ref[...]).astype(BF)
    copies[0].wait()
    hot_ref[...] = hot[...].astype(BF)
    for copy in copies[1:] + [save]:
        copy.wait()


def head_mask(heads, width):
    return iota((heads, width), 1) // HEAD_DIM == iota((heads, width), 0)


def spread_heads(values, mask, users):
    return jnp.concatenate(
        [jnp.where(mask, values[u : u + 1], 0.0) for u in range(users)], axis=0
    ).astype(BF)


def join_heads(full, mask, users):
    heads = mask.shape[0]
    parts = [
        jnp.sum(
            jnp.where(mask, full[u * heads : (u + 1) * heads], 0.0), axis=0, keepdims=True
        )
        for u in range(users)
    ]
    return jnp.concatenate(parts + [jnp.zeros((PAD - users, full.shape[1]), F32)], axis=0)


def look_up(column, fetched, hot):
    lanes = iota(column.shape, 1)
    slots = fetched.shape[0]
    picks = jnp.concatenate(
        [one_hot(column == lanes + 128 * j) for j in range(slots // 128)], axis=1
    )
    hot_picks = one_hot(column == lanes + HOT_CODE)
    return (dot(picks, fetched[...]) + dot(hot_picks, hot[...].astype(BF))).astype(BF)


def item_forward_kernel(
    users,
    fetched_ref,
    hot_ref,
    column_ref,
    item_w2,
    item_w1_hbm,
    gain_hbm,
    vectors_ref,
    inner_ref,
    outer_ref,
    item_w1,
    gain,
    sems,
):
    loads = copies_of([(item_w1_hbm, item_w1), (gain_hbm, gain)], sems)
    rows = look_up(column_ref[...], fetched_ref, hot_ref)
    loads[0].wait()
    inner = dot(rows, item_w1[...])
    inner_ref[...] = inner
    gated = (inner * jax.nn.sigmoid(inner)).astype(BF)
    loads[1].wait()
    outer = dot(gated, item_w2[...])
    outer_ref[...] = outer
    scale = lax.rsqrt(jnp.mean(outer * outer, axis=-1, keepdims=True) + EPS)
    vectors = jnp.where(iota(outer.shape, 0) < users, outer * scale * gain[...], 0.0)
    peers = vectors_ref.shape[0] // 8
    vectors_ref[...] = jnp.concatenate([vectors[0:8]] * peers, axis=0).astype(BF)


def user_forward_kernel(users, *refs):
    fetched_ref, item_kept, sources, refs = refs[0], refs[1:3], refs[3:13], refs[13:]
    vectors_ref, kept_hbm, item_kept_hbm, refs = refs[0], refs[1:6], refs[6:8], refs[8:]
    targets, kept, (in_sems, out_sems) = refs[:10], refs[10:15], refs[15:]
    column_of, hot, pos_of, norm_gain_ref, out_gain_ref = targets[:5]
    in_proj, w_query, w_key, w_value, w_out = targets[5:]
    hidden_ref, normed_ref, qk_ref, weights_ref, mixed_ref = kept
    copies = copies_of(zip(sources, targets), in_sems)
    saves = [
        pltpu.make_async_copy(a, b, out_sems.at[i])
        for i, (a, b) in enumerate(zip(kept + item_kept, kept_hbm + item_kept_hbm))
    ]
    saves[5].start()
    saves[6].start()
    hist, width = pos_of.shape
    heads = width // HEAD_DIM
    span = users * hist
    copies[0].wait()
    copies[1].wait()
    rows = look_up(column_of[0:span, :], fetched_ref, hot)
    for copy in copies[2:6]:
        copy.wait()
    pos = pos_of[...].astype(F32)
    hidden = dot(rows, in_proj[...]) + jnp.concatenate([pos] * users, axis=0)
    hidden_ref[...] = hidden
    saves[0].start()
    scale = lax.rsqrt(jnp.mean(hidden * hidden, axis=-1, keepdims=True) + EPS)
    normed = (hidden * scale * norm_gain_ref[...]).astype(BF)
    normed_ref[...] = normed
    saves[1].start()
    last = jnp.concatenate(
        [normed[(u + 1) * hist - PAD : (u + 1) * hist].astype(F32)[PAD - 1 :] for u in range(users)]
        + [jnp.zeros((PAD - users, width), F32)],
        axis=0,
    ).astype(BF)
    mask = head_mask(heads, width)
    copies[6].wait()
    query = dot(last, w_query[...]).astype(BF).astype(F32)
    copies[7].wait()
    qk = dot_nt(spread_heads(query, mask, users), w_key[...]).astype(BF)
    qk_ref[...] = qk
    saves[2].start()
    shape = (users * heads, span)
    own = iota(shape, 0) // heads == iota(shape, 1) // hist
    scores = jnp.where(own, dot_nt(qk, normed) * (1.0 / math.sqrt(HEAD_DIM)), -jnp.inf)
    raised = jnp.exp(scores - jnp.max(scores, axis=1, keepdims=True))
    weights = raised / jnp.sum(raised, axis=1, keepdims=True)
    weights_ref[...] = weights
    saves[3].start()
    mixes = dot(weights.astype(BF), normed).astype(BF)
    copies[8].wait()
    attended = join_heads(dot(mixes, w_value[...]), mask, users).astype(BF)
    copies[9].wait()
    hidden_last = jnp.concatenate(
        [hidden[(u + 1) * hist - 1 : (u + 1) * hist] for u in range(users)]
        + [jnp.zeros((PAD - users, width), F32)],
        axis=0,
    )
    mixed = hidden_last + dot(attended, w_out[...])
    mixed_ref[...] = mixed
    saves[4].start()
    scale = lax.rsqrt(jnp.mean(mixed * mixed, axis=-1, keepdims=True) + EPS)
    vectors_ref[...] = (mixed * scale * out_gain_ref[...]).astype(BF)
    for save in saves:
        save.wait()


def arrange_kernel(users, near, near_ref, vectors_ref, spread_ref):
    width = near_ref.shape[1]
    block = near * users
    part = spread_ref.shape[1] - width
    shape = (block, near * 8)
    at = iota(shape, 0)
    source = at // users * 8 + at % users
    items = dot(one_hot(iota(shape, 1) == source), near_ref[...])
    shape = (block, PAD)
    at = iota(shape, 0)
    mine = jnp.zeros((block, part), F32)
    for c in range(near):
        picks = one_hot((at % near == c) & (iota(shape, 1) == at // near))
        mine = mine + dot(picks, vectors_ref[:, c * part : (c + 1) * part])
    rows = jnp.concatenate([items, mine], axis=1).astype(BF)
    for i in range(spread_ref.shape[0] // block):
        spread_ref[i * block : (i + 1) * block, :] = rows


def softmax_kernel(
    users, near, scale, place_ref, gathered_ref, swapped_ref, d_user_ref, d_part_ref, raised_ref
):
    rows = gathered_ref.shape[0]
    width = d_user_ref.shape[1]
    items = near * users
    group = rows // near
    mine, plane = place_ref[0], place_ref[1]
    own, other = gathered_ref[:, 0:width], swapped_ref[:, 0:width]
    shape = (rows, rows)
    line = iota(shape, 0)
    picks = one_hot(iota(shape, 1) == line % group * near + line // group)

    def users_of(ref):
        parts = dot(picks, ref[:, width:])
        return jnp.concatenate([parts[c * group : (c + 1) * group] for c in range(near)], axis=1)

    group_users = jnp.concatenate([users_of(gathered_ref), users_of(swapped_ref)], axis=0).astype(BF)
    total = 2 * group

    shape = (rows, total)
    first = scale * dot_nt(own, group_users)
    second = scale * dot_nt(other, group_users)
    top = jnp.maximum(
        jnp.max(first, axis=0, keepdims=True), jnp.max(second, axis=0, keepdims=True)
    )
    raised = jnp.exp(first - top)
    raised_ref[...] = raised
    other_raised = jnp.exp(second - top)
    count = jnp.sum(raised, axis=0, keepdims=True) + jnp.sum(other_raised, axis=0, keepdims=True)
    share = 1.0 / count

    line = (items, total)
    target = (iota(line, 0) // users == plane) & (
        iota(line, 1) == mine * users + iota(line, 0) % users
    )
    near_raised = raised_ref[pl.ds(pl.multiple_of(mine * items, 8), items), :]
    slope = (near_raised * share - jnp.where(target, 1.0, 0.0)).astype(BF)
    apart = (near * 8, items)
    at = iota(apart, 0)
    apart = one_hot((at % 8 < users) & (iota(apart, 1) == at // 8 * users + at % 8))
    d_part = scale * dot(dot(apart, slope).astype(BF), group_users)

    who = iota(shape, 1) - mine * users
    target = (who >= 0) & (who < users) & (iota(shape, 0) == mine * items + plane * users + who)
    slope = (raised * share - jnp.where(target, 1.0, 0.0)).astype(BF)
    other_slope = (other_raised * share).astype(BF)
    self = (PAD, total)
    self = one_hot((iota(self, 0) < users) & (iota(self, 1) == mine * users + iota(self, 0)))
    d_user = dot(dot_nt(self, slope).astype(BF), own)
    d_user = d_user + dot(dot_nt(self, other_slope).astype(BF), other)
    d_user_ref[...] = (scale * d_user).astype(BF).astype(F32)
    each = jnp.sum(jnp.where(target, top + jnp.log(count) - first, 0.0), axis=0, keepdims=True)
    loss = jnp.sum(each, axis=1, keepdims=True)
    high = loss.astype(BF).astype(F32)
    middle = (loss - high).astype(BF).astype(F32)
    low = loss - high - middle
    shape = d_part.shape
    lanes = iota(shape, 1)
    loss = jnp.where(lanes == 0, high, jnp.where(lanes == 1, middle, jnp.where(lanes == 2, low, 0.0)))
    d_part_ref[...] = jnp.where(iota(shape, 0) % 8 == users, loss, d_part).astype(BF)


def norm_backward(values, cotangent, gain):
    inverse = lax.rsqrt(jnp.mean(values * values, axis=-1, keepdims=True) + EPS)
    pulled = cotangent * gain
    along = jnp.mean(pulled * values, axis=-1, keepdims=True)
    return inverse * pulled - values * (inverse * inverse * inverse * along)


def user_backward_kernel(users, d_user_ref, *refs):
    sources, refs = refs[:18], refs[18:]
    d_rows_ref, ahead, refs = refs[0], refs[1:7], refs[7:]
    targets, sems = refs[:12], refs[12]
    mixed_ref, out_gain_ref, w_out, w_value, normed_ref, weights_ref, qk_ref = targets[:7]
    hidden_ref, norm_gain_ref, in_proj, w_key, w_query = targets[7:]
    copies = copies_of(zip(sources, tuple(targets) + tuple(ahead)), sems)
    span, width = hidden_ref.shape
    hist = span // users
    heads = width // HEAD_DIM
    mask = head_mask(heads, width)
    for copy in copies[:3]:
        copy.wait()
    d_mixed = norm_backward(mixed_ref[...], d_user_ref[...], out_gain_ref[...])
    d_attended = dot_nt(d_mixed.astype(BF), w_out[...])
    copies[3].wait()
    d_mixes = dot_nt(spread_heads(d_attended, mask, users), w_value[...]).astype(BF)
    for copy in copies[4:7]:
        copy.wait()
    normed = normed_ref[...]
    weights = weights_ref[...]
    shape = weights.shape
    own = iota(shape, 0) // heads == iota(shape, 1) // hist
    d_weights = jnp.where(own, dot_nt(d_mixes, normed), 0.0)
    d_scores = weights * (d_weights - jnp.sum(weights * d_weights, axis=1, keepdims=True))
    d_scores = (d_scores * (1.0 / math.sqrt(HEAD_DIM))).astype(BF)
    d_normed = dot_tn(
        jnp.concatenate([weights.astype(BF), d_scores], axis=0),
        jnp.concatenate([d_mixes, qk_ref[...]], axis=0),
    )
    d_qk = dot(d_scores, normed).astype(BF)
    for copy in copies[7:11]:
        copy.wait()
    hidden, gain = hidden_ref[...], norm_gain_ref[...]
    d_rows = dot_nt(norm_backward(hidden, d_normed, gain).astype(BF), in_proj[...])
    d_query = join_heads(dot(d_qk, w_key[...]), mask, users).astype(BF)
    copies[11].wait()
    d_last = dot_nt(d_query, w_query[...])
    last = jnp.concatenate(
        [hidden[(u + 1) * hist - 1 : (u + 1) * hist] for u in range(users)]
        + [jnp.zeros((PAD - users, width), F32)],
        axis=0,
    )
    d_last = norm_backward(last, d_last, gain) + d_mixed
    d_last = dot_nt(d_last.astype(BF), in_proj[...]).astype(BF)
    shape = (span, PAD)
    at = iota(shape, 1)
    place = one_hot((at < users) & (iota(shape, 0) == (at + 1) * hist - 1))
    d_rows_ref[...] = (d_rows + dot(place, d_last)).astype(BF)
    for copy in copies[12:]:
        copy.wait()


def item_backward_kernel(users, core_ref, parts_ref, d_rows_ref, *refs):
    row_ref, gain, inner_ref, item_w2, item_w1, outer_ref, refs = *refs[:6], refs[6:]
    d_all_ref, send_ref, keep_ref, loss_ref = refs
    span, emb = d_rows_ref.shape
    wide = row_ref.shape[1]
    peers = parts_ref.shape[0]
    shape = (PAD, peers)
    sums = dot(one_hot(iota(shape, 1) % 8 == iota(shape, 0)), parts_ref[...])
    shape = (1, 128)
    loss = jnp.where(iota(shape, 1) < 3, sums[users : users + 1, 0:128], 0.0)
    loss_ref[...] = jnp.broadcast_to(jnp.sum(loss, axis=1, keepdims=True), loss_ref.shape)
    d_item = jnp.where(iota(sums.shape, 0) < users, sums, 0.0).astype(BF).astype(F32)
    d_all_ref[0:span, :] = d_rows_ref[...]
    half = keep_ref.shape[0]
    first = HOT_CODE + core_ref[0] * half
    picks = one_hot(iota((half, wide), 0) + first == row_ref[0:1, :])
    keep = dot(picks[:, 0:span], d_rows_ref[...])
    first = HOT_CODE + (1 - core_ref[0]) * half
    other_picks = one_hot(iota((half, wide), 0) + first == row_ref[0:1, :])
    send = dot(other_picks[:, 0:span], d_rows_ref[...])
    d_outer = norm_backward(outer_ref[...], d_item, gain[...])
    inner = inner_ref[...]
    gate = jax.nn.sigmoid(inner)
    d_inner = dot_nt(d_outer.astype(BF), item_w2[...]) * (gate * (1.0 + inner * (1.0 - gate)))
    d_items = dot_nt(d_inner.astype(BF), item_w1[...])
    d_items = jnp.concatenate([d_items, jnp.zeros((wide - span - PAD, emb), F32)], axis=0).astype(BF)
    d_all_ref[span:, :] = d_items
    keep_ref[...] = keep + dot(picks[:, span:], d_items)
    send_ref[...] = send + dot(other_picks[:, span:], d_items)


def rare_kernel(d_all_ref, row_ref, rare_ref):
    shape = (rare_ref.shape[0], row_ref.shape[1])
    rare_ref[...] = dot(one_hot(iota(shape, 0) == row_ref[0:1, :]), d_all_ref[...]).astype(BF)


def outgoing_kernel(rare_ref, keep_ref, got_ref, outgoing_ref):
    half = keep_ref.shape[0]
    slots = rare_ref.shape[0]
    shape = (slots, half)
    line = iota(shape, 0)
    owner, slot = line // SLOTS, line % SLOTS - HOT_SLOT
    held = owner // 8 * 2 + owner % 2 + slot * (half // 2)
    held = one_hot((slot >= 0) & (slot < 2) & (iota(shape, 1) == held))
    hot = dot(held, (keep_ref[...] + got_ref[...]).astype(BF))
    outgoing_ref[...] = (rare_ref[...].astype(F32) + hot).astype(BF)


def scatter_kernel(returned_ref, row_ref, loss_ref, part_ref, sums_ref):
    rows, emb = part_ref.shape
    slots = returned_ref.shape[0]
    returned = returned_ref[...]
    picks = one_hot(iota((rows, slots), 0) == row_ref[0:1, :])
    part_ref[...] = dot(picks, returned).astype(BF)
    shape = (PAD, slots)
    hot = dot(one_hot((iota(shape, 0) < 2) & (iota(shape, 1) % SLOTS == iota(shape, 0) + HOT_SLOT)), returned)
    halves = [hot[i : i + 1, j : j + 128] for i in range(2) for j in range(0, emb, 128)]
    block = jnp.concatenate(halves + [loss_ref[0 : 8 - len(halves), :]], axis=0)
    sums_ref[...] = jnp.concatenate([block] * (sums_ref.shape[0] // 8), axis=0)


def finish_kernel(count, core_ref, sums_ref, other_ref, hot_ref, loss_ref):
    rows, emb = hot_ref.shape
    groups = sums_ref.shape[0] // 8
    for core, ref in ((core_ref[0], sums_ref), (1 - core_ref[0], other_ref)):
        row = 0
        for i in range(2):
            at = pl.ds(pl.multiple_of(core * (rows // 2) + i * groups, groups), groups)
            for j in range(0, emb, 128):
                hot_ref[at, j : j + 128] = ref[pl.ds(row, groups, stride=8), :]
                row += 1
    at = pl.ds(row, groups, stride=8)
    losses = sums_ref[at, :] + other_ref[at, :]
    loss_ref[...] = jnp.sum(losses[:, 0:1], axis=0, keepdims=True) / count


def shards(
    history,
    item_ids,
    hot_table,
    rare_table,
    in_proj,
    pos_embed,
    norm_gain,
    w_query,
    w_key,
    w_value,
    w_out,
    out_gain,
    item_w1,
    item_w2,
    item_gain,
):
    users, hist = history.shape
    emb = hot_table.shape[1]
    rare_count = rare_table.shape[0]
    width = in_proj.shape[1]
    heads = width // HEAD_DIM
    scale = 4.0 / math.sqrt(width)
    owners = lax.axis_size(SHARD)
    towers = lax.axis_size("tower")
    near = lax.axis_size(LINE)
    total = users * towers * owners
    slots = owners * SLOTS
    span = users * hist
    wide = -(-(span + PAD) // 128) * 128
    swap = [(i, towers - 1 - i) for i in range(towers)]
    shape = jax.ShapeDtypeStruct
    sems = lambda n: pltpu.SemaphoreType.DMA((n,))
    vmem = lambda a: pltpu.VMEM(a.shape, a.dtype)
    hbm = lambda a: pltpu.HBM(a.shape, a.dtype)
    in_hbm = lambda a: pltpu.with_memory_space_constraint(a, pltpu.HBM)
    in_vmem = lambda a: pltpu.with_memory_space_constraint(a, pltpu.VMEM)
    like = lambda arrays: [pltpu.VMEM(a.shape, a.dtype) for a in arrays]
    exchange = functools.partial(lax.all_to_all, split_axis=0, concat_axis=0, tiled=True)

    places = (shape((8, wide), jnp.int32), shape((wide, 128), jnp.int32))
    loads = (history, item_ids.reshape(1, users), rare_table)
    request, known, row, column = pl.pallas_call(
        functools.partial(index_kernel, owners),
        out_shape=(
            shape((owners, 128), jnp.int32),
            pltpu.VMEM((rare_count, emb), BF),
            *map(vmem, places),
        ),
        in_specs=[HBM] * 3,
        out_specs=(VMEM,) * 4,
        scratch_shapes=like(loads) + [sems(3)],
        compiler_params=params(24),
        name="index",
    )(*map(in_hbm, loads))
    asked = exchange(request, SHARD)
    served, hot_ready, item_column, asked_row, row, column = pl.pallas_call(
        serve_kernel,
        out_shape=(
            shape((slots, emb), BF),
            pltpu.VMEM(hot_table.shape, BF),
            pltpu.VMEM((PAD, 128), jnp.int32),
            pltpu.HBM((8, slots), jnp.int32),
            *map(hbm, places),
        ),
        in_specs=[VMEM] * 4 + [HBM],
        out_specs=(VMEM, VMEM, VMEM, HBM, HBM, HBM),
        scratch_shapes=[
            pltpu.VMEM(hot_table.shape, F32),
            pltpu.VMEM((8, slots), jnp.int32),
            sems(4),
        ],
        compiler_params=params(24),
        name="serve",
    )(asked, *map(in_vmem, (known, row, column)), in_hbm(hot_table))
    fetched = exchange(served, SHARD)

    norm_gain, out_gain, item_gain = (g.reshape(1, width) for g in (norm_gain, out_gain, item_gain))
    item_kept = (shape((PAD, width), F32), shape((PAD, width), F32))
    item_vec, inner, outer = pl.pallas_call(
        functools.partial(item_forward_kernel, users),
        out_shape=(shape((near * 8, width), BF), *map(vmem, item_kept)),
        in_specs=[VMEM] * 4 + [HBM] * 2,
        out_specs=(VMEM,) * 3,
        scratch_shapes=like((item_w1, item_gain)) + [sems(2)],
        compiler_params=params(24),
        name="item_forward",
    )(
        fetched,
        *map(in_vmem, (hot_ready, item_column, item_w2)),
        *map(in_hbm, (item_w1, item_gain)),
    )
    near_items = exchange(item_vec, LINE)

    loads = (column, hot_table, pos_embed, norm_gain, out_gain)
    loads += (in_proj, w_query, w_key, w_value, w_out)
    kept = (
        shape((span, width), F32),
        shape((span, width), BF),
        shape((users * heads, width), BF),
        shape((users * heads, span), F32),
        shape((PAD, width), F32),
    )
    user_vec, hidden, normed, qk, weights, mixed, inner, outer = pl.pallas_call(
        functools.partial(user_forward_kernel, users),
        out_shape=(shape((PAD, width), BF), *map(hbm, kept + item_kept)),
        in_specs=[VMEM] * 3 + [HBM] * len(loads),
        out_specs=(VMEM,) + (HBM,) * (len(kept) + 2),
        scratch_shapes=like(loads + kept) + [sems(len(loads)), sems(len(kept) + 2)],
        compiler_params=params(40),
        name="user_forward",
    )(fetched, in_vmem(inner), in_vmem(outer), *map(in_hbm, loads))

    rows = owners * users
    spread = pl.pallas_call(
        functools.partial(arrange_kernel, users, near),
        out_shape=shape((rows, width + width // near), BF),
        in_specs=[VMEM, VMEM],
        out_specs=VMEM,
        compiler_params=params(24),
        name="arrange",
    )(near_items, user_vec)
    gathered = exchange(spread, ("x", "y"))
    swapped = lax.ppermute(gathered, "tower", swap)
    place = jnp.stack([lax.axis_index(("x", "y")), lax.axis_index(LINE)]).astype(jnp.int32)
    d_user, d_part = pl.pallas_call(
        functools.partial(softmax_kernel, users, near, scale),
        out_shape=(shape((PAD, width), F32), shape((near * 8, width), BF)),
        in_specs=[SMEM, VMEM, VMEM],
        out_specs=(VMEM, VMEM),
        scratch_shapes=[pltpu.VMEM((rows, 2 * owners // near * users), F32)],
        compiler_params=params(32),
        name="softmax",
    )(place, gathered, swapped)
    parts = exchange(d_part, LINE)

    loads = (mixed, out_gain, w_out, w_value, normed, weights, qk)
    loads += (hidden, norm_gain, in_proj, w_key, w_query)
    ahead = (row, item_gain, inner, item_w2, item_w1, outer)
    d_rows, *item_ready = pl.pallas_call(
        functools.partial(user_backward_kernel, users),
        out_shape=(shape((span, emb), BF), *map(vmem, ahead)),
        in_specs=[VMEM] + [HBM] * 18,
        out_specs=(VMEM,) * 7,
        scratch_shapes=like(loads) + [sems(18)],
        compiler_params=params(40),
        name="user_backward",
    )(d_user, *map(in_hbm, loads + ahead))
    core = lax.axis_index("tower").astype(jnp.int32).reshape(1)
    row_ready = item_ready[0]
    d_all, send, keep, loss = pl.pallas_call(
        functools.partial(item_backward_kernel, users),
        out_shape=(
            shape((wide, emb), BF),
            shape((owners // 2, emb), F32),
            shape((owners // 2, emb), F32),
            shape((8, 128), F32),
        ),
        in_specs=[SMEM] + [VMEM] * 8,
        out_specs=(VMEM,) * 4,
        compiler_params=params(32),
        name="item_backward",
    )(core, parts, d_rows, *map(in_vmem, item_ready))
    got = lax.ppermute(send, "tower", swap)
    rare = pl.pallas_call(
        rare_kernel,
        out_shape=shape((slots, emb), BF),
        in_specs=[VMEM, VMEM],
        out_specs=VMEM,
        compiler_params=params(32),
        name="rare",
    )(d_all, in_vmem(row_ready))
    outgoing = pl.pallas_call(
        outgoing_kernel,
        out_shape=shape((slots, emb), BF),
        in_specs=[VMEM] * 3,
        out_specs=VMEM,
        compiler_params=params(32),
        name="outgoing",
    )(rare, keep, got)

    returned = exchange(outgoing, SHARD)
    part, mine = pl.pallas_call(
        scatter_kernel,
        out_shape=(shape((rare_count, emb), BF), shape((owners // 4 * 8, 128), F32)),
        in_specs=[VMEM, VMEM, VMEM],
        out_specs=(VMEM, VMEM),
        compiler_params=params(24),
        name="scatter",
    )(returned, asked_row, loss)
    rare_grad = part.astype(F32) + lax.ppermute(part, "tower", swap).astype(F32)
    sums = exchange(mine, GROUP)
    other_sums = lax.ppermute(sums, "tower", swap)
    hot_total, loss_total = pl.pallas_call(
        functools.partial(finish_kernel, total * 2),
        out_shape=(shape((owners, emb), F32), shape((1, 1), F32)),
        in_specs=[SMEM, VMEM, VMEM],
        out_specs=(VMEM, VMEM),
        compiler_params=params(24),
        name="finish",
    )(core, sums, other_sums)
    return (hot_total, rare_grad, loss_total[0, 0])


def solution(mesh):
    sizes = (mesh.shape["tower"], 4, 4, mesh.shape["shard"] // 32, 2)
    mesh = Mesh(mesh.devices.reshape(sizes), ("tower",) + SHARD)
    return jax.shard_map(
        shards,
        mesh=mesh,
        in_specs=(
            P(("tower",) + SHARD, None),
            P(("tower",) + SHARD),
            P(),
            P(SHARD, None),
            P(),
            P(),
            P(),
            P(),
            P(),
            P(),
            P(),
            P(),
            P(),
            P(),
            P(),
        ),
        out_specs=(P(), P(SHARD, None), P()),
        check_vma=False,
    )
```

```python
import functools
import math

import jax
import jax.numpy as jnp
from jax import lax
from jax.experimental import pallas as pl
from jax.experimental.pallas import tpu as pltpu
from jax.sharding import Mesh
from jax.sharding import PartitionSpec as P

HEAD_DIM = 64
EPS = 1e-06
SLOTS = 8
HOT_SLOT = 5
HOT_CODE = 4096
LINE = ("zh", "zl")
SHARD = ("x", "y") + LINE
GROUP = ("x", "y", "zl")
PAD = 16
BF = jnp.bfloat16
F32 = jnp.float32
VMEM = pl.BlockSpec(memory_space=pltpu.VMEM)
SMEM = pl.BlockSpec(memory_space=pltpu.SMEM)
HBM = pl.BlockSpec(memory_space=pltpu.HBM)
NT = (((1,), (1,)), ((), ()))
TN = (((0,), (0,)), ((), ()))


def dot(a, b):
    return jnp.dot(a, b, preferred_element_type=F32)


def dot_nt(a, b):
    return lax.dot_general(a, b, NT, preferred_element_type=F32)


def dot_tn(a, b):
    return lax.dot_general(a, b, TN, preferred_element_type=F32)


def iota(shape, axis):
    return lax.broadcasted_iota(jnp.int32, shape, axis)


def one_hot(mask):
    return jnp.where(mask, 1.0, 0.0).astype(BF)


def params(mib):
    return pltpu.CompilerParams(vmem_limit_bytes=mib * 1024 * 1024)


def copies_of(pairs, sems):
    copies = [pltpu.make_async_copy(a, b, sems.at[i]) for i, (a, b) in enumerate(pairs)]
    for copy in copies:
        copy.start()
    return copies


def index_kernel(
    owners,
    history_hbm,
    items_hbm,
    table_hbm,
    request_ref,
    known_ref,
    row,
    column,
    history_ref,
    items_ref,
    table,
    sems,
):
    loads = copies_of(
        [(history_hbm, history_ref), (items_hbm, items_ref), (table_hbm, table)], sems
    )
    loads[0].wait()
    loads[1].wait()
    hot_count = owners
    rare_count = table.shape[0]
    users = history_ref.shape[0]
    span = row.shape[1]
    parts = [history_ref[u : u + 1, :] for u in range(users)] + [items_ref[...]]
    filled = sum(p.shape[1] for p in parts)
    ids = jnp.concatenate(parts + [jnp.full((1, span - filled), -1, jnp.int32)], axis=1)
    is_rare = ids >= hot_count
    index = ids - hot_count
    owner = jnp.where(is_rare, index // rare_count, -1)
    value = jnp.where(is_rare, index % rare_count + 1, 0).astype(F32)
    hits = iota((owners, span), 0) == owner
    before = one_hot(iota((span, span), 0) < iota((span, span), 1))
    earlier = dot(one_hot(hits), before)
    position = jnp.sum(jnp.where(hits, earlier, 0.0), axis=0, keepdims=True).astype(jnp.int32)
    places = jnp.where(
        is_rare, owner * SLOTS + position, jnp.where(ids >= 0, ids + HOT_CODE, -1)
    )
    row[...] = jnp.broadcast_to(places, row.shape)
    column[...] = jnp.transpose(jnp.broadcast_to(places.astype(F32), (128, span))).astype(jnp.int32)
    order = jnp.where(hits, earlier, -1.0)
    lanes = iota(request_ref.shape, 1)
    request = jnp.zeros(request_ref.shape, F32)
    for slot in range(HOT_SLOT):
        wanted = jnp.sum(jnp.where(order == float(slot), value, 0.0), axis=1, keepdims=True)
        request = jnp.where(lanes == slot, wanted, request)
    request_ref[...] = request.astype(jnp.int32)
    loads[2].wait()
    known_ref[...] = table[...].astype(BF)


def serve_kernel(
    asked_ref,
    known_ref,
    row_ref,
    column_ref,
    hot_hbm,
    served,
    hot_ref,
    item_column_ref,
    asked_row_hbm,
    row_hbm,
    column_hbm,
    hot,
    row,
    sems,
):
    copies = copies_of([(hot_hbm, hot), (row_ref, row_hbm), (column_ref, column_hbm)], sems)
    span = column_ref.shape[0] - 128
    item_column_ref[...] = column_ref[span : span + PAD, :]
    slots = served.shape[0]
    sources = asked_ref.shape[0]
    asked = asked_ref[...]
    high = (asked // 2).astype(F32).astype(BF)
    low = (asked % 2).astype(F32).astype(BF)
    expand = one_hot(iota((slots, sources), 0) // SLOTS == iota((slots, sources), 1))
    wide = 2.0 * dot(expand, high) + dot(expand, low)
    mine = iota(wide.shape, 1) == iota(wide.shape, 0) % SLOTS
    index = jnp.sum(jnp.where(mine, wide, 0.0), axis=1, keepdims=True) - 1.0
    index = jnp.broadcast_to(index, wide.shape)
    row[...] = jnp.transpose(index)[0:8].astype(jnp.int32)
    save = pltpu.make_async_copy(row, asked_row_hbm, sems.at[3])
    save.start()
    index = index.astype(jnp.int32)
    lanes = iota(index.shape, 1)
    rows = known_ref.shape[0]
    picks = jnp.concatenate(
        [one_hot(index == lanes + 128 * j) for j in range(rows // 128)], axis=1
    )
    served[...] = dot(picks, known_ref[...]).astype(BF)
    copies[0].wait()
    hot_ref[...] = hot[...].astype(BF)
    for copy in copies[1:] + [save]:
        copy.wait()


def head_mask(heads, width):
    return iota((heads, width), 1) // HEAD_DIM == iota((heads, width), 0)


def spread_heads(values, mask, users):
    return jnp.concatenate(
        [jnp.where(mask, values[u : u + 1], 0.0) for u in range(users)], axis=0
    ).astype(BF)


def join_heads(full, mask, users):
    heads = mask.shape[0]
    parts = [
        jnp.sum(
            jnp.where(mask, full[u * heads : (u + 1) * heads], 0.0), axis=0, keepdims=True
        )
        for u in range(users)
    ]
    return jnp.concatenate(parts + [jnp.zeros((PAD - users, full.shape[1]), F32)], axis=0)


def look_up(column, fetched, hot):
    lanes = iota(column.shape, 1)
    slots = fetched.shape[0]
    picks = jnp.concatenate(
        [one_hot(column == lanes + 128 * j) for j in range(slots // 128)], axis=1
    )
    hot_picks = one_hot(column == lanes + HOT_CODE)
    return (dot(picks, fetched[...]) + dot(hot_picks, hot[...].astype(BF))).astype(BF)


def item_forward_kernel(
    users,
    fetched_ref,
    hot_ref,
    column_ref,
    item_w2,
    item_w1_hbm,
    gain_hbm,
    vectors_ref,
    inner_ref,
    outer_ref,
    item_w1,
    gain,
    sems,
):
    loads = copies_of([(item_w1_hbm, item_w1), (gain_hbm, gain)], sems)
    rows = look_up(column_ref[...], fetched_ref, hot_ref)
    loads[0].wait()
    inner = dot(rows, item_w1[...])
    inner_ref[...] = inner
    gated = (inner * jax.nn.sigmoid(inner)).astype(BF)
    loads[1].wait()
    outer = dot(gated, item_w2[...])
    outer_ref[...] = outer
    scale = lax.rsqrt(jnp.mean(outer * outer, axis=-1, keepdims=True) + EPS)
    vectors = jnp.where(iota(outer.shape, 0) < users, outer * scale * gain[...], 0.0)
    peers = vectors_ref.shape[0] // 8
    vectors_ref[...] = jnp.concatenate([vectors[0:8]] * peers, axis=0).astype(BF)


def user_forward_kernel(users, *refs):
    fetched_ref, item_kept, sources, refs = refs[0], refs[1:3], refs[3:13], refs[13:]
    vectors_ref, kept_hbm, item_kept_hbm, refs = refs[0], refs[1:6], refs[6:8], refs[8:]
    targets, kept, (in_sems, out_sems) = refs[:10], refs[10:15], refs[15:]
    column_of, hot, pos_of, norm_gain_ref, out_gain_ref = targets[:5]
    in_proj, w_query, w_key, w_value, w_out = targets[5:]
    hidden_ref, normed_ref, qk_ref, weights_ref, mixed_ref = kept
    copies = copies_of(zip(sources, targets), in_sems)
    saves = [
        pltpu.make_async_copy(a, b, out_sems.at[i])
        for i, (a, b) in enumerate(zip(kept + item_kept, kept_hbm + item_kept_hbm))
    ]
    saves[5].start()
    saves[6].start()
    hist, width = pos_of.shape
    heads = width // HEAD_DIM
    span = users * hist
    copies[0].wait()
    copies[1].wait()
    rows = look_up(column_of[0:span, :], fetched_ref, hot)
    for copy in copies[2:6]:
        copy.wait()
    pos = pos_of[...].astype(F32)
    hidden = dot(rows, in_proj[...]) + jnp.concatenate([pos] * users, axis=0)
    hidden_ref[...] = hidden
    saves[0].start()
    scale = lax.rsqrt(jnp.mean(hidden * hidden, axis=-1, keepdims=True) + EPS)
    normed = (hidden * scale * norm_gain_ref[...]).astype(BF)
    normed_ref[...] = normed
    saves[1].start()
    last = jnp.concatenate(
        [normed[(u + 1) * hist - PAD : (u + 1) * hist].astype(F32)[PAD - 1 :] for u in range(users)]
        + [jnp.zeros((PAD - users, width), F32)],
        axis=0,
    ).astype(BF)
    mask = head_mask(heads, width)
    copies[6].wait()
    query = dot(last, w_query[...]).astype(BF).astype(F32)
    copies[7].wait()
    qk = dot_nt(spread_heads(query, mask, users), w_key[...]).astype(BF)
    qk_ref[...] = qk
    saves[2].start()
    shape = (users * heads, span)
    own = iota(shape, 0) // heads == iota(shape, 1) // hist
    scores = jnp.where(own, dot_nt(qk, normed) * (1.0 / math.sqrt(HEAD_DIM)), -jnp.inf)
    raised = jnp.exp(scores - jnp.max(scores, axis=1, keepdims=True))
    weights = raised / jnp.sum(raised, axis=1, keepdims=True)
    weights_ref[...] = weights
    saves[3].start()
    mixes = dot(weights.astype(BF), normed).astype(BF)
    copies[8].wait()
    attended = join_heads(dot(mixes, w_value[...]), mask, users).astype(BF)
    copies[9].wait()
    hidden_last = jnp.concatenate(
        [hidden[(u + 1) * hist - 1 : (u + 1) * hist] for u in range(users)]
        + [jnp.zeros((PAD - users, width), F32)],
        axis=0,
    )
    mixed = hidden_last + dot(attended, w_out[...])
    mixed_ref[...] = mixed
    saves[4].start()
    scale = lax.rsqrt(jnp.mean(mixed * mixed, axis=-1, keepdims=True) + EPS)
    vectors_ref[...] = (mixed * scale * out_gain_ref[...]).astype(BF)
    for save in saves:
        save.wait()


def arrange_kernel(users, near, near_ref, vectors_ref, spread_ref):
    width = near_ref.shape[1]
    block = near * users
    part = spread_ref.shape[1] - width
    shape = (block, near * 8)
    at = iota(shape, 0)
    source = at // users * 8 + at % users
    items = dot(one_hot(iota(shape, 1) == source), near_ref[...])
    shape = (block, PAD)
    at = iota(shape, 0)
    mine = jnp.zeros((block, part), F32)
    for c in range(near):
        picks = one_hot((at % near == c) & (iota(shape, 1) == at // near))
        mine = mine + dot(picks, vectors_ref[:, c * part : (c + 1) * part])
    rows = jnp.concatenate([items, mine], axis=1).astype(BF)
    for i in range(spread_ref.shape[0] // block):
        spread_ref[i * block : (i + 1) * block, :] = rows


def users_of(near, width, ref):
    rows = ref.shape[0]
    group = rows // near
    line = iota((rows, rows), 0)
    picks = one_hot(iota((rows, rows), 1) == line % group * near + line // group)
    parts = dot(picks, ref[:, width:])
    return jnp.concatenate([parts[c * group : (c + 1) * group] for c in range(near)], axis=1).astype(BF)


def own_users_kernel(near, gathered_ref, own_ref):
    own_ref[...] = users_of(near, own_ref.shape[1], gathered_ref)


def softmax_kernel(
    users,
    near,
    scale,
    place_ref,
    gathered_ref,
    own_users_ref,
    swapped_ref,
    d_user_ref,
    d_part_ref,
    raised_ref,
):
    rows = gathered_ref.shape[0]
    width = d_user_ref.shape[1]
    items = near * users
    group = rows // near
    mine, plane = place_ref[0], place_ref[1]
    own, other = gathered_ref[:, 0:width], swapped_ref[:, 0:width]
    other_users = users_of(near, width, swapped_ref)
    group_users = jnp.concatenate([own_users_ref[...], other_users], axis=0)
    total = 2 * group

    shape = (rows, total)
    first = scale * dot_nt(own, group_users)
    second = scale * dot_nt(other, group_users)
    top = jnp.maximum(
        jnp.max(first, axis=0, keepdims=True), jnp.max(second, axis=0, keepdims=True)
    )
    raised = jnp.exp(first - top)
    raised_ref[...] = raised
    other_raised = jnp.exp(second - top)
    count = jnp.sum(raised, axis=0, keepdims=True) + jnp.sum(other_raised, axis=0, keepdims=True)
    share = 1.0 / count

    line = (items, total)
    target = (iota(line, 0) // users == plane) & (
        iota(line, 1) == mine * users + iota(line, 0) % users
    )
    near_raised = raised_ref[pl.ds(pl.multiple_of(mine * items, 8), items), :]
    slope = (near_raised * share - jnp.where(target, 1.0, 0.0)).astype(BF)
    apart = (near * 8, items)
    at = iota(apart, 0)
    apart = one_hot((at % 8 < users) & (iota(apart, 1) == at // 8 * users + at % 8))
    d_part = scale * dot(dot(apart, slope).astype(BF), group_users)

    who = iota(shape, 1) - mine * users
    target = (who >= 0) & (who < users) & (iota(shape, 0) == mine * items + plane * users + who)
    slope = (raised * share - jnp.where(target, 1.0, 0.0)).astype(BF)
    other_slope = (other_raised * share).astype(BF)
    self = (PAD, total)
    self = one_hot((iota(self, 0) < users) & (iota(self, 1) == mine * users + iota(self, 0)))
    d_user = dot(dot_nt(self, slope).astype(BF), own)
    d_user = d_user + dot(dot_nt(self, other_slope).astype(BF), other)
    d_user_ref[...] = (scale * d_user).astype(BF).astype(F32)
    each = jnp.sum(jnp.where(target, top + jnp.log(count) - first, 0.0), axis=0, keepdims=True)
    loss = jnp.sum(each, axis=1, keepdims=True)
    high = loss.astype(BF).astype(F32)
    middle = (loss - high).astype(BF).astype(F32)
    low = loss - high - middle
    shape = d_part.shape
    lanes = iota(shape, 1)
    loss = jnp.where(lanes == 0, high, jnp.where(lanes == 1, middle, jnp.where(lanes == 2, low, 0.0)))
    d_part_ref[...] = jnp.where(iota(shape, 0) % 8 == users, loss, d_part).astype(BF)


def norm_backward(values, cotangent, gain):
    inverse = lax.rsqrt(jnp.mean(values * values, axis=-1, keepdims=True) + EPS)
    pulled = cotangent * gain
    along = jnp.mean(pulled * values, axis=-1, keepdims=True)
    return inverse * pulled - values * (inverse * inverse * inverse * along)


def user_backward_kernel(users, d_user_ref, *refs):
    sources, refs = refs[:18], refs[18:]
    d_rows_ref, ahead, refs = refs[0], refs[1:7], refs[7:]
    targets, (d_normed, sems) = refs[:12], refs[12:]
    mixed_ref, out_gain_ref, w_out, w_value, normed_ref, weights_ref, qk_ref = targets[:7]
    w_key, w_query, hidden_ref, norm_gain_ref, in_proj = targets[7:]
    copies = copies_of(zip(sources, tuple(targets) + tuple(ahead)), sems)
    span, width = hidden_ref.shape
    hist = span // users
    heads = width // HEAD_DIM
    mask = head_mask(heads, width)
    for copy in copies[:3]:
        copy.wait()
    d_mixed = norm_backward(mixed_ref[...], d_user_ref[...], out_gain_ref[...])
    d_attended = dot_nt(d_mixed.astype(BF), w_out[...])
    copies[3].wait()
    d_mixes = dot_nt(spread_heads(d_attended, mask, users), w_value[...]).astype(BF)
    for copy in copies[4:7]:
        copy.wait()
    normed = normed_ref[...]
    weights = weights_ref[...]
    shape = weights.shape
    own = iota(shape, 0) // heads == iota(shape, 1) // hist
    d_weights = jnp.where(own, dot_nt(d_mixes, normed), 0.0)
    d_scores = weights * (d_weights - jnp.sum(weights * d_weights, axis=1, keepdims=True))
    d_scores = (d_scores * (1.0 / math.sqrt(HEAD_DIM))).astype(BF)
    d_normed[...] = dot_tn(
        jnp.concatenate([weights.astype(BF), d_scores], axis=0),
        jnp.concatenate([d_mixes, qk_ref[...]], axis=0),
    )
    d_qk = dot(d_scores, normed).astype(BF)
    copies[7].wait()
    d_query = join_heads(dot(d_qk, w_key[...]), mask, users).astype(BF)
    copies[8].wait()
    d_last = dot_nt(d_query, w_query[...])
    for u in range(users):
        at = slice((u + 1) * hist - 1, (u + 1) * hist)
        d_normed[at, :] = d_normed[at, :] + d_last[u : u + 1]
    copies[9].wait()
    copies[10].wait()
    d_normed[...] = norm_backward(hidden_ref[...], d_normed[...], norm_gain_ref[...])
    for u in range(users):
        at = slice((u + 1) * hist - 1, (u + 1) * hist)
        d_normed[at, :] = d_normed[at, :] + d_mixed[u : u + 1]
    copies[11].wait()
    d_rows_ref[...] = dot_nt(d_normed[...].astype(BF), in_proj[...]).astype(BF)
    for copy in copies[12:]:
        copy.wait()


def item_backward_kernel(users, core_ref, parts_ref, d_rows_ref, *refs):
    row_ref, gain, inner_ref, item_w2, item_w1, outer_ref, refs = *refs[:6], refs[6:]
    d_all_ref, send_ref, keep_ref, loss_ref = refs
    span, emb = d_rows_ref.shape
    wide = row_ref.shape[1]
    peers = parts_ref.shape[0]
    shape = (PAD, peers)
    sums = dot(one_hot(iota(shape, 1) % 8 == iota(shape, 0)), parts_ref[...])
    shape = (1, 128)
    loss = jnp.where(iota(shape, 1) < 3, sums[users : users + 1, 0:128], 0.0)
    loss_ref[...] = jnp.broadcast_to(jnp.sum(loss, axis=1, keepdims=True), loss_ref.shape)
    d_item = jnp.where(iota(sums.shape, 0) < users, sums, 0.0).astype(BF).astype(F32)
    d_all_ref[0:span, :] = d_rows_ref[...]
    half = keep_ref.shape[0]
    first = HOT_CODE + core_ref[0] * half
    picks = one_hot(iota((half, wide), 0) + first == row_ref[0:1, :])
    keep = dot(picks[:, 0:span], d_rows_ref[...])
    first = HOT_CODE + (1 - core_ref[0]) * half
    other_picks = one_hot(iota((half, wide), 0) + first == row_ref[0:1, :])
    send = dot(other_picks[:, 0:span], d_rows_ref[...])
    d_outer = norm_backward(outer_ref[...], d_item, gain[...])
    inner = inner_ref[...]
    gate = jax.nn.sigmoid(inner)
    d_inner = dot_nt(d_outer.astype(BF), item_w2[...]) * (gate * (1.0 + inner * (1.0 - gate)))
    d_items = dot_nt(d_inner.astype(BF), item_w1[...])
    d_items = jnp.concatenate([d_items, jnp.zeros((wide - span - PAD, emb), F32)], axis=0).astype(BF)
    d_all_ref[span:, :] = d_items
    keep_ref[...] = keep + dot(picks[:, span:], d_items)
    send_ref[...] = send + dot(other_picks[:, span:], d_items)


def rare_kernel(d_all_ref, row_ref, rare_ref):
    shape = (rare_ref.shape[0], row_ref.shape[1])
    rare_ref[...] = dot(one_hot(iota(shape, 0) == row_ref[0:1, :]), d_all_ref[...]).astype(BF)


def outgoing_kernel(rare_ref, keep_ref, got_ref, outgoing_ref):
    half = keep_ref.shape[0]
    slots = rare_ref.shape[0]
    shape = (slots, half)
    line = iota(shape, 0)
    owner, slot = line // SLOTS, line % SLOTS - HOT_SLOT
    held = owner // 8 * 2 + owner % 2 + slot * (half // 2)
    held = one_hot((slot >= 0) & (slot < 2) & (iota(shape, 1) == held))
    hot = dot(held, (keep_ref[...] + got_ref[...]).astype(BF))
    outgoing_ref[...] = (rare_ref[...].astype(F32) + hot).astype(BF)


def scatter_kernel(returned_ref, row_ref, loss_ref, part_ref, sums_ref):
    rows, emb = part_ref.shape
    slots = returned_ref.shape[0]
    returned = returned_ref[...]
    picks = one_hot(iota((rows, slots), 0) == row_ref[0:1, :])
    part_ref[...] = dot(picks, returned).astype(BF)
    shape = (PAD, slots)
    hot = dot(one_hot((iota(shape, 0) < 2) & (iota(shape, 1) % SLOTS == iota(shape, 0) + HOT_SLOT)), returned)
    halves = [hot[i : i + 1, j : j + 128] for i in range(2) for j in range(0, emb, 128)]
    block = jnp.concatenate(halves + [loss_ref[0 : 8 - len(halves), :]], axis=0)
    sums_ref[...] = jnp.concatenate([block] * (sums_ref.shape[0] // 8), axis=0)


def finish_kernel(count, core_ref, sums_ref, other_ref, hot_ref, loss_ref):
    rows, emb = hot_ref.shape
    groups = sums_ref.shape[0] // 8
    for core, ref in ((core_ref[0], sums_ref), (1 - core_ref[0], other_ref)):
        row = 0
        for i in range(2):
            at = pl.ds(pl.multiple_of(core * (rows // 2) + i * groups, groups), groups)
            for j in range(0, emb, 128):
                hot_ref[at, j : j + 128] = ref[pl.ds(row, groups, stride=8), :]
                row += 1
    at = pl.ds(row, groups, stride=8)
    losses = sums_ref[at, :] + other_ref[at, :]
    loss_ref[...] = jnp.sum(losses[:, 0:1], axis=0, keepdims=True) / count


def shards(
    history,
    item_ids,
    hot_table,
    rare_table,
    in_proj,
    pos_embed,
    norm_gain,
    w_query,
    w_key,
    w_value,
    w_out,
    out_gain,
    item_w1,
    item_w2,
    item_gain,
):
    users, hist = history.shape
    emb = hot_table.shape[1]
    rare_count = rare_table.shape[0]
    width = in_proj.shape[1]
    heads = width // HEAD_DIM
    scale = 4.0 / math.sqrt(width)
    owners = lax.axis_size(SHARD)
    towers = lax.axis_size("tower")
    near = lax.axis_size(LINE)
    total = users * towers * owners
    slots = owners * SLOTS
    span = users * hist
    wide = -(-(span + PAD) // 128) * 128
    swap = [(i, towers - 1 - i) for i in range(towers)]
    shape = jax.ShapeDtypeStruct
    sems = lambda n: pltpu.SemaphoreType.DMA((n,))
    vmem = lambda a: pltpu.VMEM(a.shape, a.dtype)
    hbm = lambda a: pltpu.HBM(a.shape, a.dtype)
    in_hbm = lambda a: pltpu.with_memory_space_constraint(a, pltpu.HBM)
    in_vmem = lambda a: pltpu.with_memory_space_constraint(a, pltpu.VMEM)
    like = lambda arrays: [pltpu.VMEM(a.shape, a.dtype) for a in arrays]
    exchange = functools.partial(lax.all_to_all, split_axis=0, concat_axis=0, tiled=True)

    places = (shape((8, wide), jnp.int32), shape((wide, 128), jnp.int32))
    loads = (history, item_ids.reshape(1, users), rare_table)
    request, known, row, column = pl.pallas_call(
        functools.partial(index_kernel, owners),
        out_shape=(
            shape((owners, 128), jnp.int32),
            pltpu.VMEM((rare_count, emb), BF),
            *map(vmem, places),
        ),
        in_specs=[HBM] * 3,
        out_specs=(VMEM,) * 4,
        scratch_shapes=like(loads) + [sems(3)],
        compiler_params=params(24),
        name="index",
    )(*map(in_hbm, loads))
    asked = exchange(request, SHARD)
    served, hot_ready, item_column, asked_row, row, column = pl.pallas_call(
        serve_kernel,
        out_shape=(
            shape((slots, emb), BF),
            pltpu.VMEM(hot_table.shape, BF),
            pltpu.VMEM((PAD, 128), jnp.int32),
            pltpu.HBM((8, slots), jnp.int32),
            *map(hbm, places),
        ),
        in_specs=[VMEM] * 4 + [HBM],
        out_specs=(VMEM, VMEM, VMEM, HBM, HBM, HBM),
        scratch_shapes=[
            pltpu.VMEM(hot_table.shape, F32),
            pltpu.VMEM((8, slots), jnp.int32),
            sems(4),
        ],
        compiler_params=params(24),
        name="serve",
    )(asked, *map(in_vmem, (known, row, column)), in_hbm(hot_table))
    fetched = exchange(served, SHARD)

    norm_gain, out_gain, item_gain = (g.reshape(1, width) for g in (norm_gain, out_gain, item_gain))
    item_kept = (shape((PAD, width), F32), shape((PAD, width), F32))
    item_vec, inner, outer = pl.pallas_call(
        functools.partial(item_forward_kernel, users),
        out_shape=(shape((near * 8, width), BF), *map(vmem, item_kept)),
        in_specs=[VMEM] * 4 + [HBM] * 2,
        out_specs=(VMEM,) * 3,
        scratch_shapes=like((item_w1, item_gain)) + [sems(2)],
        compiler_params=params(24),
        name="item_forward",
    )(
        fetched,
        *map(in_vmem, (hot_ready, item_column, item_w2)),
        *map(in_hbm, (item_w1, item_gain)),
    )
    near_items = exchange(item_vec, LINE)

    loads = (column, hot_table, pos_embed, norm_gain, out_gain)
    loads += (in_proj, w_query, w_key, w_value, w_out)
    kept = (
        shape((span, width), F32),
        shape((span, width), BF),
        shape((users * heads, width), BF),
        shape((users * heads, span), F32),
        shape((PAD, width), F32),
    )
    user_vec, hidden, normed, qk, weights, mixed, inner, outer = pl.pallas_call(
        functools.partial(user_forward_kernel, users),
        out_shape=(shape((PAD, width), BF), *map(hbm, kept + item_kept)),
        in_specs=[VMEM] * 3 + [HBM] * len(loads),
        out_specs=(VMEM,) + (HBM,) * (len(kept) + 2),
        scratch_shapes=like(loads + kept) + [sems(len(loads)), sems(len(kept) + 2)],
        compiler_params=params(40),
        name="user_forward",
    )(fetched, in_vmem(inner), in_vmem(outer), *map(in_hbm, loads))

    rows = owners * users
    spread = pl.pallas_call(
        functools.partial(arrange_kernel, users, near),
        out_shape=shape((rows, width + width // near), BF),
        in_specs=[VMEM, VMEM],
        out_specs=VMEM,
        compiler_params=params(24),
        name="arrange",
    )(near_items, user_vec)
    gathered = exchange(spread, ("x", "y"))
    swapped = lax.ppermute(gathered, "tower", swap)
    own_users = pl.pallas_call(
        functools.partial(own_users_kernel, near),
        out_shape=shape((rows // near, width), BF),
        in_specs=[VMEM],
        out_specs=VMEM,
        compiler_params=params(24),
        name="own_users",
    )(gathered)
    place = jnp.stack([lax.axis_index(("x", "y")), lax.axis_index(LINE)]).astype(jnp.int32)
    d_user, d_part = pl.pallas_call(
        functools.partial(softmax_kernel, users, near, scale),
        out_shape=(shape((PAD, width), F32), shape((near * 8, width), BF)),
        in_specs=[SMEM, VMEM, VMEM, VMEM],
        out_specs=(VMEM, VMEM),
        scratch_shapes=[pltpu.VMEM((rows, 2 * owners // near * users), F32)],
        compiler_params=params(32),
        name="softmax",
    )(place, gathered, own_users, swapped)
    parts = exchange(d_part, LINE)

    loads = (mixed, out_gain, w_out, w_value, normed, weights, qk)
    loads += (w_key, w_query, hidden, norm_gain, in_proj)
    ahead = (row, item_gain, inner, item_w2, item_w1, outer)
    d_rows, *item_ready = pl.pallas_call(
        functools.partial(user_backward_kernel, users),
        out_shape=(shape((span, emb), BF), *map(vmem, ahead)),
        in_specs=[VMEM] + [HBM] * 18,
        out_specs=(VMEM,) * 7,
        scratch_shapes=like(loads) + [pltpu.VMEM((span, width), F32), sems(18)],
        compiler_params=params(40),
        name="user_backward",
    )(d_user, *map(in_hbm, loads + ahead))
    core = lax.axis_index("tower").astype(jnp.int32).reshape(1)
    row_ready = item_ready[0]
    d_all, send, keep, loss = pl.pallas_call(
        functools.partial(item_backward_kernel, users),
        out_shape=(
            shape((wide, emb), BF),
            shape((owners // 2, emb), F32),
            shape((owners // 2, emb), F32),
            shape((8, 128), F32),
        ),
        in_specs=[SMEM] + [VMEM] * 8,
        out_specs=(VMEM,) * 4,
        compiler_params=params(32),
        name="item_backward",
    )(core, parts, d_rows, *map(in_vmem, item_ready))
    got = lax.ppermute(send, "tower", swap)
    rare = pl.pallas_call(
        rare_kernel,
        out_shape=shape((slots, emb), BF),
        in_specs=[VMEM, VMEM],
        out_specs=VMEM,
        compiler_params=params(32),
        name="rare",
    )(d_all, in_vmem(row_ready))
    outgoing = pl.pallas_call(
        outgoing_kernel,
        out_shape=shape((slots, emb), BF),
        in_specs=[VMEM] * 3,
        out_specs=VMEM,
        compiler_params=params(32),
        name="outgoing",
    )(rare, keep, got)

    returned = exchange(outgoing, SHARD)
    part, mine = pl.pallas_call(
        scatter_kernel,
        out_shape=(shape((rare_count, emb), BF), shape((owners // 4 * 8, 128), F32)),
        in_specs=[VMEM, VMEM, VMEM],
        out_specs=(VMEM, VMEM),
        compiler_params=params(24),
        name="scatter",
    )(returned, asked_row, loss)
    rare_grad = part.astype(F32) + lax.ppermute(part, "tower", swap).astype(F32)
    sums = exchange(mine, GROUP)
    other_sums = lax.ppermute(sums, "tower", swap)
    hot_total, loss_total = pl.pallas_call(
        functools.partial(finish_kernel, total * 2),
        out_shape=(shape((owners, emb), F32), shape((1, 1), F32)),
        in_specs=[SMEM, VMEM, VMEM],
        out_specs=(VMEM, VMEM),
        compiler_params=params(24),
        name="finish",
    )(core, sums, other_sums)
    return (hot_total, rare_grad, loss_total[0, 0])


def solution(mesh):
    sizes = (mesh.shape["tower"], 4, 4, mesh.shape["shard"] // 32, 2)
    mesh = Mesh(mesh.devices.reshape(sizes), ("tower",) + SHARD)
    return jax.shard_map(
        shards,
        mesh=mesh,
        in_specs=(
            P(("tower",) + SHARD, None),
            P(("tower",) + SHARD),
            P(),
            P(SHARD, None),
            P(),
            P(),
            P(),
            P(),
            P(),
            P(),
            P(),
            P(),
            P(),
            P(),
            P(),
        ),
        out_specs=(P(), P(SHARD, None), P()),
        check_vma=False,
    )
```

```python
import functools
import math

import jax
import jax.numpy as jnp
from jax import lax
from jax.experimental import pallas as pl
from jax.experimental.pallas import tpu as pltpu
from jax.sharding import Mesh
from jax.sharding import PartitionSpec as P

HEAD_DIM = 64
EPS = 1e-06
SLOTS = 8
HOT_SLOT = 5
HOT_CODE = 4096
LINE = ("zh", "zl")
SHARD = ("x", "y") + LINE
GROUP = ("x", "y", "zl")
PAD = 16
BF = jnp.bfloat16
F32 = jnp.float32
VMEM = pl.BlockSpec(memory_space=pltpu.VMEM)
SMEM = pl.BlockSpec(memory_space=pltpu.SMEM)
HBM = pl.BlockSpec(memory_space=pltpu.HBM)
NT = (((1,), (1,)), ((), ()))
TN = (((0,), (0,)), ((), ()))


def dot(a, b):
    return jnp.dot(a, b, preferred_element_type=F32)


def dot_nt(a, b):
    return lax.dot_general(a, b, NT, preferred_element_type=F32)


def dot_tn(a, b):
    return lax.dot_general(a, b, TN, preferred_element_type=F32)


def iota(shape, axis):
    return lax.broadcasted_iota(jnp.int32, shape, axis)


def one_hot(mask):
    return jnp.where(mask, 1.0, 0.0).astype(BF)


def params(mib):
    return pltpu.CompilerParams(vmem_limit_bytes=mib * 1024 * 1024)


def copies_of(pairs, sems):
    copies = [pltpu.make_async_copy(a, b, sems.at[i]) for i, (a, b) in enumerate(pairs)]
    for copy in copies:
        copy.start()
    return copies


def index_kernel(
    owners,
    history_hbm,
    items_hbm,
    table_hbm,
    request_ref,
    known_ref,
    row,
    column,
    history_ref,
    items_ref,
    table,
    sems,
):
    loads = copies_of(
        [(history_hbm, history_ref), (items_hbm, items_ref), (table_hbm, table)], sems
    )
    loads[0].wait()
    loads[1].wait()
    hot_count = owners
    rare_count = table.shape[0]
    users = history_ref.shape[0]
    span = row.shape[1]
    parts = [history_ref[u : u + 1, :] for u in range(users)] + [items_ref[...]]
    filled = sum(p.shape[1] for p in parts)
    ids = jnp.concatenate(parts + [jnp.full((1, span - filled), -1, jnp.int32)], axis=1)
    is_rare = ids >= hot_count
    index = ids - hot_count
    owner = jnp.where(is_rare, index // rare_count, -1)
    value = jnp.where(is_rare, index % rare_count + 1, 0).astype(F32)
    hits = iota((owners, span), 0) == owner
    before = one_hot(iota((span, span), 0) < iota((span, span), 1))
    earlier = dot(one_hot(hits), before)
    position = jnp.sum(jnp.where(hits, earlier, 0.0), axis=0, keepdims=True).astype(jnp.int32)
    places = jnp.where(
        is_rare, owner * SLOTS + position, jnp.where(ids >= 0, ids + HOT_CODE, -1)
    )
    row[...] = jnp.broadcast_to(places, row.shape)
    column[...] = jnp.transpose(jnp.broadcast_to(places.astype(F32), (128, span))).astype(jnp.int32)
    order = jnp.where(hits, earlier, -1.0)
    lanes = iota(request_ref.shape, 1)
    request = jnp.zeros(request_ref.shape, F32)
    for slot in range(HOT_SLOT):
        wanted = jnp.sum(jnp.where(order == float(slot), value, 0.0), axis=1, keepdims=True)
        request = jnp.where(lanes == slot, wanted, request)
    request_ref[...] = request.astype(jnp.int32)
    loads[2].wait()
    known_ref[...] = table[...].astype(BF)


def serve_kernel(
    asked_ref,
    known_ref,
    row_ref,
    column_ref,
    hot_hbm,
    served,
    hot_ref,
    item_column_ref,
    asked_row_hbm,
    row_hbm,
    column_hbm,
    hot,
    row,
    sems,
):
    copies = copies_of([(hot_hbm, hot), (row_ref, row_hbm), (column_ref, column_hbm)], sems)
    span = column_ref.shape[0] - 128
    item_column_ref[...] = column_ref[span : span + PAD, :]
    slots = served.shape[0]
    sources = asked_ref.shape[0]
    asked = asked_ref[...]
    high = (asked // 2).astype(F32).astype(BF)
    low = (asked % 2).astype(F32).astype(BF)
    expand = one_hot(iota((slots, sources), 0) // SLOTS == iota((slots, sources), 1))
    wide = 2.0 * dot(expand, high) + dot(expand, low)
    mine = iota(wide.shape, 1) == iota(wide.shape, 0) % SLOTS
    index = jnp.sum(jnp.where(mine, wide, 0.0), axis=1, keepdims=True) - 1.0
    index = jnp.broadcast_to(index, wide.shape)
    row[...] = jnp.transpose(index)[0:8].astype(jnp.int32)
    save = pltpu.make_async_copy(row, asked_row_hbm, sems.at[3])
    save.start()
    index = index.astype(jnp.int32)
    lanes = iota(index.shape, 1)
    rows = known_ref.shape[0]
    picks = jnp.concatenate(
        [one_hot(index == lanes + 128 * j) for j in range(rows // 128)], axis=1
    )
    served[...] = dot(picks, known_ref[...]).astype(BF)
    copies[0].wait()
    hot_ref[...] = hot[...].astype(BF)
    for copy in copies[1:] + [save]:
        copy.wait()


def head_mask(heads, width):
    return iota((heads, width), 1) // HEAD_DIM == iota((heads, width), 0)


def spread_heads(values, mask, users):
    return jnp.concatenate(
        [jnp.where(mask, values[u : u + 1], 0.0) for u in range(users)], axis=0
    ).astype(BF)


def join_heads(full, mask, users):
    heads = mask.shape[0]
    parts = [
        jnp.sum(
            jnp.where(mask, full[u * heads : (u + 1) * heads], 0.0), axis=0, keepdims=True
        )
        for u in range(users)
    ]
    return jnp.concatenate(parts + [jnp.zeros((PAD - users, full.shape[1]), F32)], axis=0)


def look_up(column, fetched, hot):
    lanes = iota(column.shape, 1)
    slots = fetched.shape[0]
    picks = jnp.concatenate(
        [one_hot(column == lanes + 128 * j) for j in range(slots // 128)], axis=1
    )
    hot_picks = one_hot(column == lanes + HOT_CODE)
    return (dot(picks, fetched[...]) + dot(hot_picks, hot[...].astype(BF))).astype(BF)


def item_forward_kernel(
    users,
    fetched_ref,
    hot_ref,
    column_ref,
    item_w2,
    item_w1_hbm,
    gain_hbm,
    vectors_ref,
    inner_ref,
    outer_ref,
    item_w1,
    gain,
    sems,
):
    loads = copies_of([(item_w1_hbm, item_w1), (gain_hbm, gain)], sems)
    rows = look_up(column_ref[...], fetched_ref, hot_ref)
    loads[0].wait()
    inner = dot(rows, item_w1[...])
    inner_ref[...] = inner
    gated = (inner * jax.nn.sigmoid(inner)).astype(BF)
    loads[1].wait()
    outer = dot(gated, item_w2[...])
    outer_ref[...] = outer
    scale = lax.rsqrt(jnp.mean(outer * outer, axis=-1, keepdims=True) + EPS)
    vectors = jnp.where(iota(outer.shape, 0) < users, outer * scale * gain[...], 0.0)
    peers = vectors_ref.shape[0] // 8
    vectors_ref[...] = jnp.concatenate([vectors[0:8]] * peers, axis=0).astype(BF)


def user_forward_kernel(users, *refs):
    fetched_ref, item_kept, sources, refs = refs[0], refs[1:3], refs[3:13], refs[13:]
    vectors_ref, kept_hbm, item_kept_hbm, refs = refs[0], refs[1:6], refs[6:8], refs[8:]
    targets, kept, (in_sems, out_sems) = refs[:10], refs[10:15], refs[15:]
    column_of, hot, pos_of, norm_gain_ref, out_gain_ref = targets[:5]
    in_proj, w_query, w_key, w_value, w_out = targets[5:]
    hidden_ref, normed_ref, qk_ref, weights_ref, mixed_ref = kept
    copies = copies_of(zip(sources, targets), in_sems)
    saves = [
        pltpu.make_async_copy(a, b, out_sems.at[i])
        for i, (a, b) in enumerate(zip(kept + item_kept, kept_hbm + item_kept_hbm))
    ]
    saves[5].start()
    saves[6].start()
    hist, width = pos_of.shape
    heads = width // HEAD_DIM
    span = users * hist
    copies[0].wait()
    copies[1].wait()
    rows = look_up(column_of[0:span, :], fetched_ref, hot)
    for copy in copies[2:6]:
        copy.wait()
    pos = pos_of[...].astype(F32)
    hidden = dot(rows, in_proj[...]) + jnp.concatenate([pos] * users, axis=0)
    hidden_ref[...] = hidden.astype(BF)
    saves[0].start()
    scale = lax.rsqrt(jnp.mean(hidden * hidden, axis=-1, keepdims=True) + EPS)
    normed = (hidden * scale * norm_gain_ref[...]).astype(BF)
    normed_ref[...] = normed
    saves[1].start()
    last = jnp.concatenate(
        [normed[(u + 1) * hist - PAD : (u + 1) * hist].astype(F32)[PAD - 1 :] for u in range(users)]
        + [jnp.zeros((PAD - users, width), F32)],
        axis=0,
    ).astype(BF)
    mask = head_mask(heads, width)
    copies[6].wait()
    query = dot(last, w_query[...]).astype(BF).astype(F32)
    copies[7].wait()
    qk = dot_nt(spread_heads(query, mask, users), w_key[...]).astype(BF)
    qk_ref[...] = qk
    saves[2].start()
    shape = (users * heads, span)
    own = iota(shape, 0) // heads == iota(shape, 1) // hist
    scores = jnp.where(own, dot_nt(qk, normed) * (1.0 / math.sqrt(HEAD_DIM)), -jnp.inf)
    raised = jnp.exp(scores - jnp.max(scores, axis=1, keepdims=True))
    weights = raised / jnp.sum(raised, axis=1, keepdims=True)
    weights_ref[...] = weights
    saves[3].start()
    mixes = dot(weights.astype(BF), normed).astype(BF)
    copies[8].wait()
    attended = join_heads(dot(mixes, w_value[...]), mask, users).astype(BF)
    copies[9].wait()
    hidden_last = jnp.concatenate(
        [hidden[(u + 1) * hist - 1 : (u + 1) * hist] for u in range(users)]
        + [jnp.zeros((PAD - users, width), F32)],
        axis=0,
    )
    mixed = hidden_last + dot(attended, w_out[...])
    mixed_ref[...] = mixed
    saves[4].start()
    scale = lax.rsqrt(jnp.mean(mixed * mixed, axis=-1, keepdims=True) + EPS)
    vectors_ref[...] = (mixed * scale * out_gain_ref[...]).astype(BF)
    for save in saves:
        save.wait()


def arrange_kernel(users, near, near_ref, vectors_ref, spread_ref):
    width = near_ref.shape[1]
    block = near * users
    part = spread_ref.shape[1] - width
    shape = (block, near * 8)
    at = iota(shape, 0)
    source = at // users * 8 + at % users
    items = dot(one_hot(iota(shape, 1) == source), near_ref[...])
    shape = (block, PAD)
    at = iota(shape, 0)
    mine = jnp.zeros((block, part), F32)
    for c in range(near):
        picks = one_hot((at % near == c) & (iota(shape, 1) == at // near))
        mine = mine + dot(picks, vectors_ref[:, c * part : (c + 1) * part])
    rows = jnp.concatenate([items, mine], axis=1).astype(BF)
    for i in range(spread_ref.shape[0] // block):
        spread_ref[i * block : (i + 1) * block, :] = rows


def users_of(near, width, ref):
    rows = ref.shape[0]
    group = rows // near
    line = iota((rows, rows), 0)
    picks = one_hot(iota((rows, rows), 1) == line % group * near + line // group)
    parts = dot(picks, ref[:, width:])
    return jnp.concatenate([parts[c * group : (c + 1) * group] for c in range(near)], axis=1).astype(BF)


def own_users_kernel(near, gathered_ref, own_ref):
    own_ref[...] = users_of(near, own_ref.shape[1], gathered_ref)


def softmax_kernel(
    users,
    near,
    scale,
    place_ref,
    gathered_ref,
    own_users_ref,
    swapped_ref,
    d_user_ref,
    d_part_ref,
    raised_ref,
):
    rows = gathered_ref.shape[0]
    width = d_user_ref.shape[1]
    items = near * users
    group = rows // near
    mine, plane = place_ref[0], place_ref[1]
    own, other = gathered_ref[:, 0:width], swapped_ref[:, 0:width]
    other_users = users_of(near, width, swapped_ref)
    group_users = jnp.concatenate([own_users_ref[...], other_users], axis=0)
    total = 2 * group

    shape = (rows, total)
    first = scale * dot_nt(own, group_users)
    second = scale * dot_nt(other, group_users)
    top = jnp.maximum(
        jnp.max(first, axis=0, keepdims=True), jnp.max(second, axis=0, keepdims=True)
    )
    raised = jnp.exp(first - top)
    raised_ref[...] = raised
    other_raised = jnp.exp(second - top)
    count = jnp.sum(raised, axis=0, keepdims=True) + jnp.sum(other_raised, axis=0, keepdims=True)
    share = 1.0 / count

    line = (items, total)
    target = (iota(line, 0) // users == plane) & (
        iota(line, 1) == mine * users + iota(line, 0) % users
    )
    near_raised = raised_ref[pl.ds(pl.multiple_of(mine * items, 8), items), :]
    slope = (near_raised * share - jnp.where(target, 1.0, 0.0)).astype(BF)
    apart = (near * 8, items)
    at = iota(apart, 0)
    apart = one_hot((at % 8 < users) & (iota(apart, 1) == at // 8 * users + at % 8))
    d_part = scale * dot(dot(apart, slope).astype(BF), group_users)

    who = iota(shape, 1) - mine * users
    target = (who >= 0) & (who < users) & (iota(shape, 0) == mine * items + plane * users + who)
    slope = (raised * share - jnp.where(target, 1.0, 0.0)).astype(BF)
    other_slope = (other_raised * share).astype(BF)
    self = (PAD, total)
    self = one_hot((iota(self, 0) < users) & (iota(self, 1) == mine * users + iota(self, 0)))
    d_user = dot(dot_nt(self, slope).astype(BF), own)
    d_user = d_user + dot(dot_nt(self, other_slope).astype(BF), other)
    d_user_ref[...] = (scale * d_user).astype(BF).astype(F32)
    each = jnp.sum(jnp.where(target, top + jnp.log(count) - first, 0.0), axis=0, keepdims=True)
    loss = jnp.sum(each, axis=1, keepdims=True)
    high = loss.astype(BF).astype(F32)
    middle = (loss - high).astype(BF).astype(F32)
    low = loss - high - middle
    shape = d_part.shape
    lanes = iota(shape, 1)
    loss = jnp.where(lanes == 0, high, jnp.where(lanes == 1, middle, jnp.where(lanes == 2, low, 0.0)))
    d_part_ref[...] = jnp.where(iota(shape, 0) % 8 == users, loss, d_part).astype(BF)


def norm_backward(values, cotangent, gain):
    inverse = lax.rsqrt(jnp.mean(values * values, axis=-1, keepdims=True) + EPS)
    pulled = cotangent * gain
    along = jnp.mean(pulled * values, axis=-1, keepdims=True)
    return inverse * pulled - values * (inverse * inverse * inverse * along)


def user_backward_kernel(users, d_user_ref, *refs):
    sources, refs = refs[:18], refs[18:]
    d_rows_ref, ahead, refs = refs[0], refs[1:7], refs[7:]
    targets, (d_normed, sems) = refs[:12], refs[12:]
    mixed_ref, out_gain_ref, w_out, w_value, normed_ref, weights_ref, qk_ref = targets[:7]
    w_key, w_query, hidden_ref, norm_gain_ref, in_proj = targets[7:]
    copies = copies_of(zip(sources, tuple(targets) + tuple(ahead)), sems)
    span, width = hidden_ref.shape
    hist = span // users
    heads = width // HEAD_DIM
    mask = head_mask(heads, width)
    for copy in copies[:3]:
        copy.wait()
    d_mixed = norm_backward(mixed_ref[...], d_user_ref[...], out_gain_ref[...])
    d_attended = dot_nt(d_mixed.astype(BF), w_out[...])
    copies[3].wait()
    d_mixes = dot_nt(spread_heads(d_attended, mask, users), w_value[...]).astype(BF)
    for copy in copies[4:7]:
        copy.wait()
    normed = normed_ref[...]
    weights = weights_ref[...]
    shape = weights.shape
    own = iota(shape, 0) // heads == iota(shape, 1) // hist
    d_weights = jnp.where(own, dot_nt(d_mixes, normed), 0.0)
    d_scores = weights * (d_weights - jnp.sum(weights * d_weights, axis=1, keepdims=True))
    d_scores = (d_scores * (1.0 / math.sqrt(HEAD_DIM))).astype(BF)
    d_normed[...] = dot_tn(
        jnp.concatenate([weights.astype(BF), d_scores], axis=0),
        jnp.concatenate([d_mixes, qk_ref[...]], axis=0),
    )
    d_qk = dot(d_scores, normed).astype(BF)
    copies[7].wait()
    d_query = join_heads(dot(d_qk, w_key[...]), mask, users).astype(BF)
    copies[8].wait()
    d_last = dot_nt(d_query, w_query[...])
    for u in range(users):
        at = slice((u + 1) * hist - 1, (u + 1) * hist)
        d_normed[at, :] = d_normed[at, :] + d_last[u : u + 1]
    copies[9].wait()
    copies[10].wait()
    d_normed[...] = norm_backward(hidden_ref[...].astype(F32), d_normed[...], norm_gain_ref[...])
    for u in range(users):
        at = slice((u + 1) * hist - 1, (u + 1) * hist)
        d_normed[at, :] = d_normed[at, :] + d_mixed[u : u + 1]
    copies[11].wait()
    d_rows_ref[...] = dot_nt(d_normed[...].astype(BF), in_proj[...]).astype(BF)
    for copy in copies[12:]:
        copy.wait()


def item_backward_kernel(users, core_ref, parts_ref, d_rows_ref, *refs):
    row_ref, gain, inner_ref, item_w2, item_w1, outer_ref, refs = *refs[:6], refs[6:]
    d_all_ref, send_ref, keep_ref, loss_ref = refs
    span, emb = d_rows_ref.shape
    wide = row_ref.shape[1]
    peers = parts_ref.shape[0]
    shape = (PAD, peers)
    sums = dot(one_hot(iota(shape, 1) % 8 == iota(shape, 0)), parts_ref[...])
    shape = (1, 128)
    loss = jnp.where(iota(shape, 1) < 3, sums[users : users + 1, 0:128], 0.0)
    loss_ref[...] = jnp.broadcast_to(jnp.sum(loss, axis=1, keepdims=True), loss_ref.shape)
    d_item = jnp.where(iota(sums.shape, 0) < users, sums, 0.0).astype(BF).astype(F32)
    d_all_ref[0:span, :] = d_rows_ref[...]
    half = keep_ref.shape[0]
    first = HOT_CODE + core_ref[0] * half
    picks = one_hot(iota((half, wide), 0) + first == row_ref[0:1, :])
    keep = dot(picks[:, 0:span], d_rows_ref[...])
    first = HOT_CODE + (1 - core_ref[0]) * half
    other_picks = one_hot(iota((half, wide), 0) + first == row_ref[0:1, :])
    send = dot(other_picks[:, 0:span], d_rows_ref[...])
    d_outer = norm_backward(outer_ref[...], d_item, gain[...])
    inner = inner_ref[...]
    gate = jax.nn.sigmoid(inner)
    d_inner = dot_nt(d_outer.astype(BF), item_w2[...]) * (gate * (1.0 + inner * (1.0 - gate)))
    d_items = dot_nt(d_inner.astype(BF), item_w1[...])
    d_items = jnp.concatenate([d_items, jnp.zeros((wide - span - PAD, emb), F32)], axis=0).astype(BF)
    d_all_ref[span:, :] = d_items
    keep_ref[...] = keep + dot(picks[:, span:], d_items)
    send_ref[...] = (send + dot(other_picks[:, span:], d_items)).astype(BF)


def rare_kernel(d_all_ref, row_ref, rare_ref):
    shape = (rare_ref.shape[0], row_ref.shape[1])
    rare_ref[...] = dot(one_hot(iota(shape, 0) == row_ref[0:1, :]), d_all_ref[...]).astype(BF)


def outgoing_kernel(rare_ref, keep_ref, got_ref, outgoing_ref):
    half = keep_ref.shape[0]
    slots = rare_ref.shape[0]
    shape = (slots, half)
    line = iota(shape, 0)
    owner, slot = line // SLOTS, line % SLOTS - HOT_SLOT
    held = owner // 8 * 2 + owner % 2 + slot * (half // 2)
    held = one_hot((slot >= 0) & (slot < 2) & (iota(shape, 1) == held))
    hot = dot(held, (keep_ref[...] + got_ref[...].astype(F32)).astype(BF))
    outgoing_ref[...] = (rare_ref[...].astype(F32) + hot).astype(BF)


def scatter_kernel(returned_ref, row_ref, loss_ref, part_ref, sums_ref):
    rows, emb = part_ref.shape
    slots = returned_ref.shape[0]
    returned = returned_ref[...]
    picks = one_hot(iota((rows, slots), 0) == row_ref[0:1, :])
    part_ref[...] = dot(picks, returned).astype(BF)
    shape = (PAD, slots)
    hot = dot(one_hot((iota(shape, 0) < 2) & (iota(shape, 1) % SLOTS == iota(shape, 0) + HOT_SLOT)), returned)
    halves = [hot[i : i + 1, j : j + 128] for i in range(2) for j in range(0, emb, 128)]
    block = jnp.concatenate(halves + [loss_ref[0 : 8 - len(halves), :]], axis=0)
    sums_ref[...] = jnp.concatenate([block] * (sums_ref.shape[0] // 8), axis=0)


def finish_kernel(count, core_ref, sums_ref, other_ref, hot_ref, loss_ref):
    rows, emb = hot_ref.shape
    groups = sums_ref.shape[0] // 8
    for core, ref in ((core_ref[0], sums_ref), (1 - core_ref[0], other_ref)):
        row = 0
        for i in range(2):
            at = pl.ds(pl.multiple_of(core * (rows // 2) + i * groups, groups), groups)
            for j in range(0, emb, 128):
                hot_ref[at, j : j + 128] = ref[pl.ds(row, groups, stride=8), :]
                row += 1
    at = pl.ds(row, groups, stride=8)
    losses = sums_ref[at, :] + other_ref[at, :]
    loss_ref[...] = jnp.sum(losses[:, 0:1], axis=0, keepdims=True) / count


def shards(
    history,
    item_ids,
    hot_table,
    rare_table,
    in_proj,
    pos_embed,
    norm_gain,
    w_query,
    w_key,
    w_value,
    w_out,
    out_gain,
    item_w1,
    item_w2,
    item_gain,
):
    users, hist = history.shape
    emb = hot_table.shape[1]
    rare_count = rare_table.shape[0]
    width = in_proj.shape[1]
    heads = width // HEAD_DIM
    scale = 4.0 / math.sqrt(width)
    owners = lax.axis_size(SHARD)
    towers = lax.axis_size("tower")
    near = lax.axis_size(LINE)
    total = users * towers * owners
    slots = owners * SLOTS
    span = users * hist
    wide = -(-(span + PAD) // 128) * 128
    swap = [(i, towers - 1 - i) for i in range(towers)]
    shape = jax.ShapeDtypeStruct
    sems = lambda n: pltpu.SemaphoreType.DMA((n,))
    vmem = lambda a: pltpu.VMEM(a.shape, a.dtype)
    hbm = lambda a: pltpu.HBM(a.shape, a.dtype)
    in_hbm = lambda a: pltpu.with_memory_space_constraint(a, pltpu.HBM)
    in_vmem = lambda a: pltpu.with_memory_space_constraint(a, pltpu.VMEM)
    like = lambda arrays: [pltpu.VMEM(a.shape, a.dtype) for a in arrays]
    exchange = functools.partial(lax.all_to_all, split_axis=0, concat_axis=0, tiled=True)

    places = (shape((8, wide), jnp.int32), shape((wide, 128), jnp.int32))
    loads = (history, item_ids.reshape(1, users), rare_table)
    request, known, row, column = pl.pallas_call(
        functools.partial(index_kernel, owners),
        out_shape=(
            shape((owners, 128), jnp.int32),
            pltpu.VMEM((rare_count, emb), BF),
            *map(vmem, places),
        ),
        in_specs=[HBM] * 3,
        out_specs=(VMEM,) * 4,
        scratch_shapes=like(loads) + [sems(3)],
        compiler_params=params(24),
        name="index",
    )(*map(in_hbm, loads))
    asked = exchange(request, SHARD)
    served, hot_ready, item_column, asked_row, row, column = pl.pallas_call(
        serve_kernel,
        out_shape=(
            shape((slots, emb), BF),
            pltpu.VMEM(hot_table.shape, BF),
            pltpu.VMEM((PAD, 128), jnp.int32),
            pltpu.HBM((8, slots), jnp.int32),
            *map(hbm, places),
        ),
        in_specs=[VMEM] * 4 + [HBM],
        out_specs=(VMEM, VMEM, VMEM, HBM, HBM, HBM),
        scratch_shapes=[
            pltpu.VMEM(hot_table.shape, F32),
            pltpu.VMEM((8, slots), jnp.int32),
            sems(4),
        ],
        compiler_params=params(24),
        name="serve",
    )(asked, *map(in_vmem, (known, row, column)), in_hbm(hot_table))
    fetched = exchange(served, SHARD)

    norm_gain, out_gain, item_gain = (g.reshape(1, width) for g in (norm_gain, out_gain, item_gain))
    item_kept = (shape((PAD, width), F32), shape((PAD, width), F32))
    item_vec, inner, outer = pl.pallas_call(
        functools.partial(item_forward_kernel, users),
        out_shape=(shape((near * 8, width), BF), *map(vmem, item_kept)),
        in_specs=[VMEM] * 4 + [HBM] * 2,
        out_specs=(VMEM,) * 3,
        scratch_shapes=like((item_w1, item_gain)) + [sems(2)],
        compiler_params=params(24),
        name="item_forward",
    )(
        fetched,
        *map(in_vmem, (hot_ready, item_column, item_w2)),
        *map(in_hbm, (item_w1, item_gain)),
    )
    near_items = exchange(item_vec, LINE)

    loads = (column, hot_table, pos_embed, norm_gain, out_gain)
    loads += (in_proj, w_query, w_key, w_value, w_out)
    kept = (
        shape((span, width), BF),
        shape((span, width), BF),
        shape((users * heads, width), BF),
        shape((users * heads, span), F32),
        shape((PAD, width), F32),
    )
    user_vec, hidden, normed, qk, weights, mixed, inner, outer = pl.pallas_call(
        functools.partial(user_forward_kernel, users),
        out_shape=(shape((PAD, width), BF), *map(hbm, kept + item_kept)),
        in_specs=[VMEM] * 3 + [HBM] * len(loads),
        out_specs=(VMEM,) + (HBM,) * (len(kept) + 2),
        scratch_shapes=like(loads + kept) + [sems(len(loads)), sems(len(kept) + 2)],
        compiler_params=params(40),
        name="user_forward",
    )(fetched, in_vmem(inner), in_vmem(outer), *map(in_hbm, loads))

    rows = owners * users
    spread = pl.pallas_call(
        functools.partial(arrange_kernel, users, near),
        out_shape=shape((rows, width + width // near), BF),
        in_specs=[VMEM, VMEM],
        out_specs=VMEM,
        compiler_params=params(24),
        name="arrange",
    )(near_items, user_vec)
    gathered = exchange(spread, ("x", "y"))
    swapped = lax.ppermute(gathered, "tower", swap)
    own_users = pl.pallas_call(
        functools.partial(own_users_kernel, near),
        out_shape=shape((rows // near, width), BF),
        in_specs=[VMEM],
        out_specs=VMEM,
        compiler_params=params(24),
        name="own_users",
    )(gathered)
    place = jnp.stack([lax.axis_index(("x", "y")), lax.axis_index(LINE)]).astype(jnp.int32)
    d_user, d_part = pl.pallas_call(
        functools.partial(softmax_kernel, users, near, scale),
        out_shape=(shape((PAD, width), F32), shape((near * 8, width), BF)),
        in_specs=[SMEM, VMEM, VMEM, VMEM],
        out_specs=(VMEM, VMEM),
        scratch_shapes=[pltpu.VMEM((rows, 2 * owners // near * users), F32)],
        compiler_params=params(32),
        name="softmax",
    )(place, gathered, own_users, swapped)
    parts = exchange(d_part, LINE)

    loads = (mixed, out_gain, w_out, w_value, normed, weights, qk)
    loads += (w_key, w_query, hidden, norm_gain, in_proj)
    ahead = (row, item_gain, inner, item_w2, item_w1, outer)
    d_rows, *item_ready = pl.pallas_call(
        functools.partial(user_backward_kernel, users),
        out_shape=(shape((span, emb), BF), *map(vmem, ahead)),
        in_specs=[VMEM] + [HBM] * 18,
        out_specs=(VMEM,) * 7,
        scratch_shapes=like(loads) + [pltpu.VMEM((span, width), F32), sems(18)],
        compiler_params=params(40),
        name="user_backward",
    )(d_user, *map(in_hbm, loads + ahead))
    core = lax.axis_index("tower").astype(jnp.int32).reshape(1)
    row_ready = item_ready[0]
    d_all, send, keep, loss = pl.pallas_call(
        functools.partial(item_backward_kernel, users),
        out_shape=(
            shape((wide, emb), BF),
            shape((owners // 2, emb), BF),
            shape((owners // 2, emb), F32),
            shape((8, 128), F32),
        ),
        in_specs=[SMEM] + [VMEM] * 8,
        out_specs=(VMEM,) * 4,
        compiler_params=params(32),
        name="item_backward",
    )(core, parts, d_rows, *map(in_vmem, item_ready))
    got = lax.ppermute(send, "tower", swap)
    rare = pl.pallas_call(
        rare_kernel,
        out_shape=shape((slots, emb), BF),
        in_specs=[VMEM, VMEM],
        out_specs=VMEM,
        compiler_params=params(32),
        name="rare",
    )(d_all, in_vmem(row_ready))
    outgoing = pl.pallas_call(
        outgoing_kernel,
        out_shape=shape((slots, emb), BF),
        in_specs=[VMEM] * 3,
        out_specs=VMEM,
        compiler_params=params(32),
        name="outgoing",
    )(rare, keep, got)

    returned = exchange(outgoing, SHARD)
    part, mine = pl.pallas_call(
        scatter_kernel,
        out_shape=(shape((rare_count, emb), BF), shape((owners // 4 * 8, 128), F32)),
        in_specs=[VMEM, VMEM, VMEM],
        out_specs=(VMEM, VMEM),
        compiler_params=params(24),
        name="scatter",
    )(returned, asked_row, loss)
    rare_grad = part.astype(F32) + lax.ppermute(part, "tower", swap).astype(F32)
    sums = exchange(mine, GROUP)
    other_sums = lax.ppermute(sums, "tower", swap)
    hot_total, loss_total = pl.pallas_call(
        functools.partial(finish_kernel, total * 2),
        out_shape=(shape((owners, emb), F32), shape((1, 1), F32)),
        in_specs=[SMEM, VMEM, VMEM],
        out_specs=(VMEM, VMEM),
        compiler_params=params(24),
        name="finish",
    )(core, sums, other_sums)
    return (hot_total, rare_grad, loss_total[0, 0])


def solution(mesh):
    sizes = (mesh.shape["tower"], 4, 4, mesh.shape["shard"] // 32, 2)
    mesh = Mesh(mesh.devices.reshape(sizes), ("tower",) + SHARD)
    return jax.shard_map(
        shards,
        mesh=mesh,
        in_specs=(
            P(("tower",) + SHARD, None),
            P(("tower",) + SHARD),
            P(),
            P(SHARD, None),
            P(),
            P(),
            P(),
            P(),
            P(),
            P(),
            P(),
            P(),
            P(),
            P(),
            P(),
        ),
        out_specs=(P(), P(SHARD, None), P()),
        check_vma=False,
    )
```
